128 devices in a mesh: section: 2 (over x_hi), dp: 8 (over z, core), fsdp: 8 (over x_lo, y).
Axes of the slice: x: 4 (x_hi: 2, x_lo: 2; x = x_hi * 2 + x_lo), y: 4, z: 4, core: 2. Of those that a mesh axis runs over, the one named last changes fastest.
Arguments:
- inputs: bfloat16 [2, 8, 1024, 960], P(None, 'dp', 'fsdp'), may hold values from -6 to 6
- positions: int32 [2, 8, 1024], P(None, 'dp', 'fsdp'), may hold values from 0 to 2046, as said below
- plan: int32 [8, 2], P('dp'), may hold values from 0 to 1, as said below
- attend_in: bfloat16 [2, 960, 1600], P('section', 'fsdp'), may hold values from -0.1875 to 0.1875
- attend_out: bfloat16 [2, 960, 960], P('section', 'fsdp'), may hold values from -1 to 1
- gate_up: bfloat16 [2, 960, 5120], P('section', 'fsdp'), may hold values from -0.1875 to 0.1875
- down_weight: bfloat16 [2, 2560, 960], P('section', 'fsdp'), may hold values from -0.25 to 0.25
- norm_gains: bfloat16 [2, 2, 960], P('section', None, 'fsdp'), may hold values from 0.25 to 1.75
- cotangent: bfloat16 [2, 8, 1024, 960], P(None, 'dp', 'fsdp'), may hold values from -6 to 6
Outputs:
- activations: bfloat16 [2, 2, 8, 1024, 960], P('section', None, 'dp', 'fsdp')
- input_grads: float32 [2, 2, 8, 1024, 960], P('section', None, 'dp', 'fsdp')
- attend_in_gradient: float32 [2, 960, 1600], P('section', 'fsdp')
- attend_out_gradient: float32 [2, 960, 960], P('section', 'fsdp')
- gate_up_gradient: float32 [2, 960, 5120], P('section', 'fsdp')
- down_gradient: float32 [2, 2560, 960], P('section', 'fsdp')
- gains_gradient: float32 [2, 2, 960], P('section', None, 'fsdp')
The draws below stay inside these ranges and needn't reach their ends.
Inputs may be any that keep to these rules, and one draw needn't show every extreme that they name: Along each sequence the positions start at 0, rise by 1 to 3 from token to token, and end at 2046. `plan`: each row is a permutation of 0 .. 1.
All inputs are finite; a program needn't handle non-finite values.
Results may differ from the reference program's by a relative error of at most 0.025.
Values may be sent and summed in bfloat16 or wider, within the bound.
A program may use at most 256 MiB of HBM per device.

```python
from functools import partial
import jax
import jax.numpy as jnp
from jax import lax

D = 960
QUERY_HEADS = 15
KEY_VALUE_HEADS = 5
HEAD_WIDTH = 64
FF = 2560
SEQUENCE_TOKENS = 1024
MB = 2
SECTIONS = 2
BATCH = 8
QUERY_PER_KEY = 3
QUERY_WIDTH_ALL = 960
KEY_WIDTH_TOTAL = 320
QKV = 1600


def draw_positions(key, part):
    key = jax.random.fold_in(key, 11)
    half = (SEQUENCE_TOKENS - 1) // 2
    base = jnp.concatenate([jnp.ones((half,), jnp.int32), -jnp.ones((half,), jnp.int32), jnp.zeros((SEQUENCE_TOKENS - 1 - 2 * half,), jnp.int32)])
    seq_keys = jax.random.split(key, MB * BATCH)
    mixed = jax.vmap(lambda seq_key: jax.random.permutation(seq_key, base))(seq_keys)
    steps = (2 + mixed).astype(jnp.int32)
    total = jnp.concatenate([jnp.zeros((MB * BATCH, 1), jnp.int32), jnp.cumsum(steps, axis=-1)], -1)
    return total.reshape(MB, BATCH, SEQUENCE_TOKENS).astype(jnp.int32)


def draw_plan(key, part):
    key = jax.random.fold_in(key, 23)
    lane_keys = jax.random.split(key, BATCH)
    return jax.vmap(lambda lane_key: jax.random.permutation(lane_key, MB))(lane_keys).astype(jnp.int32)


def level_of(own_key, extent, cuts, least, largest):
    factor_of, own = 1.0, jax.random.fold_in(own_key, 6)
    for axis_at, blocks in cuts:
        draws = jnp.exp(jax.random.uniform(jax.random.fold_in(own, axis_at), (blocks,), jnp.float32, least / len(cuts), largest / len(cuts)))
        factor_of = factor_of * jnp.repeat(draws, extent[axis_at] // blocks).reshape([-1 if axis == axis_at else 1 for axis in range(len(extent))])
    return factor_of


def bell_draw(stream_key, extent, deviation, bound, cuts=(), dtype=jnp.bfloat16):
    factor_of = level_of(stream_key, extent, cuts, -0.22, 0.18) if cuts else 1.0
    drawn = jax.random.normal(stream_key, extent, jnp.float32) * deviation * factor_of
    return jnp.minimum(jnp.maximum(drawn, -bound), bound).astype(dtype)


def setup_inputs(seed: int = 0) -> dict:
    keys = jax.random.split(jax.random.key(seed), 10)
    inputs = bell_draw(keys[0], (MB, BATCH, SEQUENCE_TOKENS, D), 1.0, 6.0, ((1, 8), (2, 8)))
    positions = draw_positions(jax.random.fold_in(keys[9], 71), 0)
    plan = draw_plan(jax.random.fold_in(keys[9], 71), 0)
    attend_in = bell_draw(keys[3], (SECTIONS, D, QKV), D ** -0.5, 0.1875, ((0, 2), (1, 8)))
    attend_out = bell_draw(keys[4], (SECTIONS, QUERY_WIDTH_ALL, D), (QUERY_WIDTH_ALL // 32) ** -0.5, 1.0, ((0, 2), (1, 8)))
    gate_up = bell_draw(keys[5], (SECTIONS, D, 2 * FF), D ** -0.5, 0.1875, ((0, 2), (1, 8)))
    down_weight = bell_draw(keys[6], (SECTIONS, FF, D), (FF // 4) ** -0.5, 0.25, ((0, 2), (1, 8)))
    norm_gains = jnp.clip(1.0 + 0.15 * jax.random.normal(keys[7], (SECTIONS, 2, D), jnp.float32), 0.25, 1.75).astype(jnp.bfloat16)
    cotangent = bell_draw(keys[8], (MB, BATCH, SEQUENCE_TOKENS, D), 1.0, 6.0, ((1, 8), (2, 8)))
    return {"inputs": inputs, "positions": positions, "plan": plan, "attend_in": attend_in, "attend_out": attend_out, "gate_up": gate_up, "down_weight": down_weight, "norm_gains": norm_gains, "cotangent": cotangent}


EPSILON = 1e-05
BASE = 10000.0

@jax.custom_vjp
def low(v):
    return lax.optimization_barrier(v.astype(jnp.bfloat16)).astype(jnp.float32)

@jax.custom_vjp
def low_back(v):
    return v

def low_keep(v):
    return (low(v), None)

def low_pass(kept, grad):
    return (grad,)

def back_keep(v):
    return (v, None)

def back_low(kept, grad):
    return (low(grad),)
low.defvjp(low_keep, low_pass)
low_back.defvjp(back_keep, back_low)

def highest_dot(left, right):
    return jnp.dot(left, right, precision=lax.Precision.HIGHEST, preferred_element_type=jnp.float32)

def rotary_tables(places):
    half = HEAD_WIDTH // 2
    frequency = BASE ** (-(jnp.arange(half).astype(jnp.float32) * (2.0 / HEAD_WIDTH)))
    angle = places.astype(jnp.float32)[:, None] * frequency[None, :]
    cosine_table = jnp.cos(angle)
    sine_table = jnp.sin(angle)
    return (jnp.concatenate([cosine_table, cosine_table], -1), jnp.concatenate([sine_table, sine_table], -1))

def apply_rotation(values, cosine_table, sine_table):
    half = values.shape[-1] // 2
    turned = jnp.concatenate([-values[..., half:], values[..., :half]], -1)
    return values * cosine_table[:, None, :] + turned * sine_table[:, None, :]

def normed(values, gain):
    return values * lax.rsqrt(lax.optimization_barrier(jnp.mean(values * values, -1, keepdims=True)) + EPSILON) * gain

def layer(params, values, places):
    attend_in, attend_out, gate_up, down_weight, gains = params
    first_norm = low(normed(values, gains[0]))
    projected_output = low_back(highest_dot(first_norm, attend_in))
    cosine_table, sine_table = rotary_tables(places)
    query_matrix = projected_output[:, :QUERY_WIDTH_ALL].reshape(SEQUENCE_TOKENS, QUERY_HEADS, HEAD_WIDTH)
    key_rows = projected_output[:, QUERY_WIDTH_ALL:QUERY_WIDTH_ALL + KEY_WIDTH_TOTAL].reshape(SEQUENCE_TOKENS, KEY_VALUE_HEADS, HEAD_WIDTH)
    value_rows = projected_output[:, QUERY_WIDTH_ALL + KEY_WIDTH_TOTAL:].reshape(SEQUENCE_TOKENS, KEY_VALUE_HEADS, HEAD_WIDTH)
    query_matrix = low(apply_rotation(query_matrix, cosine_table, sine_table)).reshape(SEQUENCE_TOKENS, KEY_VALUE_HEADS, QUERY_PER_KEY, HEAD_WIDTH)
    key_rows = low(apply_rotation(key_rows, cosine_table, sine_table))
    value_rows = low(value_rows)
    scores = jnp.einsum('tgqd,sgd->gqts', query_matrix, key_rows, precision=lax.Precision.HIGHEST) * HEAD_WIDTH ** (-0.5)
    scores = low_back(scores)
    causal = jnp.arange(SEQUENCE_TOKENS)[:, None] >= jnp.arange(SEQUENCE_TOKENS)[None, :]
    scores = jnp.where(causal[None, None], scores, -1e+30)
    total = jax.scipy.special.logsumexp(scores, axis=-1, keepdims=True)
    probs = low(jnp.exp(scores - total))
    mixed = jnp.einsum('gqts,sgd->tgqd', probs, value_rows, precision=lax.Precision.HIGHEST)
    mixed = low(low_back(mixed)).reshape(SEQUENCE_TOKENS, QUERY_WIDTH_ALL)
    hidden = values + low_back(highest_dot(mixed, attend_out))
    second_norm = low(normed(hidden, gains[1]))
    gated = low_back(highest_dot(second_norm, gate_up))
    act = low(jax.nn.silu(gated[:, :FF]) * gated[:, FF:])
    return hidden + low_back(highest_dot(act, down_weight))

def run_section(params, data, places, first, last):

    def one(item):
        return jax.checkpoint(layer)(params, item[0], item[1])
    entry = data if first else low_back(data)
    result = lax.map(one, (entry, places))
    return result if last else low(result)

def reference(inputs, positions, plan, attend_in, attend_out, gate_up, down_weight, norm_gains, cotangent):
    lanes = jnp.arange(BATCH)[None, :]
    slots = jnp.transpose(plan)
    data = inputs[slots, lanes].astype(jnp.float32).reshape(MB * BATCH, SEQUENCE_TOKENS, D)
    places = positions[slots, lanes].reshape(MB * BATCH, SEQUENCE_TOKENS)
    outputs = []
    pulls = []
    for section in range(SECTIONS):
        params = (attend_in[section].astype(jnp.float32), attend_out[section].astype(jnp.float32), gate_up[section].astype(jnp.float32), down_weight[section].astype(jnp.float32), norm_gains[section].astype(jnp.float32))
        section_fn = partial(run_section, places=places, first=section == 0, last=section == SECTIONS - 1)
        data, pull = jax.vjp(section_fn, params, data)
        outputs.append(data.astype(jnp.bfloat16).reshape(MB, BATCH, SEQUENCE_TOKENS, D))
        pulls.append(pull)
    upstream = cotangent.astype(jnp.float32).reshape(MB * BATCH, SEQUENCE_TOKENS, D)
    input_list = [None] * SECTIONS
    weight_list = [None] * SECTIONS
    for section in range(SECTIONS - 1, -1, -1):
        weight_grads, upstream = pulls[section](upstream)
        by_slot = upstream.reshape(MB, BATCH, SEQUENCE_TOKENS, D)
        input_list[section] = jnp.zeros((MB, BATCH, SEQUENCE_TOKENS, D), jnp.float32).at[slots, lanes].set(by_slot)
        weight_list[section] = weight_grads
    stacked = [jnp.stack([weight_list[s][i] for s in range(SECTIONS)]) for i in range(5)]
    return (jnp.stack(outputs), jnp.stack(input_list), stacked[0], stacked[1], stacked[2], stacked[3], stacked[4])
```

```python
import functools

import jax
import jax.numpy as jnp
from jax import lax
from jax.experimental import pallas as pl
from jax.experimental.pallas import tpu as pltpu
from jax.sharding import PartitionSpec as P

D = 960
QUERY_HEADS = 15
KEY_VALUE_HEADS = 5
HEAD_WIDTH = 64
FF = 2560
QUERY_WIDTH = QUERY_HEADS * HEAD_WIDTH
KEY_WIDTH = KEY_VALUE_HEADS * HEAD_WIDTH
QKV = QUERY_WIDTH + 2 * KEY_WIDTH
SHARDS = 8
ROWS = D // SHARDS
PADDED = 128
DOWN_COLUMNS = 1024

EPSILON = 1e-05
BASE = 10000.0

MESH = pl.DeviceIdType.MESH
ANY = pl.BlockSpec(memory_space=pl.ANY)

GATE_UP = (PADDED, 2 * FF, "columns")
DOWN = (FF // SHARDS, DOWN_COLUMNS, "columns")
ATTEND_IN = (PADDED, QKV, "rows")
ATTEND_OUT = (PADDED, D, "rows")
SHAPES = (GATE_UP, DOWN, ATTEND_IN, ATTEND_OUT)


def half_shape(shape):
    rows, columns, kind = shape
    return (rows // 2, columns) if kind == "rows" else (rows, columns // 2)


def half_view(shape, core, start, count):
    rows, columns, kind = shape
    if kind == "rows":
        first = pl.multiple_of(core * (rows // 2) + start, 16)
        return (pl.ds(first, count), slice(None))
    first = pl.multiple_of(core * (columns // 2), 128)
    return (pl.ds(pl.multiple_of(start, 16), count), pl.ds(first, columns // 2))


def places():
    dp = lax.axis_index("dp")
    fsdp = lax.axis_index("fsdp")
    return dp // 2, dp % 2, fsdp // 4, fsdp % 4


def peer_ids():
    z, core, x, y = places()
    return {
        "X": {"fsdp": (1 - x) * 4 + y},
        "Yp": {"fsdp": x * 4 + (y + 1) % 4},
        "Ym": {"fsdp": x * 4 + (y + 3) % 4},
        "C": {"dp": z * 2 + 1 - core},
        "Z1": {"dp": ((z + 1) % 4) * 2 + core},
        "Z2": {"dp": ((z + 2) % 4) * 2 + core},
        "Z3": {"dp": ((z + 3) % 4) * 2 + core},
    }


def greet(ids, names):
    barrier = pltpu.get_barrier_semaphore()
    for name in names:
        pl.semaphore_signal(barrier, inc=1, device_id=ids[name], device_id_type=MESH)
    pl.semaphore_wait(barrier, len(names))


GATHER = (
    ("X", 0, 0, "f"),
    ("Yp", 0, 0, "f"),
    ("Ym", 0, 0, "f"),
    ("Ym", 0, 1, 0),
    ("X", 0, 1, 0),
    ("Yp", 0, 3, 1),
    ("X", 0, 3, 0),
    ("Yp", 1, 0, 1),
    ("Ym", 1, 0, 1),
    ("Ym", 1, 1, 0),
    ("Yp", 1, 3, 1),
)
GATHER_NEXT = {1: (5, 6), 2: (3, 4), 0: (7, 8), 4: (9,), 7: (10,)}
GATHER_ORDER = (1, 2, 0, 4, 7, 3, 5, 6, 8, 9, 10)


def seen_by_receiver(peer, column, step):
    if peer == "X":
        return 1 - column, step
    if peer == "Yp":
        return column, (step + 3) % 4
    if peer == "Ym":
        return column, (step + 1) % 4
    return column, step


def part_rows(shape, part):
    rows = half_shape(shape)[0]
    return (0, rows) if part == "f" else (part * (rows // 2), rows // 2)


def gather_kernel(*refs):
    count = len(SHAPES)
    shards, outs = refs[:count], refs[count : 2 * count]
    local_sem, send_sem, recv_sem = refs[2 * count :]
    z, core, x, y = places()
    ids = peer_ids()
    mine = x * 4 + y

    def owner(column, step):
        return ((x + column) % 2) * 4 + (y + step) % 4

    def view(array, column, step, part, which):
        start, rows = part_rows(SHAPES[array], part)
        return outs[array].at[(owner(column, step),) + half_view(SHAPES[array], which, start, rows)]

    def copy(array, edge):
        peer, column, step, part = GATHER[edge % 11]
        if edge < 11:
            target = view(array, column, step, part, core)
            source = target
            if (column, step) == (0, 0):
                start, rows = part_rows(SHAPES[array], part)
                source = shards[array].at[half_view(SHAPES[array], core, start, rows)]
        else:
            peer, (column, step) = "C", seen_by_receiver(peer, column, step)
            source = target = view(array, column, step, part, core)
        return pltpu.make_async_remote_copy(
            src_ref=source,
            dst_ref=target,
            send_sem=send_sem.at[array, edge],
            recv_sem=recv_sem.at[array, edge],
            device_id=ids[peer],
            device_id_type=MESH,
        )

    def wait_for(array, edge):
        peer, column, step, part = GATHER[edge % 11]
        column, step = seen_by_receiver(peer, column, step)
        which = core if edge < 11 else 1 - core
        landed = view(array, column, step, part, which)
        pltpu.make_async_remote_copy(
            src_ref=landed,
            dst_ref=landed,
            send_sem=send_sem.at[array, edge],
            recv_sem=recv_sem.at[array, edge],
            device_id=ids["C"],
            device_id_type=MESH,
        ).wait_recv()

    greet(ids, ("X", "Yp", "Ym", "C"))
    own = [
        pltpu.make_async_copy(shards[array], outs[array].at[mine], local_sem.at[array])
        for array in range(count)
    ]
    for array in range(count):
        for edge in (0, 1, 2):
            copy(array, edge).start()
        own[array].start()
    for array in range(count):
        for edge in GATHER_ORDER:
            wait_for(array, edge)
            for later in GATHER_NEXT.get(edge, ()):
                copy(array, later).start()
            copy(array, 11 + edge).start()
    for array in range(count):
        for edge in range(11):
            wait_for(array, 11 + edge)
        for edge in range(22):
            copy(array, edge).wait_send()
        own[array].wait()


def gather_weights(shards):
    count = len(SHAPES)
    return pl.pallas_call(
        gather_kernel,
        name="gather_weights",
        out_shape=[
            jax.ShapeDtypeStruct((SHARDS, rows, columns), jnp.bfloat16)
            for rows, columns, _ in SHAPES
        ],
        in_specs=[ANY] * count,
        out_specs=[ANY] * count,
        scratch_shapes=[
            pltpu.SemaphoreType.DMA((count,)),
            pltpu.SemaphoreType.DMA((count, 22)),
            pltpu.SemaphoreType.DMA((count, 22)),
        ],
        compiler_params=pltpu.CompilerParams(collective_id=0, has_side_effects=True),
    )(*shards)


REDUCE = (
    ("Yp", 0, 2, 0, ()),
    ("Ym", 0, 2, 1, ()),
    ("Yp", 1, 2, 0, ()),
    ("Ym", 1, 2, 1, ()),
    ("X", 1, 3, 0, ()),
    ("Yp", 1, 1, 1, ()),
    ("X", 1, 1, 0, (2,)),
    ("Ym", 1, 3, 1, (3,)),
    ("Yp", 0, 1, "f", (0, 6)),
    ("Ym", 0, 3, "f", (1, 4)),
    ("X", 1, 0, "f", (5, 7)),
)
REDUCE_STAGES = ((0, 1, 2, 3, 4, 5), (6, 7), (8, 9, 10))


def reduce_kernel(*refs):
    count = len(SHAPES)
    terms, outs = refs[:count], refs[count : 2 * count]
    scratch = refs[2 * count :]
    totals = scratch[:count]
    wholes = scratch[count : 2 * count]
    parts = scratch[2 * count : 3 * count]
    quarters = scratch[3 * count : 4 * count]
    local_sem, send_sem, recv_sem = scratch[4 * count :]
    z, core, x, y = places()
    ids = peer_ids()
    mine = x * 4 + y

    def owner(column, step):
        return ((x + column) % 2) * 4 + (y + step) % 4

    def piece(array, edge):
        _, column, step, part, _ = REDUCE[edge]
        start, rows = part_rows(SHAPES[array], part)
        return totals[array].at[owner(column, step), pl.ds(start, rows), :]

    def slot(array, edge):
        return parts[array].at[edge] if edge < 8 else wholes[array].at[edge - 8]

    def add(array, into, start, rows, source):
        @pl.loop(0, rows // 16)
        def _(index):
            offset = pl.multiple_of(index * 16, 16)
            at = pl.ds(pl.multiple_of(start + offset, 16), 16)
            totals[array][into, at, :] = (
                totals[array][into, at, :].astype(jnp.float32)
                + source[pl.ds(offset, 16), :].astype(jnp.float32)
            ).astype(jnp.bfloat16)

    def quarter(array, index):
        rows = half_shape(SHAPES[array])[0] // 4
        return pl.multiple_of(index * rows, 16), rows

    def out_view(array, index, which):
        start, rows = quarter(array, index)
        return outs[array].at[half_view(SHAPES[array], which, start, rows)]

    def copy(array, edge):
        if edge < 11:
            peer, source, target = REDUCE[edge][0], piece(array, edge), slot(array, edge)
        elif edge < 14:
            step = edge - 10
            peer = f"Z{step}"
            start, rows = quarter(array, (z + step) % 4)
            source = totals[array].at[mine, pl.ds(start, rows), :]
            target = quarters[array].at[step - 1]
        elif edge < 17:
            peer = f"Z{edge - 13}"
            start, rows = quarter(array, z)
            source = totals[array].at[mine, pl.ds(start, rows), :]
            target = out_view(array, z, core)
        else:
            peer = "C"
            at = (z + edge - 17) % 4
            source = target = out_view(array, at, core)
            if edge == 17:
                start, rows = quarter(array, z)
                source = totals[array].at[mine, pl.ds(start, rows), :]
        return pltpu.make_async_remote_copy(
            src_ref=source,
            dst_ref=target,
            send_sem=send_sem.at[array, edge],
            recv_sem=recv_sem.at[array, edge],
            device_id=ids[peer],
            device_id_type=MESH,
        )

    def wait_for(array, edge):
        if edge < 11:
            landed = slot(array, edge)
        elif edge < 14:
            landed = quarters[array].at[edge - 11]
        elif edge < 17:
            landed = out_view(array, (z + 4 - (edge - 13)) % 4, core)
        else:
            landed = out_view(array, (z + edge - 17) % 4, 1 - core)
        pltpu.make_async_remote_copy(
            src_ref=landed,
            dst_ref=landed,
            send_sem=send_sem.at[array, edge],
            recv_sem=recv_sem.at[array, edge],
            device_id=ids["C"],
            device_id_type=MESH,
        ).wait_recv()

    def receive(array, edge):
        wait_for(array, edge)
        peer, column, step, part, _ = REDUCE[edge]
        column, step = seen_by_receiver(peer, column, step)
        start, rows = part_rows(SHAPES[array], part)
        add(array, owner(column, step), start, rows, slot(array, edge))

    loads = [
        pltpu.make_async_copy(terms[array], totals[array], local_sem.at[array])
        for array in range(count)
    ]
    for load in loads:
        load.start()
    greet(ids, ("X", "Yp", "Ym", "C", "Z1", "Z2", "Z3"))
    for stage in REDUCE_STAGES:
        for array in range(count):
            if stage == REDUCE_STAGES[0]:
                loads[array].wait()
            for edge in stage:
                for earlier in REDUCE[edge][4]:
                    receive(array, earlier)
                copy(array, edge).start()
    for array in range(count):
        for edge in (8, 9, 10):
            receive(array, edge)
        for edge in (11, 12, 13):
            copy(array, edge).start()
    stores = []
    for array in range(count):
        start, rows = quarter(array, z)
        for edge in (11, 12, 13):
            wait_for(array, edge)
            add(array, mine, start, rows, quarters[array].at[edge - 11])
        for edge in (14, 15, 16, 17):
            copy(array, edge).start()
        store = pltpu.make_async_copy(
            totals[array].at[mine, pl.ds(start, rows), :],
            out_view(array, z, core),
            local_sem.at[array],
        )
        store.start()
        stores.append(store)
    for array in range(count):
        for edge in (14, 15, 16):
            wait_for(array, edge)
            copy(array, 17 + (17 - edge)).start()
    for array in range(count):
        for edge in range(17, 21):
            wait_for(array, edge)
        for edge in range(21):
            copy(array, edge).wait_send()
        stores[array].wait()


def reduce_gradients(terms):
    count = len(SHAPES)
    halves = [half_shape(shape) for shape in SHAPES]
    return pl.pallas_call(
        reduce_kernel,
        name="reduce_gradients",
        out_shape=[
            jax.ShapeDtypeStruct((rows, columns), jnp.bfloat16) for rows, columns, _ in SHAPES
        ],
        in_specs=[ANY] * count,
        out_specs=[ANY] * count,
        scratch_shapes=[pltpu.VMEM((SHARDS,) + half, jnp.bfloat16) for half in halves]
        + [pltpu.VMEM((3,) + half, jnp.bfloat16) for half in halves]
        + [pltpu.VMEM((8, half[0] // 2, half[1]), jnp.bfloat16) for half in halves]
        + [pltpu.VMEM((3, half[0] // 4, half[1]), jnp.bfloat16) for half in halves]
        + [
            pltpu.SemaphoreType.DMA((count,)),
            pltpu.SemaphoreType.DMA((count, 21)),
            pltpu.SemaphoreType.DMA((count, 21)),
        ],
        compiler_params=pltpu.CompilerParams(
            collective_id=1, has_side_effects=True, vmem_limit_bytes=48 * 2**20
        ),
    )(*terms)


def rotary_tables(positions):
    half = HEAD_WIDTH // 2
    frequency = BASE ** (-(jnp.arange(half).astype(jnp.float32) * (2.0 / HEAD_WIDTH)))
    angle = positions.astype(jnp.float32)[..., None] * frequency
    cosine_table = jnp.cos(angle)
    sine_table = jnp.sin(angle)
    return (
        jnp.concatenate([cosine_table, cosine_table], -1)[..., None, :],
        jnp.concatenate([sine_table, sine_table], -1)[..., None, :],
    )


def apply_rotation(values, cosine_table, sine_table):
    half = values.shape[-1] // 2
    turned = jnp.concatenate([-values[..., half:], values[..., :half]], -1)
    return values * cosine_table + turned * sine_table


def reverse_rotation(values, cosine_table, sine_table):
    half = values.shape[-1] // 2
    shifted = values * sine_table
    turned = jnp.concatenate([-shifted[..., half:], shifted[..., :half]], -1)
    return values * cosine_table - turned


def normed(values, gain):
    return values * lax.rsqrt(jnp.mean(values * values, -1, keepdims=True) + EPSILON) * gain


def norm_backward(values, gain, upstream):
    row_scale = lax.rsqrt(jnp.mean(values * values, -1, keepdims=True) + EPSILON)
    unit = values * row_scale
    gain_slope = jnp.sum(upstream * unit, 0)
    inner = upstream * gain
    return (row_scale * (inner - unit * jnp.mean(inner * unit, -1, keepdims=True)), gain_slope)


def pad_shards(values):
    split = values.reshape(values.shape[0], SHARDS, ROWS)
    return jnp.pad(split, ((0, 0), (0, 0), (0, PADDED - ROWS))).reshape(values.shape[0], -1)


def unpad_shards(values):
    split = values.reshape(values.shape[0], SHARDS, PADDED)
    return split[:, :, :ROWS].reshape(values.shape[0], D)


def heads(values):
    return values.reshape(values.shape[:-1] + (-1, HEAD_WIDTH))


def masked_scores(query_matrix, key_value_pair, shard_index):
    batches, local_count = query_matrix.shape[:2]
    token_length = key_value_pair.shape[1]
    grouped_heads = query_matrix.reshape(
        batches, local_count, KEY_VALUE_HEADS, QUERY_HEADS // KEY_VALUE_HEADS, HEAD_WIDTH
    )
    key_rows = heads(key_value_pair[..., :KEY_WIDTH])
    scores = jnp.einsum(
        "btgqd,bsgd->bgqts", grouped_heads, key_rows, preferred_element_type=jnp.float32
    ) * HEAD_WIDTH ** (-0.5)
    query_rows = shard_index * local_count + jnp.arange(local_count)
    causal = query_rows[:, None] >= jnp.arange(token_length)[None, :]
    return jnp.where(causal, scores, -1e30)


def forward_layer(layer_in, tables, weights, shard_index):
    attend_in, attend_out, gate_up, down_weight, gains = weights
    batches, local_count = layer_in.shape[:2]
    rows = batches * local_count
    values = layer_in.reshape(rows, D).astype(jnp.float32)
    first_norm = pad_shards(normed(values, gains[0]).astype(jnp.bfloat16))
    projected = jnp.dot(first_norm, attend_in, preferred_element_type=jnp.float32)
    projected = projected.reshape(batches, local_count, QKV)
    rotated = apply_rotation(heads(projected[..., : QUERY_WIDTH + KEY_WIDTH]), *tables)
    rotated = rotated.astype(jnp.bfloat16).reshape(batches, local_count, -1)
    query_matrix = rotated[..., :QUERY_WIDTH]
    own_pair = jnp.concatenate(
        [rotated[..., QUERY_WIDTH:], projected[..., QUERY_WIDTH + KEY_WIDTH :].astype(jnp.bfloat16)],
        -1,
    )
    key_value_pair = lax.all_gather(own_pair, "fsdp", axis=1, tiled=True)
    scores = masked_scores(query_matrix, key_value_pair, shard_index)
    highest = jnp.max(scores, -1)
    totals = highest + jnp.log(jnp.sum(jnp.exp(scores - highest[..., None]), -1))
    probs = jnp.exp(scores - totals[..., None]).astype(jnp.bfloat16)
    mixed = jnp.einsum(
        "bgqts,bsgd->btgqd",
        probs,
        heads(key_value_pair[..., KEY_WIDTH:]),
        preferred_element_type=jnp.float32,
    )
    mixed = pad_shards(mixed.astype(jnp.bfloat16).reshape(rows, QUERY_WIDTH))
    hidden = values + jnp.dot(mixed, attend_out, preferred_element_type=jnp.float32)
    second_norm = pad_shards(normed(hidden, gains[1]).astype(jnp.bfloat16))
    gated = jnp.dot(second_norm, gate_up, preferred_element_type=jnp.float32)
    act = (jax.nn.silu(gated[:, :FF]) * gated[:, FF:]).astype(jnp.bfloat16)
    result = hidden + jnp.dot(act, down_weight, preferred_element_type=jnp.float32)[:, :D]
    kept = (
        values,
        first_norm,
        query_matrix,
        key_value_pair,
        totals,
        mixed,
        hidden,
        second_norm,
        gated,
        act,
    )
    return (result.astype(jnp.bfloat16).reshape(layer_in.shape), kept)


def backward_layer(upstream, kept, tables, weights, shard_index):
    attend_in, attend_out, gate_up, down_weight, gains = weights
    (
        values,
        first_norm,
        query_matrix,
        key_value_pair,
        totals,
        mixed,
        hidden,
        second_norm,
        gated,
        act,
    ) = kept
    batches, local_count = upstream.shape[:2]
    rows = batches * local_count
    token_length = key_value_pair.shape[1]
    scale = HEAD_WIDTH ** (-0.5)
    upstream = upstream.reshape(rows, D)
    down_in = jnp.pad(upstream, ((0, 0), (0, DOWN_COLUMNS - D)))
    upstream = upstream.astype(jnp.float32)
    act_slope = jnp.einsum("td,fd->tf", down_in, down_weight, preferred_element_type=jnp.float32)
    gate_part = gated[:, :FF]
    up_part = gated[:, FF:]
    sigma = jax.nn.sigmoid(gate_part)
    gate_slope = act_slope * up_part * sigma * (1.0 + gate_part * (1.0 - sigma))
    up_slope = act_slope * gate_part * sigma
    gated_slope = jnp.concatenate([gate_slope, up_slope], 1).astype(jnp.bfloat16)
    second_slope = unpad_shards(
        jnp.einsum("tf,df->td", gated_slope, gate_up, preferred_element_type=jnp.float32)
    )
    hidden_part, second_gain = norm_backward(hidden, gains[1], second_slope)
    hidden_slope = upstream + hidden_part
    branch_slope = hidden_slope.astype(jnp.bfloat16)
    mixed_gradient = unpad_shards(
        jnp.einsum(
            "td,qd->tq", branch_slope, attend_out, preferred_element_type=jnp.float32
        ).astype(jnp.bfloat16)
    )
    mixed_gradient = mixed_gradient.reshape(
        batches, local_count, KEY_VALUE_HEADS, QUERY_HEADS // KEY_VALUE_HEADS, HEAD_WIDTH
    )
    scores = masked_scores(query_matrix, key_value_pair, shard_index)
    probs = jnp.exp(scores - totals[..., None])
    probs_low = probs.astype(jnp.bfloat16)
    complete_keys = heads(key_value_pair[..., :KEY_WIDTH])
    complete_values = heads(key_value_pair[..., KEY_WIDTH:])
    prob_slope = jnp.einsum(
        "btgqd,bsgd->bgqts", mixed_gradient, complete_values, preferred_element_type=jnp.float32
    )
    score_slope = probs * (prob_slope - jnp.sum(probs * prob_slope, -1, keepdims=True))
    score_slope = score_slope.astype(jnp.bfloat16)
    query_slope = (
        jnp.einsum(
            "bgqts,bsgd->btgqd", score_slope, complete_keys, preferred_element_type=jnp.float32
        )
        * scale
    )
    grouped_heads = query_matrix.reshape(mixed_gradient.shape)
    key_part = (
        jnp.einsum(
            "bgqts,btgqd->bsgd", score_slope, grouped_heads, preferred_element_type=jnp.float32
        )
        * scale
    )
    val_part = jnp.einsum(
        "bgqts,btgqd->bsgd", probs_low, mixed_gradient, preferred_element_type=jnp.float32
    )
    owned_part = lax.psum_scatter(
        jnp.concatenate(
            [
                key_part.reshape(batches, token_length, KEY_WIDTH),
                val_part.reshape(batches, token_length, KEY_WIDTH),
            ],
            -1,
        ).astype(jnp.bfloat16),
        "fsdp",
        scatter_dimension=1,
        tiled=True,
    ).astype(jnp.float32)
    query_raw = reverse_rotation(
        query_slope.reshape(batches, local_count, QUERY_HEADS, HEAD_WIDTH), *tables
    ).reshape(rows, QUERY_WIDTH)
    unrotated_key = reverse_rotation(heads(owned_part[..., :KEY_WIDTH]), *tables)
    projected_slope = jnp.concatenate(
        [
            query_raw,
            unrotated_key.reshape(rows, KEY_WIDTH),
            owned_part[..., KEY_WIDTH:].reshape(rows, KEY_WIDTH),
        ],
        1,
    ).astype(jnp.bfloat16)
    first_slope = unpad_shards(
        jnp.einsum("tf,df->td", projected_slope, attend_in, preferred_element_type=jnp.float32)
    )
    input_part, first_gain = norm_backward(values, gains[0], first_slope)
    input_slope = hidden_slope + input_part
    slopes = (projected_slope, branch_slope, gated_slope, down_in)
    return (
        input_slope.reshape(batches, local_count, D),
        slopes,
        jnp.stack([first_gain, second_gain]),
    )


def passed_along(value, steps):
    return lax.ppermute(value, "section", [(0, 1)] if steps > 0 else [(1, 0)])


def with_other_core(value):
    size = lax.axis_size("dp")
    other = lax.ppermute(value, "dp", [(index, index ^ 1) for index in range(size)])
    return other


def weight_terms(kept, slopes, gain_slopes):
    core = lax.axis_index("dp") % 2
    first_norm, mixed, second_norm, act = (kept[1], kept[5], kept[7], kept[9])
    projected_slope, branch_slope, gated_slope, down_in = slopes
    tokens = act.shape[0]

    def halved(values, axis):
        extent = values.shape[axis] // 2
        keep = lax.dynamic_slice_in_dim(values, core * extent, extent, axis)
        send = lax.dynamic_slice_in_dim(values, (1 - core) * extent, extent, axis)
        return jnp.concatenate([keep, with_other_core(send)], 0)

    def whole(values):
        return jnp.concatenate([values, with_other_core(values)], 0)

    def term(left, right):
        split = left.reshape(2 * tokens, SHARDS, -1)
        return jnp.einsum(
            "tkr,tn->krn", split, right, preferred_element_type=jnp.float32
        ).astype(jnp.bfloat16)

    in_rows = halved(first_norm.reshape(tokens, SHARDS, PADDED), 2)
    out_rows = halved(mixed.reshape(tokens, SHARDS, PADDED), 2)
    in_term = term(in_rows, whole(projected_slope))
    gains = (gain_slopes + with_other_core(gain_slopes)).reshape(2, SHARDS, ROWS).swapaxes(0, 1)
    spare = PADDED // 2 - (PADDED - ROWS)
    in_term = in_term.at[:, spare : spare + 2, :ROWS].add(
        jnp.where(core == 1, gains, 0.0).astype(jnp.bfloat16)
    )
    return (
        term(whole(second_norm), halved(gated_slope, 1)),
        term(whole(act), halved(down_in, 1)),
        in_term,
        term(out_rows, whole(branch_slope)),
    )


def body(
    inputs, positions, plan, attend_in, attend_out, gate_up, down_weight, norm_gains, cotangent
):
    section_index = lax.axis_index("section")
    shard_index = lax.axis_index("fsdp")
    extra = PADDED - ROWS
    in_shard = jnp.concatenate(
        [
            attend_in[0],
            jnp.pad(norm_gains[0], ((0, extra - 2), (0, QKV - ROWS))),
        ],
        0,
    )
    gathered = gather_weights(
        (
            jnp.pad(gate_up[0], ((0, extra), (0, 0))),
            jnp.pad(down_weight[0], ((0, 0), (0, DOWN_COLUMNS - D))),
            in_shard,
            jnp.pad(attend_out[0], ((0, extra), (0, 0))),
        )
    )
    gains = gathered[2][:, ROWS : ROWS + 2, :ROWS].swapaxes(0, 1).reshape(2, D)
    weights = (
        gathered[2].reshape(-1, QKV),
        gathered[3].reshape(-1, D),
        gathered[0].reshape(-1, 2 * FF),
        gathered[1].reshape(-1, DOWN_COLUMNS),
        gains.astype(jnp.float32),
    )
    plan_row = plan[0]
    fresh = jnp.take(inputs[:, 0], plan_row, axis=0)
    tables = rotary_tables(jnp.take(positions[:, 0], plan_row, axis=0))
    given = cotangent[:, 0]
    result, _ = forward_layer(fresh, tables, weights, shard_index)
    layer_in = jnp.where(section_index == 0, fresh, passed_along(result, 1))
    outputs, kept = forward_layer(layer_in, tables, weights, shard_index)
    input_slope, _, _ = backward_layer(given, kept, tables, weights, shard_index)
    back = passed_along(input_slope.astype(jnp.bfloat16), -1)
    upstream = jnp.where(section_index == 1, given, back)
    input_slope, slopes, gain_slopes = backward_layer(upstream, kept, tables, weights, shard_index)
    reported = jnp.where(
        section_index == 0, input_slope, input_slope.astype(jnp.bfloat16).astype(jnp.float32)
    )
    input_slopes = jnp.take(reported, plan_row, axis=0)
    summed = reduce_gradients(weight_terms(kept, slopes, gain_slopes))
    full = [value.astype(jnp.float32) for value in summed]
    return (
        outputs[None, :, None],
        input_slopes[None, :, None],
        full[2][None, :ROWS],
        full[3][None, :ROWS],
        full[0][None, :ROWS],
        full[1][None, :, :D],
        full[2][None, ROWS : ROWS + 2, :ROWS],
    )


def solution(mesh):
    in_specs = (
        P(None, "dp", "fsdp", None),
        P(None, "dp", "fsdp"),
        P("dp", None),
        P("section", "fsdp", None),
        P("section", "fsdp", None),
        P("section", "fsdp", None),
        P("section", "fsdp", None),
        P("section", None, "fsdp"),
        P(None, "dp", "fsdp", None),
    )
    out_specs = (
        P("section", None, "dp", "fsdp", None),
        P("section", None, "dp", "fsdp", None),
        P("section", "fsdp", None),
        P("section", "fsdp", None),
        P("section", "fsdp", None),
        P("section", "fsdp", None),
        P("section", None, "fsdp"),
    )
    return jax.shard_map(body, mesh=mesh, in_specs=in_specs, out_specs=out_specs, check_vma=False)
```

```python
import functools

import jax
import jax.numpy as jnp
from jax import lax
from jax.experimental import pallas as pl
from jax.experimental.pallas import tpu as pltpu
from jax.sharding import PartitionSpec as P

D = 960
QUERY_HEADS = 15
KEY_VALUE_HEADS = 5
HEAD_WIDTH = 64
FF = 2560
QUERY_WIDTH = QUERY_HEADS * HEAD_WIDTH
KEY_WIDTH = KEY_VALUE_HEADS * HEAD_WIDTH
QKV = QUERY_WIDTH + 2 * KEY_WIDTH
SHARDS = 8
ROWS = D // SHARDS
PADDED = 128
DOWN_COLUMNS = 1024

EPSILON = 1e-05
BASE = 10000.0

MESH = pl.DeviceIdType.MESH
ANY = pl.BlockSpec(memory_space=pl.ANY)

GATE_UP = (PADDED, 2 * FF, "columns")
DOWN = (FF // SHARDS, DOWN_COLUMNS, "columns")
ATTEND_IN = (PADDED, QKV, "rows")
ATTEND_OUT = (PADDED, D, "rows")
SHAPES = (GATE_UP, DOWN, ATTEND_IN, ATTEND_OUT)


def half_shape(shape):
    rows, columns, kind = shape
    return (rows // 2, columns) if kind == "rows" else (rows, columns // 2)


def half_view(shape, core, start, count):
    rows, columns, kind = shape
    if kind == "rows":
        first = pl.multiple_of(core * (rows // 2) + start, 16)
        return (pl.ds(first, count), slice(None))
    first = pl.multiple_of(core * (columns // 2), 128)
    return (pl.ds(pl.multiple_of(start, 16), count), pl.ds(first, columns // 2))


def places():
    dp = lax.axis_index("dp")
    fsdp = lax.axis_index("fsdp")
    return dp // 2, dp % 2, fsdp // 4, fsdp % 4


def peer_ids():
    z, core, x, y = places()
    return {
        "X": {"fsdp": (1 - x) * 4 + y},
        "Yp": {"fsdp": x * 4 + (y + 1) % 4},
        "Ym": {"fsdp": x * 4 + (y + 3) % 4},
        "C": {"dp": z * 2 + 1 - core},
        "Z1": {"dp": ((z + 1) % 4) * 2 + core},
        "Z2": {"dp": ((z + 2) % 4) * 2 + core},
        "Z3": {"dp": ((z + 3) % 4) * 2 + core},
    }


def greet(ids, names):
    barrier = pltpu.get_barrier_semaphore()
    for name in names:
        pl.semaphore_signal(barrier, inc=1, device_id=ids[name], device_id_type=MESH)
    pl.semaphore_wait(barrier, len(names))


GATHER = (
    ("X", 0, 0, "f"),
    ("Yp", 0, 0, "f"),
    ("Ym", 0, 0, "f"),
    ("Ym", 0, 1, 0),
    ("X", 0, 1, 0),
    ("Yp", 0, 3, 1),
    ("X", 0, 3, 0),
    ("Yp", 1, 0, 1),
    ("Ym", 1, 0, 1),
    ("Ym", 1, 1, 0),
    ("Yp", 1, 3, 1),
)
GATHER_NEXT = {1: (5, 6), 2: (3, 4), 0: (7, 8), 4: (9,), 7: (10,)}
GATHER_ORDER = (1, 2, 0, 4, 7, 3, 5, 6, 8, 9, 10)


def seen_by_receiver(peer, column, step):
    if peer == "X":
        return 1 - column, step
    if peer == "Yp":
        return column, (step + 3) % 4
    if peer == "Ym":
        return column, (step + 1) % 4
    return column, step


def part_rows(shape, part):
    rows = half_shape(shape)[0]
    return (0, rows) if part == "f" else (part * (rows // 2), rows // 2)


def gather_kernel(*refs):
    count = len(SHAPES)
    shards, outs = refs[:count], refs[count : 2 * count]
    local_sem, send_sem, recv_sem = refs[2 * count :]
    z, core, x, y = places()
    ids = peer_ids()
    mine = x * 4 + y

    def owner(column, step):
        return ((x + column) % 2) * 4 + (y + step) % 4

    def view(array, column, step, part, which):
        start, rows = part_rows(SHAPES[array], part)
        return outs[array].at[(owner(column, step),) + half_view(SHAPES[array], which, start, rows)]

    def copy(array, edge):
        peer, column, step, part = GATHER[edge % 11]
        if edge < 11:
            target = view(array, column, step, part, core)
            source = target
            if (column, step) == (0, 0):
                start, rows = part_rows(SHAPES[array], part)
                source = shards[array].at[half_view(SHAPES[array], core, start, rows)]
        else:
            peer, (column, step) = "C", seen_by_receiver(peer, column, step)
            source = target = view(array, column, step, part, core)
        return pltpu.make_async_remote_copy(
            src_ref=source,
            dst_ref=target,
            send_sem=send_sem.at[array, edge],
            recv_sem=recv_sem.at[array, edge],
            device_id=ids[peer],
            device_id_type=MESH,
        )

    def wait_for(array, edge):
        peer, column, step, part = GATHER[edge % 11]
        column, step = seen_by_receiver(peer, column, step)
        which = core if edge < 11 else 1 - core
        landed = view(array, column, step, part, which)
        pltpu.make_async_remote_copy(
            src_ref=landed,
            dst_ref=landed,
            send_sem=send_sem.at[array, edge],
            recv_sem=recv_sem.at[array, edge],
            device_id=ids["C"],
            device_id_type=MESH,
        ).wait_recv()

    greet(ids, ("X", "Yp", "Ym", "C"))
    own = [
        pltpu.make_async_copy(shards[array], outs[array].at[mine], local_sem.at[array])
        for array in range(count)
    ]
    for array in range(count):
        for edge in (0, 1, 2):
            copy(array, edge).start()
        own[array].start()
    for array in range(count):
        for edge in GATHER_ORDER:
            wait_for(array, edge)
            for later in GATHER_NEXT.get(edge, ()):
                copy(array, later).start()
            copy(array, 11 + edge).start()
    for array in range(count):
        for edge in range(11):
            wait_for(array, 11 + edge)
        for edge in range(22):
            copy(array, edge).wait_send()
        own[array].wait()


def gather_weights(shards):
    count = len(SHAPES)
    return pl.pallas_call(
        gather_kernel,
        name="gather_weights",
        out_shape=[
            jax.ShapeDtypeStruct((SHARDS, rows, columns), jnp.bfloat16)
            for rows, columns, _ in SHAPES
        ],
        in_specs=[ANY] * count,
        out_specs=[ANY] * count,
        scratch_shapes=[
            pltpu.SemaphoreType.DMA((count,)),
            pltpu.SemaphoreType.DMA((count, 22)),
            pltpu.SemaphoreType.DMA((count, 22)),
        ],
        compiler_params=pltpu.CompilerParams(collective_id=0, has_side_effects=True),
    )(*shards)


REDUCE = (
    ("Yp", 0, 2, 0, ()),
    ("Ym", 0, 2, 1, ()),
    ("Yp", 1, 2, 0, ()),
    ("Ym", 1, 2, 1, ()),
    ("X", 1, 3, 0, ()),
    ("Yp", 1, 1, 1, ()),
    ("X", 1, 1, 0, (2,)),
    ("Ym", 1, 3, 1, (3,)),
    ("Yp", 0, 1, "f", (0, 6)),
    ("Ym", 0, 3, "f", (1, 4)),
    ("X", 1, 0, "f", (5, 7)),
)
REDUCE_STAGES = ((0, 1, 2, 3, 4, 5), (6, 7), (8, 9, 10))


def reduce_kernel(*refs):
    count = len(SHAPES)
    terms, outs = refs[:count], refs[count : 2 * count]
    scratch = refs[2 * count :]
    totals = scratch[:count]
    wholes = scratch[count : 2 * count]
    parts = scratch[2 * count : 3 * count]
    quarters = scratch[3 * count : 4 * count]
    local_sem, send_sem, recv_sem = scratch[4 * count :]
    z, core, x, y = places()
    ids = peer_ids()
    mine = x * 4 + y

    def owner(column, step):
        return ((x + column) % 2) * 4 + (y + step) % 4

    def piece(array, edge):
        _, column, step, part, _ = REDUCE[edge]
        start, rows = part_rows(SHAPES[array], part)
        return totals[array].at[owner(column, step), pl.ds(start, rows), :]

    def slot(array, edge):
        return parts[array].at[edge] if edge < 8 else wholes[array].at[edge - 8]

    def add(array, into, start, rows, source):
        @pl.loop(0, rows // 16)
        def _(index):
            offset = pl.multiple_of(index * 16, 16)
            at = pl.ds(pl.multiple_of(start + offset, 16), 16)
            totals[array][into, at, :] = (
                totals[array][into, at, :].astype(jnp.float32)
                + source[pl.ds(offset, 16), :].astype(jnp.float32)
            ).astype(jnp.bfloat16)

    def quarter(array, index):
        rows = half_shape(SHAPES[array])[0] // 4
        return pl.multiple_of(index * rows, 16), rows

    def out_view(array, index, which):
        start, rows = quarter(array, index)
        return outs[array].at[half_view(SHAPES[array], which, start, rows)]

    def copy(array, edge):
        if edge < 11:
            peer, source, target = REDUCE[edge][0], piece(array, edge), slot(array, edge)
        elif edge < 14:
            step = edge - 10
            peer = f"Z{step}"
            start, rows = quarter(array, (z + step) % 4)
            source = totals[array].at[mine, pl.ds(start, rows), :]
            target = quarters[array].at[step - 1]
        elif edge < 17:
            peer = f"Z{edge - 13}"
            start, rows = quarter(array, z)
            source = totals[array].at[mine, pl.ds(start, rows), :]
            target = out_view(array, z, core)
        else:
            peer = "C"
            at = (z + edge - 17) % 4
            source = target = out_view(array, at, core)
            if edge == 17:
                start, rows = quarter(array, z)
                source = totals[array].at[mine, pl.ds(start, rows), :]
        return pltpu.make_async_remote_copy(
            src_ref=source,
            dst_ref=target,
            send_sem=send_sem.at[array, edge],
            recv_sem=recv_sem.at[array, edge],
            device_id=ids[peer],
            device_id_type=MESH,
        )

    def wait_for(array, edge):
        if edge < 11:
            landed = slot(array, edge)
        elif edge < 14:
            landed = quarters[array].at[edge - 11]
        elif edge < 17:
            landed = out_view(array, (z + 4 - (edge - 13)) % 4, core)
        else:
            landed = out_view(array, (z + edge - 17) % 4, 1 - core)
        pltpu.make_async_remote_copy(
            src_ref=landed,
            dst_ref=landed,
            send_sem=send_sem.at[array, edge],
            recv_sem=recv_sem.at[array, edge],
            device_id=ids["C"],
            device_id_type=MESH,
        ).wait_recv()

    def receive(array, edge):
        wait_for(array, edge)
        peer, column, step, part, _ = REDUCE[edge]
        column, step = seen_by_receiver(peer, column, step)
        start, rows = part_rows(SHAPES[array], part)
        add(array, owner(column, step), start, rows, slot(array, edge))

    loads = [
        pltpu.make_async_copy(terms[array], totals[array], local_sem.at[array])
        for array in range(count)
    ]
    for load in loads:
        load.start()
    greet(ids, ("X", "Yp", "Ym", "C", "Z1", "Z2", "Z3"))
    for stage in REDUCE_STAGES:
        for array in range(count):
            if stage == REDUCE_STAGES[0]:
                loads[array].wait()
            for edge in stage:
                for earlier in REDUCE[edge][4]:
                    receive(array, earlier)
                copy(array, edge).start()
    for array in range(count):
        for edge in (8, 9, 10):
            receive(array, edge)
        for edge in (11, 12, 13):
            copy(array, edge).start()
    stores = []
    for array in range(count):
        start, rows = quarter(array, z)
        for edge in (11, 12, 13):
            wait_for(array, edge)
            add(array, mine, start, rows, quarters[array].at[edge - 11])
        for edge in (14, 15, 16, 17):
            copy(array, edge).start()
        store = pltpu.make_async_copy(
            totals[array].at[mine, pl.ds(start, rows), :],
            out_view(array, z, core),
            local_sem.at[array],
        )
        store.start()
        stores.append(store)
    for array in range(count):
        for edge in (14, 15, 16):
            wait_for(array, edge)
            copy(array, 17 + (17 - edge)).start()
    for array in range(count):
        for edge in range(17, 21):
            wait_for(array, edge)
        for edge in range(21):
            copy(array, edge).wait_send()
        stores[array].wait()


def reduce_gradients(terms):
    count = len(SHAPES)
    halves = [half_shape(shape) for shape in SHAPES]
    return pl.pallas_call(
        reduce_kernel,
        name="reduce_gradients",
        out_shape=[
            jax.ShapeDtypeStruct((rows, columns), jnp.bfloat16) for rows, columns, _ in SHAPES
        ],
        in_specs=[ANY] * count,
        out_specs=[ANY] * count,
        scratch_shapes=[pltpu.VMEM((SHARDS,) + half, jnp.bfloat16) for half in halves]
        + [pltpu.VMEM((3,) + half, jnp.bfloat16) for half in halves]
        + [pltpu.VMEM((8, half[0] // 2, half[1]), jnp.bfloat16) for half in halves]
        + [pltpu.VMEM((3, half[0] // 4, half[1]), jnp.bfloat16) for half in halves]
        + [
            pltpu.SemaphoreType.DMA((count,)),
            pltpu.SemaphoreType.DMA((count, 21)),
            pltpu.SemaphoreType.DMA((count, 21)),
        ],
        compiler_params=pltpu.CompilerParams(
            collective_id=1, has_side_effects=True, vmem_limit_bytes=48 * 2**20
        ),
    )(*terms)


TOKENS = 1024
LOCAL = TOKENS // SHARDS
SLOTS = 2
BLOCK = 256
PAIR = 2 * HEAD_WIDTH
NEGATIVE = -1e30


def two_groups(device):
    return (device == 1) | (device == 4)


def group_lanes(device, which):
    return pl.ds(pl.multiple_of(((2 * device) // 3 + which) * PAIR, PAIR), PAIR)


def pair_lanes(device):
    return pl.ds(pl.multiple_of(device * PAIR, PAIR), PAIR)


def token_rows(device):
    return pl.ds(pl.multiple_of(device * LOCAL, LOCAL), LOCAL)


def ring(me):
    return [(step, (me + step) % SHARDS, (me + SHARDS - step) % SHARDS) for step in range(1, SHARDS)]


def greet_all(me):
    barrier = pltpu.get_barrier_semaphore()
    for _, target, _ in ring(me):
        pl.semaphore_signal(barrier, inc=1, device_id={"fsdp": target}, device_id_type=MESH)
    pl.semaphore_wait(barrier, SHARDS - 1)


def sent(source, target, send_sem, recv_sem, device):
    return pltpu.make_async_remote_copy(
        src_ref=source,
        dst_ref=target,
        send_sem=send_sem,
        recv_sem=recv_sem,
        device_id={"fsdp": device},
        device_id_type=MESH,
    )


def causal_mask(values):
    length = values.shape[1]
    row = lax.broadcasted_iota(jnp.int32, (BLOCK, BLOCK), 0)
    column = lax.broadcasted_iota(jnp.int32, (BLOCK, BLOCK), 1)
    own = jnp.where(column <= row, values[:, length - BLOCK :], NEGATIVE)
    if length == BLOCK:
        return own
    return jnp.concatenate([values[:, : length - BLOCK], own], 1)


def dot_t(left, right):
    return lax.dot_general(
        left, right, (((1,), (1,)), ((), ())), preferred_element_type=jnp.float32
    )


def dot_first(left, right):
    return lax.dot_general(
        left, right, (((0,), (0,)), ((), ())), preferred_element_type=jnp.float32
    )


def attend_kernel(
    q_ref, kv_ref, mixed_ref, q_kept, kv_kept, lse_kept,
    q_all, kv_all, lse_all, mixed_all, local_sem, send_sem, recv_sem,
):
    me = lax.axis_index("fsdp")
    both = two_groups(me)
    second = jnp.where(both, 1, 0)

    def incoming(slot, step, device, sender):
        rows = token_rows(sender)
        return [
            sent(
                q_ref.at[slot, :, pair_lanes(device)], q_all.at[slot, rows, :],
                send_sem.at[0, slot, step], recv_sem.at[0, slot, step], device,
            ),
            sent(
                kv_ref.at[slot, :, group_lanes(device, 0)], kv_all.at[0, slot, rows, :],
                send_sem.at[1, slot, step], recv_sem.at[1, slot, step], device,
            ),
        ]

    def extra(slot, step, device, sender):
        group = jnp.where(two_groups(device), 1, 0)
        return sent(
            kv_ref.at[slot, :, group_lanes(device, group)], kv_all.at[1, slot, token_rows(sender), :],
            send_sem.at[2, slot, step], recv_sem.at[2, slot, step], device,
        )

    def outgoing(slot, step, device, sender):
        return sent(
            mixed_all.at[slot, token_rows(device), :], mixed_ref.at[slot, :, pair_lanes(sender)],
            send_sem.at[3, slot, step], recv_sem.at[3, slot, step], device,
        )

    def own_copies(slot):
        rows = token_rows(me)
        group = jnp.where(both, 1, 0)
        return [
            pltpu.make_async_copy(
                q_ref.at[slot, :, pair_lanes(me)], q_all.at[slot, rows, :], local_sem.at[0, slot]
            ),
            pltpu.make_async_copy(
                kv_ref.at[slot, :, group_lanes(me, 0)], kv_all.at[0, slot, rows, :],
                local_sem.at[1, slot],
            ),
            pltpu.make_async_copy(
                kv_ref.at[slot, :, group_lanes(me, group)], kv_all.at[1, slot, rows, :],
                local_sem.at[2, slot],
            ),
        ]

    def own_result(slot):
        return pltpu.make_async_copy(
            mixed_all.at[slot, token_rows(me), :], mixed_ref.at[slot, :, pair_lanes(me)],
            local_sem.at[3, slot],
        )

    greet_all(me)
    for slot in range(SLOTS):
        for step, target, _ in ring(me):
            for copy in incoming(slot, step, target, me):
                copy.start()

            @pl.when(two_groups(target))
            def _():
                extra(slot, step, target, me).start()

        for copy in own_copies(slot):
            copy.start()

    @pl.loop(0, SLOTS)
    def _(slot):
        for step, _, source in ring(me):
            for copy in incoming(slot, step, source, source):
                copy.wait_recv()

            @pl.when(both)
            def _():
                extra(slot, step, source, source).wait_recv()

        for copy in own_copies(slot):
            copy.wait()
        for block in range(TOKENS // BLOCK):
            rows = pl.ds(block * BLOCK, BLOCK)
            length = (block + 1) * BLOCK
            outs, totals = [], []
            for head in range(2):
                group = 0 if head == 0 else second
                lanes = slice(head * HEAD_WIDTH, (head + 1) * HEAD_WIDTH)
                query = q_all[slot, rows, lanes]
                keys = kv_all[group, slot, :length, :HEAD_WIDTH]
                values = kv_all[group, slot, :length, HEAD_WIDTH:]
                scores = causal_mask(dot_t(query, keys))
                highest = jnp.max(scores, -1, keepdims=True)
                weights = jnp.exp(scores - highest)
                total = jnp.sum(weights, -1, keepdims=True)
                out = jnp.dot(
                    weights.astype(jnp.bfloat16), values, preferred_element_type=jnp.float32
                )
                outs.append(out / total)
                totals.append(
                    jnp.broadcast_to(highest + jnp.log(total), (BLOCK, HEAD_WIDTH))
                )
            mixed_all[slot, rows, :] = jnp.concatenate(outs, 1).astype(jnp.bfloat16)
            lse_all[slot, rows, :] = jnp.concatenate(totals, 1)
        for step, target, _ in ring(me):
            outgoing(slot, step, target, me).start()
        own_result(slot).start()

    keep = [
        pltpu.make_async_copy(q_all, q_kept, local_sem.at[4, 0]),
        pltpu.make_async_copy(kv_all, kv_kept, local_sem.at[4, 1]),
        pltpu.make_async_copy(lse_all, lse_kept, local_sem.at[5, 0]),
    ]
    for copy in keep:
        copy.start()
    for slot in range(SLOTS):
        for step, target, source in ring(me):
            outgoing(slot, step, source, source).wait_recv()
            outgoing(slot, step, target, me).wait_send()
            for copy in incoming(slot, step, target, me):
                copy.wait_send()

            @pl.when(two_groups(target))
            def _():
                extra(slot, step, target, me).wait_send()

        own_result(slot).wait()
    for copy in keep:
        copy.wait()


Q_ALL = (SLOTS, TOKENS, PAIR)
KV_ALL = (2, SLOTS, TOKENS, PAIR)
FULL = SHARDS * PAIR


def attend(query_rows, key_values):
    bf16 = jnp.bfloat16
    return pl.pallas_call(
        attend_kernel,
        name="attend",
        out_shape=[
            jax.ShapeDtypeStruct((SLOTS, LOCAL, FULL), bf16),
            jax.ShapeDtypeStruct(Q_ALL, bf16),
            jax.ShapeDtypeStruct(KV_ALL, bf16),
            jax.ShapeDtypeStruct(Q_ALL, jnp.float32),
        ],
        in_specs=[ANY] * 2,
        out_specs=[ANY] * 4,
        scratch_shapes=[
            pltpu.VMEM(Q_ALL, bf16),
            pltpu.VMEM(KV_ALL, bf16),
            pltpu.VMEM(Q_ALL, jnp.float32),
            pltpu.VMEM(Q_ALL, bf16),
            pltpu.SemaphoreType.DMA((6, SLOTS)),
            pltpu.SemaphoreType.DMA((4, SLOTS, SHARDS)),
            pltpu.SemaphoreType.DMA((4, SLOTS, SHARDS)),
        ],
        compiler_params=pltpu.CompilerParams(
            collective_id=2, has_side_effects=True, vmem_limit_bytes=40 * 2**20
        ),
    )(query_rows, key_values)


def attend_back_kernel(
    slope_ref, q_ref, kv_ref, lse_ref, dq_ref, dkv_ref, dkv_extra_ref,
    slope_all, q_all, kv_all, lse_all, dq_all, dkv_total, dkv_all,
    local_sem, send_sem, recv_sem,
):
    me = lax.axis_index("fsdp")
    both = two_groups(me)
    second = jnp.where(both, 1, 0)
    extra_at = me // 4

    def incoming(slot, step, device, sender):
        return sent(
            slope_ref.at[slot, :, pair_lanes(device)], slope_all.at[slot, token_rows(sender), :],
            send_sem.at[0, slot, step], recv_sem.at[0, slot, step], device,
        )

    def outgoing(slot, step, device, sender):
        rows = token_rows(device)
        return [
            sent(
                dq_all.at[slot, rows, :], dq_ref.at[slot, :, pair_lanes(sender)],
                send_sem.at[1, slot, step], recv_sem.at[1, slot, step], device,
            ),
            sent(
                dkv_all.at[0, slot, rows, :], dkv_ref.at[sender, slot],
                send_sem.at[2, slot, step], recv_sem.at[2, slot, step], device,
            ),
        ]

    def extra(slot, step, device, sender):
        return sent(
            dkv_all.at[1, slot, token_rows(device), :], dkv_extra_ref.at[sender // 4, slot],
            send_sem.at[3, slot, step], recv_sem.at[3, slot, step], device,
        )

    def own_slope(slot):
        return pltpu.make_async_copy(
            slope_ref.at[slot, :, pair_lanes(me)], slope_all.at[slot, token_rows(me), :],
            local_sem.at[0, slot],
        )

    def own_results(slot):
        rows = token_rows(me)
        return [
            pltpu.make_async_copy(
                dq_all.at[slot, rows, :], dq_ref.at[slot, :, pair_lanes(me)], local_sem.at[1, slot]
            ),
            pltpu.make_async_copy(
                dkv_all.at[0, slot, rows, :], dkv_ref.at[me, slot], local_sem.at[2, slot]
            ),
        ]

    def own_extra(slot):
        return pltpu.make_async_copy(
            dkv_all.at[1, slot, token_rows(me), :], dkv_extra_ref.at[extra_at, slot],
            local_sem.at[3, slot],
        )

    loads = [
        pltpu.make_async_copy(q_ref, q_all, local_sem.at[4, 0]),
        pltpu.make_async_copy(kv_ref, kv_all, local_sem.at[4, 1]),
        pltpu.make_async_copy(lse_ref, lse_all, local_sem.at[5, 0]),
    ]
    for copy in loads:
        copy.start()
    greet_all(me)
    for slot in range(SLOTS):
        for step, target, _ in ring(me):
            incoming(slot, step, target, me).start()
        own_slope(slot).start()
    for copy in loads:
        copy.wait()

    @pl.loop(0, SLOTS)
    def _(slot):
        for step, _, source in ring(me):
            incoming(slot, step, source, source).wait_recv()
        own_slope(slot).wait()
        dkv_total[...] = jnp.zeros_like(dkv_total)
        for block in range(TOKENS // BLOCK):
            rows = pl.ds(block * BLOCK, BLOCK)
            length = (block + 1) * BLOCK
            outs = []
            for head in range(2):
                group = 0 if head == 0 else second
                lanes = slice(head * HEAD_WIDTH, (head + 1) * HEAD_WIDTH)
                query = q_all[slot, rows, lanes]
                slope = slope_all[slot, rows, lanes]
                lse = lse_all[slot, rows, head * HEAD_WIDTH : head * HEAD_WIDTH + 1]
                keys = kv_all[group, slot, :length, :HEAD_WIDTH]
                values = kv_all[group, slot, :length, HEAD_WIDTH:]
                probs = jnp.exp(causal_mask(dot_t(query, keys)) - lse)
                prob_slope = dot_t(slope, values)
                inner = jnp.sum(probs * prob_slope, -1, keepdims=True)
                score_slope = (probs * (prob_slope - inner)).astype(jnp.bfloat16)
                outs.append(
                    jnp.dot(score_slope, keys, preferred_element_type=jnp.float32)
                    * HEAD_WIDTH ** (-0.5)
                )
                dkv_total[group, :length, :] += jnp.concatenate(
                    [dot_first(score_slope, query), dot_first(probs.astype(jnp.bfloat16), slope)], 1
                )
            dq_all[slot, rows, :] = jnp.concatenate(outs, 1).astype(jnp.bfloat16)
        dkv_all[0, slot] = dkv_total[0].astype(jnp.bfloat16)
        dkv_all[1, slot] = dkv_total[1].astype(jnp.bfloat16)
        for step, target, _ in ring(me):
            for copy in outgoing(slot, step, target, me):
                copy.start()

            @pl.when(both)
            def _():
                extra(slot, step, target, me).start()

        for copy in own_results(slot):
            copy.start()

        @pl.when(both)
        def _():
            own_extra(slot).start()

    for slot in range(SLOTS):
        for step, target, source in ring(me):
            incoming(slot, step, target, me).wait_send()
            for copy in outgoing(slot, step, source, source):
                copy.wait_recv()
            for copy in outgoing(slot, step, target, me):
                copy.wait_send()

            @pl.when(two_groups(source))
            def _():
                extra(slot, step, source, source).wait_recv()

            @pl.when(both)
            def _():
                extra(slot, step, target, me).wait_send()

        for copy in own_results(slot):
            copy.wait()

        @pl.when(both)
        def _():
            own_extra(slot).wait()


def attend_back(slope, kept):
    bf16 = jnp.bfloat16
    return pl.pallas_call(
        attend_back_kernel,
        name="attend_back",
        out_shape=[
            jax.ShapeDtypeStruct((SLOTS, LOCAL, FULL), bf16),
            jax.ShapeDtypeStruct((SHARDS, SLOTS, LOCAL, PAIR), bf16),
            jax.ShapeDtypeStruct((2, SLOTS, LOCAL, PAIR), bf16),
        ],
        in_specs=[ANY] * 4,
        out_specs=[ANY] * 3,
        scratch_shapes=[
            pltpu.VMEM(Q_ALL, bf16),
            pltpu.VMEM(Q_ALL, bf16),
            pltpu.VMEM(KV_ALL, bf16),
            pltpu.VMEM(Q_ALL, jnp.float32),
            pltpu.VMEM(Q_ALL, bf16),
            pltpu.VMEM((2, TOKENS, PAIR), jnp.float32),
            pltpu.VMEM(KV_ALL, bf16),
            pltpu.SemaphoreType.DMA((6, SLOTS)),
            pltpu.SemaphoreType.DMA((4, SLOTS, SHARDS)),
            pltpu.SemaphoreType.DMA((4, SLOTS, SHARDS)),
        ],
        compiler_params=pltpu.CompilerParams(
            collective_id=3, has_side_effects=True, vmem_limit_bytes=48 * 2**20
        ),
    )(slope, *kept)


def rotary_tables(positions):
    half = HEAD_WIDTH // 2
    frequency = BASE ** (-(jnp.arange(half).astype(jnp.float32) * (2.0 / HEAD_WIDTH)))
    angle = positions.astype(jnp.float32)[..., None] * frequency
    cosine_table = jnp.cos(angle)
    sine_table = jnp.sin(angle)
    return (
        jnp.concatenate([cosine_table, cosine_table], -1)[..., None, :],
        jnp.concatenate([sine_table, sine_table], -1)[..., None, :],
    )


def apply_rotation(values, cosine_table, sine_table):
    half = values.shape[-1] // 2
    turned = jnp.concatenate([-values[..., half:], values[..., :half]], -1)
    return values * cosine_table + turned * sine_table


def reverse_rotation(values, cosine_table, sine_table):
    half = values.shape[-1] // 2
    shifted = values * sine_table
    turned = jnp.concatenate([-shifted[..., half:], shifted[..., :half]], -1)
    return values * cosine_table - turned


def normed(values, gain):
    return values * lax.rsqrt(jnp.mean(values * values, -1, keepdims=True) + EPSILON) * gain


def norm_backward(values, gain, upstream):
    row_scale = lax.rsqrt(jnp.mean(values * values, -1, keepdims=True) + EPSILON)
    unit = values * row_scale
    gain_slope = jnp.sum(upstream * unit, 0)
    inner = upstream * gain
    return (row_scale * (inner - unit * jnp.mean(inner * unit, -1, keepdims=True)), gain_slope)


def pad_shards(values):
    split = values.reshape(values.shape[0], SHARDS, ROWS)
    return jnp.pad(split, ((0, 0), (0, 0), (0, PADDED - ROWS))).reshape(values.shape[0], -1)


def unpad_shards(values):
    split = values.reshape(values.shape[0], SHARDS, PADDED)
    return split[:, :, :ROWS].reshape(values.shape[0], D)


def heads(values):
    return values.reshape(values.shape[:-1] + (-1, HEAD_WIDTH))


def forward_layer(layer_in, tables, weights):
    attend_in, attend_out, gate_up, down_weight, gains = weights
    batches, local_count = layer_in.shape[:2]
    rows = batches * local_count
    values = layer_in.reshape(rows, D).astype(jnp.float32)
    first_norm = pad_shards(normed(values, gains[0]).astype(jnp.bfloat16))
    projected = jnp.dot(first_norm, attend_in, preferred_element_type=jnp.float32)
    projected = projected.reshape(batches, local_count, QKV)
    rotated = apply_rotation(heads(projected[..., : QUERY_WIDTH + KEY_WIDTH]), *tables)
    query_rows = rotated[..., :QUERY_HEADS, :].astype(jnp.bfloat16) * HEAD_WIDTH ** (-0.5)
    query_rows = jnp.pad(
        query_rows.reshape(batches, local_count, QUERY_WIDTH), ((0, 0), (0, 0), (0, HEAD_WIDTH))
    )
    key_values = jnp.concatenate(
        [rotated[..., QUERY_HEADS:, :], heads(projected[..., QUERY_WIDTH + KEY_WIDTH :])], -1
    )
    key_values = key_values.astype(jnp.bfloat16).reshape(batches, local_count, 2 * KEY_WIDTH)
    mixed, *attended = attend(query_rows, key_values)
    mixed = mixed.reshape(rows, FULL)
    hidden = values + jnp.dot(mixed, attend_out, preferred_element_type=jnp.float32)
    second_norm = pad_shards(normed(hidden, gains[1]).astype(jnp.bfloat16))
    gated = jnp.dot(second_norm, gate_up, preferred_element_type=jnp.float32)
    act = (jax.nn.silu(gated[:, :FF]) * gated[:, FF:]).astype(jnp.bfloat16)
    result = hidden + jnp.dot(act, down_weight, preferred_element_type=jnp.float32)[:, :D]
    kept = (
        values,
        first_norm,
        attended,
        mixed,
        hidden,
        second_norm,
        gated,
        act,
    )
    return (result.astype(jnp.bfloat16).reshape(layer_in.shape), kept)


def backward_layer(upstream, kept, tables, weights):
    attend_in, attend_out, gate_up, down_weight, gains = weights
    (
        values,
        first_norm,
        attended,
        mixed,
        hidden,
        second_norm,
        gated,
        act,
    ) = kept
    batches, local_count = upstream.shape[:2]
    rows = batches * local_count
    upstream = upstream.reshape(rows, D)
    down_in = jnp.pad(upstream, ((0, 0), (0, DOWN_COLUMNS - D)))
    upstream = upstream.astype(jnp.float32)
    act_slope = jnp.einsum("td,fd->tf", down_in, down_weight, preferred_element_type=jnp.float32)
    gate_part = gated[:, :FF]
    up_part = gated[:, FF:]
    sigma = jax.nn.sigmoid(gate_part)
    gate_slope = act_slope * up_part * sigma * (1.0 + gate_part * (1.0 - sigma))
    up_slope = act_slope * gate_part * sigma
    gated_slope = jnp.concatenate([gate_slope, up_slope], 1).astype(jnp.bfloat16)
    second_slope = unpad_shards(
        jnp.einsum("tf,df->td", gated_slope, gate_up, preferred_element_type=jnp.float32)
    )
    hidden_part, second_gain = norm_backward(hidden, gains[1], second_slope)
    hidden_slope = upstream + hidden_part
    branch_slope = hidden_slope.astype(jnp.bfloat16)
    mixed_gradient = jnp.einsum(
        "td,qd->tq", branch_slope, attend_out, preferred_element_type=jnp.float32
    ).astype(jnp.bfloat16)
    query_slope, pair_slopes, extra_slopes = attend_back(
        mixed_gradient.reshape(batches, local_count, FULL), attended
    )
    pair_slopes = pair_slopes.astype(jnp.float32)
    extra_slopes = extra_slopes.astype(jnp.float32)
    group_slopes = jnp.stack(
        [
            pair_slopes[0] + pair_slopes[1],
            extra_slopes[0] + pair_slopes[2],
            pair_slopes[3] + pair_slopes[4],
            extra_slopes[1] + pair_slopes[5],
            pair_slopes[6] + pair_slopes[7],
        ],
        2,
    )
    query_slope = query_slope[..., :QUERY_WIDTH].astype(jnp.float32)
    query_raw = reverse_rotation(
        query_slope.reshape(batches, local_count, QUERY_HEADS, HEAD_WIDTH), *tables
    ).reshape(rows, QUERY_WIDTH)
    unrotated_key = reverse_rotation(group_slopes[..., :HEAD_WIDTH], *tables)
    projected_slope = jnp.concatenate(
        [
            query_raw,
            unrotated_key.reshape(rows, KEY_WIDTH),
            group_slopes[..., HEAD_WIDTH:].reshape(rows, KEY_WIDTH),
        ],
        1,
    ).astype(jnp.bfloat16)
    first_slope = unpad_shards(
        jnp.einsum("tf,df->td", projected_slope, attend_in, preferred_element_type=jnp.float32)
    )
    input_part, first_gain = norm_backward(values, gains[0], first_slope)
    input_slope = hidden_slope + input_part
    slopes = (projected_slope, branch_slope, gated_slope, down_in)
    return (
        input_slope.reshape(batches, local_count, D),
        slopes,
        jnp.stack([first_gain, second_gain]),
    )


def passed_along(value, steps):
    return lax.ppermute(value, "section", [(0, 1)] if steps > 0 else [(1, 0)])


def with_other_core(value):
    size = lax.axis_size("dp")
    other = lax.ppermute(value, "dp", [(index, index ^ 1) for index in range(size)])
    return other


def weight_terms(kept, slopes, gain_slopes):
    core = lax.axis_index("dp") % 2
    first_norm, mixed, second_norm, act = (kept[1], kept[3], kept[5], kept[7])
    mixed = pad_shards(mixed[:, :QUERY_WIDTH])
    projected_slope, branch_slope, gated_slope, down_in = slopes
    tokens = act.shape[0]

    def halved(values, axis):
        extent = values.shape[axis] // 2
        keep = lax.dynamic_slice_in_dim(values, core * extent, extent, axis)
        send = lax.dynamic_slice_in_dim(values, (1 - core) * extent, extent, axis)
        return jnp.concatenate([keep, with_other_core(send)], 0)

    def whole(values):
        return jnp.concatenate([values, with_other_core(values)], 0)

    def term(left, right):
        split = left.reshape(2 * tokens, SHARDS, -1)
        return jnp.einsum(
            "tkr,tn->krn", split, right, preferred_element_type=jnp.float32
        ).astype(jnp.bfloat16)

    in_rows = halved(first_norm.reshape(tokens, SHARDS, PADDED), 2)
    out_rows = halved(mixed.reshape(tokens, SHARDS, PADDED), 2)
    in_term = term(in_rows, whole(projected_slope))
    gains = (gain_slopes + with_other_core(gain_slopes)).reshape(2, SHARDS, ROWS).swapaxes(0, 1)
    spare = PADDED // 2 - (PADDED - ROWS)
    in_term = in_term.at[:, spare : spare + 2, :ROWS].add(
        jnp.where(core == 1, gains, 0.0).astype(jnp.bfloat16)
    )
    return (
        term(whole(second_norm), halved(gated_slope, 1)),
        term(whole(act), halved(down_in, 1)),
        in_term,
        term(out_rows, whole(branch_slope)),
    )


def body(
    inputs, positions, plan, attend_in, attend_out, gate_up, down_weight, norm_gains, cotangent
):
    section_index = lax.axis_index("section")
    extra = PADDED - ROWS
    in_shard = jnp.concatenate(
        [
            attend_in[0],
            jnp.pad(norm_gains[0], ((0, extra - 2), (0, QKV - ROWS))),
        ],
        0,
    )
    gathered = gather_weights(
        (
            jnp.pad(gate_up[0], ((0, extra), (0, 0))),
            jnp.pad(down_weight[0], ((0, 0), (0, DOWN_COLUMNS - D))),
            in_shard,
            jnp.pad(attend_out[0], ((0, extra), (0, 0))),
        )
    )
    gains = gathered[2][:, ROWS : ROWS + 2, :ROWS].swapaxes(0, 1).reshape(2, D)
    weights = (
        gathered[2].reshape(-1, QKV),
        jnp.pad(gathered[3][:, :ROWS].reshape(QUERY_WIDTH, D), ((0, FULL - QUERY_WIDTH), (0, 0))),
        gathered[0].reshape(-1, 2 * FF),
        gathered[1].reshape(-1, DOWN_COLUMNS),
        gains.astype(jnp.float32),
    )
    plan_row = plan[0]
    fresh = jnp.take(inputs[:, 0], plan_row, axis=0)
    tables = rotary_tables(jnp.take(positions[:, 0], plan_row, axis=0))
    given = cotangent[:, 0]
    result, _ = forward_layer(fresh, tables, weights)
    layer_in = jnp.where(section_index == 0, fresh, passed_along(result, 1))
    outputs, kept = forward_layer(layer_in, tables, weights)
    input_slope, _, _ = backward_layer(given, kept, tables, weights)
    back = passed_along(input_slope.astype(jnp.bfloat16), -1)
    upstream = jnp.where(section_index == 1, given, back)
    input_slope, slopes, gain_slopes = backward_layer(upstream, kept, tables, weights)
    reported = jnp.where(
        section_index == 0, input_slope, input_slope.astype(jnp.bfloat16).astype(jnp.float32)
    )
    input_slopes = jnp.take(reported, plan_row, axis=0)
    summed = reduce_gradients(weight_terms(kept, slopes, gain_slopes))
    full = [value.astype(jnp.float32) for value in summed]
    return (
        outputs[None, :, None],
        input_slopes[None, :, None],
        full[2][None, :ROWS],
        full[3][None, :ROWS],
        full[0][None, :ROWS],
        full[1][None, :, :D],
        full[2][None, ROWS : ROWS + 2, :ROWS],
    )


def solution(mesh):
    in_specs = (
        P(None, "dp", "fsdp", None),
        P(None, "dp", "fsdp"),
        P("dp", None),
        P("section", "fsdp", None),
        P("section", "fsdp", None),
        P("section", "fsdp", None),
        P("section", "fsdp", None),
        P("section", None, "fsdp"),
        P(None, "dp", "fsdp", None),
    )
    out_specs = (
        P("section", None, "dp", "fsdp", None),
        P("section", None, "dp", "fsdp", None),
        P("section", "fsdp", None),
        P("section", "fsdp", None),
        P("section", "fsdp", None),
        P("section", "fsdp", None),
        P("section", None, "fsdp"),
    )
    return jax.shard_map(body, mesh=mesh, in_specs=in_specs, out_specs=out_specs, check_vma=False)
```

```python
import functools

import jax
import jax.numpy as jnp
from jax import lax
from jax.experimental import pallas as pl
from jax.experimental.pallas import tpu as pltpu
from jax.sharding import PartitionSpec as P

D = 960
QUERY_HEADS = 15
KEY_VALUE_HEADS = 5
HEAD_WIDTH = 64
FF = 2560
QUERY_WIDTH = QUERY_HEADS * HEAD_WIDTH
KEY_WIDTH = KEY_VALUE_HEADS * HEAD_WIDTH
QKV = QUERY_WIDTH + 2 * KEY_WIDTH
SHARDS = 8
ROWS = D // SHARDS
PADDED = 128
DOWN_COLUMNS = 1024

EPSILON = 1e-05
BASE = 10000.0

MESH = pl.DeviceIdType.MESH
ANY = pl.BlockSpec(memory_space=pl.ANY)

GATE_UP = (PADDED, 2 * FF, "columns")
DOWN = (FF // SHARDS, DOWN_COLUMNS, "columns")
ATTEND_IN = (PADDED, QKV, "rows")
ATTEND_OUT = (PADDED, D, "rows")
SHAPES = (GATE_UP, DOWN, ATTEND_IN, ATTEND_OUT)


def half_shape(shape):
    rows, columns, kind = shape
    return (rows // 2, columns) if kind == "rows" else (rows, columns // 2)


def half_view(shape, core, start, count):
    rows, columns, kind = shape
    if kind == "rows":
        first = pl.multiple_of(core * (rows // 2) + start, 16)
        return (pl.ds(first, count), slice(None))
    first = pl.multiple_of(core * (columns // 2), 128)
    return (pl.ds(pl.multiple_of(start, 16), count), pl.ds(first, columns // 2))


def places():
    dp = lax.axis_index("dp")
    fsdp = lax.axis_index("fsdp")
    return dp // 2, dp % 2, fsdp // 4, fsdp % 4


def peer_ids():
    z, core, x, y = places()
    return {
        "X": {"fsdp": (1 - x) * 4 + y},
        "Yp": {"fsdp": x * 4 + (y + 1) % 4},
        "Ym": {"fsdp": x * 4 + (y + 3) % 4},
        "C": {"dp": z * 2 + 1 - core},
        "Z1": {"dp": ((z + 1) % 4) * 2 + core},
        "Z2": {"dp": ((z + 2) % 4) * 2 + core},
        "Z3": {"dp": ((z + 3) % 4) * 2 + core},
    }


def greet(ids, names):
    barrier = pltpu.get_barrier_semaphore()
    for name in names:
        pl.semaphore_signal(barrier, inc=1, device_id=ids[name], device_id_type=MESH)
    pl.semaphore_wait(barrier, len(names))


GATHER = (
    ("X", 0, 0, "f"),
    ("Yp", 0, 0, "f"),
    ("Ym", 0, 0, "f"),
    ("Ym", 0, 1, 0),
    ("X", 0, 1, 0),
    ("Yp", 0, 3, 1),
    ("X", 0, 3, 0),
    ("Yp", 1, 0, 1),
    ("Ym", 1, 0, 1),
    ("Ym", 1, 1, 0),
    ("Yp", 1, 3, 1),
)
GATHER_NEXT = {1: (5, 6), 2: (3, 4), 0: (7, 8), 4: (9,), 7: (10,)}
GATHER_ORDER = (1, 2, 0, 4, 7, 3, 5, 6, 8, 9, 10)


def seen_by_receiver(peer, column, step):
    if peer == "X":
        return 1 - column, step
    if peer == "Yp":
        return column, (step + 3) % 4
    if peer == "Ym":
        return column, (step + 1) % 4
    return column, step


def part_rows(shape, part):
    rows = half_shape(shape)[0]
    return (0, rows) if part == "f" else (part * (rows // 2), rows // 2)


SPREAD = 0
UPWARD = (0, 1, 3, 5, 7)
PLAIN_EDGES = 22
SPREAD_EDGES = 88


def gather_kernel(*refs):
    count = len(SHAPES)
    shards, outs = refs[:count], refs[count : 2 * count]
    local_sem, send_sem, recv_sem = refs[2 * count :]
    z, core, x, y = places()
    ids = peer_ids()
    mine = x * 4 + y

    def owner(column, step):
        return ((x + column) % 2) * 4 + (y + step) % 4

    def index(array, part, which, plane):
        start, rows = part_rows(SHAPES[array], part)
        if array == SPREAD:
            quarter = half_shape(SHAPES[array])[0] // 4
            start, rows = plane * quarter + start // 4, rows // 4
        return half_view(SHAPES[array], which, start, rows)

    def view(array, column, step, part, which, plane):
        return outs[array].at[(owner(column, step),) + index(array, part, which, plane)]

    def received(edge):
        group, base = edge // 11, edge % 11
        peer, column, step, part = GATHER[base]
        column, step = seen_by_receiver(peer, column, step)
        away = {0: 0, 1: 0, 2: 3, 3: 1, 4: 2, 5: 3, 6: 1, 7: 2}[group]
        return column, step, part, away

    def peer_of(edge):
        group, base = edge // 11, edge % 11
        if group == 0:
            return GATHER[base][0]
        if group in (1, 5, 6, 7):
            return "C"
        return {2: "Z1", 3: "Z3", 4: "Z1" if base in UPWARD else "Z3"}[group]

    def copy(array, edge):
        group, base = edge // 11, edge % 11
        if group == 0:
            _, column, step, part = GATHER[base]
            away = 0
        else:
            column, step, part, away = received(edge)
            if group in (2, 3):
                away = 0
            elif group == 4:
                away = 3 if base in UPWARD else 1
        target = source = view(array, column, step, part, core, (z + away) % 4)
        if group == 0 and (column, step) == (0, 0):
            source = shards[array].at[index(array, part, core, z)]
        return pltpu.make_async_remote_copy(
            src_ref=source,
            dst_ref=target,
            send_sem=send_sem.at[array, edge],
            recv_sem=recv_sem.at[array, edge],
            device_id=ids[peer_of(edge)],
            device_id_type=MESH,
        )

    def wait_for(array, edge):
        column, step, part, away = received(edge)
        which = 1 - core if edge // 11 in (1, 5, 6, 7) else core
        landed = view(array, column, step, part, which, (z + away) % 4)
        pltpu.make_async_remote_copy(
            src_ref=landed,
            dst_ref=landed,
            send_sem=send_sem.at[array, edge],
            recv_sem=recv_sem.at[array, edge],
            device_id=ids["C"],
            device_id_type=MESH,
        ).wait_recv()

    def within_plane(array):
        for edge in GATHER_ORDER:
            wait_for(array, edge)
            for later in GATHER_NEXT.get(edge, ()):
                copy(array, later).start()
            if array == SPREAD:
                copy(array, 22 + edge).start()
                copy(array, 33 + edge).start()
            copy(array, 11 + edge).start()

    greet(ids, ("X", "Yp", "Ym", "C", "Z1", "Z3"))
    own = [
        pltpu.make_async_copy(shards[array], outs[array].at[mine], local_sem.at[array])
        for array in range(count)
    ]
    for array in range(count):
        for edge in (0, 1, 2):
            copy(array, edge).start()
        own[array].start()
    within_plane(SPREAD)
    within_plane(1)
    for edge in GATHER_ORDER:
        for group in (2, 3):
            wait_for(SPREAD, 11 * group + edge)
            if (group == 2) == (edge in UPWARD):
                copy(SPREAD, 44 + edge).start()
            copy(SPREAD, 11 * (group + 3) + edge).start()
    within_plane(2)
    within_plane(3)
    for edge in GATHER_ORDER:
        wait_for(SPREAD, 44 + edge)
        copy(SPREAD, 77 + edge).start()
    for array in range(count):
        last = SPREAD_EDGES if array == SPREAD else PLAIN_EDGES
        for edge in range(last):
            if edge // 11 in (1, 5, 6, 7):
                wait_for(array, edge)
        for edge in range(last):
            copy(array, edge).wait_send()
        own[array].wait()


def gather_weights(shards):
    count = len(SHAPES)
    return pl.pallas_call(
        gather_kernel,
        name="gather_weights",
        out_shape=[
            jax.ShapeDtypeStruct((SHARDS, rows, columns), jnp.bfloat16)
            for rows, columns, _ in SHAPES
        ],
        in_specs=[ANY] * count,
        out_specs=[ANY] * count,
        scratch_shapes=[
            pltpu.SemaphoreType.DMA((count,)),
            pltpu.SemaphoreType.DMA((count, SPREAD_EDGES)),
            pltpu.SemaphoreType.DMA((count, SPREAD_EDGES)),
        ],
        compiler_params=pltpu.CompilerParams(collective_id=0, has_side_effects=True),
    )(*shards)


REDUCE = (
    ("Yp", 0, 2, 0, ()),
    ("Ym", 0, 2, 1, ()),
    ("Yp", 1, 2, 0, ()),
    ("Ym", 1, 2, 1, ()),
    ("X", 1, 3, 0, ()),
    ("Yp", 1, 1, 1, ()),
    ("X", 1, 1, 0, (2,)),
    ("Ym", 1, 3, 1, (3,)),
    ("Yp", 0, 1, "f", (0, 6)),
    ("Ym", 0, 3, "f", (1, 4)),
    ("X", 1, 0, "f", (5, 7)),
)
REDUCE_STAGES = ((0, 1, 2, 3, 4, 5), (6, 7), (8, 9, 10))
SHARD_ORDER = ((0, 2), (1, 2), (1, 3), (1, 1), (0, 1), (0, 3), (1, 0), (0, 0))
REDUCE_EDGES = 45


def reduce_kernel(*refs):
    count = len(SHAPES)
    terms, outs = refs[:count], refs[count : 2 * count]
    scratch = refs[2 * count :]
    totals = scratch[:count]
    wholes = scratch[count : 2 * count]
    parts = scratch[2 * count : 3 * count]
    quarters = scratch[3 * count : 4 * count]
    rounds, local_sem, send_sem, recv_sem = scratch[4 * count :]
    z, core, x, y = places()
    ids = peer_ids()
    mine = x * 4 + y

    def owner(column, step):
        return ((x + column) % 2) * 4 + (y + step) % 4

    def piece_rows(array, part):
        start, rows = part_rows(SHAPES[array], part)
        if array == SPREAD:
            start, rows = pl.multiple_of(z * (half_shape(SHAPES[array])[0] // 4) + start // 4, 16), rows // 4
        return start, rows

    def piece(array, edge):
        _, column, step, part, _ = REDUCE[edge]
        start, rows = piece_rows(array, part)
        return totals[array].at[owner(column, step), pl.ds(start, rows), :]

    def slot(array, edge):
        return parts[array].at[edge] if edge < 8 else wholes[array].at[edge - 8]

    def add(array, into, start, rows, source):
        @pl.loop(0, rows // 16)
        def _(index):
            offset = pl.multiple_of(index * 16, 16)
            at = pl.ds(pl.multiple_of(start + offset, 16), 16)
            totals[array][into, at, :] = (
                totals[array][into, at, :].astype(jnp.float32)
                + source[pl.ds(offset, 16), :].astype(jnp.float32)
            ).astype(jnp.bfloat16)

    def quarter(array, index):
        rows = half_shape(SHAPES[array])[0] // 4
        return pl.multiple_of(index * rows, 16), rows

    def out_view(array, index, which):
        start, rows = quarter(array, index)
        return outs[array].at[half_view(SHAPES[array], which, start, rows)]

    def copy(array, edge):
        if edge < 11:
            peer, source, target = REDUCE[edge][0], piece(array, edge), slot(array, edge)
        elif edge < 14:
            step = edge - 10
            peer = f"Z{step}"
            start, rows = quarter(array, (z + step) % 4)
            source = totals[array].at[mine, pl.ds(start, rows), :]
            target = quarters[array].at[step - 1]
        elif edge < 17:
            peer = f"Z{edge - 13}"
            start, rows = quarter(array, z)
            source = totals[array].at[mine, pl.ds(start, rows), :]
            target = out_view(array, z, core)
        elif edge < 21:
            peer = "C"
            at = (z + edge - 17) % 4
            source = target = out_view(array, at, core)
            if edge == 17:
                start, rows = quarter(array, z)
                source = totals[array].at[mine, pl.ds(start, rows), :]
        else:
            kind, shard = (edge - 21) // 8, (edge - 21) % 8
            away = (2, 1, 3)[kind]
            peer = ("Z1" if shard % 2 == 0 else "Z3", "Z1", "Z3")[kind]
            start, rows = quarter(array, (z + away) % 4)
            source = totals[array].at[owner(*SHARD_ORDER[shard]), pl.ds(start, rows), :]
            target = rounds.at[edge - 21]
        return pltpu.make_async_remote_copy(
            src_ref=source,
            dst_ref=target,
            send_sem=send_sem.at[array, edge],
            recv_sem=recv_sem.at[array, edge],
            device_id=ids[peer],
            device_id_type=MESH,
        )

    def wait_for(array, edge):
        if edge < 11:
            landed = slot(array, edge)
        elif edge < 14:
            landed = quarters[array].at[edge - 11]
        elif edge < 17:
            landed = out_view(array, (z + 4 - (edge - 13)) % 4, core)
        elif edge < 21:
            landed = out_view(array, (z + edge - 17) % 4, 1 - core)
        else:
            landed = rounds.at[edge - 21]
        pltpu.make_async_remote_copy(
            src_ref=landed,
            dst_ref=landed,
            send_sem=send_sem.at[array, edge],
            recv_sem=recv_sem.at[array, edge],
            device_id=ids["C"],
            device_id_type=MESH,
        ).wait_recv()

    def receive(array, edge):
        wait_for(array, edge)
        peer, column, step, part, _ = REDUCE[edge]
        column, step = seen_by_receiver(peer, column, step)
        start, rows = piece_rows(array, part)
        add(array, owner(column, step), start, rows, slot(array, edge))

    def receive_round(kind, shard):
        edge = 21 + 8 * kind + shard
        wait_for(SPREAD, edge)
        away = 0 if kind > 0 else (1 if shard % 2 == 0 else 3)
        start, rows = quarter(SPREAD, (z + away) % 4)
        add(SPREAD, owner(*SHARD_ORDER[shard]), start, rows, rounds.at[edge - 21])

    def stage(array, number):
        for edge in REDUCE_STAGES[number]:
            for earlier in REDUCE[edge][4]:
                receive(array, earlier)
            copy(array, edge).start()

    plain = [array for array in range(count) if array != SPREAD]
    loads = [
        pltpu.make_async_copy(terms[array], totals[array], local_sem.at[array])
        for array in range(count)
    ]
    for load in loads:
        load.start()
    greet(ids, ("X", "Yp", "Ym", "C", "Z1", "Z2", "Z3"))
    loads[SPREAD].wait()
    for shard in range(SHARDS):
        copy(SPREAD, 21 + shard).start()
    for array in plain:
        loads[array].wait()
        stage(array, 0)
    for shard in range(SHARDS):
        receive_round(0, shard)
        copy(SPREAD, 29 + shard).start()
        copy(SPREAD, 37 + shard).start()
    for array in plain:
        stage(array, 1)
    for shard in range(4):
        receive_round(1, shard)
        receive_round(2, shard)
    stage(SPREAD, 0)
    for shard in range(4, SHARDS):
        receive_round(1, shard)
        receive_round(2, shard)
    for array in plain:
        stage(array, 2)
    stage(SPREAD, 1)
    stage(SPREAD, 2)
    for array in plain:
        for edge in (8, 9, 10):
            receive(array, edge)
        for edge in (11, 12, 13):
            copy(array, edge).start()
    for edge in (8, 9, 10):
        receive(SPREAD, edge)
    stores = []
    for array in range(count):
        start, rows = quarter(array, z)
        for edge in (11, 12, 13) if array != SPREAD else ():
            wait_for(array, edge)
            add(array, mine, start, rows, quarters[array].at[edge - 11])
        for edge in (14, 15, 16, 17):
            copy(array, edge).start()
        store = pltpu.make_async_copy(
            totals[array].at[mine, pl.ds(start, rows), :],
            out_view(array, z, core),
            local_sem.at[array],
        )
        store.start()
        stores.append(store)
    for array in range(count):
        for edge in (14, 15, 16):
            wait_for(array, edge)
            copy(array, 17 + (17 - edge)).start()
    for array in range(count):
        for edge in range(17, 21):
            wait_for(array, edge)
        for edge in range(REDUCE_EDGES):
            if (edge not in (11, 12, 13)) if array == SPREAD else (edge < 21):
                copy(array, edge).wait_send()
        stores[array].wait()


def reduce_gradients(terms):
    count = len(SHAPES)
    halves = [half_shape(shape) for shape in SHAPES]
    pieces = [
        (half[0] // 4, half[1]) if array == SPREAD else half for array, half in enumerate(halves)
    ]
    return pl.pallas_call(
        reduce_kernel,
        name="reduce_gradients",
        out_shape=[
            jax.ShapeDtypeStruct((rows, columns), jnp.bfloat16) for rows, columns, _ in SHAPES
        ],
        in_specs=[ANY] * count,
        out_specs=[ANY] * count,
        scratch_shapes=[pltpu.VMEM((SHARDS,) + half, jnp.bfloat16) for half in halves]
        + [pltpu.VMEM((3, half[0], half[1]), jnp.bfloat16) for half in pieces]
        + [pltpu.VMEM((8, half[0] // 2, half[1]), jnp.bfloat16) for half in pieces]
        + [pltpu.VMEM((3, half[0] // 4, half[1]), jnp.bfloat16) for half in halves]
        + [
            pltpu.VMEM((3 * SHARDS,) + pieces[SPREAD], jnp.bfloat16),
            pltpu.SemaphoreType.DMA((count,)),
            pltpu.SemaphoreType.DMA((count, REDUCE_EDGES)),
            pltpu.SemaphoreType.DMA((count, REDUCE_EDGES)),
        ],
        compiler_params=pltpu.CompilerParams(
            collective_id=1, has_side_effects=True, vmem_limit_bytes=48 * 2**20
        ),
    )(*terms)


TOKENS = 1024
LOCAL = TOKENS // SHARDS
SLOTS = 2
BLOCK = 256
PAIR = 2 * HEAD_WIDTH
NEGATIVE = -1e30


def two_groups(device):
    return (device == 1) | (device == 4)


def group_lanes(device, which):
    return pl.ds(pl.multiple_of(((2 * device) // 3 + which) * PAIR, PAIR), PAIR)


def pair_lanes(device):
    return pl.ds(pl.multiple_of(device * PAIR, PAIR), PAIR)


def token_rows(device):
    return pl.ds(pl.multiple_of(device * LOCAL, LOCAL), LOCAL)


def ring(me):
    return [(step, (me + step) % SHARDS, (me + SHARDS - step) % SHARDS) for step in range(1, SHARDS)]


def greet_all(me):
    barrier = pltpu.get_barrier_semaphore()
    for _, target, _ in ring(me):
        pl.semaphore_signal(barrier, inc=1, device_id={"fsdp": target}, device_id_type=MESH)
    pl.semaphore_wait(barrier, SHARDS - 1)


def sent(source, target, send_sem, recv_sem, device):
    return pltpu.make_async_remote_copy(
        src_ref=source,
        dst_ref=target,
        send_sem=send_sem,
        recv_sem=recv_sem,
        device_id={"fsdp": device},
        device_id_type=MESH,
    )


def causal_mask(values):
    length = values.shape[1]
    row = lax.broadcasted_iota(jnp.int32, (BLOCK, BLOCK), 0)
    column = lax.broadcasted_iota(jnp.int32, (BLOCK, BLOCK), 1)
    own = jnp.where(column <= row, values[:, length - BLOCK :], NEGATIVE)
    if length == BLOCK:
        return own
    return jnp.concatenate([values[:, : length - BLOCK], own], 1)


def dot_t(left, right):
    return lax.dot_general(
        left, right, (((1,), (1,)), ((), ())), preferred_element_type=jnp.float32
    )


def dot_first(left, right):
    return lax.dot_general(
        left, right, (((0,), (0,)), ((), ())), preferred_element_type=jnp.float32
    )


def attend_kernel(
    q_ref, kv_ref, mixed_ref, q_kept, kv_kept, lse_kept,
    q_all, kv_all, lse_all, mixed_all, local_sem, send_sem, recv_sem,
):
    me = lax.axis_index("fsdp")
    both = two_groups(me)
    second = jnp.where(both, 1, 0)

    def incoming(slot, step, device, sender):
        rows = token_rows(sender)
        return [
            sent(
                q_ref.at[slot, :, pair_lanes(device)], q_all.at[slot, rows, :],
                send_sem.at[0, slot, step], recv_sem.at[0, slot, step], device,
            ),
            sent(
                kv_ref.at[slot, :, group_lanes(device, 0)], kv_all.at[0, slot, rows, :],
                send_sem.at[1, slot, step], recv_sem.at[1, slot, step], device,
            ),
        ]

    def extra(slot, step, device, sender):
        group = jnp.where(two_groups(device), 1, 0)
        return sent(
            kv_ref.at[slot, :, group_lanes(device, group)], kv_all.at[1, slot, token_rows(sender), :],
            send_sem.at[2, slot, step], recv_sem.at[2, slot, step], device,
        )

    def outgoing(slot, step, device, sender):
        return sent(
            mixed_all.at[slot, token_rows(device), :], mixed_ref.at[slot, :, pair_lanes(sender)],
            send_sem.at[3, slot, step], recv_sem.at[3, slot, step], device,
        )

    def own_copies(slot):
        rows = token_rows(me)
        group = jnp.where(both, 1, 0)
        return [
            pltpu.make_async_copy(
                q_ref.at[slot, :, pair_lanes(me)], q_all.at[slot, rows, :], local_sem.at[0, slot]
            ),
            pltpu.make_async_copy(
                kv_ref.at[slot, :, group_lanes(me, 0)], kv_all.at[0, slot, rows, :],
                local_sem.at[1, slot],
            ),
            pltpu.make_async_copy(
                kv_ref.at[slot, :, group_lanes(me, group)], kv_all.at[1, slot, rows, :],
                local_sem.at[2, slot],
            ),
        ]

    def own_result(slot):
        return pltpu.make_async_copy(
            mixed_all.at[slot, token_rows(me), :], mixed_ref.at[slot, :, pair_lanes(me)],
            local_sem.at[3, slot],
        )

    greet_all(me)
    for slot in range(SLOTS):
        for step, target, _ in ring(me):
            for copy in incoming(slot, step, target, me):
                copy.start()

            @pl.when(two_groups(target))
            def _():
                extra(slot, step, target, me).start()

        for copy in own_copies(slot):
            copy.start()

    @pl.loop(0, SLOTS)
    def _(slot):
        for step, _, source in ring(me):
            for copy in incoming(slot, step, source, source):
                copy.wait_recv()

            @pl.when(both)
            def _():
                extra(slot, step, source, source).wait_recv()

        for copy in own_copies(slot):
            copy.wait()
        for block in range(TOKENS // BLOCK):
            rows = pl.ds(block * BLOCK, BLOCK)
            length = (block + 1) * BLOCK
            outs, totals = [], []
            for head in range(2):
                group = 0 if head == 0 else second
                lanes = slice(head * HEAD_WIDTH, (head + 1) * HEAD_WIDTH)
                query = q_all[slot, rows, lanes]
                keys = kv_all[group, slot, :length, :HEAD_WIDTH]
                values = kv_all[group, slot, :length, HEAD_WIDTH:]
                scores = causal_mask(dot_t(query, keys))
                highest = jnp.max(scores, -1, keepdims=True)
                weights = jnp.exp(scores - highest)
                total = jnp.sum(weights, -1, keepdims=True)
                out = jnp.dot(
                    weights.astype(jnp.bfloat16), values, preferred_element_type=jnp.float32
                )
                outs.append(out / total)
                totals.append(
                    jnp.broadcast_to(highest + jnp.log(total), (BLOCK, HEAD_WIDTH))
                )
            mixed_all[slot, rows, :] = jnp.concatenate(outs, 1).astype(jnp.bfloat16)
            lse_all[slot, rows, :] = jnp.concatenate(totals, 1)
        for step, target, _ in ring(me):
            outgoing(slot, step, target, me).start()
        own_result(slot).start()

    keep = [
        pltpu.make_async_copy(q_all, q_kept, local_sem.at[4, 0]),
        pltpu.make_async_copy(kv_all, kv_kept, local_sem.at[4, 1]),
        pltpu.make_async_copy(lse_all, lse_kept, local_sem.at[5, 0]),
    ]
    for copy in keep:
        copy.start()
    for slot in range(SLOTS):
        for step, target, source in ring(me):
            outgoing(slot, step, source, source).wait_recv()
            outgoing(slot, step, target, me).wait_send()
            for copy in incoming(slot, step, target, me):
                copy.wait_send()

            @pl.when(two_groups(target))
            def _():
                extra(slot, step, target, me).wait_send()

        own_result(slot).wait()
    for copy in keep:
        copy.wait()


Q_ALL = (SLOTS, TOKENS, PAIR)
KV_ALL = (2, SLOTS, TOKENS, PAIR)
FULL = SHARDS * PAIR


def attend(query_rows, key_values):
    bf16 = jnp.bfloat16
    return pl.pallas_call(
        attend_kernel,
        name="attend",
        out_shape=[
            jax.ShapeDtypeStruct((SLOTS, LOCAL, FULL), bf16),
            jax.ShapeDtypeStruct(Q_ALL, bf16),
            jax.ShapeDtypeStruct(KV_ALL, bf16),
            jax.ShapeDtypeStruct(Q_ALL, jnp.float32),
        ],
        in_specs=[ANY] * 2,
        out_specs=[ANY] * 4,
        scratch_shapes=[
            pltpu.VMEM(Q_ALL, bf16),
            pltpu.VMEM(KV_ALL, bf16),
            pltpu.VMEM(Q_ALL, jnp.float32),
            pltpu.VMEM(Q_ALL, bf16),
            pltpu.SemaphoreType.DMA((6, SLOTS)),
            pltpu.SemaphoreType.DMA((4, SLOTS, SHARDS)),
            pltpu.SemaphoreType.DMA((4, SLOTS, SHARDS)),
        ],
        compiler_params=pltpu.CompilerParams(
            collective_id=2, has_side_effects=True, vmem_limit_bytes=40 * 2**20
        ),
    )(query_rows, key_values)


def attend_back_kernel(
    slope_ref, q_ref, kv_ref, lse_ref, dq_ref, dkv_ref, dkv_extra_ref,
    slope_all, q_all, kv_all, lse_all, dq_all, dkv_total, dkv_all,
    local_sem, send_sem, recv_sem,
):
    me = lax.axis_index("fsdp")
    both = two_groups(me)
    second = jnp.where(both, 1, 0)
    extra_at = me // 4

    def incoming(slot, step, device, sender):
        return sent(
            slope_ref.at[slot, :, pair_lanes(device)], slope_all.at[slot, token_rows(sender), :],
            send_sem.at[0, slot, step], recv_sem.at[0, slot, step], device,
        )

    def outgoing(slot, step, device, sender):
        rows = token_rows(device)
        return [
            sent(
                dq_all.at[slot, rows, :], dq_ref.at[slot, :, pair_lanes(sender)],
                send_sem.at[1, slot, step], recv_sem.at[1, slot, step], device,
            ),
            sent(
                dkv_all.at[0, slot, rows, :], dkv_ref.at[sender, slot],
                send_sem.at[2, slot, step], recv_sem.at[2, slot, step], device,
            ),
        ]

    def extra(slot, step, device, sender):
        return sent(
            dkv_all.at[1, slot, token_rows(device), :], dkv_extra_ref.at[sender // 4, slot],
            send_sem.at[3, slot, step], recv_sem.at[3, slot, step], device,
        )

    def own_slope(slot):
        return pltpu.make_async_copy(
            slope_ref.at[slot, :, pair_lanes(me)], slope_all.at[slot, token_rows(me), :],
            local_sem.at[0, slot],
        )

    def own_results(slot):
        rows = token_rows(me)
        return [
            pltpu.make_async_copy(
                dq_all.at[slot, rows, :], dq_ref.at[slot, :, pair_lanes(me)], local_sem.at[1, slot]
            ),
            pltpu.make_async_copy(
                dkv_all.at[0, slot, rows, :], dkv_ref.at[me, slot], local_sem.at[2, slot]
            ),
        ]

    def own_extra(slot):
        return pltpu.make_async_copy(
            dkv_all.at[1, slot, token_rows(me), :], dkv_extra_ref.at[extra_at, slot],
            local_sem.at[3, slot],
        )

    loads = [
        pltpu.make_async_copy(q_ref, q_all, local_sem.at[4, 0]),
        pltpu.make_async_copy(kv_ref, kv_all, local_sem.at[4, 1]),
        pltpu.make_async_copy(lse_ref, lse_all, local_sem.at[5, 0]),
    ]
    for copy in loads:
        copy.start()
    greet_all(me)
    for slot in range(SLOTS):
        for step, target, _ in ring(me):
            incoming(slot, step, target, me).start()
        own_slope(slot).start()
    for copy in loads:
        copy.wait()

    @pl.loop(0, SLOTS)
    def _(slot):
        for step, _, source in ring(me):
            incoming(slot, step, source, source).wait_recv()
        own_slope(slot).wait()
        dkv_total[...] = jnp.zeros_like(dkv_total)
        for block in range(TOKENS // BLOCK):
            rows = pl.ds(block * BLOCK, BLOCK)
            length = (block + 1) * BLOCK
            outs = []
            for head in range(2):
                group = 0 if head == 0 else second
                lanes = slice(head * HEAD_WIDTH, (head + 1) * HEAD_WIDTH)
                query = q_all[slot, rows, lanes]
                slope = slope_all[slot, rows, lanes]
                lse = lse_all[slot, rows, head * HEAD_WIDTH : head * HEAD_WIDTH + 1]
                keys = kv_all[group, slot, :length, :HEAD_WIDTH]
                values = kv_all[group, slot, :length, HEAD_WIDTH:]
                probs = jnp.exp(causal_mask(dot_t(query, keys)) - lse)
                prob_slope = dot_t(slope, values)
                inner = jnp.sum(probs * prob_slope, -1, keepdims=True)
                score_slope = (probs * (prob_slope - inner)).astype(jnp.bfloat16)
                outs.append(
                    jnp.dot(score_slope, keys, preferred_element_type=jnp.float32)
                    * HEAD_WIDTH ** (-0.5)
                )
                dkv_total[group, :length, :] += jnp.concatenate(
                    [dot_first(score_slope, query), dot_first(probs.astype(jnp.bfloat16), slope)], 1
                )
            dq_all[slot, rows, :] = jnp.concatenate(outs, 1).astype(jnp.bfloat16)
        dkv_all[0, slot] = dkv_total[0].astype(jnp.bfloat16)
        dkv_all[1, slot] = dkv_total[1].astype(jnp.bfloat16)
        for step, target, _ in ring(me):
            for copy in outgoing(slot, step, target, me):
                copy.start()

            @pl.when(both)
            def _():
                extra(slot, step, target, me).start()

        for copy in own_results(slot):
            copy.start()

        @pl.when(both)
        def _():
            own_extra(slot).start()

    for slot in range(SLOTS):
        for step, target, source in ring(me):
            incoming(slot, step, target, me).wait_send()
            for copy in outgoing(slot, step, source, source):
                copy.wait_recv()
            for copy in outgoing(slot, step, target, me):
                copy.wait_send()

            @pl.when(two_groups(source))
            def _():
                extra(slot, step, source, source).wait_recv()

            @pl.when(both)
            def _():
                extra(slot, step, target, me).wait_send()

        for copy in own_results(slot):
            copy.wait()

        @pl.when(both)
        def _():
            own_extra(slot).wait()


def attend_back(slope, kept):
    bf16 = jnp.bfloat16
    return pl.pallas_call(
        attend_back_kernel,
        name="attend_back",
        out_shape=[
            jax.ShapeDtypeStruct((SLOTS, LOCAL, FULL), bf16),
            jax.ShapeDtypeStruct((SHARDS, SLOTS, LOCAL, PAIR), bf16),
            jax.ShapeDtypeStruct((2, SLOTS, LOCAL, PAIR), bf16),
        ],
        in_specs=[ANY] * 4,
        out_specs=[ANY] * 3,
        scratch_shapes=[
            pltpu.VMEM(Q_ALL, bf16),
            pltpu.VMEM(Q_ALL, bf16),
            pltpu.VMEM(KV_ALL, bf16),
            pltpu.VMEM(Q_ALL, jnp.float32),
            pltpu.VMEM(Q_ALL, bf16),
            pltpu.VMEM((2, TOKENS, PAIR), jnp.float32),
            pltpu.VMEM(KV_ALL, bf16),
            pltpu.SemaphoreType.DMA((6, SLOTS)),
            pltpu.SemaphoreType.DMA((4, SLOTS, SHARDS)),
            pltpu.SemaphoreType.DMA((4, SLOTS, SHARDS)),
        ],
        compiler_params=pltpu.CompilerParams(
            collective_id=3, has_side_effects=True, vmem_limit_bytes=48 * 2**20
        ),
    )(slope, *kept)


def rotary_tables(positions):
    half = HEAD_WIDTH // 2
    frequency = BASE ** (-(jnp.arange(half).astype(jnp.float32) * (2.0 / HEAD_WIDTH)))
    angle = positions.astype(jnp.float32)[..., None] * frequency
    cosine_table = jnp.cos(angle)
    sine_table = jnp.sin(angle)
    return (
        jnp.concatenate([cosine_table, cosine_table], -1)[..., None, :],
        jnp.concatenate([sine_table, sine_table], -1)[..., None, :],
    )


def apply_rotation(values, cosine_table, sine_table):
    half = values.shape[-1] // 2
    turned = jnp.concatenate([-values[..., half:], values[..., :half]], -1)
    return values * cosine_table + turned * sine_table


def reverse_rotation(values, cosine_table, sine_table):
    half = values.shape[-1] // 2
    shifted = values * sine_table
    turned = jnp.concatenate([-shifted[..., half:], shifted[..., :half]], -1)
    return values * cosine_table - turned


def normed(values, gain):
    return values * lax.rsqrt(jnp.mean(values * values, -1, keepdims=True) + EPSILON) * gain


def norm_backward(values, gain, upstream):
    row_scale = lax.rsqrt(jnp.mean(values * values, -1, keepdims=True) + EPSILON)
    unit = values * row_scale
    gain_slope = jnp.sum(upstream * unit, 0)
    inner = upstream * gain
    return (row_scale * (inner - unit * jnp.mean(inner * unit, -1, keepdims=True)), gain_slope)


def pad_shards(values):
    split = values.reshape(values.shape[0], SHARDS, ROWS)
    return jnp.pad(split, ((0, 0), (0, 0), (0, PADDED - ROWS))).reshape(values.shape[0], -1)


def unpad_shards(values):
    split = values.reshape(values.shape[0], SHARDS, PADDED)
    return split[:, :, :ROWS].reshape(values.shape[0], D)


def heads(values):
    return values.reshape(values.shape[:-1] + (-1, HEAD_WIDTH))


def forward_layer(layer_in, tables, weights):
    attend_in, attend_out, gate_up, down_weight, gains = weights
    batches, local_count = layer_in.shape[:2]
    rows = batches * local_count
    values = layer_in.reshape(rows, D).astype(jnp.float32)
    first_norm = pad_shards(normed(values, gains[0]).astype(jnp.bfloat16))
    projected = jnp.dot(first_norm, attend_in, preferred_element_type=jnp.float32)
    projected = projected.reshape(batches, local_count, QKV)
    rotated = apply_rotation(heads(projected[..., : QUERY_WIDTH + KEY_WIDTH]), *tables)
    query_rows = rotated[..., :QUERY_HEADS, :].astype(jnp.bfloat16) * HEAD_WIDTH ** (-0.5)
    query_rows = jnp.pad(
        query_rows.reshape(batches, local_count, QUERY_WIDTH), ((0, 0), (0, 0), (0, HEAD_WIDTH))
    )
    key_values = jnp.concatenate(
        [rotated[..., QUERY_HEADS:, :], heads(projected[..., QUERY_WIDTH + KEY_WIDTH :])], -1
    )
    key_values = key_values.astype(jnp.bfloat16).reshape(batches, local_count, 2 * KEY_WIDTH)
    mixed, *attended = attend(query_rows, key_values)
    mixed = mixed.reshape(rows, FULL)
    hidden = values + jnp.dot(mixed, attend_out, preferred_element_type=jnp.float32)
    second_norm = pad_shards(normed(hidden, gains[1]).astype(jnp.bfloat16))
    gated = jnp.dot(second_norm, gate_up, preferred_element_type=jnp.float32)
    act = (jax.nn.silu(gated[:, :FF]) * gated[:, FF:]).astype(jnp.bfloat16)
    result = hidden + jnp.dot(act, down_weight, preferred_element_type=jnp.float32)[:, :D]
    kept = (
        values,
        first_norm,
        attended,
        mixed,
        hidden,
        second_norm,
        gated,
        act,
    )
    return (result.astype(jnp.bfloat16).reshape(layer_in.shape), kept)


def backward_layer(upstream, kept, tables, weights):
    attend_in, attend_out, gate_up, down_weight, gains = weights
    (
        values,
        first_norm,
        attended,
        mixed,
        hidden,
        second_norm,
        gated,
        act,
    ) = kept
    batches, local_count = upstream.shape[:2]
    rows = batches * local_count
    upstream = upstream.reshape(rows, D)
    down_in = jnp.pad(upstream, ((0, 0), (0, DOWN_COLUMNS - D)))
    upstream = upstream.astype(jnp.float32)
    act_slope = jnp.einsum("td,fd->tf", down_in, down_weight, preferred_element_type=jnp.float32)
    gate_part = gated[:, :FF]
    up_part = gated[:, FF:]
    sigma = jax.nn.sigmoid(gate_part)
    gate_slope = act_slope * up_part * sigma * (1.0 + gate_part * (1.0 - sigma))
    up_slope = act_slope * gate_part * sigma
    gated_slope = jnp.concatenate([gate_slope, up_slope], 1).astype(jnp.bfloat16)
    second_slope = unpad_shards(
        jnp.einsum("tf,df->td", gated_slope, gate_up, preferred_element_type=jnp.float32)
    )
    hidden_part, second_gain = norm_backward(hidden, gains[1], second_slope)
    hidden_slope = upstream + hidden_part
    branch_slope = hidden_slope.astype(jnp.bfloat16)
    mixed_gradient = jnp.einsum(
        "td,qd->tq", branch_slope, attend_out, preferred_element_type=jnp.float32
    ).astype(jnp.bfloat16)
    query_slope, pair_slopes, extra_slopes = attend_back(
        mixed_gradient.reshape(batches, local_count, FULL), attended
    )
    pair_slopes = pair_slopes.astype(jnp.float32)
    extra_slopes = extra_slopes.astype(jnp.float32)
    group_slopes = jnp.stack(
        [
            pair_slopes[0] + pair_slopes[1],
            extra_slopes[0] + pair_slopes[2],
            pair_slopes[3] + pair_slopes[4],
            extra_slopes[1] + pair_slopes[5],
            pair_slopes[6] + pair_slopes[7],
        ],
        2,
    )
    query_slope = query_slope[..., :QUERY_WIDTH].astype(jnp.float32)
    query_raw = reverse_rotation(
        query_slope.reshape(batches, local_count, QUERY_HEADS, HEAD_WIDTH), *tables
    ).reshape(rows, QUERY_WIDTH)
    unrotated_key = reverse_rotation(group_slopes[..., :HEAD_WIDTH], *tables)
    projected_slope = jnp.concatenate(
        [
            query_raw,
            unrotated_key.reshape(rows, KEY_WIDTH),
            group_slopes[..., HEAD_WIDTH:].reshape(rows, KEY_WIDTH),
        ],
        1,
    ).astype(jnp.bfloat16)
    first_slope = unpad_shards(
        jnp.einsum("tf,df->td", projected_slope, attend_in, preferred_element_type=jnp.float32)
    )
    input_part, first_gain = norm_backward(values, gains[0], first_slope)
    input_slope = hidden_slope + input_part
    slopes = (projected_slope, branch_slope, gated_slope, down_in)
    return (
        input_slope.reshape(batches, local_count, D),
        slopes,
        jnp.stack([first_gain, second_gain]),
    )


def passed_along(value, steps):
    return lax.ppermute(value, "section", [(0, 1)] if steps > 0 else [(1, 0)])


def with_other_core(value):
    size = lax.axis_size("dp")
    other = lax.ppermute(value, "dp", [(index, index ^ 1) for index in range(size)])
    return other


def weight_terms(kept, slopes, gain_slopes):
    core = lax.axis_index("dp") % 2
    first_norm, mixed, second_norm, act = (kept[1], kept[3], kept[5], kept[7])
    mixed = pad_shards(mixed[:, :QUERY_WIDTH])
    projected_slope, branch_slope, gated_slope, down_in = slopes
    tokens = act.shape[0]

    def halved(values, axis):
        extent = values.shape[axis] // 2
        keep = lax.dynamic_slice_in_dim(values, core * extent, extent, axis)
        send = lax.dynamic_slice_in_dim(values, (1 - core) * extent, extent, axis)
        return jnp.concatenate([keep, with_other_core(send)], 0)

    def whole(values):
        return jnp.concatenate([values, with_other_core(values)], 0)

    def term(left, right):
        split = left.reshape(2 * tokens, SHARDS, -1)
        return jnp.einsum(
            "tkr,tn->krn", split, right, preferred_element_type=jnp.float32
        ).astype(jnp.bfloat16)

    in_rows = halved(first_norm.reshape(tokens, SHARDS, PADDED), 2)
    out_rows = halved(mixed.reshape(tokens, SHARDS, PADDED), 2)
    in_term = term(in_rows, whole(projected_slope))
    gains = (gain_slopes + with_other_core(gain_slopes)).reshape(2, SHARDS, ROWS).swapaxes(0, 1)
    spare = PADDED // 2 - (PADDED - ROWS)
    in_term = in_term.at[:, spare : spare + 2, :ROWS].add(
        jnp.where(core == 1, gains, 0.0).astype(jnp.bfloat16)
    )
    return (
        term(whole(second_norm), halved(gated_slope, 1)),
        term(whole(act), halved(down_in, 1)),
        in_term,
        term(out_rows, whole(branch_slope)),
    )


def body(
    inputs, positions, plan, attend_in, attend_out, gate_up, down_weight, norm_gains, cotangent
):
    section_index = lax.axis_index("section")
    extra = PADDED - ROWS
    in_shard = jnp.concatenate(
        [
            attend_in[0],
            jnp.pad(norm_gains[0], ((0, extra - 2), (0, QKV - ROWS))),
        ],
        0,
    )
    gathered = gather_weights(
        (
            jnp.pad(gate_up[0], ((0, extra), (0, 0))),
            jnp.pad(down_weight[0], ((0, 0), (0, DOWN_COLUMNS - D))),
            in_shard,
            jnp.pad(attend_out[0], ((0, extra), (0, 0))),
        )
    )
    gains = gathered[2][:, ROWS : ROWS + 2, :ROWS].swapaxes(0, 1).reshape(2, D)
    weights = (
        gathered[2].reshape(-1, QKV),
        jnp.pad(gathered[3][:, :ROWS].reshape(QUERY_WIDTH, D), ((0, FULL - QUERY_WIDTH), (0, 0))),
        gathered[0].reshape(-1, 2 * FF),
        gathered[1].reshape(-1, DOWN_COLUMNS),
        gains.astype(jnp.float32),
    )
    plan_row = plan[0]
    fresh = jnp.take(inputs[:, 0], plan_row, axis=0)
    tables = rotary_tables(jnp.take(positions[:, 0], plan_row, axis=0))
    given = cotangent[:, 0]
    result, _ = forward_layer(fresh, tables, weights)
    layer_in = jnp.where(section_index == 0, fresh, passed_along(result, 1))
    outputs, kept = forward_layer(layer_in, tables, weights)
    input_slope, _, _ = backward_layer(given, kept, tables, weights)
    back = passed_along(input_slope.astype(jnp.bfloat16), -1)
    upstream = jnp.where(section_index == 1, given, back)
    input_slope, slopes, gain_slopes = backward_layer(upstream, kept, tables, weights)
    reported = jnp.where(
        section_index == 0, input_slope, input_slope.astype(jnp.bfloat16).astype(jnp.float32)
    )
    input_slopes = jnp.take(reported, plan_row, axis=0)
    summed = reduce_gradients(weight_terms(kept, slopes, gain_slopes))
    full = [value.astype(jnp.float32) for value in summed]
    return (
        outputs[None, :, None],
        input_slopes[None, :, None],
        full[2][None, :ROWS],
        full[3][None, :ROWS],
        full[0][None, :ROWS],
        full[1][None, :, :D],
        full[2][None, ROWS : ROWS + 2, :ROWS],
    )


def solution(mesh):
    in_specs = (
        P(None, "dp", "fsdp", None),
        P(None, "dp", "fsdp"),
        P("dp", None),
        P("section", "fsdp", None),
        P("section", "fsdp", None),
        P("section", "fsdp", None),
        P("section", "fsdp", None),
        P("section", None, "fsdp"),
        P(None, "dp", "fsdp", None),
    )
    out_specs = (
        P("section", None, "dp", "fsdp", None),
        P("section", None, "dp", "fsdp", None),
        P("section", "fsdp", None),
        P("section", "fsdp", None),
        P("section", "fsdp", None),
        P("section", "fsdp", None),
        P("section", None, "fsdp"),
    )
    return jax.shard_map(body, mesh=mesh, in_specs=in_specs, out_specs=out_specs, check_vma=False)
```

```python
import functools

import jax
import jax.numpy as jnp
from jax import lax
from jax.experimental import pallas as pl
from jax.experimental.pallas import tpu as pltpu
from jax.sharding import PartitionSpec as P

D = 960
QUERY_HEADS = 15
KEY_VALUE_HEADS = 5
HEAD_WIDTH = 64
FF = 2560
QUERY_WIDTH = QUERY_HEADS * HEAD_WIDTH
KEY_WIDTH = KEY_VALUE_HEADS * HEAD_WIDTH
QKV = QUERY_WIDTH + 2 * KEY_WIDTH
SHARDS = 8
ROWS = D // SHARDS
PADDED = 128
DOWN_COLUMNS = 1024

EPSILON = 1e-05
BASE = 10000.0

MESH = pl.DeviceIdType.MESH
ANY = pl.BlockSpec(memory_space=pl.ANY)
VMEM = pl.BlockSpec(memory_space=pltpu.VMEM)

GATE_UP = (PADDED, 2 * FF, "columns")
DOWN = (FF // SHARDS, DOWN_COLUMNS, "columns")
ATTEND_IN = (PADDED, QKV, "rows")
ATTEND_OUT = (PADDED, D, "rows")
FEED_FORWARD = (GATE_UP, DOWN)
ATTENTION = (ATTEND_IN, ATTEND_OUT)


def half_shape(shape):
    rows, columns, kind = shape
    return (rows // 2, columns) if kind == "rows" else (rows, columns // 2)


def half_view(shape, core, start, count):
    rows, columns, kind = shape
    if kind == "rows":
        first = pl.multiple_of(core * (rows // 2) + start, 16)
        return (pl.ds(first, count), slice(None))
    first = pl.multiple_of(core * (columns // 2), 128)
    return (pl.ds(pl.multiple_of(start, 16), count), pl.ds(first, columns // 2))


def places():
    dp = lax.axis_index("dp")
    fsdp = lax.axis_index("fsdp")
    return dp // 2, dp % 2, fsdp // 4, fsdp % 4


def peer_ids():
    z, core, x, y = places()
    return {
        "X": {"fsdp": (1 - x) * 4 + y},
        "Yp": {"fsdp": x * 4 + (y + 1) % 4},
        "Ym": {"fsdp": x * 4 + (y + 3) % 4},
        "C": {"dp": z * 2 + 1 - core},
        "Z1": {"dp": ((z + 1) % 4) * 2 + core},
        "Z2": {"dp": ((z + 2) % 4) * 2 + core},
        "Z3": {"dp": ((z + 3) % 4) * 2 + core},
    }


def greet(ids, names):
    barrier = pltpu.get_barrier_semaphore()
    for name in names:
        pl.semaphore_signal(barrier, inc=1, device_id=ids[name], device_id_type=MESH)
    pl.semaphore_wait(barrier, len(names))


GATHER = (
    ("X", 0, 0, "f"),
    ("Yp", 0, 0, "f"),
    ("Ym", 0, 0, "f"),
    ("Ym", 0, 1, 0),
    ("X", 0, 1, 0),
    ("Yp", 0, 3, 1),
    ("X", 0, 3, 0),
    ("Yp", 1, 0, 1),
    ("Ym", 1, 0, 1),
    ("Ym", 1, 1, 0),
    ("Yp", 1, 3, 1),
)
GATHER_NEXT = {1: (5, 6), 2: (3, 4), 0: (7, 8), 4: (9,), 7: (10,)}
GATHER_STAGES = ((1, 2, 0), (4, 7, 3, 5, 6, 8), (9, 10))
GATHER_ORDER = (1, 2, 0, 4, 7, 3, 5, 6, 8, 9, 10)


def seen_by_receiver(peer, column, step):
    if peer == "X":
        return 1 - column, step
    if peer == "Yp":
        return column, (step + 3) % 4
    if peer == "Ym":
        return column, (step + 1) % 4
    return column, step


def part_rows(shape, part):
    rows = half_shape(shape)[0]
    return (0, rows) if part == "f" else (part * (rows // 2), rows // 2)


UPWARD = (0, 1, 3, 5, 7)
PLAIN_EDGES = 22
SPREAD_EDGES = 88


class Gather:
    def __init__(self, shapes, spread, shards, outs, sems):
        self.shapes, self.spread, self.shards, self.outs = shapes, spread, shards, outs
        self.local_sem, self.send_sem, self.recv_sem = sems
        self.z, self.core, self.x, self.y = places()
        self.ids = peer_ids()

    def owner(self, column, step):
        return ((self.x + column) % 2) * 4 + (self.y + step) % 4

    def index(self, array, part, which, plane):
        shape = self.shapes[array]
        start, rows = part_rows(shape, part)
        if array == self.spread:
            quarter = half_shape(shape)[0] // 4
            start, rows = plane * quarter + start // 4, rows // 4
        return half_view(shape, which, start, rows)

    def view(self, array, column, step, part, which, plane):
        return self.outs[array].at[
            (self.owner(column, step),) + self.index(array, part, which, plane)
        ]

    def received(self, edge):
        group, base = edge // 11, edge % 11
        peer, column, step, part = GATHER[base]
        column, step = seen_by_receiver(peer, column, step)
        return column, step, part, (0, 0, 3, 1, 2, 3, 1, 2)[group]

    def peer_of(self, edge):
        group, base = edge // 11, edge % 11
        if group == 0:
            return GATHER[base][0]
        if group in (1, 5, 6, 7):
            return "C"
        return {2: "Z1", 3: "Z3", 4: "Z1" if base in UPWARD else "Z3"}[group]

    def copy(self, array, edge):
        group, base = edge // 11, edge % 11
        if group == 0:
            _, column, step, part = GATHER[base]
            away = 0
        else:
            column, step, part, away = self.received(edge)
            if group in (2, 3):
                away = 0
            elif group == 4:
                away = 3 if base in UPWARD else 1
        target = source = self.view(array, column, step, part, self.core, (self.z + away) % 4)
        if group == 0 and (column, step) == (0, 0):
            source = self.shards[array].at[self.index(array, part, self.core, self.z)]
        return pltpu.make_async_remote_copy(
            src_ref=source,
            dst_ref=target,
            send_sem=self.send_sem.at[array, edge],
            recv_sem=self.recv_sem.at[array, edge],
            device_id=self.ids[self.peer_of(edge)],
            device_id_type=MESH,
        )

    def wait_for(self, array, edge):
        column, step, part, away = self.received(edge)
        which = 1 - self.core if edge // 11 in (1, 5, 6, 7) else self.core
        landed = self.view(array, column, step, part, which, (self.z + away) % 4)
        pltpu.make_async_remote_copy(
            src_ref=landed,
            dst_ref=landed,
            send_sem=self.send_sem.at[array, edge],
            recv_sem=self.recv_sem.at[array, edge],
            device_id=self.ids["C"],
            device_id_type=MESH,
        ).wait_recv()

    def own(self, array):
        return pltpu.make_async_copy(
            self.shards[array],
            self.outs[array].at[self.x * 4 + self.y],
            self.local_sem.at[array],
        )

    def start(self):
        for array in range(len(self.shapes)):
            for edge in (0, 1, 2):
                self.copy(array, edge).start()
            self.own(array).start()

    def within_plane(self, array, edges):
        for edge in edges:
            self.wait_for(array, edge)
            for later in GATHER_NEXT.get(edge, ()):
                self.copy(array, later).start()
            if array == self.spread:
                self.copy(array, 22 + edge).start()
                self.copy(array, 33 + edge).start()
            self.copy(array, 11 + edge).start()

    def round_z(self, edges):
        if self.spread is None:
            return
        for edge in edges:
            for group in (2, 3):
                self.wait_for(self.spread, 11 * group + edge)
                if (group == 2) == (edge in UPWARD):
                    self.copy(self.spread, 44 + edge).start()
                self.copy(self.spread, 11 * (group + 3) + edge).start()

    def steps(self):
        first, second, third = GATHER_STAGES
        arrays = range(len(self.shapes))
        steps = [functools.partial(self.within_plane, array, first) for array in arrays]
        steps.append(functools.partial(self.round_z, first))
        steps += [functools.partial(self.within_plane, array, second) for array in arrays]
        steps.append(functools.partial(self.round_z, second))
        steps += [functools.partial(self.within_plane, array, third) for array in arrays]
        steps.append(functools.partial(self.round_z, third))
        steps.append(self.finish)
        return steps

    def finish(self):
        if self.spread is not None:
            for edge in GATHER_ORDER:
                self.wait_for(self.spread, 44 + edge)
                self.copy(self.spread, 77 + edge).start()
        for array in range(len(self.shapes)):
            last = SPREAD_EDGES if array == self.spread else PLAIN_EDGES
            for edge in range(last):
                if edge // 11 in (1, 5, 6, 7):
                    self.wait_for(array, edge)
            for edge in range(last):
                self.copy(array, edge).wait_send()
            self.own(array).wait()

    @staticmethod
    def out_shapes(shapes):
        return [
            jax.ShapeDtypeStruct((SHARDS, rows, columns), jnp.bfloat16)
            for rows, columns, _ in shapes
        ]

    @staticmethod
    def scratch(shapes, spread):
        edges = PLAIN_EDGES if spread is None else SPREAD_EDGES
        return [
            pltpu.SemaphoreType.DMA((len(shapes),)),
            pltpu.SemaphoreType.DMA((len(shapes), edges)),
            pltpu.SemaphoreType.DMA((len(shapes), edges)),
        ]


def gather_kernel(shapes, *refs):
    count = len(shapes)
    gather = Gather(shapes, None, refs[:count], refs[count : 2 * count], refs[2 * count :])
    greet(gather.ids, ("X", "Yp", "Ym", "C"))
    gather.start()
    for step in gather.steps():
        step()


def gather_weights(shards):
    count = len(ATTENTION)
    return pl.pallas_call(
        functools.partial(gather_kernel, ATTENTION),
        name="gather_weights",
        out_shape=Gather.out_shapes(ATTENTION),
        in_specs=[VMEM] * count,
        out_specs=[ANY] * count,
        scratch_shapes=Gather.scratch(ATTENTION, None),
        compiler_params=pltpu.CompilerParams(collective_id=0, has_side_effects=True),
    )(*shards)


REDUCE = (
    ("Yp", 0, 2, 0, ()),
    ("Ym", 0, 2, 1, ()),
    ("Yp", 1, 2, 0, ()),
    ("Ym", 1, 2, 1, ()),
    ("X", 1, 3, 0, ()),
    ("Yp", 1, 1, 1, ()),
    ("X", 1, 1, 0, (2,)),
    ("Ym", 1, 3, 1, (3,)),
    ("Yp", 0, 1, "f", (0, 6)),
    ("Ym", 0, 3, "f", (1, 4)),
    ("X", 1, 0, "f", (5, 7)),
)
REDUCE_STAGES = ((0, 1, 2, 3, 4, 5), (6, 7), (8, 9, 10))
SHARD_ORDER = ((0, 2), (1, 2), (1, 3), (1, 1), (0, 1), (0, 3), (1, 0), (0, 0))
REDUCE_EDGES = 45


class Reduce:
    def __init__(self, shapes, spread, terms, outs, scratch):
        count = len(shapes)
        self.shapes, self.spread, self.terms, self.outs = shapes, spread, terms, outs
        self.totals = scratch[:count]
        self.wholes = scratch[count : 2 * count]
        self.parts = scratch[2 * count : 3 * count]
        self.quarters = scratch[3 * count : 4 * count]
        self.rounds = None if spread is None else scratch[4 * count]
        self.local_sem, self.send_sem, self.recv_sem = scratch[-3:]
        self.z, self.core, self.x, self.y = places()
        self.mine = self.x * 4 + self.y
        self.ids = peer_ids()
        self.plain = [array for array in range(count) if array != spread]

    @staticmethod
    def piece_shapes(shapes, spread):
        halves = [half_shape(shape) for shape in shapes]
        return halves, [
            (half[0], half[1] // 4) if array == spread else half
            for array, half in enumerate(halves)
        ]

    @staticmethod
    def out_shapes(shapes):
        return [jax.ShapeDtypeStruct((rows, columns), jnp.bfloat16) for rows, columns, _ in shapes]

    @staticmethod
    def scratch(shapes, spread):
        halves, pieces = Reduce.piece_shapes(shapes, spread)
        bf16 = jnp.bfloat16
        buffers = [pltpu.VMEM((SHARDS,) + half, bf16) for half in halves]
        buffers += [pltpu.VMEM((3,) + piece, bf16) for piece in pieces]
        buffers += [pltpu.VMEM((8, piece[0] // 2, piece[1]), bf16) for piece in pieces]
        buffers += [pltpu.VMEM((3, half[0] // 4, half[1]), bf16) for half in halves]
        if spread is not None:
            buffers.append(pltpu.VMEM((3 * SHARDS,) + pieces[spread], bf16))
        return buffers + [
            pltpu.SemaphoreType.DMA((len(shapes),)),
            pltpu.SemaphoreType.DMA((len(shapes), REDUCE_EDGES)),
            pltpu.SemaphoreType.DMA((len(shapes), REDUCE_EDGES)),
        ]

    def owner(self, column, step):
        return ((self.x + column) % 2) * 4 + (self.y + step) % 4

    def lanes(self, array, plane):
        columns = half_shape(self.shapes[array])[1]
        if array != self.spread:
            return pl.ds(0, columns)
        return pl.ds(pl.multiple_of(plane * (columns // 4), 128), columns // 4)

    def piece(self, array, edge):
        _, column, step, part, _ = REDUCE[edge]
        start, rows = part_rows(self.shapes[array], part)
        return self.totals[array].at[
            self.owner(column, step), pl.ds(start, rows), self.lanes(array, self.z)
        ]

    def slot(self, array, edge):
        return self.parts[array].at[edge] if edge < 8 else self.wholes[array].at[edge - 8]

    def add(self, array, into, start, rows, lanes, source):
        total = self.totals[array]

        @pl.loop(0, rows // 16)
        def _(index):
            offset = pl.multiple_of(index * 16, 16)
            at = pl.ds(pl.multiple_of(start + offset, 16), 16)
            total[into, at, lanes] = (
                total[into, at, lanes].astype(jnp.float32)
                + source[pl.ds(offset, 16), :].astype(jnp.float32)
            ).astype(jnp.bfloat16)

    def quarter(self, array, plane):
        rows = half_shape(self.shapes[array])[0]
        if array == self.spread:
            return 0, rows, self.lanes(array, plane)
        return pl.multiple_of(plane * (rows // 4), 16), rows // 4, self.lanes(array, plane)

    def summed(self, array, plane):
        start, rows, lanes = self.quarter(array, plane)
        return self.totals[array].at[self.mine, pl.ds(start, rows), lanes]

    def out_view(self, array, plane, which):
        shape = self.shapes[array]
        if array == self.spread:
            rows, columns = half_shape(shape)
            first = pl.multiple_of(which * columns + plane * (columns // 4), 128)
            return self.outs[array].at[pl.ds(0, rows), pl.ds(first, columns // 4)]
        start, rows, _ = self.quarter(array, plane)
        return self.outs[array].at[half_view(shape, which, start, rows)]

    def copy(self, array, edge):
        z = self.z
        if edge < 11:
            peer, source, target = REDUCE[edge][0], self.piece(array, edge), self.slot(array, edge)
        elif edge < 14:
            step = edge - 10
            peer, source = f"Z{step}", self.summed(array, (z + step) % 4)
            target = self.quarters[array].at[step - 1]
        elif edge < 17:
            peer, source = f"Z{edge - 13}", self.summed(array, z)
            target = self.out_view(array, z, self.core)
        elif edge < 21:
            peer = "C"
            source = target = self.out_view(array, (z + edge - 17) % 4, self.core)
            if edge == 17:
                source = self.summed(array, z)
        else:
            kind, shard = (edge - 21) // 8, (edge - 21) % 8
            peer = ("Z1" if shard % 2 == 0 else "Z3", "Z1", "Z3")[kind]
            lanes = self.lanes(array, (z + (2, 1, 3)[kind]) % 4)
            source = self.totals[array].at[self.owner(*SHARD_ORDER[shard]), :, lanes]
            target = self.rounds.at[edge - 21]
        return pltpu.make_async_remote_copy(
            src_ref=source,
            dst_ref=target,
            send_sem=self.send_sem.at[array, edge],
            recv_sem=self.recv_sem.at[array, edge],
            device_id=self.ids[peer],
            device_id_type=MESH,
        )

    def wait_for(self, array, edge):
        z = self.z
        if edge < 11:
            landed = self.slot(array, edge)
        elif edge < 14:
            landed = self.quarters[array].at[edge - 11]
        elif edge < 17:
            landed = self.out_view(array, (z + 4 - (edge - 13)) % 4, self.core)
        elif edge < 21:
            landed = self.out_view(array, (z + edge - 17) % 4, 1 - self.core)
        else:
            landed = self.rounds.at[edge - 21]
        pltpu.make_async_remote_copy(
            src_ref=landed,
            dst_ref=landed,
            send_sem=self.send_sem.at[array, edge],
            recv_sem=self.recv_sem.at[array, edge],
            device_id=self.ids["C"],
            device_id_type=MESH,
        ).wait_recv()

    def receive(self, array, edge):
        self.wait_for(array, edge)
        peer, column, step, part, _ = REDUCE[edge]
        column, step = seen_by_receiver(peer, column, step)
        start, rows = part_rows(self.shapes[array], part)
        lanes = self.lanes(array, self.z)
        self.add(array, self.owner(column, step), start, rows, lanes, self.slot(array, edge))

    def receive_round(self, kind, shard):
        edge = 21 + 8 * kind + shard
        array = self.spread
        self.wait_for(array, edge)
        away = 0 if kind > 0 else (1 if shard % 2 == 0 else 3)
        rows = half_shape(self.shapes[array])[0]
        lanes = self.lanes(array, (self.z + away) % 4)
        self.add(
            array, self.owner(*SHARD_ORDER[shard]), 0, rows, lanes, self.rounds.at[edge - 21]
        )

    def stage(self, array, number):
        for edge in REDUCE_STAGES[number]:
            for earlier in REDUCE[edge][4]:
                self.receive(array, earlier)
            self.copy(array, edge).start()

    def load(self, array):
        return pltpu.make_async_copy(
            self.terms[array], self.totals[array], self.local_sem.at[array]
        )

    def store(self, array):
        return pltpu.make_async_copy(
            self.summed(array, self.z), self.out_view(array, self.z, self.core),
            self.local_sem.at[array],
        )

    def start_loads(self):
        for array in range(len(self.shapes)):
            self.load(array).start()

    def start(self):
        if self.spread is not None:
            self.load(self.spread).wait()
            for shard in range(SHARDS):
                self.copy(self.spread, 21 + shard).start()
        for array in self.plain:
            self.load(array).wait()
            self.stage(array, 0)

    def first_round(self):
        for shard in range(SHARDS):
            self.receive_round(0, shard)
            self.copy(self.spread, 29 + shard).start()
            self.copy(self.spread, 37 + shard).start()

    def second_round(self, shards):
        for shard in shards:
            self.receive_round(1, shard)
            self.receive_round(2, shard)

    def end_plane(self, array):
        for edge in (8, 9, 10):
            self.receive(array, edge)
        for edge in (11, 12, 13) if array != self.spread else ():
            self.copy(array, edge).start()

    def end_z(self, array):
        if array != self.spread:
            start, rows, lanes = self.quarter(array, self.z)
            for edge in (11, 12, 13):
                self.wait_for(array, edge)
                self.add(
                    array, self.mine, start, rows, lanes, self.quarters[array].at[edge - 11]
                )
        for edge in (14, 15, 16, 17):
            self.copy(array, edge).start()
        self.store(array).start()

    def finish(self):
        for array in range(len(self.shapes)):
            for edge in (14, 15, 16):
                self.wait_for(array, edge)
                self.copy(array, 34 - edge).start()
        for array in range(len(self.shapes)):
            for edge in range(17, 21):
                self.wait_for(array, edge)
            for edge in range(REDUCE_EDGES):
                if (edge not in (11, 12, 13)) if array == self.spread else (edge < 21):
                    self.copy(array, edge).wait_send()
            self.store(array).wait()

    def steps(self):
        call = functools.partial
        steps = []
        if self.spread is not None:
            steps.append(self.first_round)
        steps += [call(self.stage, array, 1) for array in self.plain]
        if self.spread is not None:
            steps.append(call(self.second_round, range(4)))
            steps.append(call(self.stage, self.spread, 0))
            steps.append(call(self.second_round, range(4, SHARDS)))
            steps.append(call(self.stage, self.spread, 1))
        steps += [call(self.stage, array, 2) for array in self.plain]
        if self.spread is not None:
            steps.append(call(self.stage, self.spread, 2))
        steps += [call(self.end_plane, array) for array in self.plain]
        if self.spread is not None:
            steps.append(call(self.end_plane, self.spread))
            steps.append(call(self.end_z, self.spread))
        steps += [call(self.end_z, array) for array in self.plain]
        steps.append(self.finish)
        return steps


def reduce_kernel(shapes, *refs):
    count = len(shapes)
    reduce = Reduce(shapes, None, refs[:count], refs[count : 2 * count], refs[2 * count :])
    reduce.start_loads()
    greet(reduce.ids, ("X", "Yp", "Ym", "C", "Z1", "Z2", "Z3"))
    reduce.start()
    for step in reduce.steps():
        step()


def reduce_gradients(terms):
    count = len(ATTENTION)
    return pl.pallas_call(
        functools.partial(reduce_kernel, ATTENTION),
        name="reduce_gradients",
        out_shape=Reduce.out_shapes(ATTENTION),
        in_specs=[ANY] * count,
        out_specs=[ANY] * count,
        scratch_shapes=Reduce.scratch(ATTENTION, None),
        compiler_params=pltpu.CompilerParams(
            collective_id=1, has_side_effects=True, vmem_limit_bytes=48 * 2**20
        ),
    )(*terms)


TOKENS = 1024
LOCAL = TOKENS // SHARDS
SLOTS = 2
BLOCK = 256
PAIR = 2 * HEAD_WIDTH
NEGATIVE = -1e30


def two_groups(device):
    return (device == 1) | (device == 4)


def group_lanes(device, which):
    return pl.ds(pl.multiple_of(((2 * device) // 3 + which) * PAIR, PAIR), PAIR)


def pair_lanes(device):
    return pl.ds(pl.multiple_of(device * PAIR, PAIR), PAIR)


def token_rows(device):
    return pl.ds(pl.multiple_of(device * LOCAL, LOCAL), LOCAL)


def ring(me):
    return [(step, (me + step) % SHARDS, (me + SHARDS - step) % SHARDS) for step in range(1, SHARDS)]


def greet_all(me, others=()):
    barrier = pltpu.get_barrier_semaphore()
    ids = peer_ids()
    for device in [{"fsdp": target} for _, target, _ in ring(me)] + [ids[name] for name in others]:
        pl.semaphore_signal(barrier, inc=1, device_id=device, device_id_type=MESH)
    pl.semaphore_wait(barrier, SHARDS - 1 + len(others))


def sent(source, target, send_sem, recv_sem, device):
    return pltpu.make_async_remote_copy(
        src_ref=source,
        dst_ref=target,
        send_sem=send_sem,
        recv_sem=recv_sem,
        device_id={"fsdp": device},
        device_id_type=MESH,
    )


def causal_mask(values):
    length = values.shape[1]
    row = lax.broadcasted_iota(jnp.int32, (BLOCK, BLOCK), 0)
    column = lax.broadcasted_iota(jnp.int32, (BLOCK, BLOCK), 1)
    own = jnp.where(column <= row, values[:, length - BLOCK :], NEGATIVE)
    if length == BLOCK:
        return own
    return jnp.concatenate([values[:, : length - BLOCK], own], 1)


def dot_t(left, right):
    return lax.dot_general(
        left, right, (((1,), (1,)), ((), ())), preferred_element_type=jnp.float32
    )


def dot_first(left, right):
    return lax.dot_general(
        left, right, (((0,), (0,)), ((), ())), preferred_element_type=jnp.float32
    )


def attend_kernel(with_gather, *refs):
    count = len(FEED_FORWARD) if with_gather else 0
    q_ref, kv_ref, mixed_ref, q_kept, kv_kept, lse_kept = refs[:2] + refs[2 + count : 6 + count]
    q_all, kv_all, lse_all, mixed_all, local_sem, send_sem, recv_sem = refs[
        6 + 2 * count : 13 + 2 * count
    ]
    background = None
    if with_gather:
        background = Gather(
            FEED_FORWARD, 0, refs[2 : 2 + count], refs[6 + count : 6 + 2 * count], refs[-3:]
        )
    me = lax.axis_index("fsdp")
    both = two_groups(me)
    second = jnp.where(both, 1, 0)

    def incoming(slot, step, device, sender):
        rows = token_rows(sender)
        return [
            sent(
                q_ref.at[slot, :, pair_lanes(device)], q_all.at[slot, rows, :],
                send_sem.at[0, slot, step], recv_sem.at[0, slot, step], device,
            ),
            sent(
                kv_ref.at[slot, :, group_lanes(device, 0)], kv_all.at[0, slot, rows, :],
                send_sem.at[1, slot, step], recv_sem.at[1, slot, step], device,
            ),
        ]

    def extra(slot, step, device, sender):
        group = jnp.where(two_groups(device), 1, 0)
        return sent(
            kv_ref.at[slot, :, group_lanes(device, group)], kv_all.at[1, slot, token_rows(sender), :],
            send_sem.at[2, slot, step], recv_sem.at[2, slot, step], device,
        )

    def outgoing(slot, step, device, sender):
        return sent(
            mixed_all.at[slot, token_rows(device), :], mixed_ref.at[slot, :, pair_lanes(sender)],
            send_sem.at[3, slot, step], recv_sem.at[3, slot, step], device,
        )

    def own_copies(slot):
        rows = token_rows(me)
        group = jnp.where(both, 1, 0)
        return [
            pltpu.make_async_copy(
                q_ref.at[slot, :, pair_lanes(me)], q_all.at[slot, rows, :], local_sem.at[0, slot]
            ),
            pltpu.make_async_copy(
                kv_ref.at[slot, :, group_lanes(me, 0)], kv_all.at[0, slot, rows, :],
                local_sem.at[1, slot],
            ),
            pltpu.make_async_copy(
                kv_ref.at[slot, :, group_lanes(me, group)], kv_all.at[1, slot, rows, :],
                local_sem.at[2, slot],
            ),
        ]

    def own_result(slot):
        return pltpu.make_async_copy(
            mixed_all.at[slot, token_rows(me), :], mixed_ref.at[slot, :, pair_lanes(me)],
            local_sem.at[3, slot],
        )

    greet_all(me, ("C", "Z1", "Z3") if background else ())
    for slot in range(SLOTS):
        for step, target, _ in ring(me):
            for copy in incoming(slot, step, target, me):
                copy.start()

            @pl.when(two_groups(target))
            def _():
                extra(slot, step, target, me).start()

        for copy in own_copies(slot):
            copy.start()

    pending = []
    if background:
        background.start()
        pending = background.steps()

    def do_pending(number):
        for _ in range(min(number, len(pending))):
            pending.pop(0)()

    def work(slot):
        for step, _, source in ring(me):
            for copy in incoming(slot, step, source, source):
                copy.wait_recv()

            @pl.when(both)
            def _():
                extra(slot, step, source, source).wait_recv()

        for copy in own_copies(slot):
            copy.wait()
        if background and slot == 0:
            do_pending(1)
        for block in range(TOKENS // BLOCK):
            rows = pl.ds(block * BLOCK, BLOCK)
            length = (block + 1) * BLOCK
            outs, totals = [], []
            for head in range(2):
                group = 0 if head == 0 else second
                lanes = slice(head * HEAD_WIDTH, (head + 1) * HEAD_WIDTH)
                query = q_all[slot, rows, lanes]
                keys = kv_all[group, slot, :length, :HEAD_WIDTH]
                values = kv_all[group, slot, :length, HEAD_WIDTH:]
                scores = causal_mask(dot_t(query, keys))
                highest = jnp.max(scores, -1, keepdims=True)
                weights = jnp.exp(scores - highest)
                total = jnp.sum(weights, -1, keepdims=True)
                out = jnp.dot(
                    weights.astype(jnp.bfloat16), values, preferred_element_type=jnp.float32
                )
                outs.append(out / total)
                totals.append(
                    jnp.broadcast_to(highest + jnp.log(total), (BLOCK, HEAD_WIDTH))
                )
            mixed_all[slot, rows, :] = jnp.concatenate(outs, 1).astype(jnp.bfloat16)
            lse_all[slot, rows, :] = jnp.concatenate(totals, 1)
        for step, target, _ in ring(me):
            outgoing(slot, step, target, me).start()
        own_result(slot).start()

    if background:
        work(0)
        do_pending(3)
        work(1)
    else:
        pl.loop(0, SLOTS)(work)
    do_pending(len(pending))
    keep = [
        pltpu.make_async_copy(q_all, q_kept, local_sem.at[4, 0]),
        pltpu.make_async_copy(kv_all, kv_kept, local_sem.at[4, 1]),
        pltpu.make_async_copy(lse_all, lse_kept, local_sem.at[5, 0]),
    ]
    for copy in keep:
        copy.start()
    for slot in range(SLOTS):
        for step, target, source in ring(me):
            outgoing(slot, step, source, source).wait_recv()
            outgoing(slot, step, target, me).wait_send()
            for copy in incoming(slot, step, target, me):
                copy.wait_send()

            @pl.when(two_groups(target))
            def _():
                extra(slot, step, target, me).wait_send()

        own_result(slot).wait()
    for copy in keep:
        copy.wait()


Q_ALL = (SLOTS, TOKENS, PAIR)
KV_ALL = (2, SLOTS, TOKENS, PAIR)
FULL = SHARDS * PAIR


def attend(query_rows, key_values, shards=()):
    bf16 = jnp.bfloat16
    with_gather = bool(shards)
    return pl.pallas_call(
        functools.partial(attend_kernel, with_gather),
        name="attend_gather" if with_gather else "attend",
        out_shape=[
            jax.ShapeDtypeStruct((SLOTS, LOCAL, FULL), bf16),
            jax.ShapeDtypeStruct(Q_ALL, bf16),
            jax.ShapeDtypeStruct(KV_ALL, bf16),
            jax.ShapeDtypeStruct(Q_ALL, jnp.float32),
        ]
        + (Gather.out_shapes(FEED_FORWARD) if with_gather else []),
        in_specs=[ANY] * 2 + [VMEM] * len(shards),
        out_specs=[ANY] * (4 + len(shards)),
        scratch_shapes=[
            pltpu.VMEM(Q_ALL, bf16),
            pltpu.VMEM(KV_ALL, bf16),
            pltpu.VMEM(Q_ALL, jnp.float32),
            pltpu.VMEM(Q_ALL, bf16),
            pltpu.SemaphoreType.DMA((6, SLOTS)),
            pltpu.SemaphoreType.DMA((4, SLOTS, SHARDS)),
            pltpu.SemaphoreType.DMA((4, SLOTS, SHARDS)),
        ]
        + (Gather.scratch(FEED_FORWARD, 0) if with_gather else []),
        compiler_params=pltpu.CompilerParams(
            collective_id=4 if with_gather else 2,
            has_side_effects=True,
            vmem_limit_bytes=40 * 2**20,
        ),
    )(query_rows, key_values, *shards)


def attend_back_kernel(with_reduce, *refs):
    count = len(FEED_FORWARD) if with_reduce else 0
    slope_ref, q_ref, kv_ref, lse_ref = refs[:4]
    dq_ref, dkv_ref, dkv_extra_ref = refs[4 + count : 7 + count]
    scratch = refs[7 + 2 * count :]
    slope_all, q_all, kv_all, lse_all, dq_all, dkv_total, dkv_all = scratch[:7]
    local_sem, send_sem, recv_sem = scratch[7:10]
    background = None
    if with_reduce:
        background = Reduce(
            FEED_FORWARD, None, refs[4 : 4 + count], refs[7 + count : 7 + 2 * count], scratch[10:]
        )
    me = lax.axis_index("fsdp")
    both = two_groups(me)
    second = jnp.where(both, 1, 0)
    extra_at = me // 4

    def incoming(slot, step, device, sender):
        return sent(
            slope_ref.at[slot, :, pair_lanes(device)], slope_all.at[slot, token_rows(sender), :],
            send_sem.at[0, slot, step], recv_sem.at[0, slot, step], device,
        )

    def outgoing(slot, step, device, sender):
        rows = token_rows(device)
        return [
            sent(
                dq_all.at[slot, rows, :], dq_ref.at[slot, :, pair_lanes(sender)],
                send_sem.at[1, slot, step], recv_sem.at[1, slot, step], device,
            ),
            sent(
                dkv_all.at[0, slot, rows, :], dkv_ref.at[sender, slot],
                send_sem.at[2, slot, step], recv_sem.at[2, slot, step], device,
            ),
        ]

    def extra(slot, step, device, sender):
        return sent(
            dkv_all.at[1, slot, token_rows(device), :], dkv_extra_ref.at[sender // 4, slot],
            send_sem.at[3, slot, step], recv_sem.at[3, slot, step], device,
        )

    def own_slope(slot):
        return pltpu.make_async_copy(
            slope_ref.at[slot, :, pair_lanes(me)], slope_all.at[slot, token_rows(me), :],
            local_sem.at[0, slot],
        )

    def own_results(slot):
        rows = token_rows(me)
        return [
            pltpu.make_async_copy(
                dq_all.at[slot, rows, :], dq_ref.at[slot, :, pair_lanes(me)], local_sem.at[1, slot]
            ),
            pltpu.make_async_copy(
                dkv_all.at[0, slot, rows, :], dkv_ref.at[me, slot], local_sem.at[2, slot]
            ),
        ]

    def own_extra(slot):
        return pltpu.make_async_copy(
            dkv_all.at[1, slot, token_rows(me), :], dkv_extra_ref.at[extra_at, slot],
            local_sem.at[3, slot],
        )

    loads = [
        pltpu.make_async_copy(q_ref, q_all, local_sem.at[4, 0]),
        pltpu.make_async_copy(kv_ref, kv_all, local_sem.at[4, 1]),
        pltpu.make_async_copy(lse_ref, lse_all, local_sem.at[5, 0]),
    ]
    for copy in loads:
        copy.start()
    if background:
        background.start_loads()
    greet_all(me, ("C", "Z1", "Z2", "Z3") if background else ())
    for slot in range(SLOTS):
        for step, target, _ in ring(me):
            incoming(slot, step, target, me).start()
        own_slope(slot).start()
    pending = []
    if background:
        background.start()
        pending = background.steps()
    for copy in loads:
        copy.wait()

    def work(slot):
        for step, _, source in ring(me):
            incoming(slot, step, source, source).wait_recv()
        own_slope(slot).wait()
        dkv_total[...] = jnp.zeros_like(dkv_total)
        for block in range(TOKENS // BLOCK):
            rows = pl.ds(block * BLOCK, BLOCK)
            length = (block + 1) * BLOCK
            outs = []
            for head in range(2):
                group = 0 if head == 0 else second
                lanes = slice(head * HEAD_WIDTH, (head + 1) * HEAD_WIDTH)
                query = q_all[slot, rows, lanes]
                slope = slope_all[slot, rows, lanes]
                lse = lse_all[slot, rows, head * HEAD_WIDTH : head * HEAD_WIDTH + 1]
                keys = kv_all[group, slot, :length, :HEAD_WIDTH]
                values = kv_all[group, slot, :length, HEAD_WIDTH:]
                probs = jnp.exp(causal_mask(dot_t(query, keys)) - lse)
                prob_slope = dot_t(slope, values)
                inner = jnp.sum(probs * prob_slope, -1, keepdims=True)
                score_slope = (probs * (prob_slope - inner)).astype(jnp.bfloat16)
                outs.append(
                    jnp.dot(score_slope, keys, preferred_element_type=jnp.float32)
                    * HEAD_WIDTH ** (-0.5)
                )
                dkv_total[group, :length, :] += jnp.concatenate(
                    [dot_first(score_slope, query), dot_first(probs.astype(jnp.bfloat16), slope)], 1
                )
            dq_all[slot, rows, :] = jnp.concatenate(outs, 1).astype(jnp.bfloat16)
        dkv_all[0, slot] = dkv_total[0].astype(jnp.bfloat16)
        dkv_all[1, slot] = dkv_total[1].astype(jnp.bfloat16)
        for step, target, _ in ring(me):
            for copy in outgoing(slot, step, target, me):
                copy.start()

            @pl.when(both)
            def _():
                extra(slot, step, target, me).start()

        for copy in own_results(slot):
            copy.start()

        @pl.when(both)
        def _():
            own_extra(slot).start()

    if background:
        work(0)
        for step in pending[:2]:
            step()
        work(1)
        for step in pending[2:]:
            step()
    else:
        pl.loop(0, SLOTS)(work)

    for slot in range(SLOTS):
        for step, target, source in ring(me):
            incoming(slot, step, target, me).wait_send()
            for copy in outgoing(slot, step, source, source):
                copy.wait_recv()
            for copy in outgoing(slot, step, target, me):
                copy.wait_send()

            @pl.when(two_groups(source))
            def _():
                extra(slot, step, source, source).wait_recv()

            @pl.when(both)
            def _():
                extra(slot, step, target, me).wait_send()

        for copy in own_results(slot):
            copy.wait()

        @pl.when(both)
        def _():
            own_extra(slot).wait()


def attend_back(slope, kept, terms=()):
    bf16 = jnp.bfloat16
    with_reduce = bool(terms)
    return pl.pallas_call(
        functools.partial(attend_back_kernel, with_reduce),
        name="attend_back_reduce" if with_reduce else "attend_back",
        out_shape=[
            jax.ShapeDtypeStruct((SLOTS, LOCAL, FULL), bf16),
            jax.ShapeDtypeStruct((SHARDS, SLOTS, LOCAL, PAIR), bf16),
            jax.ShapeDtypeStruct((2, SLOTS, LOCAL, PAIR), bf16),
        ]
        + (Reduce.out_shapes(FEED_FORWARD) if with_reduce else []),
        in_specs=[ANY] * (4 + len(terms)),
        out_specs=[ANY] * (3 + len(terms)),
        scratch_shapes=[
            pltpu.VMEM(Q_ALL, bf16),
            pltpu.VMEM(Q_ALL, bf16),
            pltpu.VMEM(KV_ALL, bf16),
            pltpu.VMEM(Q_ALL, jnp.float32),
            pltpu.VMEM(Q_ALL, bf16),
            pltpu.VMEM((2, TOKENS, PAIR), jnp.float32),
            pltpu.VMEM(KV_ALL, bf16),
            pltpu.SemaphoreType.DMA((6, SLOTS)),
            pltpu.SemaphoreType.DMA((4, SLOTS, SHARDS)),
            pltpu.SemaphoreType.DMA((4, SLOTS, SHARDS)),
        ]
        + (Reduce.scratch(FEED_FORWARD, None) if with_reduce else []),
        compiler_params=pltpu.CompilerParams(
            collective_id=5 if with_reduce else 3,
            has_side_effects=True,
            vmem_limit_bytes=(56 if with_reduce else 48) * 2**20,
        ),
    )(slope, *kept, *terms)


def rotary_tables(positions):
    half = HEAD_WIDTH // 2
    frequency = BASE ** (-(jnp.arange(half).astype(jnp.float32) * (2.0 / HEAD_WIDTH)))
    angle = positions.astype(jnp.float32)[..., None] * frequency
    cosine_table = jnp.cos(angle)
    sine_table = jnp.sin(angle)
    return (
        jnp.concatenate([cosine_table, cosine_table], -1)[..., None, :],
        jnp.concatenate([sine_table, sine_table], -1)[..., None, :],
    )


def apply_rotation(values, cosine_table, sine_table):
    half = values.shape[-1] // 2
    turned = jnp.concatenate([-values[..., half:], values[..., :half]], -1)
    return values * cosine_table + turned * sine_table


def reverse_rotation(values, cosine_table, sine_table):
    half = values.shape[-1] // 2
    shifted = values * sine_table
    turned = jnp.concatenate([-shifted[..., half:], shifted[..., :half]], -1)
    return values * cosine_table - turned


def normed(values, gain):
    return values * lax.rsqrt(jnp.mean(values * values, -1, keepdims=True) + EPSILON) * gain


def norm_backward(values, gain, upstream):
    row_scale = lax.rsqrt(jnp.mean(values * values, -1, keepdims=True) + EPSILON)
    unit = values * row_scale
    gain_slope = jnp.sum(upstream * unit, 0)
    inner = upstream * gain
    return (row_scale * (inner - unit * jnp.mean(inner * unit, -1, keepdims=True)), gain_slope)


def pad_shards(values):
    split = values.reshape(values.shape[0], SHARDS, ROWS)
    return jnp.pad(split, ((0, 0), (0, 0), (0, PADDED - ROWS))).reshape(values.shape[0], -1)


def unpad_shards(values):
    split = values.reshape(values.shape[0], SHARDS, PADDED)
    return split[:, :, :ROWS].reshape(values.shape[0], D)


def heads(values):
    return values.reshape(values.shape[:-1] + (-1, HEAD_WIDTH))


def forward_layer(layer_in, tables, weights, shards=()):
    attend_in, attend_out, gate_up, down_weight, gains = weights
    batches, local_count = layer_in.shape[:2]
    rows = batches * local_count
    values = layer_in.reshape(rows, D).astype(jnp.float32)
    first_norm = pad_shards(normed(values, gains[0]).astype(jnp.bfloat16))
    projected = jnp.dot(first_norm, attend_in, preferred_element_type=jnp.float32)
    projected = projected.reshape(batches, local_count, QKV)
    rotated = apply_rotation(heads(projected[..., : QUERY_WIDTH + KEY_WIDTH]), *tables)
    query_rows = rotated[..., :QUERY_HEADS, :].astype(jnp.bfloat16) * HEAD_WIDTH ** (-0.5)
    query_rows = jnp.pad(
        query_rows.reshape(batches, local_count, QUERY_WIDTH), ((0, 0), (0, 0), (0, HEAD_WIDTH))
    )
    key_values = jnp.concatenate(
        [rotated[..., QUERY_HEADS:, :], heads(projected[..., QUERY_WIDTH + KEY_WIDTH :])], -1
    )
    key_values = key_values.astype(jnp.bfloat16).reshape(batches, local_count, 2 * KEY_WIDTH)
    mixed, *attended = attend(query_rows, key_values, shards)
    if shards:
        *attended, gate_up, down_weight = attended
        gate_up = gate_up.reshape(-1, 2 * FF)
        down_weight = down_weight.reshape(-1, DOWN_COLUMNS)
    mixed = mixed.reshape(rows, FULL)
    hidden = values + jnp.dot(mixed, attend_out, preferred_element_type=jnp.float32)
    second_norm = pad_shards(normed(hidden, gains[1]).astype(jnp.bfloat16))
    gated = jnp.dot(second_norm, gate_up, preferred_element_type=jnp.float32)
    act = (jax.nn.silu(gated[:, :FF]) * gated[:, FF:]).astype(jnp.bfloat16)
    result = hidden + jnp.dot(act, down_weight, preferred_element_type=jnp.float32)[:, :D]
    kept = (
        values,
        first_norm,
        attended,
        mixed,
        hidden,
        second_norm,
        gated,
        act,
    )
    weights = (attend_in, attend_out, gate_up, down_weight, gains)
    return (result.astype(jnp.bfloat16).reshape(layer_in.shape), kept, weights)


def backward_layer(upstream, kept, tables, weights, last=False):
    attend_in, attend_out, gate_up, down_weight, gains = weights
    (
        values,
        first_norm,
        attended,
        mixed,
        hidden,
        second_norm,
        gated,
        act,
    ) = kept
    batches, local_count = upstream.shape[:2]
    rows = batches * local_count
    upstream = upstream.reshape(rows, D)
    down_in = jnp.pad(upstream, ((0, 0), (0, DOWN_COLUMNS - D)))
    upstream = upstream.astype(jnp.float32)
    act_slope = jnp.einsum("td,fd->tf", down_in, down_weight, preferred_element_type=jnp.float32)
    gate_part = gated[:, :FF]
    up_part = gated[:, FF:]
    sigma = jax.nn.sigmoid(gate_part)
    gate_slope = act_slope * up_part * sigma * (1.0 + gate_part * (1.0 - sigma))
    up_slope = act_slope * gate_part * sigma
    gated_slope = jnp.concatenate([gate_slope, up_slope], 1).astype(jnp.bfloat16)
    second_slope = unpad_shards(
        jnp.einsum("tf,df->td", gated_slope, gate_up, preferred_element_type=jnp.float32)
    )
    hidden_part, second_gain = norm_backward(hidden, gains[1], second_slope)
    hidden_slope = upstream + hidden_part
    branch_slope = hidden_slope.astype(jnp.bfloat16)
    mixed_gradient = jnp.einsum(
        "td,qd->tq", branch_slope, attend_out, preferred_element_type=jnp.float32
    ).astype(jnp.bfloat16)
    terms = feed_forward_terms(second_norm, act, gated_slope, down_in) if last else ()
    query_slope, pair_slopes, extra_slopes, *summed = attend_back(
        mixed_gradient.reshape(batches, local_count, FULL), attended, terms
    )
    pair_slopes = pair_slopes.astype(jnp.float32)
    extra_slopes = extra_slopes.astype(jnp.float32)
    group_slopes = jnp.stack(
        [
            pair_slopes[0] + pair_slopes[1],
            extra_slopes[0] + pair_slopes[2],
            pair_slopes[3] + pair_slopes[4],
            extra_slopes[1] + pair_slopes[5],
            pair_slopes[6] + pair_slopes[7],
        ],
        2,
    )
    query_slope = query_slope[..., :QUERY_WIDTH].astype(jnp.float32)
    query_raw = reverse_rotation(
        query_slope.reshape(batches, local_count, QUERY_HEADS, HEAD_WIDTH), *tables
    ).reshape(rows, QUERY_WIDTH)
    unrotated_key = reverse_rotation(group_slopes[..., :HEAD_WIDTH], *tables)
    projected_slope = jnp.concatenate(
        [
            query_raw,
            unrotated_key.reshape(rows, KEY_WIDTH),
            group_slopes[..., HEAD_WIDTH:].reshape(rows, KEY_WIDTH),
        ],
        1,
    ).astype(jnp.bfloat16)
    first_slope = unpad_shards(
        jnp.einsum("tf,df->td", projected_slope, attend_in, preferred_element_type=jnp.float32)
    )
    input_part, first_gain = norm_backward(values, gains[0], first_slope)
    input_slope = hidden_slope + input_part
    input_slope = input_slope.reshape(batches, local_count, D)
    if not last:
        return input_slope
    gain_slopes = jnp.stack([first_gain, second_gain])
    terms = attention_terms(first_norm, mixed, projected_slope, branch_slope, gain_slopes)
    return (input_slope, (*reduce_gradients(terms), *summed))


def passed_along(value, steps):
    return lax.ppermute(value, "section", [(0, 1)] if steps > 0 else [(1, 0)])


def with_other_core(value):
    size = lax.axis_size("dp")
    other = lax.ppermute(value, "dp", [(index, index ^ 1) for index in range(size)])
    return other


def halved(values, axis):
    core = lax.axis_index("dp") % 2
    extent = values.shape[axis] // 2
    keep = lax.dynamic_slice_in_dim(values, core * extent, extent, axis)
    send = lax.dynamic_slice_in_dim(values, (1 - core) * extent, extent, axis)
    return jnp.concatenate([keep, with_other_core(send)], 0)


def whole(values):
    return jnp.concatenate([values, with_other_core(values)], 0)


def term(left, right):
    split = left.reshape(left.shape[0], SHARDS, -1)
    return jnp.einsum("tkr,tn->krn", split, right, preferred_element_type=jnp.float32).astype(
        jnp.bfloat16
    )


def feed_forward_terms(second_norm, act, gated_slope, down_in):
    return (
        term(whole(second_norm), halved(gated_slope, 1)),
        term(whole(act), halved(down_in, 1)),
    )


def attention_terms(first_norm, mixed, projected_slope, branch_slope, gain_slopes):
    core = lax.axis_index("dp") % 2
    by_shard = (-1, SHARDS, PADDED)
    in_rows = halved(first_norm.reshape(by_shard), 2)
    out_rows = halved(pad_shards(mixed[:, :QUERY_WIDTH]).reshape(by_shard), 2)
    in_term = term(in_rows, whole(projected_slope))
    gains = (gain_slopes + with_other_core(gain_slopes)).reshape(2, SHARDS, ROWS).swapaxes(0, 1)
    spare = PADDED // 2 - (PADDED - ROWS)
    in_term = in_term.at[:, spare : spare + 2, :ROWS].add(
        jnp.where(core == 1, gains, 0.0).astype(jnp.bfloat16)
    )
    return (in_term, term(out_rows, whole(branch_slope)))


def body(
    inputs, positions, plan, attend_in, attend_out, gate_up, down_weight, norm_gains, cotangent
):
    section_index = lax.axis_index("section")
    extra = PADDED - ROWS
    in_shard = jnp.concatenate(
        [
            attend_in[0],
            jnp.pad(norm_gains[0], ((0, extra - 2), (0, QKV - ROWS))),
        ],
        0,
    )
    gathered = gather_weights((in_shard, jnp.pad(attend_out[0], ((0, extra), (0, 0)))))
    gains = gathered[0][:, ROWS : ROWS + 2, :ROWS].swapaxes(0, 1).reshape(2, D)
    out_weight = gathered[1][:, :ROWS].reshape(QUERY_WIDTH, D)
    weights = (
        gathered[0].reshape(-1, QKV),
        jnp.pad(out_weight, ((0, FULL - QUERY_WIDTH), (0, 0))),
        None,
        None,
        gains.astype(jnp.float32),
    )
    shards = (
        jnp.pad(gate_up[0], ((0, extra), (0, 0))),
        jnp.pad(down_weight[0], ((0, 0), (0, DOWN_COLUMNS - D))),
    )
    plan_row = plan[0]
    fresh = jnp.take(inputs[:, 0], plan_row, axis=0)
    tables = rotary_tables(jnp.take(positions[:, 0], plan_row, axis=0))
    given = cotangent[:, 0]
    result, _, weights = forward_layer(fresh, tables, weights, shards)
    layer_in = jnp.where(section_index == 0, fresh, passed_along(result, 1))
    outputs, kept, _ = forward_layer(layer_in, tables, weights)
    input_slope = backward_layer(given, kept, tables, weights)
    back = passed_along(input_slope.astype(jnp.bfloat16), -1)
    upstream = jnp.where(section_index == 1, given, back)
    input_slope, summed = backward_layer(upstream, kept, tables, weights, True)
    reported = jnp.where(
        section_index == 0, input_slope, input_slope.astype(jnp.bfloat16).astype(jnp.float32)
    )
    input_slopes = jnp.take(reported, plan_row, axis=0)
    full = [value.astype(jnp.float32) for value in summed]
    return (
        outputs[None, :, None],
        input_slopes[None, :, None],
        full[0][None, :ROWS],
        full[1][None, :ROWS],
        full[2][None, :ROWS],
        full[3][None, :, :D],
        full[0][None, ROWS : ROWS + 2, :ROWS],
    )


def solution(mesh):
    in_specs = (
        P(None, "dp", "fsdp", None),
        P(None, "dp", "fsdp"),
        P("dp", None),
        P("section", "fsdp", None),
        P("section", "fsdp", None),
        P("section", "fsdp", None),
        P("section", "fsdp", None),
        P("section", None, "fsdp"),
        P(None, "dp", "fsdp", None),
    )
    out_specs = (
        P("section", None, "dp", "fsdp", None),
        P("section", None, "dp", "fsdp", None),
        P("section", "fsdp", None),
        P("section", "fsdp", None),
        P("section", "fsdp", None),
        P("section", "fsdp", None),
        P("section", None, "fsdp"),
    )
    return jax.shard_map(body, mesh=mesh, in_specs=in_specs, out_specs=out_specs, check_vma=False)
```

```python
import functools

import jax
import jax.numpy as jnp
from jax import lax
from jax.experimental import pallas as pl
from jax.experimental.pallas import tpu as pltpu
from jax.sharding import PartitionSpec as P

D = 960
QUERY_HEADS = 15
KEY_VALUE_HEADS = 5
HEAD_WIDTH = 64
FF = 2560
QUERY_WIDTH = QUERY_HEADS * HEAD_WIDTH
KEY_WIDTH = KEY_VALUE_HEADS * HEAD_WIDTH
QKV = QUERY_WIDTH + 2 * KEY_WIDTH
SHARDS = 8
ROWS = D // SHARDS
PADDED = 128
MODEL = 1024
PAIR = 2 * HEAD_WIDTH
FULL = SHARDS * PAIR
WIDE = FULL + KEY_VALUE_HEADS * PAIR

EPSILON = 1e-05
BASE = 10000.0

MESH = pl.DeviceIdType.MESH
ANY = pl.BlockSpec(memory_space=pl.ANY)
VMEM = pl.BlockSpec(memory_space=pltpu.VMEM)

GATE_UP = (PADDED, 2 * FF, "columns", FF, 0)
GATE_UP_FIRST = (PADDED, FF, "columns", FF, 0)
GATE_UP_SECOND = (PADDED, FF, "columns", FF, FF // 2)
DOWN = (FF // SHARDS, SHARDS * PADDED, "columns", SHARDS * PADDED // 2, 0)
ATTEND_IN = (PADDED, WIDE, "rows", 0, 0)
ATTEND_OUT = (PADDED, SHARDS * PADDED, "rows", 0, 0)
FEED_FORWARD = (GATE_UP, DOWN)
FEED_FORWARD_BACK = (GATE_UP_FIRST, GATE_UP_SECOND, DOWN)
ATTENTION = (ATTEND_IN, ATTEND_OUT)


def half_lanes(shape, core):
    _, columns, _, stride, offset = shape
    return pl.ds(pl.multiple_of(core * stride + offset, 128), columns // 2)


def half_shape(shape):
    rows, columns, kind = shape[:3]
    return (rows // 2, columns) if kind == "rows" else (rows, columns // 2)


def half_view(shape, core, start, count):
    rows, columns, kind = shape[:3]
    if kind == "rows":
        first = pl.multiple_of(core * (rows // 2) + start, 16)
        return (pl.ds(first, count), slice(None))
    return (pl.ds(pl.multiple_of(start, 16), count), half_lanes(shape, core))


def places():
    dp = lax.axis_index("dp")
    fsdp = lax.axis_index("fsdp")
    return dp // 2, dp % 2, fsdp // 4, fsdp % 4


def peer_ids():
    z, core, x, y = places()
    return {
        "X": {"fsdp": (1 - x) * 4 + y},
        "Yp": {"fsdp": x * 4 + (y + 1) % 4},
        "Ym": {"fsdp": x * 4 + (y + 3) % 4},
        "C": {"dp": z * 2 + 1 - core},
        "Z1": {"dp": ((z + 1) % 4) * 2 + core},
        "Z2": {"dp": ((z + 2) % 4) * 2 + core},
        "Z3": {"dp": ((z + 3) % 4) * 2 + core},
    }


def greet(ids, names):
    barrier = pltpu.get_barrier_semaphore()
    for name in names:
        pl.semaphore_signal(barrier, inc=1, device_id=ids[name], device_id_type=MESH)
    pl.semaphore_wait(barrier, len(names))


GATHER = (
    ("X", 0, 0, "f"),
    ("Yp", 0, 0, "f"),
    ("Ym", 0, 0, "f"),
    ("Ym", 0, 1, 0),
    ("X", 0, 1, 0),
    ("Yp", 0, 3, 1),
    ("X", 0, 3, 0),
    ("Yp", 1, 0, 1),
    ("Ym", 1, 0, 1),
    ("Ym", 1, 1, 0),
    ("Yp", 1, 3, 1),
)
GATHER_NEXT = {1: (5, 6), 2: (3, 4), 0: (7, 8), 4: (9,), 7: (10,)}
GATHER_STAGES = ((1, 2, 0), (4, 7, 3, 5, 6, 8), (9, 10))
GATHER_ORDER = (1, 2, 0, 4, 7, 3, 5, 6, 8, 9, 10)


def seen_by_receiver(peer, column, step):
    if peer == "X":
        return 1 - column, step
    if peer == "Yp":
        return column, (step + 3) % 4
    if peer == "Ym":
        return column, (step + 1) % 4
    return column, step


def part_rows(shape, part):
    rows = half_shape(shape)[0]
    return (0, rows) if part == "f" else (part * (rows // 2), rows // 2)


UPWARD = (0, 1, 3, 5, 7)
PLAIN_EDGES = 22
SPREAD_EDGES = 88


class Gather:
    def __init__(self, shapes, spread, shards, outs, sems):
        self.shapes, self.spread, self.shards, self.outs = shapes, spread, shards, outs
        self.local_sem, self.send_sem, self.recv_sem = sems
        self.z, self.core, self.x, self.y = places()
        self.ids = peer_ids()

    def owner(self, column, step):
        return ((self.x + column) % 2) * 4 + (self.y + step) % 4

    def index(self, array, part, which, plane):
        shape = self.shapes[array]
        start, rows = part_rows(shape, part)
        if array == self.spread:
            quarter = half_shape(shape)[0] // 4
            start, rows = plane * quarter + start // 4, rows // 4
        return half_view(shape, which, start, rows)

    def view(self, array, column, step, part, which, plane):
        return self.outs[array].at[
            (self.owner(column, step),) + self.index(array, part, which, plane)
        ]

    def received(self, edge):
        group, base = edge // 11, edge % 11
        peer, column, step, part = GATHER[base]
        column, step = seen_by_receiver(peer, column, step)
        return column, step, part, (0, 0, 3, 1, 2, 3, 1, 2)[group]

    def peer_of(self, edge):
        group, base = edge // 11, edge % 11
        if group == 0:
            return GATHER[base][0]
        if group in (1, 5, 6, 7):
            return "C"
        return {2: "Z1", 3: "Z3", 4: "Z1" if base in UPWARD else "Z3"}[group]

    def copy(self, array, edge):
        group, base = edge // 11, edge % 11
        if group == 0:
            _, column, step, part = GATHER[base]
            away = 0
        else:
            column, step, part, away = self.received(edge)
            if group in (2, 3):
                away = 0
            elif group == 4:
                away = 3 if base in UPWARD else 1
        target = source = self.view(array, column, step, part, self.core, (self.z + away) % 4)
        if group == 0 and (column, step) == (0, 0):
            source = self.shards[array].at[self.index(array, part, self.core, self.z)]
        return pltpu.make_async_remote_copy(
            src_ref=source,
            dst_ref=target,
            send_sem=self.send_sem.at[array, edge],
            recv_sem=self.recv_sem.at[array, edge],
            device_id=self.ids[self.peer_of(edge)],
            device_id_type=MESH,
        )

    def wait_for(self, array, edge):
        column, step, part, away = self.received(edge)
        which = 1 - self.core if edge // 11 in (1, 5, 6, 7) else self.core
        landed = self.view(array, column, step, part, which, (self.z + away) % 4)
        pltpu.make_async_remote_copy(
            src_ref=landed,
            dst_ref=landed,
            send_sem=self.send_sem.at[array, edge],
            recv_sem=self.recv_sem.at[array, edge],
            device_id=self.ids["C"],
            device_id_type=MESH,
        ).wait_recv()

    def own(self, array):
        return pltpu.make_async_copy(
            self.shards[array],
            self.outs[array].at[self.x * 4 + self.y],
            self.local_sem.at[array],
        )

    def start(self):
        for array in range(len(self.shapes)):
            for edge in (0, 1, 2):
                self.copy(array, edge).start()
            self.own(array).start()

    def within_plane(self, array, edges):
        for edge in edges:
            self.wait_for(array, edge)
            for later in GATHER_NEXT.get(edge, ()):
                self.copy(array, later).start()
            if array == self.spread:
                self.copy(array, 22 + edge).start()
                self.copy(array, 33 + edge).start()
            self.copy(array, 11 + edge).start()

    def round_z(self, edges):
        if self.spread is None:
            return
        for edge in edges:
            for group in (2, 3):
                self.wait_for(self.spread, 11 * group + edge)
                if (group == 2) == (edge in UPWARD):
                    self.copy(self.spread, 44 + edge).start()
                self.copy(self.spread, 11 * (group + 3) + edge).start()

    def steps(self):
        first, second, third = GATHER_STAGES
        arrays = range(len(self.shapes))
        steps = [functools.partial(self.within_plane, array, first) for array in arrays]
        steps.append(functools.partial(self.round_z, first))
        steps += [functools.partial(self.within_plane, array, second) for array in arrays]
        steps.append(functools.partial(self.round_z, second))
        steps += [functools.partial(self.within_plane, array, third) for array in arrays]
        steps.append(functools.partial(self.round_z, third))
        steps.append(self.finish)
        return steps

    def finish(self):
        if self.spread is not None:
            for edge in GATHER_ORDER:
                self.wait_for(self.spread, 44 + edge)
                self.copy(self.spread, 77 + edge).start()
        for array in range(len(self.shapes)):
            last = SPREAD_EDGES if array == self.spread else PLAIN_EDGES
            for edge in range(last):
                if edge // 11 in (1, 5, 6, 7):
                    self.wait_for(array, edge)
            for edge in range(last):
                self.copy(array, edge).wait_send()
            self.own(array).wait()

    @staticmethod
    def out_shapes(shapes):
        return [
            jax.ShapeDtypeStruct((SHARDS, rows, columns), jnp.bfloat16)
            for rows, columns, *_ in shapes
        ]

    @staticmethod
    def scratch(shapes, spread):
        edges = PLAIN_EDGES if spread is None else SPREAD_EDGES
        return [
            pltpu.SemaphoreType.DMA((len(shapes),)),
            pltpu.SemaphoreType.DMA((len(shapes), edges)),
            pltpu.SemaphoreType.DMA((len(shapes), edges)),
        ]


def gather_kernel(shapes, *refs):
    count = len(shapes)
    gather = Gather(shapes, None, refs[:count], refs[count : 2 * count], refs[2 * count :])
    greet(gather.ids, ("X", "Yp", "Ym", "C"))
    gather.start()
    for step in gather.steps():
        step()


def gather_weights(shards):
    count = len(ATTENTION)
    return pl.pallas_call(
        functools.partial(gather_kernel, ATTENTION),
        name="gather_weights",
        out_shape=Gather.out_shapes(ATTENTION),
        in_specs=[VMEM] * count,
        out_specs=[ANY] * count,
        scratch_shapes=Gather.scratch(ATTENTION, None),
        compiler_params=pltpu.CompilerParams(collective_id=0, has_side_effects=True),
    )(*shards)


REDUCE = (
    ("Yp", 0, 2, 0, ()),
    ("Ym", 0, 2, 1, ()),
    ("Yp", 1, 2, 0, ()),
    ("Ym", 1, 2, 1, ()),
    ("X", 1, 3, 0, ()),
    ("Yp", 1, 1, 1, ()),
    ("X", 1, 1, 0, (2,)),
    ("Ym", 1, 3, 1, (3,)),
    ("Yp", 0, 1, "f", (0, 6)),
    ("Ym", 0, 3, "f", (1, 4)),
    ("X", 1, 0, "f", (5, 7)),
)
REDUCE_STAGES = ((0, 1, 2, 3, 4, 5), (6, 7), (8, 9, 10))
SHARD_ORDER = ((0, 2), (1, 2), (1, 3), (1, 1), (0, 1), (0, 3), (1, 0), (0, 0))
REDUCE_EDGES = 47
SLOTS = 2
ROWS_HERE = 256


class Reduce:
    def __init__(self, shapes, spread, lefts, rights, extra, outs, scratch):
        count = len(shapes)
        if len(lefts) < count:
            lefts, rights, outs = ((refs[0],) + tuple(refs) for refs in (lefts, rights, outs))
        self.shapes, self.spread, self.outs = shapes, spread, outs
        self.lefts, self.rights, self.extra = lefts, rights, extra
        self.totals = scratch[:count]
        self.wholes = scratch[count : 2 * count]
        self.parts = scratch[2 * count : 3 * count]
        self.quarters = scratch[3 * count : 4 * count]
        self.rounds = None if spread is None else scratch[4 * count]
        self.left_all = list(scratch[-4 - 2 * count : -4 - count])
        self.sides = [(0, 1)] * count
        if shapes[0] is GATE_UP_FIRST:
            self.left_all[1] = self.left_all[0]
            self.sides[1] = (1,)
        self.right_all = scratch[-4 - count : -4]
        self.operand_sem, self.local_sem, self.send_sem, self.recv_sem = scratch[-4:]
        self.z, self.core, self.x, self.y = places()
        self.mine = self.x * 4 + self.y
        self.ids = peer_ids()
        self.plain = [array for array in range(count) if array != spread]

    @staticmethod
    def piece_shapes(shapes, spread):
        halves = [half_shape(shape) for shape in shapes]
        return halves, [
            (half[0], half[1] // 4) if array == spread else half
            for array, half in enumerate(halves)
        ]

    @staticmethod
    def left_shape(shape, half):
        if shape is GATE_UP_SECOND:
            return (16, 128)
        if half[0] == PADDED:
            return (ROWS_HERE, SHARDS * PADDED)
        return (SHARDS, ROWS_HERE, half[0])

    @staticmethod
    def out_shapes(shapes):
        return [jax.ShapeDtypeStruct((rows, columns), jnp.bfloat16) for rows, columns, *_ in shapes]

    @staticmethod
    def scratch(shapes, spread):
        halves, pieces = Reduce.piece_shapes(shapes, spread)
        bf16 = jnp.bfloat16
        buffers = [pltpu.VMEM((SHARDS,) + half, bf16) for half in halves]
        buffers += [pltpu.VMEM((3,) + piece, bf16) for piece in pieces]
        buffers += [pltpu.VMEM((8, piece[0] // 2, piece[1]), bf16) for piece in pieces]
        buffers += [pltpu.VMEM((3, half[0] // 4, half[1]), bf16) for half in halves]
        if spread is not None:
            buffers.append(pltpu.VMEM((3 * SHARDS,) + pieces[spread], bf16))
        buffers += [
            pltpu.VMEM((2,) + Reduce.left_shape(shape, half), bf16)
            for shape, half in zip(shapes, halves)
        ]
        buffers += [pltpu.VMEM((2, ROWS_HERE, half[1]), bf16) for half in halves]
        return buffers + [
            pltpu.SemaphoreType.DMA((len(shapes), 2)),
            pltpu.SemaphoreType.DMA((len(shapes),)),
            pltpu.SemaphoreType.DMA((len(shapes), REDUCE_EDGES)),
            pltpu.SemaphoreType.DMA((len(shapes), REDUCE_EDGES)),
        ]

    def owner(self, column, step):
        return ((self.x + column) % 2) * 4 + (self.y + step) % 4

    def lanes(self, array, plane):
        columns = half_shape(self.shapes[array])[1]
        if array != self.spread:
            return pl.ds(0, columns)
        return pl.ds(pl.multiple_of(plane * (columns // 4), 128), columns // 4)

    def piece(self, array, edge):
        _, column, step, part, _ = REDUCE[edge]
        start, rows = part_rows(self.shapes[array], part)
        return self.totals[array].at[
            self.owner(column, step), pl.ds(start, rows), self.lanes(array, self.z)
        ]

    def slot(self, array, edge):
        return self.parts[array].at[edge] if edge < 8 else self.wholes[array].at[edge - 8]

    def add(self, array, into, start, rows, lanes, source):
        total = self.totals[array]

        @pl.loop(0, rows // 16)
        def _(index):
            offset = pl.multiple_of(index * 16, 16)
            at = pl.ds(pl.multiple_of(start + offset, 16), 16)
            total[into, at, lanes] = (
                total[into, at, lanes].astype(jnp.float32)
                + source[pl.ds(offset, 16), :].astype(jnp.float32)
            ).astype(jnp.bfloat16)

    def quarter(self, array, plane):
        rows = half_shape(self.shapes[array])[0]
        if array == self.spread:
            return 0, rows, self.lanes(array, plane)
        return pl.multiple_of(plane * (rows // 4), 16), rows // 4, self.lanes(array, plane)

    def summed(self, array, plane):
        start, rows, lanes = self.quarter(array, plane)
        return self.totals[array].at[self.mine, pl.ds(start, rows), lanes]

    def out_view(self, array, plane, which):
        shape = self.shapes[array]
        if array == self.spread:
            rows, columns = half_shape(shape)
            first = pl.multiple_of(which * shape[3] + shape[4] + plane * (columns // 4), 128)
            return self.outs[array].at[pl.ds(0, rows), pl.ds(first, columns // 4)]
        start, rows, _ = self.quarter(array, plane)
        return self.outs[array].at[half_view(shape, which, start, rows)]

    def copy(self, array, edge):
        z = self.z
        if edge < 11:
            peer, source, target = REDUCE[edge][0], self.piece(array, edge), self.slot(array, edge)
        elif edge < 14:
            step = edge - 10
            peer, source = f"Z{step}", self.summed(array, (z + step) % 4)
            target = self.quarters[array].at[step - 1]
        elif edge < 17:
            peer, source = f"Z{edge - 13}", self.summed(array, z)
            target = self.out_view(array, z, self.core)
        elif edge < 21:
            peer = "C"
            source = target = self.out_view(array, (z + edge - 17) % 4, self.core)
            if edge == 17:
                source = self.summed(array, z)
        elif edge >= 45:
            peer, source = "C", self.operand(array, edge - 45, 1 - self.core)
            target = (self.left_all, self.right_all)[edge - 45][array].at[1]
        else:
            kind, shard = (edge - 21) // 8, (edge - 21) % 8
            peer = ("Z1" if shard % 2 == 0 else "Z3", "Z1", "Z3")[kind]
            lanes = self.lanes(array, (z + (2, 1, 3)[kind]) % 4)
            source = self.totals[array].at[self.owner(*SHARD_ORDER[shard]), :, lanes]
            target = self.rounds.at[edge - 21]
        return pltpu.make_async_remote_copy(
            src_ref=source,
            dst_ref=target,
            send_sem=self.send_sem.at[array, edge],
            recv_sem=self.recv_sem.at[array, edge],
            device_id=self.ids[peer],
            device_id_type=MESH,
        )

    def wait_for(self, array, edge):
        z = self.z
        if edge < 11:
            landed = self.slot(array, edge)
        elif edge < 14:
            landed = self.quarters[array].at[edge - 11]
        elif edge < 17:
            landed = self.out_view(array, (z + 4 - (edge - 13)) % 4, self.core)
        elif edge < 21:
            landed = self.out_view(array, (z + edge - 17) % 4, 1 - self.core)
        elif edge >= 45:
            landed = (self.left_all, self.right_all)[edge - 45][array].at[1]
        else:
            landed = self.rounds.at[edge - 21]
        pltpu.make_async_remote_copy(
            src_ref=landed,
            dst_ref=landed,
            send_sem=self.send_sem.at[array, edge],
            recv_sem=self.recv_sem.at[array, edge],
            device_id=self.ids["C"],
            device_id_type=MESH,
        ).wait_recv()

    def receive(self, array, edge):
        self.wait_for(array, edge)
        peer, column, step, part, _ = REDUCE[edge]
        column, step = seen_by_receiver(peer, column, step)
        start, rows = part_rows(self.shapes[array], part)
        lanes = self.lanes(array, self.z)
        self.add(array, self.owner(column, step), start, rows, lanes, self.slot(array, edge))

    def receive_round(self, kind, shard):
        edge = 21 + 8 * kind + shard
        array = self.spread
        self.wait_for(array, edge)
        away = 0 if kind > 0 else (1 if shard % 2 == 0 else 3)
        rows = half_shape(self.shapes[array])[0]
        lanes = self.lanes(array, (self.z + away) % 4)
        self.add(
            array, self.owner(*SHARD_ORDER[shard]), 0, rows, lanes, self.rounds.at[edge - 21]
        )

    def stage(self, array, number):
        for edge in REDUCE_STAGES[number]:
            for earlier in REDUCE[edge][4]:
                self.receive(array, earlier)
            self.copy(array, edge).start()

    def operand(self, array, side, core):
        kind = self.shapes[array][2]
        if side == 0:
            return self.lefts[array].at[core] if kind == "rows" else self.lefts[array]
        if kind == "rows":
            return self.rights[array]
        return self.rights[array].at[:, half_lanes(self.shapes[array], core)]

    def load(self, array, side):
        return pltpu.make_async_copy(
            self.operand(array, side, self.core),
            (self.left_all, self.right_all)[side][array].at[0],
            self.operand_sem.at[array, side],
        )

    def make(self, array, shards):
        columns = half_shape(self.shapes[array])[1]
        left, right, total = self.left_all[array], self.right_all[array], self.totals[array]
        for shard in shards:
            owner = self.owner(*SHARD_ORDER[shard])

            def chunk(lanes):
                if len(left.shape) == 3:
                    at = pl.ds(pl.multiple_of(owner * PADDED, PADDED), PADDED)
                    mine, other = left[0, :, at], left[1, :, at]
                else:
                    mine, other = left[0, owner], left[1, owner]
                total[owner, :, lanes] = (
                    dot_first(mine, right[0, :, lanes]) + dot_first(other, right[1, :, lanes])
                ).astype(jnp.bfloat16)

            if columns % 640 == 0 and columns > 640:

                @pl.loop(0, columns // 640)
                def _(index):
                    chunk(pl.ds(pl.multiple_of(index * 640, 128), 640))

            else:
                for first in range(0, columns, 512):
                    chunk(pl.ds(first, min(512, columns - first)))
            if self.extra is not None and array == 0:
                at = pl.ds(half_shape(self.shapes[array])[0] - 16, 16)
                total[owner, at, :128] += self.extra[owner]

    def store(self, array):
        return pltpu.make_async_copy(
            self.summed(array, self.z), self.out_view(array, self.z, self.core),
            self.local_sem.at[array],
        )

    def start_loads(self):
        for array in range(len(self.shapes)):
            for side in self.sides[array]:
                self.load(array, side).start()

    def start_exchange(self):
        for array in range(len(self.shapes)):
            for side in self.sides[array]:
                self.copy(array, 45 + side).start()

    def start(self):
        order = ([] if self.spread is None else [self.spread]) + self.plain
        for array in order:
            for side in self.sides[array]:
                self.load(array, side).wait()
                self.wait_for(array, 45 + side)
            if array == self.spread:
                self.make(array, range(SHARDS))
                for shard in range(SHARDS):
                    self.copy(array, 21 + shard).start()
            else:
                self.make(array, range(4))
                self.stage(array, 0)
        for array in self.plain:
            self.make(array, range(4, SHARDS))

    def first_round(self):
        for shard in range(SHARDS):
            self.receive_round(0, shard)
            self.copy(self.spread, 29 + shard).start()
            self.copy(self.spread, 37 + shard).start()

    def second_round(self, shards):
        for shard in shards:
            self.receive_round(1, shard)
            self.receive_round(2, shard)

    def end_plane(self, array):
        for edge in (8, 9, 10):
            self.receive(array, edge)
        for edge in (11, 12, 13) if array != self.spread else ():
            self.copy(array, edge).start()

    def end_z(self, array):
        if array != self.spread:
            start, rows, lanes = self.quarter(array, self.z)
            for edge in (11, 12, 13):
                self.wait_for(array, edge)
                self.add(
                    array, self.mine, start, rows, lanes, self.quarters[array].at[edge - 11]
                )
        for edge in (14, 15, 16, 17):
            self.copy(array, edge).start()
        self.store(array).start()

    def finish(self):
        for array in range(len(self.shapes)):
            for edge in (14, 15, 16):
                self.wait_for(array, edge)
                self.copy(array, 34 - edge).start()
        for array in range(len(self.shapes)):
            for edge in range(17, 21):
                self.wait_for(array, edge)
            for edge in range(REDUCE_EDGES):
                if edge >= 45:
                    started = edge - 45 in self.sides[array]
                elif array == self.spread:
                    started = edge not in (11, 12, 13)
                else:
                    started = edge < 21
                if started:
                    self.copy(array, edge).wait_send()
            self.store(array).wait()

    def steps(self):
        call = functools.partial
        steps = []
        if self.spread is not None:
            steps.append(self.first_round)
        steps += [call(self.stage, array, 1) for array in self.plain]
        if self.spread is not None:
            steps.append(call(self.second_round, range(4)))
            steps.append(call(self.stage, self.spread, 0))
            steps.append(call(self.second_round, range(4, SHARDS)))
            steps.append(call(self.stage, self.spread, 1))
        steps += [call(self.stage, array, 2) for array in self.plain]
        if self.spread is not None:
            steps.append(call(self.stage, self.spread, 2))
        steps += [call(self.end_plane, array) for array in self.plain]
        if self.spread is not None:
            steps.append(call(self.end_plane, self.spread))
            steps.append(call(self.end_z, self.spread))
        steps += [call(self.end_z, array) for array in self.plain]
        steps.append(self.finish)
        return steps


def reduce_kernel(shapes, *refs):
    count = len(shapes)
    lefts, rights, extra = refs[:count], refs[count : 2 * count], refs[2 * count]
    outs, scratch = refs[2 * count + 1 : 3 * count + 1], refs[3 * count + 1 :]
    reduce = Reduce(shapes, None, lefts, rights, extra, outs, scratch)
    reduce.start_loads()
    greet(reduce.ids, ("X", "Yp", "Ym", "C", "Z1", "Z2", "Z3"))
    reduce.start_exchange()
    reduce.start()
    for step in reduce.steps():
        step()


def reduce_gradients(lefts, rights, extra):
    count = len(ATTENTION)
    return pl.pallas_call(
        functools.partial(reduce_kernel, ATTENTION),
        name="reduce_gradients",
        out_shape=Reduce.out_shapes(ATTENTION),
        in_specs=[ANY] * (2 * count) + [VMEM],
        out_specs=[ANY] * count,
        scratch_shapes=Reduce.scratch(ATTENTION, None),
        compiler_params=pltpu.CompilerParams(
            collective_id=1, has_side_effects=True, vmem_limit_bytes=48 * 2**20
        ),
    )(*lefts, *rights, extra)


TOKENS = 1024
LOCAL = TOKENS // SHARDS
BLOCK = 256
NEGATIVE = -1e30


def two_groups(device):
    return (device == 1) | (device == 4)


def group_lanes(device, which):
    return pl.ds(pl.multiple_of(((2 * device) // 3 + which) * PAIR, PAIR), PAIR)


def pair_lanes(device):
    return pl.ds(pl.multiple_of(device * PAIR, PAIR), PAIR)


def token_rows(device):
    return pl.ds(pl.multiple_of(device * LOCAL, LOCAL), LOCAL)


def ring(me):
    return [(step, (me + step) % SHARDS, (me + SHARDS - step) % SHARDS) for step in range(1, SHARDS)]


def greet_all(me, others=()):
    barrier = pltpu.get_barrier_semaphore()
    ids = peer_ids()
    for device in [{"fsdp": target} for _, target, _ in ring(me)] + [ids[name] for name in others]:
        pl.semaphore_signal(barrier, inc=1, device_id=device, device_id_type=MESH)
    pl.semaphore_wait(barrier, SHARDS - 1 + len(others))


def turned(values):
    lane = lax.broadcasted_iota(jnp.int32, values.shape, 1)
    half = HEAD_WIDTH // 2
    ahead, behind = pltpu.roll(values, PAIR - half, 1), pltpu.roll(values, half, 1)
    return jnp.where(lane % HEAD_WIDTH < half, -ahead, behind)


def sent(source, target, send_sem, recv_sem, device):
    return pltpu.make_async_remote_copy(
        src_ref=source,
        dst_ref=target,
        send_sem=send_sem,
        recv_sem=recv_sem,
        device_id={"fsdp": device},
        device_id_type=MESH,
    )


def causal_mask(values):
    length = values.shape[1]
    row = lax.broadcasted_iota(jnp.int32, (BLOCK, BLOCK), 0)
    column = lax.broadcasted_iota(jnp.int32, (BLOCK, BLOCK), 1)
    own = jnp.where(column <= row, values[:, length - BLOCK :], NEGATIVE)
    if length == BLOCK:
        return own
    return jnp.concatenate([values[:, : length - BLOCK], own], 1)


def dot_t(left, right):
    return lax.dot_general(
        left, right, (((1,), (1,)), ((), ())), preferred_element_type=jnp.float32
    )


def dot_first(left, right):
    return lax.dot_general(
        left, right, (((0,), (0,)), ((), ())), preferred_element_type=jnp.float32
    )


def attend_kernel(with_gather, *refs):
    count = len(FEED_FORWARD) if with_gather else 0
    norm_ref, weight_ref, table_ref = refs[:3]
    mixed_ref, q_kept, kv_kept, lse_kept = refs[3 + count : 7 + count]
    q_ref, kv_ref, q_all, kv_all, lse_all, mixed_all, local_sem, send_sem, recv_sem = refs[
        7 + 2 * count : 16 + 2 * count
    ]
    background = None
    if with_gather:
        background = Gather(
            FEED_FORWARD, 0, refs[3 : 3 + count], refs[7 + count : 7 + 2 * count], refs[-3:]
        )
    me = lax.axis_index("fsdp")
    both = two_groups(me)
    second = jnp.where(both, 1, 0)

    def incoming(slot, step, device, sender):
        rows = token_rows(sender)
        return [
            sent(
                q_ref.at[slot, :, pair_lanes(device)], q_all.at[slot, rows, :],
                send_sem.at[0, slot, step], recv_sem.at[0, slot, step], device,
            ),
            sent(
                kv_ref.at[slot, :, group_lanes(device, 0)], kv_all.at[0, slot, rows, :],
                send_sem.at[1, slot, step], recv_sem.at[1, slot, step], device,
            ),
        ]

    def extra(slot, step, device, sender):
        group = jnp.where(two_groups(device), 1, 0)
        return sent(
            kv_ref.at[slot, :, group_lanes(device, group)], kv_all.at[1, slot, token_rows(sender), :],
            send_sem.at[2, slot, step], recv_sem.at[2, slot, step], device,
        )

    def outgoing(slot, step, device, sender):
        return sent(
            mixed_all.at[slot, token_rows(device), :], mixed_ref.at[slot, :, pair_lanes(sender)],
            send_sem.at[3, slot, step], recv_sem.at[3, slot, step], device,
        )

    def own_copies(slot):
        rows = token_rows(me)
        group = jnp.where(both, 1, 0)
        return [
            pltpu.make_async_copy(
                q_ref.at[slot, :, pair_lanes(me)], q_all.at[slot, rows, :], local_sem.at[0, slot]
            ),
            pltpu.make_async_copy(
                kv_ref.at[slot, :, group_lanes(me, 0)], kv_all.at[0, slot, rows, :],
                local_sem.at[1, slot],
            ),
            pltpu.make_async_copy(
                kv_ref.at[slot, :, group_lanes(me, group)], kv_all.at[1, slot, rows, :],
                local_sem.at[2, slot],
            ),
        ]

    def own_result(slot):
        return pltpu.make_async_copy(
            mixed_all.at[slot, token_rows(me), :], mixed_ref.at[slot, :, pair_lanes(me)],
            local_sem.at[3, slot],
        )

    greet_all(me, ("C", "Z1", "Z3") if background else ())
    pending = []
    if background:
        background.start()
        pending = background.steps()
    for first in range(0, WIDE, 2 * PAIR):
        width = min(2 * PAIR, WIDE - first)
        projected = jnp.dot(
            norm_ref[...], weight_ref[:, first : first + width], preferred_element_type=jnp.float32
        )
        for lane in range(first, first + width, PAIR):
            is_query = lane < FULL
            for slot in range(SLOTS):
                values = projected[
                    slot * LOCAL : (slot + 1) * LOCAL, lane - first : lane - first + PAIR
                ]
                cosine, sine = (table_ref[(0 if is_query else 2) + which, slot] for which in (0, 1))
                rotated = values * cosine + turned(values) * sine
                if is_query:
                    q_ref[slot, :, lane : lane + PAIR] = (rotated * HEAD_WIDTH ** (-0.5)).astype(
                        jnp.bfloat16
                    )
                else:
                    kv_ref[slot, :, lane - FULL : lane - FULL + PAIR] = rotated.astype(jnp.bfloat16)
    for slot in range(SLOTS):
        for step, target, _ in ring(me):
            for copy in incoming(slot, step, target, me):
                copy.start()

            @pl.when(two_groups(target))
            def _():
                extra(slot, step, target, me).start()

        for copy in own_copies(slot):
            copy.start()

    def do_pending(number):
        for _ in range(min(number, len(pending))):
            pending.pop(0)()

    def work(slot):
        for step, _, source in ring(me):
            for copy in incoming(slot, step, source, source):
                copy.wait_recv()

            @pl.when(both)
            def _():
                extra(slot, step, source, source).wait_recv()

        for copy in own_copies(slot):
            copy.wait()
        for block in range(TOKENS // BLOCK):
            rows = pl.ds(block * BLOCK, BLOCK)
            length = (block + 1) * BLOCK
            outs, totals = [], []
            for head in range(2):
                group = 0 if head == 0 else second
                lanes = slice(head * HEAD_WIDTH, (head + 1) * HEAD_WIDTH)
                query = q_all[slot, rows, lanes]
                keys = kv_all[group, slot, :length, :HEAD_WIDTH]
                values = kv_all[group, slot, :length, HEAD_WIDTH:]
                scores = causal_mask(dot_t(query, keys))
                highest = jnp.max(scores, -1, keepdims=True)
                weights = jnp.exp(scores - highest)
                total = jnp.sum(weights, -1, keepdims=True)
                out = jnp.dot(
                    weights.astype(jnp.bfloat16), values, preferred_element_type=jnp.float32
                )
                outs.append(out / total)
                totals.append(
                    jnp.broadcast_to(highest + jnp.log(total), (BLOCK, HEAD_WIDTH))
                )
            mixed_all[slot, rows, :] = jnp.concatenate(outs, 1).astype(jnp.bfloat16)
            lse_all[slot, rows, :] = jnp.concatenate(totals, 1)
        for step, target, _ in ring(me):
            outgoing(slot, step, target, me).start()
        own_result(slot).start()

    if background:
        do_pending(2)
        work(0)
        do_pending(3)
        work(1)
    else:
        pl.loop(0, SLOTS)(work)
    do_pending(len(pending))
    keep = [
        pltpu.make_async_copy(q_all, q_kept, local_sem.at[4, 0]),
        pltpu.make_async_copy(kv_all, kv_kept, local_sem.at[4, 1]),
        pltpu.make_async_copy(lse_all, lse_kept, local_sem.at[5, 0]),
    ]
    for copy in keep:
        copy.start()
    for slot in range(SLOTS):
        for step, target, source in ring(me):
            outgoing(slot, step, source, source).wait_recv()
            outgoing(slot, step, target, me).wait_send()
            for copy in incoming(slot, step, target, me):
                copy.wait_send()

            @pl.when(two_groups(target))
            def _():
                extra(slot, step, target, me).wait_send()

        own_result(slot).wait()
    for copy in keep:
        copy.wait()


Q_ALL = (SLOTS, TOKENS, PAIR)
KV_ALL = (2, SLOTS, TOKENS, PAIR)


def attend(norm, weight, tables, shards=()):
    bf16 = jnp.bfloat16
    with_gather = bool(shards)
    return pl.pallas_call(
        functools.partial(attend_kernel, with_gather),
        name="attend_gather" if with_gather else "attend",
        out_shape=[
            jax.ShapeDtypeStruct((SLOTS, LOCAL, FULL), bf16),
            jax.ShapeDtypeStruct(Q_ALL, bf16),
            jax.ShapeDtypeStruct(KV_ALL, bf16),
            jax.ShapeDtypeStruct(Q_ALL, jnp.float32),
        ]
        + (Gather.out_shapes(FEED_FORWARD) if with_gather else []),
        in_specs=[VMEM] * (3 + len(shards)),
        out_specs=[ANY] * (4 + len(shards)),
        scratch_shapes=[
            pltpu.VMEM((SLOTS, LOCAL, FULL), bf16),
            pltpu.VMEM((SLOTS, LOCAL, WIDE - FULL), bf16),
            pltpu.VMEM(Q_ALL, bf16),
            pltpu.VMEM(KV_ALL, bf16),
            pltpu.VMEM(Q_ALL, jnp.float32),
            pltpu.VMEM(Q_ALL, bf16),
            pltpu.SemaphoreType.DMA((6, SLOTS)),
            pltpu.SemaphoreType.DMA((4, SLOTS, SHARDS)),
            pltpu.SemaphoreType.DMA((4, SLOTS, SHARDS)),
        ]
        + (Gather.scratch(FEED_FORWARD, 0) if with_gather else []),
        compiler_params=pltpu.CompilerParams(
            collective_id=4 if with_gather else 2,
            has_side_effects=True,
            vmem_limit_bytes=40 * 2**20,
        ),
    )(norm, weight, tables, *shards)


def attend_back_kernel(with_reduce, *refs):
    count = len(FEED_FORWARD) if with_reduce else 0
    slope_ref, q_ref, kv_ref, lse_ref, weight_ref, table_ref = refs[:6]
    dqkv_ref, norm_slope_ref = refs[6 + 2 * count : 8 + 2 * count]
    scratch = refs[8 + 3 * count :]
    slope_all, q_all, kv_all, lse_all, dq_all, dkv_total, dkv_all = scratch[:7]
    dq_ref, dkv_ref, dkv_extra_ref, local_sem, send_sem, recv_sem = scratch[7:13]
    background = None
    if with_reduce:
        background = Reduce(
            FEED_FORWARD_BACK,
            REDUCE_SPREAD,
            refs[6 : 6 + count],
            refs[6 + count : 6 + 2 * count],
            None,
            refs[8 + 2 * count : 8 + 3 * count],
            scratch[13:],
        )
    me = lax.axis_index("fsdp")
    both = two_groups(me)
    second = jnp.where(both, 1, 0)
    extra_at = me // 4

    def incoming(slot, step, device, sender):
        return sent(
            slope_ref.at[slot, :, pair_lanes(device)], slope_all.at[slot, token_rows(sender), :],
            send_sem.at[0, slot, step], recv_sem.at[0, slot, step], device,
        )

    def outgoing(slot, step, device, sender):
        rows = token_rows(device)
        return [
            sent(
                dq_all.at[slot, rows, :], dq_ref.at[slot, :, pair_lanes(sender)],
                send_sem.at[1, slot, step], recv_sem.at[1, slot, step], device,
            ),
            sent(
                dkv_all.at[0, slot, rows, :], dkv_ref.at[sender, slot],
                send_sem.at[2, slot, step], recv_sem.at[2, slot, step], device,
            ),
        ]

    def extra(slot, step, device, sender):
        return sent(
            dkv_all.at[1, slot, token_rows(device), :], dkv_extra_ref.at[sender // 4, slot],
            send_sem.at[3, slot, step], recv_sem.at[3, slot, step], device,
        )

    def own_slope(slot):
        return pltpu.make_async_copy(
            slope_ref.at[slot, :, pair_lanes(me)], slope_all.at[slot, token_rows(me), :],
            local_sem.at[0, slot],
        )

    def own_results(slot):
        rows = token_rows(me)
        return [
            pltpu.make_async_copy(
                dq_all.at[slot, rows, :], dq_ref.at[slot, :, pair_lanes(me)], local_sem.at[1, slot]
            ),
            pltpu.make_async_copy(
                dkv_all.at[0, slot, rows, :], dkv_ref.at[me, slot], local_sem.at[2, slot]
            ),
        ]

    def own_extra(slot):
        return pltpu.make_async_copy(
            dkv_all.at[1, slot, token_rows(me), :], dkv_extra_ref.at[extra_at, slot],
            local_sem.at[3, slot],
        )

    loads = [
        pltpu.make_async_copy(q_ref, q_all, local_sem.at[4, 0]),
        pltpu.make_async_copy(kv_ref, kv_all, local_sem.at[4, 1]),
        pltpu.make_async_copy(lse_ref, lse_all, local_sem.at[5, 0]),
    ]
    for copy in loads:
        copy.start()
    if background:
        background.start_loads()
    greet_all(me, ("C", "Z1", "Z2", "Z3") if background else ())
    for slot in range(SLOTS):
        for step, target, _ in ring(me):
            incoming(slot, step, target, me).start()
        own_slope(slot).start()
    pending = []
    if background:
        background.start_exchange()
        background.start()
        pending = background.steps()
    for copy in loads:
        copy.wait()

    def work(slot):
        for step, _, source in ring(me):
            incoming(slot, step, source, source).wait_recv()
        own_slope(slot).wait()
        dkv_total[...] = jnp.zeros_like(dkv_total)
        for block in range(TOKENS // BLOCK):
            rows = pl.ds(block * BLOCK, BLOCK)
            length = (block + 1) * BLOCK
            outs = []
            for head in range(2):
                group = 0 if head == 0 else second
                lanes = slice(head * HEAD_WIDTH, (head + 1) * HEAD_WIDTH)
                query = q_all[slot, rows, lanes]
                slope = slope_all[slot, rows, lanes]
                lse = lse_all[slot, rows, head * HEAD_WIDTH : head * HEAD_WIDTH + 1]
                keys = kv_all[group, slot, :length, :HEAD_WIDTH]
                values = kv_all[group, slot, :length, HEAD_WIDTH:]
                probs = jnp.exp(causal_mask(dot_t(query, keys)) - lse)
                prob_slope = dot_t(slope, values)
                inner = jnp.sum(probs * prob_slope, -1, keepdims=True)
                score_slope = (probs * (prob_slope - inner)).astype(jnp.bfloat16)
                outs.append(
                    jnp.dot(score_slope, keys, preferred_element_type=jnp.float32)
                    * HEAD_WIDTH ** (-0.5)
                )
                dkv_total[group, :length, :] += jnp.concatenate(
                    [dot_first(score_slope, query), dot_first(probs.astype(jnp.bfloat16), slope)], 1
                )
            dq_all[slot, rows, :] = jnp.concatenate(outs, 1).astype(jnp.bfloat16)
        dkv_all[0, slot] = dkv_total[0].astype(jnp.bfloat16)
        dkv_all[1, slot] = dkv_total[1].astype(jnp.bfloat16)
        for step, target, _ in ring(me):
            for copy in outgoing(slot, step, target, me):
                copy.start()

            @pl.when(both)
            def _():
                extra(slot, step, target, me).start()

        for copy in own_results(slot):
            copy.start()

        @pl.when(both)
        def _():
            own_extra(slot).start()

    if background:
        work(0)
        for step in pending[:BACK_POINT]:
            step()
        work(1)
    else:
        pl.loop(0, SLOTS)(work)

    def collect():
        for slot in range(SLOTS):
            for step, _, source in ring(me):
                for copy in outgoing(slot, step, source, source):
                    copy.wait_recv()

                @pl.when(two_groups(source))
                def _():
                    extra(slot, step, source, source).wait_recv()

            for copy in own_results(slot):
                copy.wait()

            @pl.when(both)
            def _():
                own_extra(slot).wait()

            rows = pl.ds(slot * LOCAL, LOCAL)

            def reversed_rotation(values, table):
                return values * table_ref[table, slot] - turned(values * table_ref[table + 1, slot])

            for lane in range(0, FULL, PAIR):
                values = dq_ref[slot, :, lane : lane + PAIR].astype(jnp.float32)
                dqkv_ref[rows, lane : lane + PAIR] = reversed_rotation(values, 0).astype(
                    jnp.bfloat16
                )
            pairs = (
                (dkv_ref[0, slot], dkv_ref[1, slot]),
                (dkv_extra_ref[0, slot], dkv_ref[2, slot]),
                (dkv_ref[3, slot], dkv_ref[4, slot]),
                (dkv_extra_ref[1, slot], dkv_ref[5, slot]),
                (dkv_ref[6, slot], dkv_ref[7, slot]),
            )
            for group, (one, two) in enumerate(pairs):
                values = one.astype(jnp.float32) + two.astype(jnp.float32)
                lane = FULL + group * PAIR
                dqkv_ref[rows, lane : lane + PAIR] = reversed_rotation(values, 2).astype(
                    jnp.bfloat16
                )
        for first in range(0, FULL, 2 * PAIR):
            norm_slope_ref[:, first : first + 2 * PAIR] = dot_t(
                dqkv_ref[...], weight_ref[first : first + 2 * PAIR, :]
            )

    if background:
        for step in pending[BACK_POINT:BACK_COLLECT]:
            step()
        collect()
        for step in pending[BACK_COLLECT:]:
            step()
    else:
        collect()
    for slot in range(SLOTS):
        for step, target, source in ring(me):
            incoming(slot, step, target, me).wait_send()
            for copy in outgoing(slot, step, target, me):
                copy.wait_send()

            @pl.when(both)
            def _():
                extra(slot, step, target, me).wait_send()


REDUCE_SPREAD = 2
BACK_POINT = 3
BACK_COLLECT = 8


def attend_back(slope, kept, weight, tables, lefts=(), rights=()):
    bf16 = jnp.bfloat16
    with_reduce = bool(lefts)
    return pl.pallas_call(
        functools.partial(attend_back_kernel, with_reduce),
        name="attend_back_reduce" if with_reduce else "attend_back",
        out_shape=[
            jax.ShapeDtypeStruct((ROWS_HERE, WIDE), bf16),
            jax.ShapeDtypeStruct((ROWS_HERE, FULL), jnp.float32),
        ]
        + (Reduce.out_shapes(FEED_FORWARD) if with_reduce else []),
        in_specs=[ANY] * 4 + [VMEM] * 2 + [ANY] * (2 * len(lefts)),
        out_specs=[VMEM] * 2 + [ANY] * len(lefts),
        scratch_shapes=[
            pltpu.VMEM(Q_ALL, bf16),
            pltpu.VMEM(Q_ALL, bf16),
            pltpu.VMEM(KV_ALL, bf16),
            pltpu.VMEM(Q_ALL, jnp.float32),
            pltpu.VMEM(Q_ALL, bf16),
            pltpu.VMEM((2, TOKENS, PAIR), jnp.float32),
            pltpu.VMEM(KV_ALL, bf16),
            pltpu.VMEM((SLOTS, LOCAL, FULL), bf16),
            pltpu.VMEM((SHARDS, SLOTS, LOCAL, PAIR), bf16),
            pltpu.VMEM((2, SLOTS, LOCAL, PAIR), bf16),
            pltpu.SemaphoreType.DMA((6, SLOTS)),
            pltpu.SemaphoreType.DMA((4, SLOTS, SHARDS)),
            pltpu.SemaphoreType.DMA((4, SLOTS, SHARDS)),
        ]
        + (Reduce.scratch(FEED_FORWARD_BACK, REDUCE_SPREAD) if with_reduce else []),
        compiler_params=pltpu.CompilerParams(
            collective_id=5 if with_reduce else 3,
            has_side_effects=True,
            vmem_limit_bytes=(58 if with_reduce else 48) * 2**20,
        ),
    )(slope, *kept, weight, tables, *lefts, *rights)


def rotary_tables(positions):
    half = HEAD_WIDTH // 2
    frequency = BASE ** (-(jnp.arange(half).astype(jnp.float32) * (2.0 / HEAD_WIDTH)))
    angle = positions.astype(jnp.float32)[..., None] * frequency
    cosine, sine = jnp.cos(angle), jnp.sin(angle)
    one, zero = jnp.ones_like(cosine), jnp.zeros_like(sine)
    return jnp.stack(
        [
            jnp.concatenate(parts, -1)
            for parts in (
                [cosine] * 4,
                [sine] * 4,
                [cosine, cosine, one, one],
                [sine, sine, zero, zero],
            )
        ]
    )


def widened(values):
    lead = values.shape[:-1]
    split = values[..., QUERY_WIDTH:].reshape(lead + (2, KEY_VALUE_HEADS, HEAD_WIDTH))
    return jnp.concatenate(
        [
            values[..., :QUERY_WIDTH],
            jnp.zeros(lead + (FULL - QUERY_WIDTH,), values.dtype),
            jnp.swapaxes(split, -2, -3).reshape(lead + (2 * KEY_WIDTH,)),
        ],
        -1,
    )


def narrowed(values):
    lead = values.shape[:-1]
    split = values[..., FULL:].reshape(lead + (KEY_VALUE_HEADS, 2, HEAD_WIDTH))
    return jnp.concatenate(
        [values[..., :QUERY_WIDTH], jnp.swapaxes(split, -2, -3).reshape(lead + (2 * KEY_WIDTH,))],
        -1,
    )


def mean(values):
    return jnp.sum(values, -1, keepdims=True) * (1.0 / D)


def normed(values, gain):
    return values * lax.rsqrt(mean(values * values) + EPSILON) * gain


def norm_backward(values, gain, upstream):
    row_scale = lax.rsqrt(mean(values * values) + EPSILON)
    unit = values * row_scale
    gain_slope = jnp.sum(upstream * unit, 0)
    inner = upstream * gain
    return (row_scale * (inner - unit * mean(inner * unit)), gain_slope)


def padded(values):
    split = values.reshape(values.shape[:-1] + (SHARDS, ROWS))
    widths = ((0, 0),) * (split.ndim - 1) + ((0, PADDED - ROWS),)
    return jnp.pad(split, widths).reshape(values.shape[:-1] + (MODEL,))


def unpadded(values):
    split = values.reshape(values.shape[:-1] + (SHARDS, PADDED))
    return split[..., :ROWS].reshape(values.shape[:-1] + (D,))


def forward_layer(layer_in, tables, weights, shards=()):
    attend_in, attend_out, gate_up, down_weight, gains = weights
    rows = ROWS_HERE
    values = layer_in.reshape(rows, MODEL).astype(jnp.float32)
    first_norm = normed(values, gains[0]).astype(jnp.bfloat16)
    mixed, *attended = attend(first_norm, attend_in, tables, shards)
    if shards:
        *attended, gate_up, down_weight = attended
        gate_up = gate_up.reshape(-1, 2 * FF)
        down_weight = down_weight.reshape(-1, MODEL)
    mixed = mixed.reshape(rows, FULL)
    hidden = values + jnp.dot(mixed, attend_out, preferred_element_type=jnp.float32)
    second_norm = normed(hidden, gains[1]).astype(jnp.bfloat16)
    gated = jnp.dot(second_norm, gate_up, preferred_element_type=jnp.float32)
    act = (jax.nn.silu(gated[:, :FF]) * gated[:, FF:]).astype(jnp.bfloat16)
    result = hidden + jnp.dot(act, down_weight, preferred_element_type=jnp.float32)
    kept = (
        values,
        first_norm,
        attended,
        mixed,
        hidden,
        second_norm,
        gated,
        act,
    )
    weights = (attend_in, attend_out, gate_up, down_weight, gains)
    return (result.astype(jnp.bfloat16).reshape(layer_in.shape), kept, weights)


def backward_layer(upstream, kept, tables, weights, last=False):
    attend_in, attend_out, gate_up, down_weight, gains = weights
    (
        values,
        first_norm,
        attended,
        mixed,
        hidden,
        second_norm,
        gated,
        act,
    ) = kept
    batches, local_count = upstream.shape[:2]
    rows = batches * local_count
    down_in = upstream.reshape(rows, MODEL)
    upstream = down_in.astype(jnp.float32)
    act_slope = jnp.einsum("td,fd->tf", down_in, down_weight, preferred_element_type=jnp.float32)
    gate_part = gated[:, :FF]
    up_part = gated[:, FF:]
    sigma = jax.nn.sigmoid(gate_part)
    gate_slope = act_slope * up_part * sigma * (1.0 + gate_part * (1.0 - sigma))
    up_slope = act_slope * gate_part * sigma
    gated_slope = jnp.concatenate([gate_slope, up_slope], 1).astype(jnp.bfloat16)
    second_slope = jnp.einsum("tf,df->td", gated_slope, gate_up, preferred_element_type=jnp.float32)
    hidden_part, second_gain = norm_backward(hidden, gains[1], second_slope)
    hidden_slope = upstream + hidden_part
    branch_slope = hidden_slope.astype(jnp.bfloat16)
    mixed_gradient = jnp.einsum(
        "td,qd->tq", branch_slope, attend_out, preferred_element_type=jnp.float32
    ).astype(jnp.bfloat16)
    lefts, rights = (), ()
    if last:
        lefts = (second_norm, by_shard(act))
        rights = (gated_slope, down_in)
    projected_slope, first_slope, *summed = attend_back(
        mixed_gradient.reshape(batches, local_count, FULL),
        attended,
        attend_in,
        tables,
        lefts,
        rights,
    )
    input_part, first_gain = norm_backward(values, gains[0], first_slope)
    input_slope = hidden_slope + input_part
    input_slope = input_slope.reshape(batches, local_count, MODEL)
    if not last:
        return input_slope
    gain_slopes = jnp.stack([first_gain, second_gain])
    lefts = (by_core(first_norm), by_core(padded(mixed[:, :QUERY_WIDTH])))
    rights = (projected_slope, branch_slope)
    return (input_slope, (*reduce_gradients(lefts, rights, spare_rows(gain_slopes)), *summed))


def passed_along(value, steps):
    return lax.ppermute(value, "section", [(0, 1)] if steps > 0 else [(1, 0)])


def with_other_core(value):
    size = lax.axis_size("dp")
    other = lax.ppermute(value, "dp", [(index, index ^ 1) for index in range(size)])
    return other


def by_shard(values):
    return values.reshape(ROWS_HERE, SHARDS, -1).swapaxes(0, 1)


def by_core(values):
    return values.reshape(ROWS_HERE, SHARDS, 2, -1).transpose(2, 1, 0, 3)


def spare_rows(gain_slopes):
    core = lax.axis_index("dp") % 2
    gains = (gain_slopes + with_other_core(gain_slopes)).reshape(2, SHARDS, PADDED).swapaxes(0, 1)
    gains = jnp.where(core == 1, gains, 0.0).astype(jnp.bfloat16)
    return jnp.pad(gains, ((0, 0), (8, 6), (0, 0)))


def body(
    inputs, positions, plan, attend_in, attend_out, gate_up, down_weight, norm_gains, cotangent
):
    section_index = lax.axis_index("section")
    extra = PADDED - ROWS
    in_shard = jnp.concatenate(
        [
            widened(attend_in[0]),
            jnp.pad(norm_gains[0], ((0, extra - 2), (0, WIDE - ROWS))),
        ],
        0,
    )
    gathered = gather_weights((in_shard, jnp.pad(padded(attend_out[0]), ((0, extra), (0, 0)))))
    gains = gathered[0][:, ROWS : ROWS + 2, :PADDED].swapaxes(0, 1).reshape(2, MODEL)
    out_weight = gathered[1][:, :ROWS].reshape(QUERY_WIDTH, MODEL)
    weights = (
        gathered[0].reshape(-1, WIDE),
        jnp.pad(out_weight, ((0, FULL - QUERY_WIDTH), (0, 0))),
        None,
        None,
        gains.astype(jnp.float32),
    )
    shards = (
        jnp.pad(gate_up[0], ((0, extra), (0, 0))),
        padded(down_weight[0]),
    )
    plan_row = plan[0]
    fresh = padded(jnp.take(inputs[:, 0], plan_row, axis=0))
    tables = rotary_tables(jnp.take(positions[:, 0], plan_row, axis=0))
    given = padded(cotangent[:, 0])
    result, _, weights = forward_layer(fresh, tables, weights, shards)
    layer_in = jnp.where(section_index == 0, fresh, passed_along(result, 1))
    outputs, kept, _ = forward_layer(layer_in, tables, weights)
    input_slope = backward_layer(given, kept, tables, weights)
    back = passed_along(input_slope.astype(jnp.bfloat16), -1)
    upstream = jnp.where(section_index == 1, given, back)
    input_slope, summed = backward_layer(upstream, kept, tables, weights, True)
    reported = jnp.where(
        section_index == 0, input_slope, input_slope.astype(jnp.bfloat16).astype(jnp.float32)
    )
    input_slopes = unpadded(jnp.take(reported, plan_row, axis=0))
    full = [value.astype(jnp.float32) for value in summed]
    return (
        unpadded(outputs)[None, :, None],
        input_slopes[None, :, None],
        narrowed(full[0])[None, :ROWS],
        unpadded(full[1][:ROWS])[None],
        full[2][None, :ROWS],
        unpadded(full[3])[None],
        full[0][None, ROWS : ROWS + 2, :ROWS],
    )


def solution(mesh):
    in_specs = (
        P(None, "dp", "fsdp", None),
        P(None, "dp", "fsdp"),
        P("dp", None),
        P("section", "fsdp", None),
        P("section", "fsdp", None),
        P("section", "fsdp", None),
        P("section", "fsdp", None),
        P("section", None, "fsdp"),
        P(None, "dp", "fsdp", None),
    )
    out_specs = (
        P("section", None, "dp", "fsdp", None),
        P("section", None, "dp", "fsdp", None),
        P("section", "fsdp", None),
        P("section", "fsdp", None),
        P("section", "fsdp", None),
        P("section", "fsdp", None),
        P("section", None, "fsdp"),
    )
    return jax.shard_map(body, mesh=mesh, in_specs=in_specs, out_specs=out_specs, check_vma=False)
```

```python
import functools

import jax
import jax.numpy as jnp
from jax import lax
from jax.experimental import pallas as pl
from jax.experimental.pallas import tpu as pltpu
from jax.sharding import PartitionSpec as P

D = 960
QUERY_HEADS = 15
KEY_VALUE_HEADS = 5
HEAD_WIDTH = 64
FF = 2560
QUERY_WIDTH = QUERY_HEADS * HEAD_WIDTH
KEY_WIDTH = KEY_VALUE_HEADS * HEAD_WIDTH
QKV = QUERY_WIDTH + 2 * KEY_WIDTH
SHARDS = 8
ROWS = D // SHARDS
PADDED = 128
MODEL = 1024
PAIR = 2 * HEAD_WIDTH
FULL = SHARDS * PAIR
WIDE = FULL + KEY_VALUE_HEADS * PAIR

EPSILON = 1e-05
BASE = 10000.0

MESH = pl.DeviceIdType.MESH
ANY = pl.BlockSpec(memory_space=pl.ANY)
VMEM = pl.BlockSpec(memory_space=pltpu.VMEM)

GATE_UP = (PADDED, 2 * FF, "columns", FF, 0)
GATE_UP_FIRST = (PADDED, FF, "columns", FF, 0)
GATE_UP_SECOND = (PADDED, FF, "columns", FF, FF // 2)
DOWN = (FF // SHARDS, SHARDS * PADDED, "columns", SHARDS * PADDED // 2, 0)
ATTEND_IN = (PADDED, WIDE, "rows", 0, 0)
ATTEND_OUT = (PADDED, SHARDS * PADDED, "rows", 0, 0)
FEED_FORWARD = (GATE_UP, DOWN)
FEED_FORWARD_BACK = (GATE_UP_FIRST, GATE_UP_SECOND, DOWN)
ATTENTION = (ATTEND_IN, ATTEND_OUT)


def half_lanes(shape, core):
    _, columns, _, stride, offset = shape
    return pl.ds(pl.multiple_of(core * stride + offset, 128), columns // 2)


def half_shape(shape):
    rows, columns, kind = shape[:3]
    return (rows // 2, columns) if kind == "rows" else (rows, columns // 2)


def half_view(shape, core, start, count):
    rows, columns, kind = shape[:3]
    if kind == "rows":
        first = pl.multiple_of(core * (rows // 2) + start, 16)
        return (pl.ds(first, count), slice(None))
    return (pl.ds(pl.multiple_of(start, 16), count), half_lanes(shape, core))


def places():
    dp = lax.axis_index("dp")
    fsdp = lax.axis_index("fsdp")
    return dp // 2, dp % 2, fsdp // 4, fsdp % 4


def peer_ids():
    z, core, x, y = places()
    return {
        "X": {"fsdp": (1 - x) * 4 + y},
        "Yp": {"fsdp": x * 4 + (y + 1) % 4},
        "Ym": {"fsdp": x * 4 + (y + 3) % 4},
        "C": {"dp": z * 2 + 1 - core},
        "Z1": {"dp": ((z + 1) % 4) * 2 + core},
        "Z2": {"dp": ((z + 2) % 4) * 2 + core},
        "Z3": {"dp": ((z + 3) % 4) * 2 + core},
    }


def greet(ids, names):
    barrier = pltpu.get_barrier_semaphore()
    for name in names:
        pl.semaphore_signal(barrier, inc=1, device_id=ids[name], device_id_type=MESH)
    pl.semaphore_wait(barrier, len(names))


GATHER = (
    ("X", 0, 0, "f"),
    ("Yp", 0, 0, "f"),
    ("Ym", 0, 0, "f"),
    ("Ym", 0, 1, 0),
    ("X", 0, 1, 0),
    ("Yp", 0, 3, 1),
    ("X", 0, 3, 0),
    ("Yp", 1, 0, 1),
    ("Ym", 1, 0, 1),
    ("Ym", 1, 1, 0),
    ("Yp", 1, 3, 1),
)
GATHER_NEXT = {1: (5, 6), 2: (3, 4), 0: (7, 8), 4: (9,), 7: (10,)}
GATHER_STAGES = ((1, 2, 0), (4, 7, 3, 5, 6, 8), (9, 10))
GATHER_ORDER = (1, 2, 0, 4, 7, 3, 5, 6, 8, 9, 10)


def seen_by_receiver(peer, column, step):
    if peer == "X":
        return 1 - column, step
    if peer == "Yp":
        return column, (step + 3) % 4
    if peer == "Ym":
        return column, (step + 1) % 4
    return column, step


def part_rows(shape, part):
    rows = half_shape(shape)[0]
    return (0, rows) if part == "f" else (part * (rows // 2), rows // 2)


UPWARD = (0, 1, 3, 5, 7)
PLAIN_EDGES = 22
SPREAD_EDGES = 88


class Gather:
    def __init__(self, shapes, spread, shards, outs, sems):
        self.shapes, self.spread, self.shards, self.outs = shapes, spread, shards, outs
        self.local_sem, self.send_sem, self.recv_sem = sems
        self.z, self.core, self.x, self.y = places()
        self.ids = peer_ids()

    def owner(self, column, step):
        return ((self.x + column) % 2) * 4 + (self.y + step) % 4

    def index(self, array, part, which, plane):
        shape = self.shapes[array]
        start, rows = part_rows(shape, part)
        if array == self.spread:
            quarter = half_shape(shape)[0] // 4
            start, rows = plane * quarter + start // 4, rows // 4
        return half_view(shape, which, start, rows)

    def view(self, array, column, step, part, which, plane):
        return self.outs[array].at[
            (self.owner(column, step),) + self.index(array, part, which, plane)
        ]

    def received(self, edge):
        group, base = edge // 11, edge % 11
        peer, column, step, part = GATHER[base]
        column, step = seen_by_receiver(peer, column, step)
        return column, step, part, (0, 0, 3, 1, 2, 3, 1, 2)[group]

    def peer_of(self, edge):
        group, base = edge // 11, edge % 11
        if group == 0:
            return GATHER[base][0]
        if group in (1, 5, 6, 7):
            return "C"
        return {2: "Z1", 3: "Z3", 4: "Z1" if base in UPWARD else "Z3"}[group]

    def copy(self, array, edge):
        group, base = edge // 11, edge % 11
        if group == 0:
            _, column, step, part = GATHER[base]
            away = 0
        else:
            column, step, part, away = self.received(edge)
            if group in (2, 3):
                away = 0
            elif group == 4:
                away = 3 if base in UPWARD else 1
        target = source = self.view(array, column, step, part, self.core, (self.z + away) % 4)
        if group == 0 and (column, step) == (0, 0):
            source = self.shards[array].at[self.index(array, part, self.core, self.z)]
        return pltpu.make_async_remote_copy(
            src_ref=source,
            dst_ref=target,
            send_sem=self.send_sem.at[array, edge],
            recv_sem=self.recv_sem.at[array, edge],
            device_id=self.ids[self.peer_of(edge)],
            device_id_type=MESH,
        )

    def wait_for(self, array, edge):
        column, step, part, away = self.received(edge)
        which = 1 - self.core if edge // 11 in (1, 5, 6, 7) else self.core
        landed = self.view(array, column, step, part, which, (self.z + away) % 4)
        pltpu.make_async_remote_copy(
            src_ref=landed,
            dst_ref=landed,
            send_sem=self.send_sem.at[array, edge],
            recv_sem=self.recv_sem.at[array, edge],
            device_id=self.ids["C"],
            device_id_type=MESH,
        ).wait_recv()

    def own(self, array):
        return pltpu.make_async_copy(
            self.shards[array],
            self.outs[array].at[self.x * 4 + self.y],
            self.local_sem.at[array],
        )

    def start(self):
        for array in range(len(self.shapes)):
            for edge in (0, 1, 2):
                self.copy(array, edge).start()
            self.own(array).start()

    def within_plane(self, array, edges):
        for edge in edges:
            self.wait_for(array, edge)
            for later in GATHER_NEXT.get(edge, ()):
                self.copy(array, later).start()
            if array == self.spread:
                self.copy(array, 22 + edge).start()
                self.copy(array, 33 + edge).start()
            self.copy(array, 11 + edge).start()

    def round_z(self, edges):
        if self.spread is None:
            return
        for edge in edges:
            for group in (2, 3):
                self.wait_for(self.spread, 11 * group + edge)
                if (group == 2) == (edge in UPWARD):
                    self.copy(self.spread, 44 + edge).start()
                self.copy(self.spread, 11 * (group + 3) + edge).start()

    def steps(self):
        first, second, third = GATHER_STAGES
        arrays = range(len(self.shapes))
        steps = [functools.partial(self.within_plane, array, first) for array in arrays]
        steps.append(functools.partial(self.round_z, first))
        steps += [functools.partial(self.within_plane, array, second) for array in arrays]
        steps.append(functools.partial(self.round_z, second))
        steps += [functools.partial(self.within_plane, array, third) for array in arrays]
        steps.append(functools.partial(self.round_z, third))
        steps.append(self.finish)
        return steps

    def finish(self):
        if self.spread is not None:
            for edge in GATHER_ORDER:
                self.wait_for(self.spread, 44 + edge)
                self.copy(self.spread, 77 + edge).start()
        for array in range(len(self.shapes)):
            last = SPREAD_EDGES if array == self.spread else PLAIN_EDGES
            for edge in range(last):
                if edge // 11 in (1, 5, 6, 7):
                    self.wait_for(array, edge)
            for edge in range(last):
                self.copy(array, edge).wait_send()
            self.own(array).wait()

    @staticmethod
    def out_shapes(shapes):
        return [
            jax.ShapeDtypeStruct((SHARDS, rows, columns), jnp.bfloat16)
            for rows, columns, *_ in shapes
        ]

    @staticmethod
    def scratch(shapes, spread):
        edges = PLAIN_EDGES if spread is None else SPREAD_EDGES
        return [
            pltpu.SemaphoreType.DMA((len(shapes),)),
            pltpu.SemaphoreType.DMA((len(shapes), edges)),
            pltpu.SemaphoreType.DMA((len(shapes), edges)),
        ]


def gather_kernel(shapes, *refs):
    count = len(shapes)
    gather = Gather(shapes, None, refs[:count], refs[count : 2 * count], refs[2 * count :])
    greet(gather.ids, ("X", "Yp", "Ym", "C"))
    gather.start()
    for step in gather.steps():
        step()


def gather_weights(shards):
    count = len(ATTENTION)
    return pl.pallas_call(
        functools.partial(gather_kernel, ATTENTION),
        name="gather_weights",
        out_shape=Gather.out_shapes(ATTENTION),
        in_specs=[VMEM] * count,
        out_specs=[ANY] * count,
        scratch_shapes=Gather.scratch(ATTENTION, None),
        compiler_params=pltpu.CompilerParams(collective_id=0, has_side_effects=True),
    )(*shards)


REDUCE = (
    ("Yp", 0, 2, 0, ()),
    ("Ym", 0, 2, 1, ()),
    ("Yp", 1, 2, 0, ()),
    ("Ym", 1, 2, 1, ()),
    ("X", 1, 3, 0, ()),
    ("Yp", 1, 1, 1, ()),
    ("X", 1, 1, 0, (2,)),
    ("Ym", 1, 3, 1, (3,)),
    ("Yp", 0, 1, "f", (0, 6)),
    ("Ym", 0, 3, "f", (1, 4)),
    ("X", 1, 0, "f", (5, 7)),
)
REDUCE_STAGES = ((0, 1, 2, 3, 4, 5), (6, 7), (8, 9, 10))
SHARD_ORDER = ((0, 2), (1, 2), (1, 3), (1, 1), (0, 1), (0, 3), (1, 0), (0, 0))
REDUCE_EDGES = 47
SLOTS = 2
ROWS_HERE = 256


class Reduce:
    def __init__(self, shapes, spread, lefts, rights, extra, outs, scratch):
        count = len(shapes)
        if len(lefts) < count:
            lefts, rights, outs = ((refs[0],) + tuple(refs) for refs in (lefts, rights, outs))
        self.shapes, self.spread, self.outs = shapes, spread, outs
        self.lefts, self.rights, self.extra = lefts, rights, extra
        self.totals = scratch[:count]
        self.wholes = scratch[count : 2 * count]
        self.parts = scratch[2 * count : 3 * count]
        self.quarters = scratch[3 * count : 4 * count]
        self.rounds = None if spread is None else scratch[4 * count]
        self.left_all = list(scratch[-4 - 2 * count : -4 - count])
        self.sides = [(0, 1)] * count
        if shapes[0] is GATE_UP_FIRST:
            self.left_all[1] = self.left_all[0]
            self.sides[1] = (1,)
        self.right_all = scratch[-4 - count : -4]
        self.operand_sem, self.local_sem, self.send_sem, self.recv_sem = scratch[-4:]
        self.z, self.core, self.x, self.y = places()
        self.mine = self.x * 4 + self.y
        self.ids = peer_ids()
        self.plain = [array for array in range(count) if array != spread]

    @staticmethod
    def piece_shapes(shapes, spread):
        halves = [half_shape(shape) for shape in shapes]
        return halves, [
            (half[0], half[1] // 4) if array == spread else half
            for array, half in enumerate(halves)
        ]

    @staticmethod
    def left_shape(shape, half):
        if shape is GATE_UP_SECOND:
            return (16, 128)
        if half[0] == PADDED:
            return (ROWS_HERE, SHARDS * PADDED)
        return (SHARDS, ROWS_HERE, half[0])

    @staticmethod
    def out_shapes(shapes):
        return [jax.ShapeDtypeStruct((rows, columns), jnp.bfloat16) for rows, columns, *_ in shapes]

    @staticmethod
    def scratch(shapes, spread):
        halves, pieces = Reduce.piece_shapes(shapes, spread)
        bf16 = jnp.bfloat16
        buffers = [pltpu.VMEM((SHARDS,) + half, bf16) for half in halves]
        buffers += [pltpu.VMEM((3,) + piece, bf16) for piece in pieces]
        buffers += [pltpu.VMEM((8, piece[0] // 2, piece[1]), bf16) for piece in pieces]
        buffers += [pltpu.VMEM((3, half[0] // 4, half[1]), bf16) for half in halves]
        if spread is not None:
            buffers.append(pltpu.VMEM((3 * SHARDS,) + pieces[spread], bf16))
        buffers += [
            pltpu.VMEM((2,) + Reduce.left_shape(shape, half), bf16)
            for shape, half in zip(shapes, halves)
        ]
        buffers += [pltpu.VMEM((2, ROWS_HERE, half[1]), bf16) for half in halves]
        return buffers + [
            pltpu.SemaphoreType.DMA((len(shapes), 2)),
            pltpu.SemaphoreType.DMA((len(shapes),)),
            pltpu.SemaphoreType.DMA((len(shapes), REDUCE_EDGES)),
            pltpu.SemaphoreType.DMA((len(shapes), REDUCE_EDGES)),
        ]

    def owner(self, column, step):
        return ((self.x + column) % 2) * 4 + (self.y + step) % 4

    def lanes(self, array, plane):
        columns = half_shape(self.shapes[array])[1]
        if array != self.spread:
            return pl.ds(0, columns)
        return pl.ds(pl.multiple_of(plane * (columns // 4), 128), columns // 4)

    def piece(self, array, edge):
        _, column, step, part, _ = REDUCE[edge]
        start, rows = part_rows(self.shapes[array], part)
        return self.totals[array].at[
            self.owner(column, step), pl.ds(start, rows), self.lanes(array, self.z)
        ]

    def slot(self, array, edge):
        return self.parts[array].at[edge] if edge < 8 else self.wholes[array].at[edge - 8]

    def add(self, array, into, start, rows, lanes, source):
        total = self.totals[array]

        @pl.loop(0, rows // 16)
        def _(index):
            offset = pl.multiple_of(index * 16, 16)
            at = pl.ds(pl.multiple_of(start + offset, 16), 16)
            total[into, at, lanes] = (
                total[into, at, lanes].astype(jnp.float32)
                + source[pl.ds(offset, 16), :].astype(jnp.float32)
            ).astype(jnp.bfloat16)

    def quarter(self, array, plane):
        rows = half_shape(self.shapes[array])[0]
        if array == self.spread:
            return 0, rows, self.lanes(array, plane)
        return pl.multiple_of(plane * (rows // 4), 16), rows // 4, self.lanes(array, plane)

    def summed(self, array, plane):
        start, rows, lanes = self.quarter(array, plane)
        return self.totals[array].at[self.mine, pl.ds(start, rows), lanes]

    def out_view(self, array, plane, which):
        shape = self.shapes[array]
        if array == self.spread:
            rows, columns = half_shape(shape)
            first = pl.multiple_of(which * shape[3] + shape[4] + plane * (columns // 4), 128)
            return self.outs[array].at[pl.ds(0, rows), pl.ds(first, columns // 4)]
        start, rows, _ = self.quarter(array, plane)
        return self.outs[array].at[half_view(shape, which, start, rows)]

    def copy(self, array, edge):
        z = self.z
        if edge < 11:
            peer, source, target = REDUCE[edge][0], self.piece(array, edge), self.slot(array, edge)
        elif edge < 14:
            step = edge - 10
            peer, source = f"Z{step}", self.summed(array, (z + step) % 4)
            target = self.quarters[array].at[step - 1]
        elif edge < 17:
            peer, source = f"Z{edge - 13}", self.summed(array, z)
            target = self.out_view(array, z, self.core)
        elif edge < 21:
            peer = "C"
            source = target = self.out_view(array, (z + edge - 17) % 4, self.core)
            if edge == 17:
                source = self.summed(array, z)
        elif edge >= 45:
            peer, source = "C", self.operand(array, edge - 45, 1 - self.core)
            target = (self.left_all, self.right_all)[edge - 45][array].at[1]
        else:
            kind, shard = (edge - 21) // 8, (edge - 21) % 8
            peer = ("Z1" if shard % 2 == 0 else "Z3", "Z1", "Z3")[kind]
            lanes = self.lanes(array, (z + (2, 1, 3)[kind]) % 4)
            source = self.totals[array].at[self.owner(*SHARD_ORDER[shard]), :, lanes]
            target = self.rounds.at[edge - 21]
        return pltpu.make_async_remote_copy(
            src_ref=source,
            dst_ref=target,
            send_sem=self.send_sem.at[array, edge],
            recv_sem=self.recv_sem.at[array, edge],
            device_id=self.ids[peer],
            device_id_type=MESH,
        )

    def wait_for(self, array, edge):
        z = self.z
        if edge < 11:
            landed = self.slot(array, edge)
        elif edge < 14:
            landed = self.quarters[array].at[edge - 11]
        elif edge < 17:
            landed = self.out_view(array, (z + 4 - (edge - 13)) % 4, self.core)
        elif edge < 21:
            landed = self.out_view(array, (z + edge - 17) % 4, 1 - self.core)
        elif edge >= 45:
            landed = (self.left_all, self.right_all)[edge - 45][array].at[1]
        else:
            landed = self.rounds.at[edge - 21]
        pltpu.make_async_remote_copy(
            src_ref=landed,
            dst_ref=landed,
            send_sem=self.send_sem.at[array, edge],
            recv_sem=self.recv_sem.at[array, edge],
            device_id=self.ids["C"],
            device_id_type=MESH,
        ).wait_recv()

    def receive(self, array, edge):
        self.wait_for(array, edge)
        peer, column, step, part, _ = REDUCE[edge]
        column, step = seen_by_receiver(peer, column, step)
        start, rows = part_rows(self.shapes[array], part)
        lanes = self.lanes(array, self.z)
        self.add(array, self.owner(column, step), start, rows, lanes, self.slot(array, edge))

    def receive_round(self, kind, shard):
        edge = 21 + 8 * kind + shard
        array = self.spread
        self.wait_for(array, edge)
        away = 0 if kind > 0 else (1 if shard % 2 == 0 else 3)
        rows = half_shape(self.shapes[array])[0]
        lanes = self.lanes(array, (self.z + away) % 4)
        self.add(
            array, self.owner(*SHARD_ORDER[shard]), 0, rows, lanes, self.rounds.at[edge - 21]
        )

    def stage(self, array, number):
        for edge in REDUCE_STAGES[number]:
            for earlier in REDUCE[edge][4]:
                self.receive(array, earlier)
            self.copy(array, edge).start()

    def operand(self, array, side, core):
        kind = self.shapes[array][2]
        if side == 0:
            return self.lefts[array].at[core] if kind == "rows" else self.lefts[array]
        right = self.rights[array]
        if kind == "rows":
            return right
        if len(right.shape) == 3:
            _, columns, _, _, offset = self.shapes[array]
            return right.at[core, :, pl.ds(offset, columns // 2)]
        return right.at[:, half_lanes(self.shapes[array], core)]

    def load(self, array, side):
        return pltpu.make_async_copy(
            self.operand(array, side, self.core),
            (self.left_all, self.right_all)[side][array].at[0],
            self.operand_sem.at[array, side],
        )

    def make(self, array, shards):
        columns = half_shape(self.shapes[array])[1]
        left, right, total = self.left_all[array], self.right_all[array], self.totals[array]
        for shard in shards:
            owner = self.owner(*SHARD_ORDER[shard])

            def chunk(lanes):
                if len(left.shape) == 3:
                    at = pl.ds(pl.multiple_of(owner * PADDED, PADDED), PADDED)
                    mine, other = left[0, :, at], left[1, :, at]
                else:
                    mine, other = left[0, owner], left[1, owner]
                total[owner, :, lanes] = (
                    dot_first(mine, right[0, :, lanes]) + dot_first(other, right[1, :, lanes])
                ).astype(jnp.bfloat16)

            if columns % 640 == 0 and columns > 640:

                @pl.loop(0, columns // 640)
                def _(index):
                    chunk(pl.ds(pl.multiple_of(index * 640, 128), 640))

            else:
                for first in range(0, columns, 512):
                    chunk(pl.ds(first, min(512, columns - first)))
            if self.extra is not None and array == 0:
                at = pl.ds(half_shape(self.shapes[array])[0] - 16, 16)
                total[owner, at, :128] += self.extra[owner]

    def store(self, array):
        return pltpu.make_async_copy(
            self.summed(array, self.z), self.out_view(array, self.z, self.core),
            self.local_sem.at[array],
        )

    def start_loads(self):
        for array in range(len(self.shapes)):
            for side in self.sides[array]:
                self.load(array, side).start()

    def start_exchange(self):
        for array in range(len(self.shapes)):
            for side in self.sides[array]:
                self.copy(array, 45 + side).start()

    def start(self):
        order = ([] if self.spread is None else [self.spread]) + self.plain
        for array in order:
            for side in self.sides[array]:
                self.load(array, side).wait()
                self.wait_for(array, 45 + side)
            if array == self.spread:
                self.make(array, range(SHARDS))
                for shard in range(SHARDS):
                    self.copy(array, 21 + shard).start()
            else:
                self.make(array, range(4))
                self.stage(array, 0)
        for array in self.plain:
            self.make(array, range(4, SHARDS))

    def first_round(self):
        for shard in range(SHARDS):
            self.receive_round(0, shard)
            self.copy(self.spread, 29 + shard).start()
            self.copy(self.spread, 37 + shard).start()

    def second_round(self, shards):
        for shard in shards:
            self.receive_round(1, shard)
            self.receive_round(2, shard)

    def end_plane(self, array):
        for edge in (8, 9, 10):
            self.receive(array, edge)
        for edge in (11, 12, 13) if array != self.spread else ():
            self.copy(array, edge).start()

    def end_z(self, array):
        if array != self.spread:
            start, rows, lanes = self.quarter(array, self.z)
            for edge in (11, 12, 13):
                self.wait_for(array, edge)
                self.add(
                    array, self.mine, start, rows, lanes, self.quarters[array].at[edge - 11]
                )
        for edge in (14, 15, 16, 17):
            self.copy(array, edge).start()
        self.store(array).start()

    def finish(self):
        for array in range(len(self.shapes)):
            for edge in (14, 15, 16):
                self.wait_for(array, edge)
                self.copy(array, 34 - edge).start()
        for array in range(len(self.shapes)):
            for edge in range(17, 21):
                self.wait_for(array, edge)
            for edge in range(REDUCE_EDGES):
                if edge >= 45:
                    started = edge - 45 in self.sides[array]
                elif array == self.spread:
                    started = edge not in (11, 12, 13)
                else:
                    started = edge < 21
                if started:
                    self.copy(array, edge).wait_send()
            self.store(array).wait()

    def steps(self):
        call = functools.partial
        steps = []
        if self.spread is not None:
            steps.append(self.first_round)
        steps += [call(self.stage, array, 1) for array in self.plain]
        if self.spread is not None:
            steps.append(call(self.second_round, range(4)))
            steps.append(call(self.stage, self.spread, 0))
            steps.append(call(self.second_round, range(4, SHARDS)))
            steps.append(call(self.stage, self.spread, 1))
        steps += [call(self.stage, array, 2) for array in self.plain]
        if self.spread is not None:
            steps.append(call(self.stage, self.spread, 2))
        steps += [call(self.end_plane, array) for array in self.plain]
        if self.spread is not None:
            steps.append(call(self.end_plane, self.spread))
            steps.append(call(self.end_z, self.spread))
        steps += [call(self.end_z, array) for array in self.plain]
        steps.append(self.finish)
        return steps


def reduce_kernel(shapes, *refs):
    count = len(shapes)
    lefts, rights, extra = refs[:count], refs[count : 2 * count], refs[2 * count]
    outs, scratch = refs[2 * count + 1 : 3 * count + 1], refs[3 * count + 1 :]
    reduce = Reduce(shapes, None, lefts, rights, extra, outs, scratch)
    reduce.start_loads()
    greet(reduce.ids, ("X", "Yp", "Ym", "C", "Z1", "Z2", "Z3"))
    reduce.start_exchange()
    reduce.start()
    for step in reduce.steps():
        step()


def reduce_gradients(lefts, rights, extra):
    count = len(ATTENTION)
    return pl.pallas_call(
        functools.partial(reduce_kernel, ATTENTION),
        name="reduce_gradients",
        out_shape=Reduce.out_shapes(ATTENTION),
        in_specs=[ANY] * (2 * count) + [VMEM],
        out_specs=[ANY] * count,
        scratch_shapes=Reduce.scratch(ATTENTION, None),
        compiler_params=pltpu.CompilerParams(
            collective_id=1, has_side_effects=True, vmem_limit_bytes=48 * 2**20
        ),
    )(*lefts, *rights, extra)


TOKENS = 1024
LOCAL = TOKENS // SHARDS
BLOCK = 256
NEGATIVE = -1e30


def two_groups(device):
    return (device == 1) | (device == 4)


def group_lanes(device, which):
    return pl.ds(pl.multiple_of(((2 * device) // 3 + which) * PAIR, PAIR), PAIR)


def pair_lanes(device):
    return pl.ds(pl.multiple_of(device * PAIR, PAIR), PAIR)


def token_rows(device):
    return pl.ds(pl.multiple_of(device * LOCAL, LOCAL), LOCAL)


def ring(me):
    return [(step, (me + step) % SHARDS, (me + SHARDS - step) % SHARDS) for step in range(1, SHARDS)]


def greet_all(me, others=()):
    barrier = pltpu.get_barrier_semaphore()
    ids = peer_ids()
    for device in [{"fsdp": target} for _, target, _ in ring(me)] + [ids[name] for name in others]:
        pl.semaphore_signal(barrier, inc=1, device_id=device, device_id_type=MESH)
    pl.semaphore_wait(barrier, SHARDS - 1 + len(others))


def turned(values):
    lane = lax.broadcasted_iota(jnp.int32, values.shape, 1)
    half = HEAD_WIDTH // 2
    ahead, behind = pltpu.roll(values, PAIR - half, 1), pltpu.roll(values, half, 1)
    return jnp.where(lane % HEAD_WIDTH < half, -ahead, behind)


def sent(source, target, send_sem, recv_sem, device):
    return pltpu.make_async_remote_copy(
        src_ref=source,
        dst_ref=target,
        send_sem=send_sem,
        recv_sem=recv_sem,
        device_id={"fsdp": device},
        device_id_type=MESH,
    )


def causal_mask(values):
    length = values.shape[1]
    row = lax.broadcasted_iota(jnp.int32, (BLOCK, BLOCK), 0)
    column = lax.broadcasted_iota(jnp.int32, (BLOCK, BLOCK), 1)
    own = jnp.where(column <= row, values[:, length - BLOCK :], NEGATIVE)
    if length == BLOCK:
        return own
    return jnp.concatenate([values[:, : length - BLOCK], own], 1)


def dot_t(left, right):
    return lax.dot_general(
        left, right, (((1,), (1,)), ((), ())), preferred_element_type=jnp.float32
    )


def dot_first(left, right):
    return lax.dot_general(
        left, right, (((0,), (0,)), ((), ())), preferred_element_type=jnp.float32
    )


def attend_kernel(with_gather, *refs):
    count = len(FEED_FORWARD) if with_gather else 0
    norm_ref, weight_ref, table_ref = refs[:3]
    mixed_ref, q_kept, kv_kept, lse_kept = refs[3 + count : 7 + count]
    q_ref, kv_ref, q_all, kv_all, lse_all, mixed_all, local_sem, send_sem, recv_sem = refs[
        7 + 2 * count : 16 + 2 * count
    ]
    background = None
    if with_gather:
        background = Gather(
            FEED_FORWARD, 0, refs[3 : 3 + count], refs[7 + count : 7 + 2 * count], refs[-3:]
        )
    me = lax.axis_index("fsdp")
    both = two_groups(me)
    second = jnp.where(both, 1, 0)

    def incoming(slot, step, device, sender):
        rows = token_rows(sender)
        return [
            sent(
                q_ref.at[slot, :, pair_lanes(device)], q_all.at[slot, rows, :],
                send_sem.at[0, slot, step], recv_sem.at[0, slot, step], device,
            ),
            sent(
                kv_ref.at[slot, :, group_lanes(device, 0)], kv_all.at[0, slot, rows, :],
                send_sem.at[1, slot, step], recv_sem.at[1, slot, step], device,
            ),
        ]

    def extra(slot, step, device, sender):
        group = jnp.where(two_groups(device), 1, 0)
        return sent(
            kv_ref.at[slot, :, group_lanes(device, group)], kv_all.at[1, slot, token_rows(sender), :],
            send_sem.at[2, slot, step], recv_sem.at[2, slot, step], device,
        )

    def outgoing(slot, step, device, sender):
        return sent(
            mixed_all.at[slot, token_rows(device), :], mixed_ref.at[slot, :, pair_lanes(sender)],
            send_sem.at[3, slot, step], recv_sem.at[3, slot, step], device,
        )

    def own_copies(slot):
        rows = token_rows(me)
        group = jnp.where(both, 1, 0)
        return [
            pltpu.make_async_copy(
                q_ref.at[slot, :, pair_lanes(me)], q_all.at[slot, rows, :], local_sem.at[0, slot]
            ),
            pltpu.make_async_copy(
                kv_ref.at[slot, :, group_lanes(me, 0)], kv_all.at[0, slot, rows, :],
                local_sem.at[1, slot],
            ),
            pltpu.make_async_copy(
                kv_ref.at[slot, :, group_lanes(me, group)], kv_all.at[1, slot, rows, :],
                local_sem.at[2, slot],
            ),
        ]

    def own_result(slot):
        return pltpu.make_async_copy(
            mixed_all.at[slot, token_rows(me), :], mixed_ref.at[slot, :, pair_lanes(me)],
            local_sem.at[3, slot],
        )

    greet_all(me, ("C", "Z1", "Z3") if background else ())
    pending = []
    if background:
        background.start()
        pending = background.steps()
    for first in range(0, WIDE, 2 * PAIR):
        width = min(2 * PAIR, WIDE - first)
        projected = jnp.dot(
            norm_ref[...], weight_ref[:, first : first + width], preferred_element_type=jnp.float32
        )
        for lane in range(first, first + width, PAIR):
            is_query = lane < FULL
            for slot in range(SLOTS):
                values = projected[
                    slot * LOCAL : (slot + 1) * LOCAL, lane - first : lane - first + PAIR
                ]
                cosine, sine = (table_ref[(0 if is_query else 2) + which, slot] for which in (0, 1))
                rotated = values * cosine + turned(values) * sine
                if is_query:
                    q_ref[slot, :, lane : lane + PAIR] = (rotated * HEAD_WIDTH ** (-0.5)).astype(
                        jnp.bfloat16
                    )
                else:
                    kv_ref[slot, :, lane - FULL : lane - FULL + PAIR] = rotated.astype(jnp.bfloat16)
    for slot in range(SLOTS):
        for step, target, _ in ring(me):
            for copy in incoming(slot, step, target, me):
                copy.start()

            @pl.when(two_groups(target))
            def _():
                extra(slot, step, target, me).start()

        for copy in own_copies(slot):
            copy.start()

    def do_pending(number):
        for _ in range(min(number, len(pending))):
            pending.pop(0)()

    def work(slot):
        for step, _, source in ring(me):
            for copy in incoming(slot, step, source, source):
                copy.wait_recv()

            @pl.when(both)
            def _():
                extra(slot, step, source, source).wait_recv()

        for copy in own_copies(slot):
            copy.wait()
        for block in range(TOKENS // BLOCK):
            rows = pl.ds(block * BLOCK, BLOCK)
            length = (block + 1) * BLOCK
            outs, totals = [], []
            for head in range(2):
                group = 0 if head == 0 else second
                lanes = slice(head * HEAD_WIDTH, (head + 1) * HEAD_WIDTH)
                query = q_all[slot, rows, lanes]
                keys = kv_all[group, slot, :length, :HEAD_WIDTH]
                values = kv_all[group, slot, :length, HEAD_WIDTH:]
                scores = causal_mask(dot_t(query, keys))
                highest = jnp.max(scores, -1, keepdims=True)
                weights = jnp.exp(scores - highest)
                total = jnp.sum(weights, -1, keepdims=True)
                out = jnp.dot(
                    weights.astype(jnp.bfloat16), values, preferred_element_type=jnp.float32
                )
                outs.append(out / total)
                totals.append(
                    jnp.broadcast_to(highest + jnp.log(total), (BLOCK, HEAD_WIDTH))
                )
            mixed_all[slot, rows, :] = jnp.concatenate(outs, 1).astype(jnp.bfloat16)
            lse_all[slot, rows, :] = jnp.concatenate(totals, 1)
        for step, target, _ in ring(me):
            outgoing(slot, step, target, me).start()
        own_result(slot).start()

    if background:
        do_pending(2)
        work(0)
        do_pending(3)
        work(1)
    else:
        pl.loop(0, SLOTS)(work)
    do_pending(len(pending))
    keep = [
        pltpu.make_async_copy(q_all, q_kept, local_sem.at[4, 0]),
        pltpu.make_async_copy(kv_all, kv_kept, local_sem.at[4, 1]),
        pltpu.make_async_copy(lse_all, lse_kept, local_sem.at[5, 0]),
    ]
    for copy in keep:
        copy.start()
    for slot in range(SLOTS):
        for step, target, source in ring(me):
            outgoing(slot, step, source, source).wait_recv()
            outgoing(slot, step, target, me).wait_send()
            for copy in incoming(slot, step, target, me):
                copy.wait_send()

            @pl.when(two_groups(target))
            def _():
                extra(slot, step, target, me).wait_send()

        own_result(slot).wait()
    for copy in keep:
        copy.wait()


Q_ALL = (SLOTS, TOKENS, PAIR)
KV_ALL = (2, SLOTS, TOKENS, PAIR)


def attend(norm, weight, tables, shards=()):
    bf16 = jnp.bfloat16
    with_gather = bool(shards)
    return pl.pallas_call(
        functools.partial(attend_kernel, with_gather),
        name="attend_gather" if with_gather else "attend",
        out_shape=[
            jax.ShapeDtypeStruct((SLOTS, LOCAL, FULL), bf16),
            jax.ShapeDtypeStruct(Q_ALL, bf16),
            jax.ShapeDtypeStruct(KV_ALL, bf16),
            jax.ShapeDtypeStruct(Q_ALL, jnp.float32),
        ]
        + (Gather.out_shapes(FEED_FORWARD) if with_gather else []),
        in_specs=[VMEM] * (3 + len(shards)),
        out_specs=[ANY] * (4 + len(shards)),
        scratch_shapes=[
            pltpu.VMEM((SLOTS, LOCAL, FULL), bf16),
            pltpu.VMEM((SLOTS, LOCAL, WIDE - FULL), bf16),
            pltpu.VMEM(Q_ALL, bf16),
            pltpu.VMEM(KV_ALL, bf16),
            pltpu.VMEM(Q_ALL, jnp.float32),
            pltpu.VMEM(Q_ALL, bf16),
            pltpu.SemaphoreType.DMA((6, SLOTS)),
            pltpu.SemaphoreType.DMA((4, SLOTS, SHARDS)),
            pltpu.SemaphoreType.DMA((4, SLOTS, SHARDS)),
        ]
        + (Gather.scratch(FEED_FORWARD, 0) if with_gather else []),
        compiler_params=pltpu.CompilerParams(
            collective_id=4 if with_gather else 2,
            has_side_effects=True,
            vmem_limit_bytes=40 * 2**20,
        ),
    )(norm, weight, tables, *shards)


def attend_back_kernel(with_reduce, *refs):
    count = len(FEED_FORWARD) if with_reduce else 0
    slope_ref, q_ref, kv_ref, lse_ref, weight_ref, table_ref = refs[:6]
    dqkv_ref, norm_slope_ref = refs[6 + 2 * count : 8 + 2 * count]
    scratch = refs[8 + 3 * count :]
    slope_all, q_all, kv_all, lse_all, dq_all, dkv_total, dkv_all = scratch[:7]
    dq_ref, dkv_ref, dkv_extra_ref, local_sem, send_sem, recv_sem = scratch[7:13]
    background = None
    if with_reduce:
        background = Reduce(
            FEED_FORWARD_BACK,
            REDUCE_SPREAD,
            refs[6 : 6 + count],
            refs[6 + count : 6 + 2 * count],
            None,
            refs[8 + 2 * count : 8 + 3 * count],
            scratch[13:],
        )
    me = lax.axis_index("fsdp")
    both = two_groups(me)
    second = jnp.where(both, 1, 0)
    extra_at = me // 4

    def incoming(slot, step, device, sender):
        return sent(
            slope_ref.at[slot, :, pair_lanes(device)], slope_all.at[slot, token_rows(sender), :],
            send_sem.at[0, slot, step], recv_sem.at[0, slot, step], device,
        )

    def outgoing(slot, step, device, sender):
        rows = token_rows(device)
        return [
            sent(
                dq_all.at[slot, rows, :], dq_ref.at[slot, :, pair_lanes(sender)],
                send_sem.at[1, slot, step], recv_sem.at[1, slot, step], device,
            ),
            sent(
                dkv_all.at[0, slot, rows, :], dkv_ref.at[sender, slot],
                send_sem.at[2, slot, step], recv_sem.at[2, slot, step], device,
            ),
        ]

    def extra(slot, step, device, sender):
        return sent(
            dkv_all.at[1, slot, token_rows(device), :], dkv_extra_ref.at[sender // 4, slot],
            send_sem.at[3, slot, step], recv_sem.at[3, slot, step], device,
        )

    def own_slope(slot):
        return pltpu.make_async_copy(
            slope_ref.at[slot, :, pair_lanes(me)], slope_all.at[slot, token_rows(me), :],
            local_sem.at[0, slot],
        )

    def own_results(slot):
        rows = token_rows(me)
        return [
            pltpu.make_async_copy(
                dq_all.at[slot, rows, :], dq_ref.at[slot, :, pair_lanes(me)], local_sem.at[1, slot]
            ),
            pltpu.make_async_copy(
                dkv_all.at[0, slot, rows, :], dkv_ref.at[me, slot], local_sem.at[2, slot]
            ),
        ]

    def own_extra(slot):
        return pltpu.make_async_copy(
            dkv_all.at[1, slot, token_rows(me), :], dkv_extra_ref.at[extra_at, slot],
            local_sem.at[3, slot],
        )

    loads = [
        pltpu.make_async_copy(q_ref, q_all, local_sem.at[4, 0]),
        pltpu.make_async_copy(kv_ref, kv_all, local_sem.at[4, 1]),
        pltpu.make_async_copy(lse_ref, lse_all, local_sem.at[5, 0]),
    ]
    for copy in loads:
        copy.start()
    if background:
        background.start_loads()
    greet_all(me, ("C", "Z1", "Z2", "Z3") if background else ())
    for slot in range(SLOTS):
        for step, target, _ in ring(me):
            incoming(slot, step, target, me).start()
        own_slope(slot).start()
    pending = []
    if background:
        background.start_exchange()
        background.start()
        pending = background.steps()
    for copy in loads:
        copy.wait()

    def work(slot):
        for step, _, source in ring(me):
            incoming(slot, step, source, source).wait_recv()
        own_slope(slot).wait()
        dkv_total[...] = jnp.zeros_like(dkv_total)
        for block in range(TOKENS // BLOCK):
            rows = pl.ds(block * BLOCK, BLOCK)
            length = (block + 1) * BLOCK
            outs = []
            for head in range(2):
                group = 0 if head == 0 else second
                lanes = slice(head * HEAD_WIDTH, (head + 1) * HEAD_WIDTH)
                query = q_all[slot, rows, lanes]
                slope = slope_all[slot, rows, lanes]
                lse = lse_all[slot, rows, head * HEAD_WIDTH : head * HEAD_WIDTH + 1]
                keys = kv_all[group, slot, :length, :HEAD_WIDTH]
                values = kv_all[group, slot, :length, HEAD_WIDTH:]
                probs = jnp.exp(causal_mask(dot_t(query, keys)) - lse)
                prob_slope = dot_t(slope, values)
                inner = jnp.sum(probs * prob_slope, -1, keepdims=True)
                score_slope = (probs * (prob_slope - inner)).astype(jnp.bfloat16)
                outs.append(
                    jnp.dot(score_slope, keys, preferred_element_type=jnp.float32)
                    * HEAD_WIDTH ** (-0.5)
                )
                dkv_total[group, :length, :] += jnp.concatenate(
                    [dot_first(score_slope, query), dot_first(probs.astype(jnp.bfloat16), slope)], 1
                )
            dq_all[slot, rows, :] = jnp.concatenate(outs, 1).astype(jnp.bfloat16)
        dkv_all[0, slot] = dkv_total[0].astype(jnp.bfloat16)
        dkv_all[1, slot] = dkv_total[1].astype(jnp.bfloat16)
        for step, target, _ in ring(me):
            for copy in outgoing(slot, step, target, me):
                copy.start()

            @pl.when(both)
            def _():
                extra(slot, step, target, me).start()

        for copy in own_results(slot):
            copy.start()

        @pl.when(both)
        def _():
            own_extra(slot).start()

    if background:
        work(0)
        for step in pending[:BACK_POINT]:
            step()
        work(1)
    else:
        pl.loop(0, SLOTS)(work)

    def collect():
        for slot in range(SLOTS):
            for step, _, source in ring(me):
                for copy in outgoing(slot, step, source, source):
                    copy.wait_recv()

                @pl.when(two_groups(source))
                def _():
                    extra(slot, step, source, source).wait_recv()

            for copy in own_results(slot):
                copy.wait()

            @pl.when(both)
            def _():
                own_extra(slot).wait()

            rows = pl.ds(slot * LOCAL, LOCAL)

            def reversed_rotation(values, table):
                return values * table_ref[table, slot] - turned(values * table_ref[table + 1, slot])

            for lane in range(0, FULL, PAIR):
                values = dq_ref[slot, :, lane : lane + PAIR].astype(jnp.float32)
                dqkv_ref[rows, lane : lane + PAIR] = reversed_rotation(values, 0).astype(
                    jnp.bfloat16
                )
            pairs = (
                (dkv_ref[0, slot], dkv_ref[1, slot]),
                (dkv_extra_ref[0, slot], dkv_ref[2, slot]),
                (dkv_ref[3, slot], dkv_ref[4, slot]),
                (dkv_extra_ref[1, slot], dkv_ref[5, slot]),
                (dkv_ref[6, slot], dkv_ref[7, slot]),
            )
            for group, (one, two) in enumerate(pairs):
                values = one.astype(jnp.float32) + two.astype(jnp.float32)
                lane = FULL + group * PAIR
                dqkv_ref[rows, lane : lane + PAIR] = reversed_rotation(values, 2).astype(
                    jnp.bfloat16
                )
        for first in range(0, FULL, 2 * PAIR):
            norm_slope_ref[:, first : first + 2 * PAIR] = dot_t(
                dqkv_ref[...], weight_ref[first : first + 2 * PAIR, :]
            )

    if background:
        for step in pending[BACK_POINT:BACK_COLLECT]:
            step()
        collect()
        for step in pending[BACK_COLLECT:]:
            step()
    else:
        collect()
    for slot in range(SLOTS):
        for step, target, source in ring(me):
            incoming(slot, step, target, me).wait_send()
            for copy in outgoing(slot, step, target, me):
                copy.wait_send()

            @pl.when(both)
            def _():
                extra(slot, step, target, me).wait_send()


REDUCE_SPREAD = 2
BACK_POINT = 3
BACK_COLLECT = 8


def attend_back(slope, kept, weight, tables, lefts=(), rights=()):
    bf16 = jnp.bfloat16
    with_reduce = bool(lefts)
    return pl.pallas_call(
        functools.partial(attend_back_kernel, with_reduce),
        name="attend_back_reduce" if with_reduce else "attend_back",
        out_shape=[
            jax.ShapeDtypeStruct((ROWS_HERE, WIDE), bf16),
            jax.ShapeDtypeStruct((ROWS_HERE, FULL), jnp.float32),
        ]
        + (Reduce.out_shapes(FEED_FORWARD) if with_reduce else []),
        in_specs=[ANY] * 4 + [VMEM] * 2 + [ANY] * (2 * len(lefts)),
        out_specs=[VMEM] * 2 + [ANY] * len(lefts),
        scratch_shapes=[
            pltpu.VMEM(Q_ALL, bf16),
            pltpu.VMEM(Q_ALL, bf16),
            pltpu.VMEM(KV_ALL, bf16),
            pltpu.VMEM(Q_ALL, jnp.float32),
            pltpu.VMEM(Q_ALL, bf16),
            pltpu.VMEM((2, TOKENS, PAIR), jnp.float32),
            pltpu.VMEM(KV_ALL, bf16),
            pltpu.VMEM((SLOTS, LOCAL, FULL), bf16),
            pltpu.VMEM((SHARDS, SLOTS, LOCAL, PAIR), bf16),
            pltpu.VMEM((2, SLOTS, LOCAL, PAIR), bf16),
            pltpu.SemaphoreType.DMA((6, SLOTS)),
            pltpu.SemaphoreType.DMA((4, SLOTS, SHARDS)),
            pltpu.SemaphoreType.DMA((4, SLOTS, SHARDS)),
        ]
        + (Reduce.scratch(FEED_FORWARD_BACK, REDUCE_SPREAD) if with_reduce else []),
        compiler_params=pltpu.CompilerParams(
            collective_id=5 if with_reduce else 3,
            has_side_effects=True,
            vmem_limit_bytes=(58 if with_reduce else 48) * 2**20,
        ),
    )(slope, *kept, weight, tables, *lefts, *rights)


FF_BLOCK = 512


def feed_back_kernel(slope_ref, down_ref, gate_w_ref, up_w_ref, gate_ref, up_ref, out_ref, norm_ref):
    slope = dot_t(slope_ref[...], down_ref[...])
    gate, up = gate_ref[...], up_ref[...]
    sigma = jax.nn.sigmoid(gate)
    gate_slope = (slope * up * sigma * (1.0 + gate * (1.0 - sigma))).astype(jnp.bfloat16)
    up_slope = (slope * gate * sigma).astype(jnp.bfloat16)
    out_ref[0] = gate_slope
    out_ref[1] = up_slope
    norm_slope = dot_t(gate_slope, gate_w_ref[...]) + dot_t(up_slope, up_w_ref[...])

    @pl.when(pl.program_id(0) == 0)
    def _():
        norm_ref[...] = norm_slope

    @pl.when(pl.program_id(0) > 0)
    def _():
        norm_ref[...] += norm_slope


def feed_back(down_in, down_weight, gate_up, gated):
    blocks = FF // FF_BLOCK
    tall = pl.BlockSpec((ROWS_HERE, MODEL), lambda i: (0, 0))
    return pl.pallas_call(
        feed_back_kernel,
        name="feed_back",
        grid=(blocks,),
        out_shape=[
            jax.ShapeDtypeStruct((2, ROWS_HERE, FF), jnp.bfloat16),
            jax.ShapeDtypeStruct((ROWS_HERE, MODEL), jnp.float32),
        ],
        in_specs=[
            tall,
            pl.BlockSpec((FF_BLOCK, MODEL), lambda i: (i, 0)),
            pl.BlockSpec((MODEL, FF_BLOCK), lambda i: (0, i)),
            pl.BlockSpec((MODEL, FF_BLOCK), lambda i: (0, i + blocks)),
            pl.BlockSpec((ROWS_HERE, FF_BLOCK), lambda i: (0, i)),
            pl.BlockSpec((ROWS_HERE, FF_BLOCK), lambda i: (0, i + blocks)),
        ],
        out_specs=[pl.BlockSpec((2, ROWS_HERE, FF_BLOCK), lambda i: (0, 0, i)), tall],
        compiler_params=pltpu.CompilerParams(vmem_limit_bytes=40 * 2**20),
    )(down_in, down_weight, gate_up, gate_up, gated, gated)


def finish_kernel(
    flags_ref, hidden_slope_ref, values_ref, slope_ref, gain_ref, result_ref,
    grads_ref, outputs_ref, gain_slope_ref,
):
    swapped, first = flags_ref[0], flags_ref[1]
    slopes, gain_slope = norm_backward(values_ref[...], gain_ref[...], slope_ref[...])
    slopes += hidden_slope_ref[...]
    low = slopes.astype(jnp.bfloat16).astype(jnp.float32)
    slopes = jnp.where(first == 1, slopes, low)
    gain_slope_ref[...] = gain_slope.reshape(1, MODEL)
    for slot in range(SLOTS):
        place = jnp.where(swapped == 1, 1 - slot, slot)
        rows = slice(slot * LOCAL, (slot + 1) * LOCAL)
        for shard in range(SHARDS):
            into = slice(shard * ROWS, (shard + 1) * ROWS)
            have = slice(shard * PADDED, shard * PADDED + ROWS)
            grads_ref[place, :, into] = slopes[rows, have]
            outputs_ref[slot, :, into] = result_ref[rows, have]


def finish(flags, hidden_slope, values, slope, gain, result):
    return pl.pallas_call(
        finish_kernel,
        name="finish",
        out_shape=[
            jax.ShapeDtypeStruct((SLOTS, LOCAL, D), jnp.float32),
            jax.ShapeDtypeStruct((SLOTS, LOCAL, D), jnp.bfloat16),
            jax.ShapeDtypeStruct((1, MODEL), jnp.float32),
        ],
        in_specs=[pl.BlockSpec(memory_space=pltpu.SMEM)] + [VMEM] * 5,
        out_specs=[VMEM] * 3,
        compiler_params=pltpu.CompilerParams(vmem_limit_bytes=40 * 2**20),
    )(flags, hidden_slope, values, slope, gain, result)


def rotary_tables(positions):
    half = HEAD_WIDTH // 2
    frequency = BASE ** (-(jnp.arange(half).astype(jnp.float32) * (2.0 / HEAD_WIDTH)))
    angle = positions.astype(jnp.float32)[..., None] * frequency
    cosine, sine = jnp.cos(angle), jnp.sin(angle)
    one, zero = jnp.ones_like(cosine), jnp.zeros_like(sine)
    return jnp.stack(
        [
            jnp.concatenate(parts, -1)
            for parts in (
                [cosine] * 4,
                [sine] * 4,
                [cosine, cosine, one, one],
                [sine, sine, zero, zero],
            )
        ]
    )


def widened(values):
    lead = values.shape[:-1]
    split = values[..., QUERY_WIDTH:].reshape(lead + (2, KEY_VALUE_HEADS, HEAD_WIDTH))
    return jnp.concatenate(
        [
            values[..., :QUERY_WIDTH],
            jnp.zeros(lead + (FULL - QUERY_WIDTH,), values.dtype),
            jnp.swapaxes(split, -2, -3).reshape(lead + (2 * KEY_WIDTH,)),
        ],
        -1,
    )


def narrowed(values):
    lead = values.shape[:-1]
    split = values[..., FULL:].reshape(lead + (KEY_VALUE_HEADS, 2, HEAD_WIDTH))
    return jnp.concatenate(
        [values[..., :QUERY_WIDTH], jnp.swapaxes(split, -2, -3).reshape(lead + (2 * KEY_WIDTH,))],
        -1,
    )


def mean(values):
    return jnp.sum(values, -1, keepdims=True) * (1.0 / D)


def normed(values, gain):
    return values * lax.rsqrt(mean(values * values) + EPSILON) * gain


def norm_backward(values, gain, upstream):
    row_scale = lax.rsqrt(mean(values * values) + EPSILON)
    unit = values * row_scale
    gain_slope = jnp.sum(upstream * unit, 0)
    inner = upstream * gain
    return (row_scale * (inner - unit * mean(inner * unit)), gain_slope)


def padded(values):
    split = values.reshape(values.shape[:-1] + (SHARDS, ROWS))
    widths = ((0, 0),) * (split.ndim - 1) + ((0, PADDED - ROWS),)
    return jnp.pad(split, widths).reshape(values.shape[:-1] + (MODEL,))


def unpadded(values):
    split = values.reshape(values.shape[:-1] + (SHARDS, PADDED))
    return split[..., :ROWS].reshape(values.shape[:-1] + (D,))


def forward_layer(layer_in, tables, weights, shards=()):
    attend_in, attend_out, gate_up, down_weight, gains = weights
    rows = ROWS_HERE
    values = layer_in.reshape(rows, MODEL).astype(jnp.float32)
    first_norm = normed(values, gains[0]).astype(jnp.bfloat16)
    mixed, *attended = attend(first_norm, attend_in, tables, shards)
    if shards:
        *attended, gate_up, down_weight = attended
        gate_up = gate_up.reshape(-1, 2 * FF)
        down_weight = down_weight.reshape(-1, MODEL)
    mixed = mixed.reshape(rows, FULL)
    hidden = values + jnp.dot(mixed, attend_out, preferred_element_type=jnp.float32)
    second_norm = normed(hidden, gains[1]).astype(jnp.bfloat16)
    gated = jnp.dot(second_norm, gate_up, preferred_element_type=jnp.float32)
    act = (jax.nn.silu(gated[:, :FF]) * gated[:, FF:]).astype(jnp.bfloat16)
    result = hidden + jnp.dot(act, down_weight, preferred_element_type=jnp.float32)
    kept = (
        values,
        first_norm,
        attended,
        mixed,
        hidden,
        second_norm,
        gated,
        act,
    )
    weights = (attend_in, attend_out, gate_up, down_weight, gains)
    return (result.astype(jnp.bfloat16).reshape(layer_in.shape), kept, weights)


def backward_layer(upstream, kept, tables, weights, ending=None):
    last = ending is not None
    attend_in, attend_out, gate_up, down_weight, gains = weights
    (
        values,
        first_norm,
        attended,
        mixed,
        hidden,
        second_norm,
        gated,
        act,
    ) = kept
    batches, local_count = upstream.shape[:2]
    rows = batches * local_count
    down_in = upstream.reshape(rows, MODEL)
    upstream = down_in.astype(jnp.float32)
    gated_slope, second_slope = feed_back(down_in, down_weight, gate_up, gated)
    hidden_part, second_gain = norm_backward(hidden, gains[1], second_slope)
    hidden_slope = upstream + hidden_part
    branch_slope = hidden_slope.astype(jnp.bfloat16)
    mixed_gradient = jnp.einsum(
        "td,qd->tq", branch_slope, attend_out, preferred_element_type=jnp.float32
    ).astype(jnp.bfloat16)
    lefts, rights = (), ()
    if last:
        lefts = (second_norm, by_shard(act))
        rights = (gated_slope, down_in)
    projected_slope, first_slope, *summed = attend_back(
        mixed_gradient.reshape(batches, local_count, FULL),
        attended,
        attend_in,
        tables,
        lefts,
        rights,
    )
    if not last:
        input_part, _ = norm_backward(values, gains[0], first_slope)
        return (hidden_slope + input_part).reshape(batches, local_count, MODEL)
    flags, result = ending
    input_grads, outputs, first_gain = finish(
        flags, hidden_slope, values, first_slope, gains[:1], result.reshape(rows, MODEL)
    )
    gain_slopes = jnp.stack([first_gain[0], second_gain])
    lefts = (by_core(first_norm), by_core(padded(mixed[:, :QUERY_WIDTH])))
    rights = (projected_slope, branch_slope)
    summed = (*reduce_gradients(lefts, rights, spare_rows(gain_slopes)), *summed)
    return (input_grads, outputs, summed)


def passed_along(value, steps):
    return lax.ppermute(value, "section", [(0, 1)] if steps > 0 else [(1, 0)])


def with_other_core(value):
    size = lax.axis_size("dp")
    other = lax.ppermute(value, "dp", [(index, index ^ 1) for index in range(size)])
    return other


def by_shard(values):
    return values.reshape(ROWS_HERE, SHARDS, -1).swapaxes(0, 1)


def by_core(values):
    return values.reshape(ROWS_HERE, SHARDS, 2, -1).transpose(2, 1, 0, 3)


def spare_rows(gain_slopes):
    core = lax.axis_index("dp") % 2
    gains = (gain_slopes + with_other_core(gain_slopes)).reshape(2, SHARDS, PADDED).swapaxes(0, 1)
    gains = jnp.where(core == 1, gains, 0.0).astype(jnp.bfloat16)
    return jnp.pad(gains, ((0, 0), (8, 6), (0, 0)))


def body(
    inputs, positions, plan, attend_in, attend_out, gate_up, down_weight, norm_gains, cotangent
):
    section_index = lax.axis_index("section")
    extra = PADDED - ROWS
    in_shard = jnp.concatenate(
        [
            widened(attend_in[0]),
            jnp.pad(norm_gains[0], ((0, extra - 2), (0, WIDE - ROWS))),
        ],
        0,
    )
    gathered = gather_weights((in_shard, jnp.pad(padded(attend_out[0]), ((0, extra), (0, 0)))))
    gains = gathered[0][:, ROWS : ROWS + 2, :PADDED].swapaxes(0, 1).reshape(2, MODEL)
    out_weight = gathered[1][:, :ROWS].reshape(QUERY_WIDTH, MODEL)
    weights = (
        gathered[0].reshape(-1, WIDE),
        jnp.pad(out_weight, ((0, FULL - QUERY_WIDTH), (0, 0))),
        None,
        None,
        gains.astype(jnp.float32),
    )
    shards = (
        jnp.pad(gate_up[0], ((0, extra), (0, 0))),
        padded(down_weight[0]),
    )
    plan_row = plan[0]
    swap = plan_row[0] == 1

    def in_slots(values):
        return jnp.where(swap, values[::-1, 0], values[:, 0])

    fresh = padded(in_slots(inputs))
    tables = rotary_tables(in_slots(positions))
    given = padded(cotangent[:, 0])
    result, _, weights = forward_layer(fresh, tables, weights, shards)
    layer_in = jnp.where(section_index == 0, fresh, passed_along(result, 1))
    outputs, kept, _ = forward_layer(layer_in, tables, weights)
    input_slope = backward_layer(given, kept, tables, weights)
    back = passed_along(input_slope.astype(jnp.bfloat16), -1)
    upstream = jnp.where(section_index == 1, given, back)
    flags = jnp.stack([swap, section_index == 0]).astype(jnp.int32)
    input_slopes, outputs, summed = backward_layer(
        upstream, kept, tables, weights, (flags, outputs)
    )
    full = [value.astype(jnp.float32) for value in summed]
    return (
        outputs[None, :, None],
        input_slopes[None, :, None],
        narrowed(full[0])[None, :ROWS],
        unpadded(full[1][:ROWS])[None],
        full[2][None, :ROWS],
        unpadded(full[3])[None],
        full[0][None, ROWS : ROWS + 2, :ROWS],
    )


def solution(mesh):
    in_specs = (
        P(None, "dp", "fsdp", None),
        P(None, "dp", "fsdp"),
        P("dp", None),
        P("section", "fsdp", None),
        P("section", "fsdp", None),
        P("section", "fsdp", None),
        P("section", "fsdp", None),
        P("section", None, "fsdp"),
        P(None, "dp", "fsdp", None),
    )
    out_specs = (
        P("section", None, "dp", "fsdp", None),
        P("section", None, "dp", "fsdp", None),
        P("section", "fsdp", None),
        P("section", "fsdp", None),
        P("section", "fsdp", None),
        P("section", "fsdp", None),
        P("section", None, "fsdp"),
    )
    return jax.shard_map(body, mesh=mesh, in_specs=in_specs, out_specs=out_specs, check_vma=False)
```

```python
import functools

import jax
import jax.numpy as jnp
from jax import lax
from jax.experimental import pallas as pl
from jax.experimental.pallas import tpu as pltpu
from jax.sharding import PartitionSpec as P

D = 960
QUERY_HEADS = 15
KEY_VALUE_HEADS = 5
HEAD_WIDTH = 64
FF = 2560
QUERY_WIDTH = QUERY_HEADS * HEAD_WIDTH
KEY_WIDTH = KEY_VALUE_HEADS * HEAD_WIDTH
QKV = QUERY_WIDTH + 2 * KEY_WIDTH
SHARDS = 8
ROWS = D // SHARDS
PADDED = 128
MODEL = 1024
PAIR = 2 * HEAD_WIDTH
FULL = SHARDS * PAIR
WIDE = FULL + KEY_VALUE_HEADS * PAIR

EPSILON = 1e-05
BASE = 10000.0

MESH = pl.DeviceIdType.MESH
ANY = pl.BlockSpec(memory_space=pl.ANY)
VMEM = pl.BlockSpec(memory_space=pltpu.VMEM)

GATE_UP = (PADDED, 2 * FF, "columns", FF, 0)
GATE_UP_FIRST = (PADDED, FF, "columns", FF, 0)
GATE_UP_SECOND = (PADDED, FF, "columns", FF, FF // 2)
DOWN = (FF // SHARDS, SHARDS * PADDED, "columns", SHARDS * PADDED // 2, 0)
ATTEND_IN = (PADDED, WIDE, "rows", 0, 0)
ATTEND_OUT = (PADDED, SHARDS * PADDED, "rows", 0, 0)
FEED_FORWARD = (GATE_UP, DOWN)
FEED_FORWARD_BACK = (GATE_UP_FIRST, GATE_UP_SECOND, DOWN)
ATTENTION = (ATTEND_IN, ATTEND_OUT)


def half_lanes(shape, core):
    _, columns, _, stride, offset = shape
    return pl.ds(pl.multiple_of(core * stride + offset, 128), columns // 2)


def half_shape(shape):
    rows, columns, kind = shape[:3]
    return (rows // 2, columns) if kind == "rows" else (rows, columns // 2)


def half_view(shape, core, start, count):
    rows, columns, kind = shape[:3]
    if kind == "rows":
        first = pl.multiple_of(core * (rows // 2) + start, 16)
        return (pl.ds(first, count), slice(None))
    return (pl.ds(pl.multiple_of(start, 16), count), half_lanes(shape, core))


def places():
    dp = lax.axis_index("dp")
    fsdp = lax.axis_index("fsdp")
    return dp // 2, dp % 2, fsdp // 4, fsdp % 4


def peer_ids():
    z, core, x, y = places()
    return {
        "X": {"fsdp": (1 - x) * 4 + y},
        "Yp": {"fsdp": x * 4 + (y + 1) % 4},
        "Ym": {"fsdp": x * 4 + (y + 3) % 4},
        "C": {"dp": z * 2 + 1 - core},
        "Z1": {"dp": ((z + 1) % 4) * 2 + core},
        "Z2": {"dp": ((z + 2) % 4) * 2 + core},
        "Z3": {"dp": ((z + 3) % 4) * 2 + core},
    }


def greet(ids, names):
    barrier = pltpu.get_barrier_semaphore()
    for name in names:
        pl.semaphore_signal(barrier, inc=1, device_id=ids[name], device_id_type=MESH)
    pl.semaphore_wait(barrier, len(names))


GATHER = (
    ("X", 0, 0, "f"),
    ("Yp", 0, 0, "f"),
    ("Ym", 0, 0, "f"),
    ("Ym", 0, 1, 0),
    ("X", 0, 1, 0),
    ("Yp", 0, 3, 1),
    ("X", 0, 3, 0),
    ("Yp", 1, 0, 1),
    ("Ym", 1, 0, 1),
    ("Ym", 1, 1, 0),
    ("Yp", 1, 3, 1),
)
GATHER_NEXT = {1: (5, 6), 2: (3, 4), 0: (7, 8), 4: (9,), 7: (10,)}
GATHER_STAGES = ((1, 2, 0), (4, 7, 3, 5, 6, 8), (9, 10))
GATHER_ORDER = (1, 2, 0, 4, 7, 3, 5, 6, 8, 9, 10)


def seen_by_receiver(peer, column, step):
    if peer == "X":
        return 1 - column, step
    if peer == "Yp":
        return column, (step + 3) % 4
    if peer == "Ym":
        return column, (step + 1) % 4
    return column, step


def part_rows(shape, part):
    rows = half_shape(shape)[0]
    return (0, rows) if part == "f" else (part * (rows // 2), rows // 2)


UPWARD = (0, 1, 3, 5, 7)
PLAIN_EDGES = 22
SPREAD_EDGES = 88


class Gather:
    def __init__(self, shapes, spread, shards, outs, sems):
        self.shapes, self.spread, self.shards, self.outs = shapes, spread, shards, outs
        self.local_sem, self.send_sem, self.recv_sem = sems
        self.z, self.core, self.x, self.y = places()
        self.ids = peer_ids()

    def owner(self, column, step):
        return ((self.x + column) % 2) * 4 + (self.y + step) % 4

    def index(self, array, part, which, plane):
        shape = self.shapes[array]
        start, rows = part_rows(shape, part)
        if array == self.spread:
            quarter = half_shape(shape)[0] // 4
            start, rows = plane * quarter + start // 4, rows // 4
        return half_view(shape, which, start, rows)

    def view(self, array, column, step, part, which, plane):
        return self.outs[array].at[
            (self.owner(column, step),) + self.index(array, part, which, plane)
        ]

    def received(self, edge):
        group, base = edge // 11, edge % 11
        peer, column, step, part = GATHER[base]
        column, step = seen_by_receiver(peer, column, step)
        return column, step, part, (0, 0, 3, 1, 2, 3, 1, 2)[group]

    def peer_of(self, edge):
        group, base = edge // 11, edge % 11
        if group == 0:
            return GATHER[base][0]
        if group in (1, 5, 6, 7):
            return "C"
        return {2: "Z1", 3: "Z3", 4: "Z1" if base in UPWARD else "Z3"}[group]

    def copy(self, array, edge):
        group, base = edge // 11, edge % 11
        if group == 0:
            _, column, step, part = GATHER[base]
            away = 0
        else:
            column, step, part, away = self.received(edge)
            if group in (2, 3):
                away = 0
            elif group == 4:
                away = 3 if base in UPWARD else 1
        target = source = self.view(array, column, step, part, self.core, (self.z + away) % 4)
        if group == 0 and (column, step) == (0, 0):
            source = self.shards[array].at[self.index(array, part, self.core, self.z)]
        return pltpu.make_async_remote_copy(
            src_ref=source,
            dst_ref=target,
            send_sem=self.send_sem.at[array, edge],
            recv_sem=self.recv_sem.at[array, edge],
            device_id=self.ids[self.peer_of(edge)],
            device_id_type=MESH,
        )

    def wait_for(self, array, edge):
        column, step, part, away = self.received(edge)
        which = 1 - self.core if edge // 11 in (1, 5, 6, 7) else self.core
        landed = self.view(array, column, step, part, which, (self.z + away) % 4)
        pltpu.make_async_remote_copy(
            src_ref=landed,
            dst_ref=landed,
            send_sem=self.send_sem.at[array, edge],
            recv_sem=self.recv_sem.at[array, edge],
            device_id=self.ids["C"],
            device_id_type=MESH,
        ).wait_recv()

    def own(self, array):
        return pltpu.make_async_copy(
            self.shards[array],
            self.outs[array].at[self.x * 4 + self.y],
            self.local_sem.at[array],
        )

    def start(self):
        for array in range(len(self.shapes)):
            for edge in (0, 1, 2):
                self.copy(array, edge).start()
            self.own(array).start()

    def within_plane(self, array, edges):
        for edge in edges:
            self.wait_for(array, edge)
            for later in GATHER_NEXT.get(edge, ()):
                self.copy(array, later).start()
            if array == self.spread:
                self.copy(array, 22 + edge).start()
                self.copy(array, 33 + edge).start()
            self.copy(array, 11 + edge).start()

    def round_z(self, edges):
        if self.spread is None:
            return
        for edge in edges:
            for group in (2, 3):
                self.wait_for(self.spread, 11 * group + edge)
                if (group == 2) == (edge in UPWARD):
                    self.copy(self.spread, 44 + edge).start()
                self.copy(self.spread, 11 * (group + 3) + edge).start()

    def steps(self):
        first, second, third = GATHER_STAGES
        arrays = range(len(self.shapes))
        steps = [functools.partial(self.within_plane, array, first) for array in arrays]
        steps.append(functools.partial(self.round_z, first))
        steps += [functools.partial(self.within_plane, array, second) for array in arrays]
        steps.append(functools.partial(self.round_z, second))
        steps += [functools.partial(self.within_plane, array, third) for array in arrays]
        steps.append(functools.partial(self.round_z, third))
        steps.append(self.finish)
        return steps

    def finish(self):
        if self.spread is not None:
            for edge in GATHER_ORDER:
                self.wait_for(self.spread, 44 + edge)
                self.copy(self.spread, 77 + edge).start()
        for array in range(len(self.shapes)):
            last = SPREAD_EDGES if array == self.spread else PLAIN_EDGES
            for edge in range(last):
                if edge // 11 in (1, 5, 6, 7):
                    self.wait_for(array, edge)
            for edge in range(last):
                self.copy(array, edge).wait_send()
            self.own(array).wait()

    @staticmethod
    def out_shapes(shapes):
        return [
            jax.ShapeDtypeStruct((SHARDS, rows, columns), jnp.bfloat16)
            for rows, columns, *_ in shapes
        ]

    @staticmethod
    def scratch(shapes, spread):
        edges = PLAIN_EDGES if spread is None else SPREAD_EDGES
        return [
            pltpu.SemaphoreType.DMA((len(shapes),)),
            pltpu.SemaphoreType.DMA((len(shapes), edges)),
            pltpu.SemaphoreType.DMA((len(shapes), edges)),
        ]


def gather_kernel(shapes, *refs):
    count = len(shapes)
    gather = Gather(shapes, None, refs[:count], refs[count : 2 * count], refs[2 * count :])
    greet(gather.ids, ("X", "Yp", "Ym", "C"))
    gather.start()
    for step in gather.steps():
        step()


def gather_weights(shards):
    count = len(ATTENTION)
    return pl.pallas_call(
        functools.partial(gather_kernel, ATTENTION),
        name="gather_weights",
        out_shape=Gather.out_shapes(ATTENTION),
        in_specs=[VMEM] * count,
        out_specs=[ANY] * count,
        scratch_shapes=Gather.scratch(ATTENTION, None),
        compiler_params=pltpu.CompilerParams(collective_id=0, has_side_effects=True),
    )(*shards)


REDUCE = (
    ("Yp", 0, 2, 0, ()),
    ("Ym", 0, 2, 1, ()),
    ("Yp", 1, 2, 0, ()),
    ("Ym", 1, 2, 1, ()),
    ("X", 1, 3, 0, ()),
    ("Yp", 1, 1, 1, ()),
    ("X", 1, 1, 0, (2,)),
    ("Ym", 1, 3, 1, (3,)),
    ("Yp", 0, 1, "f", (0, 6)),
    ("Ym", 0, 3, "f", (1, 4)),
    ("X", 1, 0, "f", (5, 7)),
)
REDUCE_STAGES = ((0, 1, 2, 3, 4, 5), (6, 7), (8, 9, 10))
SHARD_ORDER = ((0, 2), (1, 2), (1, 3), (1, 1), (0, 1), (0, 3), (1, 0), (0, 0))
REDUCE_EDGES = 47
SLOTS = 2
ROWS_HERE = 256


class Reduce:
    def __init__(self, shapes, spread, lefts, rights, extra, outs, scratch):
        count = len(shapes)
        if len(lefts) < count:
            lefts, rights, outs = ((refs[0],) + tuple(refs) for refs in (lefts, rights, outs))
        self.shapes, self.spread, self.outs = shapes, spread, outs
        self.lefts, self.rights, self.extra = lefts, rights, extra
        self.totals = scratch[:count]
        self.wholes = scratch[count : 2 * count]
        self.parts = scratch[2 * count : 3 * count]
        self.quarters = scratch[3 * count : 4 * count]
        self.rounds = None if spread is None else scratch[4 * count]
        self.left_all = list(scratch[-4 - 2 * count : -4 - count])
        self.sides = [(0, 1)] * count
        if shapes[0] is GATE_UP_FIRST:
            self.left_all[1] = self.left_all[0]
            self.sides[1] = (1,)
        self.right_all = scratch[-4 - count : -4]
        self.operand_sem, self.local_sem, self.send_sem, self.recv_sem = scratch[-4:]
        self.z, self.core, self.x, self.y = places()
        self.mine = self.x * 4 + self.y
        self.ids = peer_ids()
        self.plain = [array for array in range(count) if array != spread]

    @staticmethod
    def piece_shapes(shapes, spread):
        halves = [half_shape(shape) for shape in shapes]
        return halves, [
            (half[0], half[1] // 4) if array == spread else half
            for array, half in enumerate(halves)
        ]

    @staticmethod
    def left_shape(shape, half):
        if shape is GATE_UP_SECOND:
            return (16, 128)
        if half[0] == PADDED:
            return (ROWS_HERE, SHARDS * PADDED)
        return (SHARDS, ROWS_HERE, half[0])

    @staticmethod
    def out_shapes(shapes):
        return [jax.ShapeDtypeStruct((rows, columns), jnp.bfloat16) for rows, columns, *_ in shapes]

    @staticmethod
    def scratch(shapes, spread):
        halves, pieces = Reduce.piece_shapes(shapes, spread)
        bf16 = jnp.bfloat16
        buffers = [pltpu.VMEM((SHARDS,) + half, bf16) for half in halves]
        buffers += [pltpu.VMEM((3,) + piece, bf16) for piece in pieces]
        buffers += [pltpu.VMEM((8, piece[0] // 2, piece[1]), bf16) for piece in pieces]
        buffers += [pltpu.VMEM((3, half[0] // 4, half[1]), bf16) for half in halves]
        if spread is not None:
            buffers.append(pltpu.VMEM((3 * SHARDS,) + pieces[spread], bf16))
        buffers += [
            pltpu.VMEM((2,) + Reduce.left_shape(shape, half), bf16)
            for shape, half in zip(shapes, halves)
        ]
        buffers += [pltpu.VMEM((2, ROWS_HERE, half[1]), bf16) for half in halves]
        return buffers + [
            pltpu.SemaphoreType.DMA((len(shapes), 2)),
            pltpu.SemaphoreType.DMA((len(shapes),)),
            pltpu.SemaphoreType.DMA((len(shapes), REDUCE_EDGES)),
            pltpu.SemaphoreType.DMA((len(shapes), REDUCE_EDGES)),
        ]

    def owner(self, column, step):
        return ((self.x + column) % 2) * 4 + (self.y + step) % 4

    def lanes(self, array, plane):
        columns = half_shape(self.shapes[array])[1]
        if array != self.spread:
            return pl.ds(0, columns)
        return pl.ds(pl.multiple_of(plane * (columns // 4), 128), columns // 4)

    def piece(self, array, edge):
        _, column, step, part, _ = REDUCE[edge]
        start, rows = part_rows(self.shapes[array], part)
        return self.totals[array].at[
            self.owner(column, step), pl.ds(start, rows), self.lanes(array, self.z)
        ]

    def slot(self, array, edge):
        return self.parts[array].at[edge] if edge < 8 else self.wholes[array].at[edge - 8]

    def add(self, array, into, start, rows, lanes, source):
        total = self.totals[array]

        @pl.loop(0, rows // 16)
        def _(index):
            offset = pl.multiple_of(index * 16, 16)
            at = pl.ds(pl.multiple_of(start + offset, 16), 16)
            total[into, at, lanes] = (
                total[into, at, lanes].astype(jnp.float32)
                + source[pl.ds(offset, 16), :].astype(jnp.float32)
            ).astype(jnp.bfloat16)

    def quarter(self, array, plane):
        rows = half_shape(self.shapes[array])[0]
        if array == self.spread:
            return 0, rows, self.lanes(array, plane)
        return pl.multiple_of(plane * (rows // 4), 16), rows // 4, self.lanes(array, plane)

    def summed(self, array, plane):
        start, rows, lanes = self.quarter(array, plane)
        return self.totals[array].at[self.mine, pl.ds(start, rows), lanes]

    def out_view(self, array, plane, which):
        shape = self.shapes[array]
        if array == self.spread:
            rows, columns = half_shape(shape)
            first = pl.multiple_of(which * shape[3] + shape[4] + plane * (columns // 4), 128)
            return self.outs[array].at[pl.ds(0, rows), pl.ds(first, columns // 4)]
        start, rows, _ = self.quarter(array, plane)
        return self.outs[array].at[half_view(shape, which, start, rows)]

    def copy(self, array, edge):
        z = self.z
        if edge < 11:
            peer, source, target = REDUCE[edge][0], self.piece(array, edge), self.slot(array, edge)
        elif edge < 14:
            step = edge - 10
            peer, source = f"Z{step}", self.summed(array, (z + step) % 4)
            target = self.quarters[array].at[step - 1]
        elif edge < 17:
            peer, source = f"Z{edge - 13}", self.summed(array, z)
            target = self.out_view(array, z, self.core)
        elif edge < 21:
            peer = "C"
            source = target = self.out_view(array, (z + edge - 17) % 4, self.core)
            if edge == 17:
                source = self.summed(array, z)
        elif edge >= 45:
            peer, source = "C", self.operand(array, edge - 45, 1 - self.core)
            target = (self.left_all, self.right_all)[edge - 45][array].at[1]
        else:
            kind, shard = (edge - 21) // 8, (edge - 21) % 8
            peer = ("Z1" if shard % 2 == 0 else "Z3", "Z1", "Z3")[kind]
            lanes = self.lanes(array, (z + (2, 1, 3)[kind]) % 4)
            source = self.totals[array].at[self.owner(*SHARD_ORDER[shard]), :, lanes]
            target = self.rounds.at[edge - 21]
        return pltpu.make_async_remote_copy(
            src_ref=source,
            dst_ref=target,
            send_sem=self.send_sem.at[array, edge],
            recv_sem=self.recv_sem.at[array, edge],
            device_id=self.ids[peer],
            device_id_type=MESH,
        )

    def wait_for(self, array, edge):
        z = self.z
        if edge < 11:
            landed = self.slot(array, edge)
        elif edge < 14:
            landed = self.quarters[array].at[edge - 11]
        elif edge < 17:
            landed = self.out_view(array, (z + 4 - (edge - 13)) % 4, self.core)
        elif edge < 21:
            landed = self.out_view(array, (z + edge - 17) % 4, 1 - self.core)
        elif edge >= 45:
            landed = (self.left_all, self.right_all)[edge - 45][array].at[1]
        else:
            landed = self.rounds.at[edge - 21]
        pltpu.make_async_remote_copy(
            src_ref=landed,
            dst_ref=landed,
            send_sem=self.send_sem.at[array, edge],
            recv_sem=self.recv_sem.at[array, edge],
            device_id=self.ids["C"],
            device_id_type=MESH,
        ).wait_recv()

    def receive(self, array, edge):
        self.wait_for(array, edge)
        peer, column, step, part, _ = REDUCE[edge]
        column, step = seen_by_receiver(peer, column, step)
        start, rows = part_rows(self.shapes[array], part)
        lanes = self.lanes(array, self.z)
        self.add(array, self.owner(column, step), start, rows, lanes, self.slot(array, edge))

    def receive_round(self, kind, shard):
        edge = 21 + 8 * kind + shard
        array = self.spread
        self.wait_for(array, edge)
        away = 0 if kind > 0 else (1 if shard % 2 == 0 else 3)
        rows = half_shape(self.shapes[array])[0]
        lanes = self.lanes(array, (self.z + away) % 4)
        self.add(
            array, self.owner(*SHARD_ORDER[shard]), 0, rows, lanes, self.rounds.at[edge - 21]
        )

    def stage(self, array, number):
        for edge in REDUCE_STAGES[number]:
            for earlier in REDUCE[edge][4]:
                self.receive(array, earlier)
            self.copy(array, edge).start()

    def operand(self, array, side, core):
        kind = self.shapes[array][2]
        if side == 0:
            return self.lefts[array].at[core] if kind == "rows" else self.lefts[array]
        right = self.rights[array]
        if kind == "rows":
            return right
        if len(right.shape) == 3:
            _, columns, _, _, offset = self.shapes[array]
            return right.at[core, :, pl.ds(offset, columns // 2)]
        return right.at[:, half_lanes(self.shapes[array], core)]

    def load(self, array, side):
        return pltpu.make_async_copy(
            self.operand(array, side, self.core),
            (self.left_all, self.right_all)[side][array].at[0],
            self.operand_sem.at[array, side],
        )

    def make(self, array, shards):
        columns = half_shape(self.shapes[array])[1]
        left, right, total = self.left_all[array], self.right_all[array], self.totals[array]
        for shard in shards:
            owner = self.owner(*SHARD_ORDER[shard])

            def chunk(lanes):
                if len(left.shape) == 3:
                    at = pl.ds(pl.multiple_of(owner * PADDED, PADDED), PADDED)
                    mine, other = left[0, :, at], left[1, :, at]
                else:
                    mine, other = left[0, owner], left[1, owner]
                total[owner, :, lanes] = (
                    dot_first(mine, right[0, :, lanes]) + dot_first(other, right[1, :, lanes])
                ).astype(jnp.bfloat16)

            if columns % 640 == 0 and columns > 640:

                @pl.loop(0, columns // 640)
                def _(index):
                    chunk(pl.ds(pl.multiple_of(index * 640, 128), 640))

            else:
                for first in range(0, columns, 512):
                    chunk(pl.ds(first, min(512, columns - first)))
            if self.extra is not None and array == 0:
                at = pl.ds(half_shape(self.shapes[array])[0] - 16, 16)
                total[owner, at, :128] += self.extra[owner]

    def store(self, array):
        return pltpu.make_async_copy(
            self.summed(array, self.z), self.out_view(array, self.z, self.core),
            self.local_sem.at[array],
        )

    def start_loads(self):
        for array in range(len(self.shapes)):
            for side in self.sides[array]:
                self.load(array, side).start()

    def start_exchange(self):
        for array in range(len(self.shapes)):
            for side in self.sides[array]:
                self.copy(array, 45 + side).start()

    def start(self):
        order = ([] if self.spread is None else [self.spread]) + self.plain
        for array in order:
            for side in self.sides[array]:
                self.load(array, side).wait()
                self.wait_for(array, 45 + side)
            if array == self.spread:
                self.make(array, range(SHARDS))
                for shard in range(SHARDS):
                    self.copy(array, 21 + shard).start()
            else:
                self.make(array, range(4))
                self.stage(array, 0)
        for array in self.plain:
            self.make(array, range(4, SHARDS))

    def first_round(self):
        for shard in range(SHARDS):
            self.receive_round(0, shard)
            self.copy(self.spread, 29 + shard).start()
            self.copy(self.spread, 37 + shard).start()

    def second_round(self, shards):
        for shard in shards:
            self.receive_round(1, shard)
            self.receive_round(2, shard)

    def end_plane(self, array):
        for edge in (8, 9, 10):
            self.receive(array, edge)
        for edge in (11, 12, 13) if array != self.spread else ():
            self.copy(array, edge).start()

    def end_z(self, array):
        if array != self.spread:
            start, rows, lanes = self.quarter(array, self.z)
            for edge in (11, 12, 13):
                self.wait_for(array, edge)
                self.add(
                    array, self.mine, start, rows, lanes, self.quarters[array].at[edge - 11]
                )
        for edge in (14, 15, 16, 17):
            self.copy(array, edge).start()
        self.store(array).start()

    def finish(self):
        for array in range(len(self.shapes)):
            for edge in (14, 15, 16):
                self.wait_for(array, edge)
                self.copy(array, 34 - edge).start()
        for array in range(len(self.shapes)):
            for edge in range(17, 21):
                self.wait_for(array, edge)
            for edge in range(REDUCE_EDGES):
                if edge >= 45:
                    started = edge - 45 in self.sides[array]
                elif array == self.spread:
                    started = edge not in (11, 12, 13)
                else:
                    started = edge < 21
                if started:
                    self.copy(array, edge).wait_send()
            self.store(array).wait()

    def steps(self):
        call = functools.partial
        steps = []
        if self.spread is not None:
            steps.append(self.first_round)
        steps += [call(self.stage, array, 1) for array in self.plain]
        if self.spread is not None:
            steps.append(call(self.second_round, range(4)))
            steps.append(call(self.stage, self.spread, 0))
            steps.append(call(self.second_round, range(4, SHARDS)))
            steps.append(call(self.stage, self.spread, 1))
        steps += [call(self.stage, array, 2) for array in self.plain]
        if self.spread is not None:
            steps.append(call(self.stage, self.spread, 2))
        steps += [call(self.end_plane, array) for array in self.plain]
        if self.spread is not None:
            steps.append(call(self.end_plane, self.spread))
            steps.append(call(self.end_z, self.spread))
        steps += [call(self.end_z, array) for array in self.plain]
        steps.append(self.finish)
        return steps


def reduce_kernel(shapes, *refs):
    count = len(shapes)
    lefts, rights, extra = refs[:count], refs[count : 2 * count], refs[2 * count]
    outs, scratch = refs[2 * count + 1 : 3 * count + 1], refs[3 * count + 1 :]
    reduce = Reduce(shapes, None, lefts, rights, extra, outs, scratch)
    reduce.start_loads()
    greet(reduce.ids, ("X", "Yp", "Ym", "C", "Z1", "Z2", "Z3"))
    reduce.start_exchange()
    reduce.start()
    for step in reduce.steps():
        step()


def reduce_gradients(lefts, rights, extra):
    count = len(ATTENTION)
    return pl.pallas_call(
        functools.partial(reduce_kernel, ATTENTION),
        name="reduce_gradients",
        out_shape=Reduce.out_shapes(ATTENTION),
        in_specs=[ANY] * (2 * count) + [VMEM],
        out_specs=[ANY] * count,
        scratch_shapes=Reduce.scratch(ATTENTION, None),
        compiler_params=pltpu.CompilerParams(
            collective_id=1, has_side_effects=True, vmem_limit_bytes=48 * 2**20
        ),
    )(*lefts, *rights, extra)


TOKENS = 1024
LOCAL = TOKENS // SHARDS
BLOCK = 256
NEGATIVE = -1e30


def two_groups(device):
    return (device == 1) | (device == 4)


def group_lanes(device, which):
    return pl.ds(pl.multiple_of(((2 * device) // 3 + which) * PAIR, PAIR), PAIR)


def pair_lanes(device):
    return pl.ds(pl.multiple_of(device * PAIR, PAIR), PAIR)


def token_rows(device):
    return pl.ds(pl.multiple_of(device * LOCAL, LOCAL), LOCAL)


def ring(me):
    return [(step, (me + step) % SHARDS, (me + SHARDS - step) % SHARDS) for step in range(1, SHARDS)]


def greet_all(me, others=()):
    barrier = pltpu.get_barrier_semaphore()
    ids = peer_ids()
    for device in [{"fsdp": target} for _, target, _ in ring(me)] + [ids[name] for name in others]:
        pl.semaphore_signal(barrier, inc=1, device_id=device, device_id_type=MESH)
    pl.semaphore_wait(barrier, SHARDS - 1 + len(others))


def turned(values):
    lane = lax.broadcasted_iota(jnp.int32, values.shape, 1)
    half = HEAD_WIDTH // 2
    ahead, behind = pltpu.roll(values, PAIR - half, 1), pltpu.roll(values, half, 1)
    return jnp.where(lane % HEAD_WIDTH < half, -ahead, behind)


def sent(source, target, send_sem, recv_sem, device):
    return pltpu.make_async_remote_copy(
        src_ref=source,
        dst_ref=target,
        send_sem=send_sem,
        recv_sem=recv_sem,
        device_id={"fsdp": device},
        device_id_type=MESH,
    )


def causal_mask(values):
    length = values.shape[1]
    row = lax.broadcasted_iota(jnp.int32, (BLOCK, BLOCK), 0)
    column = lax.broadcasted_iota(jnp.int32, (BLOCK, BLOCK), 1)
    own = jnp.where(column <= row, values[:, length - BLOCK :], NEGATIVE)
    if length == BLOCK:
        return own
    return jnp.concatenate([values[:, : length - BLOCK], own], 1)


def dot_t(left, right):
    return lax.dot_general(
        left, right, (((1,), (1,)), ((), ())), preferred_element_type=jnp.float32
    )


def dot_first(left, right):
    return lax.dot_general(
        left, right, (((0,), (0,)), ((), ())), preferred_element_type=jnp.float32
    )


def attend_kernel(with_gather, *refs):
    count = len(FEED_FORWARD) if with_gather else 0
    norm_ref, weight_ref, table_ref = refs[:3]
    mixed_ref, q_kept, kv_kept, lse_kept = refs[3 + count : 7 + count]
    q_ref, kv_ref, q_all, kv_all, lse_all, mixed_all, local_sem, send_sem, recv_sem = refs[
        7 + 2 * count : 16 + 2 * count
    ]
    background = None
    if with_gather:
        background = Gather(
            FEED_FORWARD, 0, refs[3 : 3 + count], refs[7 + count : 7 + 2 * count], refs[-3:]
        )
    me = lax.axis_index("fsdp")
    both = two_groups(me)
    second = jnp.where(both, 1, 0)

    def incoming(slot, step, device, sender):
        rows = token_rows(sender)
        return [
            sent(
                q_ref.at[slot, :, pair_lanes(device)], q_all.at[slot, rows, :],
                send_sem.at[0, slot, step], recv_sem.at[0, slot, step], device,
            ),
            sent(
                kv_ref.at[slot, :, group_lanes(device, 0)], kv_all.at[0, slot, rows, :],
                send_sem.at[1, slot, step], recv_sem.at[1, slot, step], device,
            ),
        ]

    def extra(slot, step, device, sender):
        group = jnp.where(two_groups(device), 1, 0)
        return sent(
            kv_ref.at[slot, :, group_lanes(device, group)], kv_all.at[1, slot, token_rows(sender), :],
            send_sem.at[2, slot, step], recv_sem.at[2, slot, step], device,
        )

    def outgoing(slot, step, device, sender):
        return sent(
            mixed_all.at[slot, token_rows(device), :], mixed_ref.at[slot, :, pair_lanes(sender)],
            send_sem.at[3, slot, step], recv_sem.at[3, slot, step], device,
        )

    def own_copies(slot):
        rows = token_rows(me)
        group = jnp.where(both, 1, 0)
        return [
            pltpu.make_async_copy(
                q_ref.at[slot, :, pair_lanes(me)], q_all.at[slot, rows, :], local_sem.at[0, slot]
            ),
            pltpu.make_async_copy(
                kv_ref.at[slot, :, group_lanes(me, 0)], kv_all.at[0, slot, rows, :],
                local_sem.at[1, slot],
            ),
            pltpu.make_async_copy(
                kv_ref.at[slot, :, group_lanes(me, group)], kv_all.at[1, slot, rows, :],
                local_sem.at[2, slot],
            ),
        ]

    def own_result(slot):
        return pltpu.make_async_copy(
            mixed_all.at[slot, token_rows(me), :], mixed_ref.at[slot, :, pair_lanes(me)],
            local_sem.at[3, slot],
        )

    greet_all(me, ("C", "Z1", "Z3") if background else ())
    pending = []
    if background:
        background.start()
        pending = background.steps()
    for first in range(0, WIDE, 2 * PAIR):
        width = min(2 * PAIR, WIDE - first)
        projected = jnp.dot(
            norm_ref[...], weight_ref[:, first : first + width], preferred_element_type=jnp.float32
        )
        for lane in range(first, first + width, PAIR):
            is_query = lane < FULL
            for slot in range(SLOTS):
                values = projected[
                    slot * LOCAL : (slot + 1) * LOCAL, lane - first : lane - first + PAIR
                ]
                cosine, sine = (table_ref[(0 if is_query else 2) + which, slot] for which in (0, 1))
                rotated = values * cosine + turned(values) * sine
                if is_query:
                    q_ref[slot, :, lane : lane + PAIR] = (rotated * HEAD_WIDTH ** (-0.5)).astype(
                        jnp.bfloat16
                    )
                else:
                    kv_ref[slot, :, lane - FULL : lane - FULL + PAIR] = rotated.astype(jnp.bfloat16)
    for slot in range(SLOTS):
        for step, target, _ in ring(me):
            for copy in incoming(slot, step, target, me):
                copy.start()

            @pl.when(two_groups(target))
            def _():
                extra(slot, step, target, me).start()

        for copy in own_copies(slot):
            copy.start()

    def do_pending(number):
        for _ in range(min(number, len(pending))):
            pending.pop(0)()

    def work(slot):
        for step, _, source in ring(me):
            for copy in incoming(slot, step, source, source):
                copy.wait_recv()

            @pl.when(both)
            def _():
                extra(slot, step, source, source).wait_recv()

        for copy in own_copies(slot):
            copy.wait()
        for block in range(TOKENS // BLOCK):
            rows = pl.ds(block * BLOCK, BLOCK)
            length = (block + 1) * BLOCK
            outs, totals = [], []
            for head in range(2):
                group = 0 if head == 0 else second
                lanes = slice(head * HEAD_WIDTH, (head + 1) * HEAD_WIDTH)
                query = q_all[slot, rows, lanes]
                keys = kv_all[group, slot, :length, :HEAD_WIDTH]
                values = kv_all[group, slot, :length, HEAD_WIDTH:]
                scores = causal_mask(dot_t(query, keys))
                highest = jnp.max(scores, -1, keepdims=True)
                weights = jnp.exp(scores - highest)
                total = jnp.sum(weights, -1, keepdims=True)
                out = jnp.dot(
                    weights.astype(jnp.bfloat16), values, preferred_element_type=jnp.float32
                )
                outs.append(out / total)
                totals.append(
                    jnp.broadcast_to(highest + jnp.log(total), (BLOCK, HEAD_WIDTH))
                )
            mixed_all[slot, rows, :] = jnp.concatenate(outs, 1).astype(jnp.bfloat16)
            lse_all[slot, rows, :] = jnp.concatenate(totals, 1)
        for step, target, _ in ring(me):
            outgoing(slot, step, target, me).start()
        own_result(slot).start()

    if background:
        do_pending(2)
        work(0)
        do_pending(3)
        work(1)
    else:
        pl.loop(0, SLOTS)(work)
    do_pending(len(pending))
    keep = [
        pltpu.make_async_copy(q_all, q_kept, local_sem.at[4, 0]),
        pltpu.make_async_copy(kv_all, kv_kept, local_sem.at[4, 1]),
        pltpu.make_async_copy(lse_all, lse_kept, local_sem.at[5, 0]),
    ]
    for copy in keep:
        copy.start()
    for slot in range(SLOTS):
        for step, target, source in ring(me):
            outgoing(slot, step, source, source).wait_recv()
            outgoing(slot, step, target, me).wait_send()
            for copy in incoming(slot, step, target, me):
                copy.wait_send()

            @pl.when(two_groups(target))
            def _():
                extra(slot, step, target, me).wait_send()

        own_result(slot).wait()
    for copy in keep:
        copy.wait()


Q_ALL = (SLOTS, TOKENS, PAIR)
KV_ALL = (2, SLOTS, TOKENS, PAIR)


def attend(norm, weight, tables, shards=()):
    bf16 = jnp.bfloat16
    with_gather = bool(shards)
    return pl.pallas_call(
        functools.partial(attend_kernel, with_gather),
        name="attend_gather" if with_gather else "attend",
        out_shape=[
            jax.ShapeDtypeStruct((SLOTS, LOCAL, FULL), bf16),
            jax.ShapeDtypeStruct(Q_ALL, bf16),
            jax.ShapeDtypeStruct(KV_ALL, bf16),
            jax.ShapeDtypeStruct(Q_ALL, jnp.float32),
        ]
        + (Gather.out_shapes(FEED_FORWARD) if with_gather else []),
        in_specs=[VMEM] * (3 + len(shards)),
        out_specs=[ANY] * (4 + len(shards)),
        scratch_shapes=[
            pltpu.VMEM((SLOTS, LOCAL, FULL), bf16),
            pltpu.VMEM((SLOTS, LOCAL, WIDE - FULL), bf16),
            pltpu.VMEM(Q_ALL, bf16),
            pltpu.VMEM(KV_ALL, bf16),
            pltpu.VMEM(Q_ALL, jnp.float32),
            pltpu.VMEM(Q_ALL, bf16),
            pltpu.SemaphoreType.DMA((6, SLOTS)),
            pltpu.SemaphoreType.DMA((4, SLOTS, SHARDS)),
            pltpu.SemaphoreType.DMA((4, SLOTS, SHARDS)),
        ]
        + (Gather.scratch(FEED_FORWARD, 0) if with_gather else []),
        compiler_params=pltpu.CompilerParams(
            collective_id=4 if with_gather else 2,
            has_side_effects=True,
            vmem_limit_bytes=40 * 2**20,
        ),
    )(norm, weight, tables, *shards)


def attend_back_kernel(with_reduce, *refs):
    count = len(FEED_FORWARD) if with_reduce else 0
    slope_ref, q_ref, kv_ref, lse_ref, weight_ref, table_ref = refs[:6]
    dqkv_ref, norm_slope_ref = refs[6 + 2 * count : 8 + 2 * count]
    scratch = refs[8 + 3 * count :]
    slope_all, q_all, kv_all, lse_all, dq_all, dkv_total, dkv_all = scratch[:7]
    dq_ref, dkv_ref, dkv_extra_ref, local_sem, send_sem, recv_sem = scratch[7:13]
    background = None
    if with_reduce:
        background = Reduce(
            FEED_FORWARD_BACK,
            REDUCE_SPREAD,
            refs[6 : 6 + count],
            refs[6 + count : 6 + 2 * count],
            None,
            refs[8 + 2 * count : 8 + 3 * count],
            scratch[13:],
        )
    me = lax.axis_index("fsdp")
    both = two_groups(me)
    second = jnp.where(both, 1, 0)
    extra_at = me // 4

    def incoming(slot, step, device, sender):
        return sent(
            slope_ref.at[slot, :, pair_lanes(device)], slope_all.at[slot, token_rows(sender), :],
            send_sem.at[0, slot, step], recv_sem.at[0, slot, step], device,
        )

    def outgoing(slot, step, device, sender):
        rows = token_rows(device)
        return [
            sent(
                dq_all.at[slot, rows, :], dq_ref.at[slot, :, pair_lanes(sender)],
                send_sem.at[1, slot, step], recv_sem.at[1, slot, step], device,
            ),
            sent(
                dkv_all.at[0, slot, rows, :], dkv_ref.at[sender, slot],
                send_sem.at[2, slot, step], recv_sem.at[2, slot, step], device,
            ),
        ]

    def extra(slot, step, device, sender):
        return sent(
            dkv_all.at[1, slot, token_rows(device), :], dkv_extra_ref.at[sender // 4, slot],
            send_sem.at[3, slot, step], recv_sem.at[3, slot, step], device,
        )

    def own_slope(slot):
        return pltpu.make_async_copy(
            slope_ref.at[slot, :, pair_lanes(me)], slope_all.at[slot, token_rows(me), :],
            local_sem.at[0, slot],
        )

    def own_results(slot):
        rows = token_rows(me)
        return [
            pltpu.make_async_copy(
                dq_all.at[slot, rows, :], dq_ref.at[slot, :, pair_lanes(me)], local_sem.at[1, slot]
            ),
            pltpu.make_async_copy(
                dkv_all.at[0, slot, rows, :], dkv_ref.at[me, slot], local_sem.at[2, slot]
            ),
        ]

    def own_extra(slot):
        return pltpu.make_async_copy(
            dkv_all.at[1, slot, token_rows(me), :], dkv_extra_ref.at[extra_at, slot],
            local_sem.at[3, slot],
        )

    loads = [
        pltpu.make_async_copy(q_ref, q_all, local_sem.at[4, 0]),
        pltpu.make_async_copy(kv_ref, kv_all, local_sem.at[4, 1]),
        pltpu.make_async_copy(lse_ref, lse_all, local_sem.at[5, 0]),
    ]
    for copy in loads:
        copy.start()
    if background:
        background.start_loads()
    greet_all(me, ("C", "Z1", "Z2", "Z3") if background else ())
    for slot in range(SLOTS):
        for step, target, _ in ring(me):
            incoming(slot, step, target, me).start()
        own_slope(slot).start()
    pending = []
    if background:
        background.start_exchange()
        background.start()
        pending = background.steps()
    for copy in loads:
        copy.wait()

    def work(slot):
        for step, _, source in ring(me):
            incoming(slot, step, source, source).wait_recv()
        own_slope(slot).wait()
        dkv_total[...] = jnp.zeros_like(dkv_total)
        for block in range(TOKENS // BLOCK):
            rows = pl.ds(block * BLOCK, BLOCK)
            length = (block + 1) * BLOCK
            outs = []
            for head in range(2):
                group = 0 if head == 0 else second
                lanes = slice(head * HEAD_WIDTH, (head + 1) * HEAD_WIDTH)
                query = q_all[slot, rows, lanes]
                slope = slope_all[slot, rows, lanes]
                lse = lse_all[slot, rows, head * HEAD_WIDTH : head * HEAD_WIDTH + 1]
                keys = kv_all[group, slot, :length, :HEAD_WIDTH]
                values = kv_all[group, slot, :length, HEAD_WIDTH:]
                probs = jnp.exp(causal_mask(dot_t(query, keys)) - lse)
                prob_slope = dot_t(slope, values)
                inner = jnp.sum(probs * prob_slope, -1, keepdims=True)
                score_slope = (probs * (prob_slope - inner)).astype(jnp.bfloat16)
                outs.append(
                    jnp.dot(score_slope, keys, preferred_element_type=jnp.float32)
                    * HEAD_WIDTH ** (-0.5)
                )
                dkv_total[group, :length, :] += jnp.concatenate(
                    [dot_first(score_slope, query), dot_first(probs.astype(jnp.bfloat16), slope)], 1
                )
            dq_all[slot, rows, :] = jnp.concatenate(outs, 1).astype(jnp.bfloat16)
        dkv_all[0, slot] = dkv_total[0].astype(jnp.bfloat16)
        dkv_all[1, slot] = dkv_total[1].astype(jnp.bfloat16)
        for step, target, _ in ring(me):
            for copy in outgoing(slot, step, target, me):
                copy.start()

            @pl.when(both)
            def _():
                extra(slot, step, target, me).start()

        for copy in own_results(slot):
            copy.start()

        @pl.when(both)
        def _():
            own_extra(slot).start()

    if background:
        work(0)
        for step in pending[:BACK_POINT]:
            step()
        work(1)
    else:
        pl.loop(0, SLOTS)(work)

    def collect():
        for slot in range(SLOTS):
            for step, _, source in ring(me):
                for copy in outgoing(slot, step, source, source):
                    copy.wait_recv()

                @pl.when(two_groups(source))
                def _():
                    extra(slot, step, source, source).wait_recv()

            for copy in own_results(slot):
                copy.wait()

            @pl.when(both)
            def _():
                own_extra(slot).wait()

            rows = pl.ds(slot * LOCAL, LOCAL)

            def reversed_rotation(values, table):
                return values * table_ref[table, slot] - turned(values * table_ref[table + 1, slot])

            for lane in range(0, FULL, PAIR):
                values = dq_ref[slot, :, lane : lane + PAIR].astype(jnp.float32)
                dqkv_ref[rows, lane : lane + PAIR] = reversed_rotation(values, 0).astype(
                    jnp.bfloat16
                )
            pairs = (
                (dkv_ref[0, slot], dkv_ref[1, slot]),
                (dkv_extra_ref[0, slot], dkv_ref[2, slot]),
                (dkv_ref[3, slot], dkv_ref[4, slot]),
                (dkv_extra_ref[1, slot], dkv_ref[5, slot]),
                (dkv_ref[6, slot], dkv_ref[7, slot]),
            )
            for group, (one, two) in enumerate(pairs):
                values = one.astype(jnp.float32) + two.astype(jnp.float32)
                lane = FULL + group * PAIR
                dqkv_ref[rows, lane : lane + PAIR] = reversed_rotation(values, 2).astype(
                    jnp.bfloat16
                )
        for first in range(0, FULL, 2 * PAIR):
            norm_slope_ref[:, first : first + 2 * PAIR] = dot_t(
                dqkv_ref[...], weight_ref[first : first + 2 * PAIR, :]
            )

    if background:
        for step in pending[BACK_POINT:BACK_COLLECT]:
            step()
        collect()
        for step in pending[BACK_COLLECT:]:
            step()
    else:
        collect()
    for slot in range(SLOTS):
        for step, target, source in ring(me):
            incoming(slot, step, target, me).wait_send()
            for copy in outgoing(slot, step, target, me):
                copy.wait_send()

            @pl.when(both)
            def _():
                extra(slot, step, target, me).wait_send()


REDUCE_SPREAD = 2
BACK_POINT = 5
BACK_COLLECT = 13


def attend_back(slope, kept, weight, tables, lefts=(), rights=()):
    bf16 = jnp.bfloat16
    with_reduce = bool(lefts)
    return pl.pallas_call(
        functools.partial(attend_back_kernel, with_reduce),
        name="attend_back_reduce" if with_reduce else "attend_back",
        out_shape=[
            jax.ShapeDtypeStruct((ROWS_HERE, WIDE), bf16),
            jax.ShapeDtypeStruct((ROWS_HERE, FULL), jnp.float32),
        ]
        + (Reduce.out_shapes(FEED_FORWARD) if with_reduce else []),
        in_specs=[ANY] * 4 + [VMEM] * 2 + [ANY] * (2 * len(lefts)),
        out_specs=[VMEM] * 2 + [ANY] * len(lefts),
        scratch_shapes=[
            pltpu.VMEM(Q_ALL, bf16),
            pltpu.VMEM(Q_ALL, bf16),
            pltpu.VMEM(KV_ALL, bf16),
            pltpu.VMEM(Q_ALL, jnp.float32),
            pltpu.VMEM(Q_ALL, bf16),
            pltpu.VMEM((2, TOKENS, PAIR), jnp.float32),
            pltpu.VMEM(KV_ALL, bf16),
            pltpu.VMEM((SLOTS, LOCAL, FULL), bf16),
            pltpu.VMEM((SHARDS, SLOTS, LOCAL, PAIR), bf16),
            pltpu.VMEM((2, SLOTS, LOCAL, PAIR), bf16),
            pltpu.SemaphoreType.DMA((6, SLOTS)),
            pltpu.SemaphoreType.DMA((4, SLOTS, SHARDS)),
            pltpu.SemaphoreType.DMA((4, SLOTS, SHARDS)),
        ]
        + (Reduce.scratch(FEED_FORWARD_BACK, REDUCE_SPREAD) if with_reduce else []),
        compiler_params=pltpu.CompilerParams(
            collective_id=5 if with_reduce else 3,
            has_side_effects=True,
            vmem_limit_bytes=(58 if with_reduce else 48) * 2**20,
        ),
    )(slope, *kept, weight, tables, *lefts, *rights)


FF_BLOCK = 512


def feed_back_kernel(slope_ref, down_ref, gate_w_ref, up_w_ref, gate_ref, up_ref, out_ref, norm_ref):
    slope = dot_t(slope_ref[...], down_ref[...])
    gate, up = gate_ref[...], up_ref[...]
    sigma = jax.nn.sigmoid(gate)
    gate_slope = (slope * up * sigma * (1.0 + gate * (1.0 - sigma))).astype(jnp.bfloat16)
    up_slope = (slope * gate * sigma).astype(jnp.bfloat16)
    out_ref[0] = gate_slope
    out_ref[1] = up_slope
    norm_slope = dot_t(gate_slope, gate_w_ref[...]) + dot_t(up_slope, up_w_ref[...])

    @pl.when(pl.program_id(0) == 0)
    def _():
        norm_ref[...] = norm_slope

    @pl.when(pl.program_id(0) > 0)
    def _():
        norm_ref[...] += norm_slope


def feed_back(down_in, down_weight, gate_up, gated):
    blocks = FF // FF_BLOCK
    tall = pl.BlockSpec((ROWS_HERE, MODEL), lambda i: (0, 0))
    return pl.pallas_call(
        feed_back_kernel,
        name="feed_back",
        grid=(blocks,),
        out_shape=[
            jax.ShapeDtypeStruct((2, ROWS_HERE, FF), jnp.bfloat16),
            jax.ShapeDtypeStruct((ROWS_HERE, MODEL), jnp.float32),
        ],
        in_specs=[
            tall,
            pl.BlockSpec((FF_BLOCK, MODEL), lambda i: (i, 0)),
            pl.BlockSpec((MODEL, FF_BLOCK), lambda i: (0, i)),
            pl.BlockSpec((MODEL, FF_BLOCK), lambda i: (0, i + blocks)),
            pl.BlockSpec((ROWS_HERE, FF_BLOCK), lambda i: (0, i)),
            pl.BlockSpec((ROWS_HERE, FF_BLOCK), lambda i: (0, i + blocks)),
        ],
        out_specs=[pl.BlockSpec((2, ROWS_HERE, FF_BLOCK), lambda i: (0, 0, i)), tall],
        compiler_params=pltpu.CompilerParams(vmem_limit_bytes=40 * 2**20),
    )(down_in, down_weight, gate_up, gate_up, gated, gated)


def begin_kernel(flags_ref, inputs_ref, cotangent_ref, fresh_ref, given_ref):
    swapped = flags_ref[0]
    fresh_ref[...] = jnp.zeros_like(fresh_ref)
    given_ref[...] = jnp.zeros_like(given_ref)
    for slot in range(SLOTS):
        place = jnp.where(swapped == 1, 1 - slot, slot)
        rows = slice(slot * LOCAL, (slot + 1) * LOCAL)
        for shard in range(SHARDS):
            have = slice(shard * ROWS, (shard + 1) * ROWS)
            into = slice(shard * PADDED, shard * PADDED + ROWS)
            fresh_ref[rows, into] = inputs_ref[place, :, have]
            given_ref[rows, into] = cotangent_ref[slot, :, have]


def begin(flags, inputs, cotangent):
    return pl.pallas_call(
        begin_kernel,
        name="begin",
        out_shape=[jax.ShapeDtypeStruct((ROWS_HERE, MODEL), jnp.bfloat16)] * 2,
        in_specs=[pl.BlockSpec(memory_space=pltpu.SMEM)] + [VMEM] * 2,
        out_specs=[VMEM] * 2,
        compiler_params=pltpu.CompilerParams(vmem_limit_bytes=40 * 2**20),
    )(flags, inputs, cotangent)


def finish_kernel(
    flags_ref, hidden_slope_ref, values_ref, slope_ref, gain_ref, result_ref,
    grads_ref, outputs_ref, gain_slope_ref,
):
    swapped, first = flags_ref[0], flags_ref[1]
    slopes, gain_slope = norm_backward(values_ref[...], gain_ref[...], slope_ref[...])
    slopes += hidden_slope_ref[...]
    low = slopes.astype(jnp.bfloat16).astype(jnp.float32)
    slopes = jnp.where(first == 1, slopes, low)
    gain_slope_ref[...] = gain_slope.reshape(1, MODEL)
    for slot in range(SLOTS):
        place = jnp.where(swapped == 1, 1 - slot, slot)
        rows = slice(slot * LOCAL, (slot + 1) * LOCAL)
        for shard in range(SHARDS):
            into = slice(shard * ROWS, (shard + 1) * ROWS)
            have = slice(shard * PADDED, shard * PADDED + ROWS)
            grads_ref[place, :, into] = slopes[rows, have]
            outputs_ref[slot, :, into] = result_ref[rows, have]


def finish(flags, hidden_slope, values, slope, gain, result):
    return pl.pallas_call(
        finish_kernel,
        name="finish",
        out_shape=[
            jax.ShapeDtypeStruct((SLOTS, LOCAL, D), jnp.float32),
            jax.ShapeDtypeStruct((SLOTS, LOCAL, D), jnp.bfloat16),
            jax.ShapeDtypeStruct((1, MODEL), jnp.float32),
        ],
        in_specs=[pl.BlockSpec(memory_space=pltpu.SMEM)] + [VMEM] * 5,
        out_specs=[VMEM] * 3,
        compiler_params=pltpu.CompilerParams(vmem_limit_bytes=40 * 2**20),
    )(flags, hidden_slope, values, slope, gain, result)


def rotary_tables(positions):
    half = HEAD_WIDTH // 2
    frequency = BASE ** (-(jnp.arange(half).astype(jnp.float32) * (2.0 / HEAD_WIDTH)))
    angle = positions.astype(jnp.float32)[..., None] * frequency
    cosine, sine = jnp.cos(angle), jnp.sin(angle)
    one, zero = jnp.ones_like(cosine), jnp.zeros_like(sine)
    return jnp.stack(
        [
            jnp.concatenate(parts, -1)
            for parts in (
                [cosine] * 4,
                [sine] * 4,
                [cosine, cosine, one, one],
                [sine, sine, zero, zero],
            )
        ]
    )


def widened(values):
    lead = values.shape[:-1]
    split = values[..., QUERY_WIDTH:].reshape(lead + (2, KEY_VALUE_HEADS, HEAD_WIDTH))
    return jnp.concatenate(
        [
            values[..., :QUERY_WIDTH],
            jnp.zeros(lead + (FULL - QUERY_WIDTH,), values.dtype),
            jnp.swapaxes(split, -2, -3).reshape(lead + (2 * KEY_WIDTH,)),
        ],
        -1,
    )


def narrowed(values):
    lead = values.shape[:-1]
    split = values[..., FULL:].reshape(lead + (KEY_VALUE_HEADS, 2, HEAD_WIDTH))
    return jnp.concatenate(
        [values[..., :QUERY_WIDTH], jnp.swapaxes(split, -2, -3).reshape(lead + (2 * KEY_WIDTH,))],
        -1,
    )


def mean(values):
    return jnp.sum(values, -1, keepdims=True) * (1.0 / D)


def normed(values, gain):
    return values * lax.rsqrt(mean(values * values) + EPSILON) * gain


def norm_backward(values, gain, upstream):
    row_scale = lax.rsqrt(mean(values * values) + EPSILON)
    unit = values * row_scale
    gain_slope = jnp.sum(upstream * unit, 0)
    inner = upstream * gain
    return (row_scale * (inner - unit * mean(inner * unit)), gain_slope)


def padded(values):
    split = values.reshape(values.shape[:-1] + (SHARDS, ROWS))
    widths = ((0, 0),) * (split.ndim - 1) + ((0, PADDED - ROWS),)
    return jnp.pad(split, widths).reshape(values.shape[:-1] + (MODEL,))


def unpadded(values):
    split = values.reshape(values.shape[:-1] + (SHARDS, PADDED))
    return split[..., :ROWS].reshape(values.shape[:-1] + (D,))


def forward_layer(layer_in, tables, weights, shards=()):
    attend_in, attend_out, gate_up, down_weight, gains = weights
    rows = ROWS_HERE
    values = layer_in.astype(jnp.float32)
    first_norm = normed(values, gains[0]).astype(jnp.bfloat16)
    mixed, *attended = attend(first_norm, attend_in, tables, shards)
    if shards:
        *attended, gate_up, down_weight = attended
        gate_up = gate_up.reshape(-1, 2 * FF)
        down_weight = down_weight.reshape(-1, MODEL)
    mixed = mixed.reshape(rows, FULL)
    hidden = values + jnp.dot(mixed, attend_out, preferred_element_type=jnp.float32)
    second_norm = normed(hidden, gains[1]).astype(jnp.bfloat16)
    gated = jnp.dot(second_norm, gate_up, preferred_element_type=jnp.float32)
    act = (jax.nn.silu(gated[:, :FF]) * gated[:, FF:]).astype(jnp.bfloat16)
    result = hidden + jnp.dot(act, down_weight, preferred_element_type=jnp.float32)
    kept = (
        values,
        first_norm,
        attended,
        mixed,
        hidden,
        second_norm,
        gated,
        act,
    )
    weights = (attend_in, attend_out, gate_up, down_weight, gains)
    return (result.astype(jnp.bfloat16), kept, weights)


def backward_layer(upstream, kept, tables, weights, ending=None):
    last = ending is not None
    attend_in, attend_out, gate_up, down_weight, gains = weights
    (
        values,
        first_norm,
        attended,
        mixed,
        hidden,
        second_norm,
        gated,
        act,
    ) = kept
    down_in = upstream
    upstream = upstream.astype(jnp.float32)
    gated_slope, second_slope = feed_back(down_in, down_weight, gate_up, gated)
    hidden_part, second_gain = norm_backward(hidden, gains[1], second_slope)
    hidden_slope = upstream + hidden_part
    branch_slope = hidden_slope.astype(jnp.bfloat16)
    mixed_gradient = jnp.einsum(
        "td,qd->tq", branch_slope, attend_out, preferred_element_type=jnp.float32
    ).astype(jnp.bfloat16)
    lefts, rights = (), ()
    if last:
        lefts = (second_norm, by_shard(act))
        rights = (gated_slope, down_in)
    projected_slope, first_slope, *summed = attend_back(
        mixed_gradient.reshape(SLOTS, LOCAL, FULL),
        attended,
        attend_in,
        tables,
        lefts,
        rights,
    )
    if not last:
        input_part, _ = norm_backward(values, gains[0], first_slope)
        return hidden_slope + input_part
    flags, result = ending
    input_grads, outputs, first_gain = finish(
        flags, hidden_slope, values, first_slope, gains[:1], result
    )
    gain_slopes = jnp.stack([first_gain[0], second_gain])
    lefts = (by_core(first_norm), by_core(padded(mixed[:, :QUERY_WIDTH])))
    rights = (projected_slope, branch_slope)
    summed = (*reduce_gradients(lefts, rights, spare_rows(gain_slopes)), *summed)
    return (input_grads, outputs, summed)


def passed_along(value, steps):
    return lax.ppermute(value, "section", [(0, 1)] if steps > 0 else [(1, 0)])


def with_other_core(value):
    size = lax.axis_size("dp")
    other = lax.ppermute(value, "dp", [(index, index ^ 1) for index in range(size)])
    return other


def by_shard(values):
    return values.reshape(ROWS_HERE, SHARDS, -1).swapaxes(0, 1)


def by_core(values):
    return values.reshape(ROWS_HERE, SHARDS, 2, -1).transpose(2, 1, 0, 3)


def spare_rows(gain_slopes):
    core = lax.axis_index("dp") % 2
    gains = (gain_slopes + with_other_core(gain_slopes)).reshape(2, SHARDS, PADDED).swapaxes(0, 1)
    gains = jnp.where(core == 1, gains, 0.0).astype(jnp.bfloat16)
    return jnp.pad(gains, ((0, 0), (8, 6), (0, 0)))


def body(
    inputs, positions, plan, attend_in, attend_out, gate_up, down_weight, norm_gains, cotangent
):
    section_index = lax.axis_index("section")
    extra = PADDED - ROWS
    in_shard = jnp.concatenate(
        [
            widened(attend_in[0]),
            jnp.pad(norm_gains[0], ((0, extra - 2), (0, WIDE - ROWS))),
        ],
        0,
    )
    gathered = gather_weights((in_shard, jnp.pad(padded(attend_out[0]), ((0, extra), (0, 0)))))
    gains = gathered[0][:, ROWS : ROWS + 2, :PADDED].swapaxes(0, 1).reshape(2, MODEL)
    out_weight = gathered[1][:, :ROWS].reshape(QUERY_WIDTH, MODEL)
    weights = (
        gathered[0].reshape(-1, WIDE),
        jnp.pad(out_weight, ((0, FULL - QUERY_WIDTH), (0, 0))),
        None,
        None,
        gains.astype(jnp.float32),
    )
    shards = (
        jnp.pad(gate_up[0], ((0, extra), (0, 0))),
        padded(down_weight[0]),
    )
    plan_row = plan[0]
    swap = plan_row[0] == 1

    def in_slots(values):
        return jnp.where(swap, values[::-1, 0], values[:, 0])

    flags = jnp.stack([swap, section_index == 0]).astype(jnp.int32)
    fresh, given = begin(flags, inputs[:, 0], cotangent[:, 0])
    tables = rotary_tables(in_slots(positions))
    result, _, weights = forward_layer(fresh, tables, weights, shards)
    layer_in = jnp.where(section_index == 0, fresh, passed_along(result, 1))
    outputs, kept, _ = forward_layer(layer_in, tables, weights)
    input_slope = backward_layer(given, kept, tables, weights)
    back = passed_along(input_slope.astype(jnp.bfloat16), -1)
    upstream = jnp.where(section_index == 1, given, back)
    input_slopes, outputs, summed = backward_layer(
        upstream, kept, tables, weights, (flags, outputs)
    )
    full = [value.astype(jnp.float32) for value in summed]
    return (
        outputs[None, :, None],
        input_slopes[None, :, None],
        narrowed(full[0])[None, :ROWS],
        unpadded(full[1][:ROWS])[None],
        full[2][None, :ROWS],
        unpadded(full[3])[None],
        full[0][None, ROWS : ROWS + 2, :ROWS],
    )


def solution(mesh):
    in_specs = (
        P(None, "dp", "fsdp", None),
        P(None, "dp", "fsdp"),
        P("dp", None),
        P("section", "fsdp", None),
        P("section", "fsdp", None),
        P("section", "fsdp", None),
        P("section", "fsdp", None),
        P("section", None, "fsdp"),
        P(None, "dp", "fsdp", None),
    )
    out_specs = (
        P("section", None, "dp", "fsdp", None),
        P("section", None, "dp", "fsdp", None),
        P("section", "fsdp", None),
        P("section", "fsdp", None),
        P("section", "fsdp", None),
        P("section", "fsdp", None),
        P("section", None, "fsdp"),
    )
    return jax.shard_map(body, mesh=mesh, in_specs=in_specs, out_specs=out_specs, check_vma=False)
```

```python
import functools

import jax
import jax.numpy as jnp
from jax import lax
from jax.experimental import pallas as pl
from jax.experimental.pallas import tpu as pltpu
from jax.sharding import PartitionSpec as P

D = 960
QUERY_HEADS = 15
KEY_VALUE_HEADS = 5
HEAD_WIDTH = 64
FF = 2560
QUERY_WIDTH = QUERY_HEADS * HEAD_WIDTH
KEY_WIDTH = KEY_VALUE_HEADS * HEAD_WIDTH
QKV = QUERY_WIDTH + 2 * KEY_WIDTH
SHARDS = 8
ROWS = D // SHARDS
PADDED = 128
MODEL = 1024
PAIR = 2 * HEAD_WIDTH
FULL = SHARDS * PAIR
WIDE = FULL + KEY_VALUE_HEADS * PAIR

EPSILON = 1e-05
BASE = 10000.0

MESH = pl.DeviceIdType.MESH
ANY = pl.BlockSpec(memory_space=pl.ANY)
VMEM = pl.BlockSpec(memory_space=pltpu.VMEM)

GATE_UP = (PADDED, 2 * FF, "columns", FF, 0)
GATE_UP_FIRST = (PADDED, FF, "columns", FF, 0)
GATE_UP_SECOND = (PADDED, FF, "columns", FF, FF // 2)
DOWN = (FF // SHARDS, SHARDS * PADDED, "columns", SHARDS * PADDED // 2, 0)
ATTEND_IN = (PADDED, WIDE, "rows", 0, 0)
ATTEND_OUT = (PADDED, SHARDS * PADDED, "rows", 0, 0)
FEED_FORWARD = (GATE_UP, DOWN)
FEED_FORWARD_BACK = (GATE_UP_FIRST, GATE_UP_SECOND, DOWN)
ATTENTION = (ATTEND_IN, ATTEND_OUT)


def half_lanes(shape, core):
    _, columns, _, stride, offset = shape
    return pl.ds(pl.multiple_of(core * stride + offset, 128), columns // 2)


def half_shape(shape):
    rows, columns, kind = shape[:3]
    return (rows // 2, columns) if kind == "rows" else (rows, columns // 2)


def half_view(shape, core, start, count):
    rows, columns, kind = shape[:3]
    if kind == "rows":
        first = pl.multiple_of(core * (rows // 2) + start, 16)
        return (pl.ds(first, count), slice(None))
    return (pl.ds(pl.multiple_of(start, 16), count), half_lanes(shape, core))


def places():
    dp = lax.axis_index("dp")
    fsdp = lax.axis_index("fsdp")
    return dp // 2, dp % 2, fsdp // 4, fsdp % 4


def peer_ids():
    z, core, x, y = places()
    return {
        "X": {"fsdp": (1 - x) * 4 + y},
        "Yp": {"fsdp": x * 4 + (y + 1) % 4},
        "Ym": {"fsdp": x * 4 + (y + 3) % 4},
        "C": {"dp": z * 2 + 1 - core},
        "Z1": {"dp": ((z + 1) % 4) * 2 + core},
        "Z2": {"dp": ((z + 2) % 4) * 2 + core},
        "Z3": {"dp": ((z + 3) % 4) * 2 + core},
    }


def greet(ids, names):
    barrier = pltpu.get_barrier_semaphore()
    for name in names:
        pl.semaphore_signal(barrier, inc=1, device_id=ids[name], device_id_type=MESH)
    pl.semaphore_wait(barrier, len(names))


GATHER = (
    ("X", 0, 0, "f"),
    ("Yp", 0, 0, "f"),
    ("Ym", 0, 0, "f"),
    ("Ym", 0, 1, 0),
    ("X", 0, 1, 0),
    ("Yp", 0, 3, 1),
    ("X", 0, 3, 0),
    ("Yp", 1, 0, 1),
    ("Ym", 1, 0, 1),
    ("Ym", 1, 1, 0),
    ("Yp", 1, 3, 1),
)
GATHER_NEXT = {1: (5, 6), 2: (3, 4), 0: (7, 8), 4: (9,), 7: (10,)}
GATHER_STAGES = ((1, 2, 0), (4, 7, 3, 5, 6, 8), (9, 10))
GATHER_ORDER = (1, 2, 0, 4, 7, 3, 5, 6, 8, 9, 10)


def seen_by_receiver(peer, column, step):
    if peer == "X":
        return 1 - column, step
    if peer == "Yp":
        return column, (step + 3) % 4
    if peer == "Ym":
        return column, (step + 1) % 4
    return column, step


def part_rows(shape, part):
    rows = half_shape(shape)[0]
    return (0, rows) if part == "f" else (part * (rows // 2), rows // 2)


UPWARD = (0, 1, 3, 5, 7)
PLAIN_EDGES = 22
SPREAD_EDGES = 88


class Gather:
    def __init__(self, shapes, spread, shards, outs, sems):
        self.shapes, self.spread, self.shards, self.outs = shapes, spread, shards, outs
        self.local_sem, self.send_sem, self.recv_sem = sems
        self.z, self.core, self.x, self.y = places()
        self.ids = peer_ids()

    def owner(self, column, step):
        return ((self.x + column) % 2) * 4 + (self.y + step) % 4

    def index(self, array, part, which, plane):
        shape = self.shapes[array]
        start, rows = part_rows(shape, part)
        if array == self.spread:
            quarter = half_shape(shape)[0] // 4
            start, rows = plane * quarter + start // 4, rows // 4
        return half_view(shape, which, start, rows)

    def view(self, array, column, step, part, which, plane):
        return self.outs[array].at[
            (self.owner(column, step),) + self.index(array, part, which, plane)
        ]

    def received(self, edge):
        group, base = edge // 11, edge % 11
        peer, column, step, part = GATHER[base]
        column, step = seen_by_receiver(peer, column, step)
        return column, step, part, (0, 0, 3, 1, 2, 3, 1, 2)[group]

    def peer_of(self, edge):
        group, base = edge // 11, edge % 11
        if group == 0:
            return GATHER[base][0]
        if group in (1, 5, 6, 7):
            return "C"
        return {2: "Z1", 3: "Z3", 4: "Z1" if base in UPWARD else "Z3"}[group]

    def copy(self, array, edge):
        group, base = edge // 11, edge % 11
        if group == 0:
            _, column, step, part = GATHER[base]
            away = 0
        else:
            column, step, part, away = self.received(edge)
            if group in (2, 3):
                away = 0
            elif group == 4:
                away = 3 if base in UPWARD else 1
        target = source = self.view(array, column, step, part, self.core, (self.z + away) % 4)
        if group == 0 and (column, step) == (0, 0):
            source = self.shards[array].at[self.index(array, part, self.core, self.z)]
        return pltpu.make_async_remote_copy(
            src_ref=source,
            dst_ref=target,
            send_sem=self.send_sem.at[array, edge],
            recv_sem=self.recv_sem.at[array, edge],
            device_id=self.ids[self.peer_of(edge)],
            device_id_type=MESH,
        )

    def wait_for(self, array, edge):
        column, step, part, away = self.received(edge)
        which = 1 - self.core if edge // 11 in (1, 5, 6, 7) else self.core
        landed = self.view(array, column, step, part, which, (self.z + away) % 4)
        pltpu.make_async_remote_copy(
            src_ref=landed,
            dst_ref=landed,
            send_sem=self.send_sem.at[array, edge],
            recv_sem=self.recv_sem.at[array, edge],
            device_id=self.ids["C"],
            device_id_type=MESH,
        ).wait_recv()

    def own(self, array):
        return pltpu.make_async_copy(
            self.shards[array],
            self.outs[array].at[self.x * 4 + self.y],
            self.local_sem.at[array],
        )

    def start(self):
        for array in range(len(self.shapes)):
            for edge in (0, 1, 2):
                self.copy(array, edge).start()
            self.own(array).start()

    def within_plane(self, array, edges):
        for edge in edges:
            self.wait_for(array, edge)
            for later in GATHER_NEXT.get(edge, ()):
                self.copy(array, later).start()
            if array == self.spread:
                self.copy(array, 22 + edge).start()
                self.copy(array, 33 + edge).start()
            self.copy(array, 11 + edge).start()

    def round_z(self, edges):
        if self.spread is None:
            return
        for edge in edges:
            for group in (2, 3):
                self.wait_for(self.spread, 11 * group + edge)
                if (group == 2) == (edge in UPWARD):
                    self.copy(self.spread, 44 + edge).start()
                self.copy(self.spread, 11 * (group + 3) + edge).start()

    def steps(self):
        first, second, third = GATHER_STAGES
        arrays = range(len(self.shapes))
        steps = [functools.partial(self.within_plane, array, first) for array in arrays]
        steps.append(functools.partial(self.round_z, first))
        steps += [functools.partial(self.within_plane, array, second) for array in arrays]
        steps.append(functools.partial(self.round_z, second))
        steps += [functools.partial(self.within_plane, array, third) for array in arrays]
        steps.append(functools.partial(self.round_z, third))
        steps.append(self.finish)
        return steps

    def finish(self):
        if self.spread is not None:
            for edge in GATHER_ORDER:
                self.wait_for(self.spread, 44 + edge)
                self.copy(self.spread, 77 + edge).start()
        for array in range(len(self.shapes)):
            last = SPREAD_EDGES if array == self.spread else PLAIN_EDGES
            for edge in range(last):
                if edge // 11 in (1, 5, 6, 7):
                    self.wait_for(array, edge)
            for edge in range(last):
                self.copy(array, edge).wait_send()
            self.own(array).wait()

    @staticmethod
    def out_shapes(shapes):
        return [
            jax.ShapeDtypeStruct((SHARDS, rows, columns), jnp.bfloat16)
            for rows, columns, *_ in shapes
        ]

    @staticmethod
    def scratch(shapes, spread):
        edges = PLAIN_EDGES if spread is None else SPREAD_EDGES
        return [
            pltpu.SemaphoreType.DMA((len(shapes),)),
            pltpu.SemaphoreType.DMA((len(shapes), edges)),
            pltpu.SemaphoreType.DMA((len(shapes), edges)),
        ]


def gather_kernel(shapes, *refs):
    count = len(shapes)
    gather = Gather(shapes, None, refs[:count], refs[count : 2 * count], refs[2 * count :])
    greet(gather.ids, ("X", "Yp", "Ym", "C"))
    gather.start()
    for step in gather.steps():
        step()


def gather_weights(shards):
    count = len(ATTENTION)
    return pl.pallas_call(
        functools.partial(gather_kernel, ATTENTION),
        name="gather_weights",
        out_shape=Gather.out_shapes(ATTENTION),
        in_specs=[VMEM] * count,
        out_specs=[ANY] * count,
        scratch_shapes=Gather.scratch(ATTENTION, None),
        compiler_params=pltpu.CompilerParams(collective_id=0, has_side_effects=True),
    )(*shards)


REDUCE = (
    ("Yp", 0, 2, 0, ()),
    ("Ym", 0, 2, 1, ()),
    ("Yp", 1, 2, 0, ()),
    ("Ym", 1, 2, 1, ()),
    ("X", 1, 3, 0, ()),
    ("Yp", 1, 1, 1, ()),
    ("X", 1, 1, 0, (2,)),
    ("Ym", 1, 3, 1, (3,)),
    ("Yp", 0, 1, "f", (0, 6)),
    ("Ym", 0, 3, "f", (1, 4)),
    ("X", 1, 0, "f", (5, 7)),
)
REDUCE_STAGES = ((0, 1, 2, 3, 4, 5), (6, 7), (8, 9, 10))
SHARD_ORDER = ((0, 2), (1, 2), (1, 3), (1, 1), (0, 1), (0, 3), (1, 0), (0, 0))
REDUCE_EDGES = 47
SLOTS = 2
ROWS_HERE = 256


class Reduce:
    def __init__(self, shapes, spread, lefts, rights, extra, outs, scratch):
        count = len(shapes)
        if len(lefts) < count:
            lefts, rights, outs = ((refs[0],) + tuple(refs) for refs in (lefts, rights, outs))
        self.shapes, self.spread, self.outs = shapes, spread, outs
        self.lefts, self.rights, self.extra = lefts, rights, extra
        self.totals = scratch[:count]
        self.wholes = scratch[count : 2 * count]
        self.parts = scratch[2 * count : 3 * count]
        self.quarters = scratch[3 * count : 4 * count]
        self.rounds = None if spread is None else scratch[4 * count]
        self.left_all = list(scratch[-4 - 2 * count : -4 - count])
        self.sides = [(0, 1)] * count
        if shapes[0] is GATE_UP_FIRST:
            self.left_all[1] = self.left_all[0]
            self.sides[1] = (1,)
        self.right_all = scratch[-4 - count : -4]
        self.operand_sem, self.local_sem, self.send_sem, self.recv_sem = scratch[-4:]
        self.z, self.core, self.x, self.y = places()
        self.mine = self.x * 4 + self.y
        self.ids = peer_ids()
        self.plain = [array for array in range(count) if array != spread]

    @staticmethod
    def piece_shapes(shapes, spread):
        halves = [half_shape(shape) for shape in shapes]
        return halves, [
            (half[0], half[1] // 4) if array == spread else half
            for array, half in enumerate(halves)
        ]

    @staticmethod
    def left_shape(shape, half):
        if shape is GATE_UP_SECOND:
            return (16, 128)
        if half[0] == PADDED:
            return (ROWS_HERE, SHARDS * PADDED)
        return (SHARDS, ROWS_HERE, half[0])

    @staticmethod
    def out_shapes(shapes):
        return [jax.ShapeDtypeStruct((rows, columns), jnp.bfloat16) for rows, columns, *_ in shapes]

    @staticmethod
    def scratch(shapes, spread):
        halves, pieces = Reduce.piece_shapes(shapes, spread)
        bf16 = jnp.bfloat16
        buffers = [pltpu.VMEM((SHARDS,) + half, bf16) for half in halves]
        buffers += [pltpu.VMEM((3,) + piece, bf16) for piece in pieces]
        buffers += [pltpu.VMEM((8, piece[0] // 2, piece[1]), bf16) for piece in pieces]
        buffers += [pltpu.VMEM((3, half[0] // 4, half[1]), bf16) for half in halves]
        if spread is not None:
            buffers.append(pltpu.VMEM((3 * SHARDS,) + pieces[spread], bf16))
        buffers += [
            pltpu.VMEM((2,) + Reduce.left_shape(shape, half), bf16)
            for shape, half in zip(shapes, halves)
        ]
        buffers += [pltpu.VMEM((2, ROWS_HERE, half[1]), bf16) for half in halves]
        return buffers + [
            pltpu.SemaphoreType.DMA((len(shapes), 2)),
            pltpu.SemaphoreType.DMA((len(shapes),)),
            pltpu.SemaphoreType.DMA((len(shapes), REDUCE_EDGES)),
            pltpu.SemaphoreType.DMA((len(shapes), REDUCE_EDGES)),
        ]

    def owner(self, column, step):
        return ((self.x + column) % 2) * 4 + (self.y + step) % 4

    def lanes(self, array, plane):
        columns = half_shape(self.shapes[array])[1]
        if array != self.spread:
            return pl.ds(0, columns)
        return pl.ds(pl.multiple_of(plane * (columns // 4), 128), columns // 4)

    def piece(self, array, edge):
        _, column, step, part, _ = REDUCE[edge]
        start, rows = part_rows(self.shapes[array], part)
        return self.totals[array].at[
            self.owner(column, step), pl.ds(start, rows), self.lanes(array, self.z)
        ]

    def slot(self, array, edge):
        return self.parts[array].at[edge] if edge < 8 else self.wholes[array].at[edge - 8]

    def add(self, array, into, start, rows, lanes, source):
        total = self.totals[array]

        @pl.loop(0, rows // 16)
        def _(index):
            offset = pl.multiple_of(index * 16, 16)
            at = pl.ds(pl.multiple_of(start + offset, 16), 16)
            total[into, at, lanes] = (
                total[into, at, lanes].astype(jnp.float32)
                + source[pl.ds(offset, 16), :].astype(jnp.float32)
            ).astype(jnp.bfloat16)

    def quarter(self, array, plane):
        rows = half_shape(self.shapes[array])[0]
        if array == self.spread:
            return 0, rows, self.lanes(array, plane)
        return pl.multiple_of(plane * (rows // 4), 16), rows // 4, self.lanes(array, plane)

    def summed(self, array, plane):
        start, rows, lanes = self.quarter(array, plane)
        return self.totals[array].at[self.mine, pl.ds(start, rows), lanes]

    def out_view(self, array, plane, which):
        shape = self.shapes[array]
        if array == self.spread:
            rows, columns = half_shape(shape)
            first = pl.multiple_of(which * shape[3] + shape[4] + plane * (columns // 4), 128)
            return self.outs[array].at[pl.ds(0, rows), pl.ds(first, columns // 4)]
        start, rows, _ = self.quarter(array, plane)
        return self.outs[array].at[half_view(shape, which, start, rows)]

    def copy(self, array, edge):
        z = self.z
        if edge < 11:
            peer, source, target = REDUCE[edge][0], self.piece(array, edge), self.slot(array, edge)
        elif edge < 14:
            step = edge - 10
            peer, source = f"Z{step}", self.summed(array, (z + step) % 4)
            target = self.quarters[array].at[step - 1]
        elif edge < 17:
            peer, source = f"Z{edge - 13}", self.summed(array, z)
            target = self.out_view(array, z, self.core)
        elif edge < 21:
            peer = "C"
            source = target = self.out_view(array, (z + edge - 17) % 4, self.core)
            if edge == 17:
                source = self.summed(array, z)
        elif edge >= 45:
            peer, source = "C", self.operand(array, edge - 45, 1 - self.core)
            target = (self.left_all, self.right_all)[edge - 45][array].at[1]
        else:
            kind, shard = (edge - 21) // 8, (edge - 21) % 8
            peer = ("Z1" if shard % 2 == 0 else "Z3", "Z1", "Z3")[kind]
            lanes = self.lanes(array, (z + (2, 1, 3)[kind]) % 4)
            source = self.totals[array].at[self.owner(*SHARD_ORDER[shard]), :, lanes]
            target = self.rounds.at[edge - 21]
        return pltpu.make_async_remote_copy(
            src_ref=source,
            dst_ref=target,
            send_sem=self.send_sem.at[array, edge],
            recv_sem=self.recv_sem.at[array, edge],
            device_id=self.ids[peer],
            device_id_type=MESH,
        )

    def wait_for(self, array, edge):
        z = self.z
        if edge < 11:
            landed = self.slot(array, edge)
        elif edge < 14:
            landed = self.quarters[array].at[edge - 11]
        elif edge < 17:
            landed = self.out_view(array, (z + 4 - (edge - 13)) % 4, self.core)
        elif edge < 21:
            landed = self.out_view(array, (z + edge - 17) % 4, 1 - self.core)
        elif edge >= 45:
            landed = (self.left_all, self.right_all)[edge - 45][array].at[1]
        else:
            landed = self.rounds.at[edge - 21]
        pltpu.make_async_remote_copy(
            src_ref=landed,
            dst_ref=landed,
            send_sem=self.send_sem.at[array, edge],
            recv_sem=self.recv_sem.at[array, edge],
            device_id=self.ids["C"],
            device_id_type=MESH,
        ).wait_recv()

    def receive(self, array, edge):
        self.wait_for(array, edge)
        peer, column, step, part, _ = REDUCE[edge]
        column, step = seen_by_receiver(peer, column, step)
        start, rows = part_rows(self.shapes[array], part)
        lanes = self.lanes(array, self.z)
        self.add(array, self.owner(column, step), start, rows, lanes, self.slot(array, edge))

    def receive_round(self, kind, shard):
        edge = 21 + 8 * kind + shard
        array = self.spread
        self.wait_for(array, edge)
        away = 0 if kind > 0 else (1 if shard % 2 == 0 else 3)
        rows = half_shape(self.shapes[array])[0]
        lanes = self.lanes(array, (self.z + away) % 4)
        self.add(
            array, self.owner(*SHARD_ORDER[shard]), 0, rows, lanes, self.rounds.at[edge - 21]
        )

    def stage(self, array, number):
        for edge in REDUCE_STAGES[number]:
            for earlier in REDUCE[edge][4]:
                self.receive(array, earlier)
            self.copy(array, edge).start()

    def operand(self, array, side, core):
        kind = self.shapes[array][2]
        if side == 0:
            return self.lefts[array].at[core] if kind == "rows" else self.lefts[array]
        right = self.rights[array]
        if kind == "rows":
            return right
        if len(right.shape) == 3:
            _, columns, _, _, offset = self.shapes[array]
            return right.at[core, :, pl.ds(offset, columns // 2)]
        return right.at[:, half_lanes(self.shapes[array], core)]

    def load(self, array, side):
        return pltpu.make_async_copy(
            self.operand(array, side, self.core),
            (self.left_all, self.right_all)[side][array].at[0],
            self.operand_sem.at[array, side],
        )

    def make(self, array, shards):
        columns = half_shape(self.shapes[array])[1]
        left, right, total = self.left_all[array], self.right_all[array], self.totals[array]
        for shard in shards:
            owner = self.owner(*SHARD_ORDER[shard])

            def chunk(lanes):
                if len(left.shape) == 3:
                    at = pl.ds(pl.multiple_of(owner * PADDED, PADDED), PADDED)
                    mine, other = left[0, :, at], left[1, :, at]
                else:
                    mine, other = left[0, owner], left[1, owner]
                total[owner, :, lanes] = (
                    dot_first(mine, right[0, :, lanes]) + dot_first(other, right[1, :, lanes])
                ).astype(jnp.bfloat16)

            if columns % 640 == 0 and columns > 640:

                @pl.loop(0, columns // 640)
                def _(index):
                    chunk(pl.ds(pl.multiple_of(index * 640, 128), 640))

            else:
                for first in range(0, columns, 512):
                    chunk(pl.ds(first, min(512, columns - first)))
            if self.extra is not None and array == 0:
                at = pl.ds(half_shape(self.shapes[array])[0] - 16, 16)
                total[owner, at, :128] += self.extra[owner]

    def store(self, array):
        return pltpu.make_async_copy(
            self.summed(array, self.z), self.out_view(array, self.z, self.core),
            self.local_sem.at[array],
        )

    def start_loads(self):
        for array in range(len(self.shapes)):
            for side in self.sides[array]:
                self.load(array, side).start()

    def start_exchange(self):
        for array in range(len(self.shapes)):
            for side in self.sides[array]:
                self.copy(array, 45 + side).start()

    def start(self):
        order = ([] if self.spread is None else [self.spread]) + self.plain
        for array in order:
            for side in self.sides[array]:
                self.load(array, side).wait()
                self.wait_for(array, 45 + side)
            if array == self.spread:
                self.make(array, range(SHARDS))
                for shard in range(SHARDS):
                    self.copy(array, 21 + shard).start()
            else:
                self.make(array, range(4))
                self.stage(array, 0)
        for array in self.plain:
            self.make(array, range(4, SHARDS))

    def first_round(self):
        for shard in range(SHARDS):
            self.receive_round(0, shard)
            self.copy(self.spread, 29 + shard).start()
            self.copy(self.spread, 37 + shard).start()

    def second_round(self, shards):
        for shard in shards:
            self.receive_round(1, shard)
            self.receive_round(2, shard)

    def end_plane(self, array):
        for edge in (8, 9, 10):
            self.receive(array, edge)
        for edge in (11, 12, 13) if array != self.spread else ():
            self.copy(array, edge).start()

    def end_z(self, array):
        if array != self.spread:
            start, rows, lanes = self.quarter(array, self.z)
            for edge in (11, 12, 13):
                self.wait_for(array, edge)
                self.add(
                    array, self.mine, start, rows, lanes, self.quarters[array].at[edge - 11]
                )
        for edge in (14, 15, 16, 17):
            self.copy(array, edge).start()
        self.store(array).start()

    def finish(self):
        for array in range(len(self.shapes)):
            for edge in (14, 15, 16):
                self.wait_for(array, edge)
                self.copy(array, 34 - edge).start()
        for array in range(len(self.shapes)):
            for edge in range(17, 21):
                self.wait_for(array, edge)
            for edge in range(REDUCE_EDGES):
                if edge >= 45:
                    started = edge - 45 in self.sides[array]
                elif array == self.spread:
                    started = edge not in (11, 12, 13)
                else:
                    started = edge < 21
                if started:
                    self.copy(array, edge).wait_send()
            self.store(array).wait()

    def steps(self):
        call = functools.partial
        steps = []
        if self.spread is not None:
            steps.append(self.first_round)
        steps += [call(self.stage, array, 1) for array in self.plain]
        if self.spread is not None:
            steps.append(call(self.second_round, range(4)))
            steps.append(call(self.stage, self.spread, 0))
            steps.append(call(self.second_round, range(4, SHARDS)))
            steps.append(call(self.stage, self.spread, 1))
        steps += [call(self.stage, array, 2) for array in self.plain]
        if self.spread is not None:
            steps.append(call(self.stage, self.spread, 2))
        steps += [call(self.end_plane, array) for array in self.plain]
        if self.spread is not None:
            steps.append(call(self.end_plane, self.spread))
            steps.append(call(self.end_z, self.spread))
        steps += [call(self.end_z, array) for array in self.plain]
        steps.append(self.finish)
        return steps


def reduce_kernel(shapes, *refs):
    count = len(shapes)
    lefts, rights, extra = refs[:count], refs[count : 2 * count], refs[2 * count]
    outs, scratch = refs[2 * count + 1 : 3 * count + 1], refs[3 * count + 1 :]
    reduce = Reduce(shapes, None, lefts, rights, extra, outs, scratch)
    reduce.start_loads()
    greet(reduce.ids, ("X", "Yp", "Ym", "C", "Z1", "Z2", "Z3"))
    reduce.start_exchange()
    reduce.start()
    for step in reduce.steps():
        step()


def reduce_gradients(lefts, rights, extra):
    count = len(ATTENTION)
    return pl.pallas_call(
        functools.partial(reduce_kernel, ATTENTION),
        name="reduce_gradients",
        out_shape=Reduce.out_shapes(ATTENTION),
        in_specs=[ANY] * (2 * count) + [VMEM],
        out_specs=[ANY] * count,
        scratch_shapes=Reduce.scratch(ATTENTION, None),
        compiler_params=pltpu.CompilerParams(
            collective_id=1, has_side_effects=True, vmem_limit_bytes=48 * 2**20
        ),
    )(*lefts, *rights, extra)


TOKENS = 1024
LOCAL = TOKENS // SHARDS
BLOCK = 256
NEGATIVE = -1e30


def two_groups(device):
    return (device == 1) | (device == 4)


def group_lanes(device, which):
    return pl.ds(pl.multiple_of(((2 * device) // 3 + which) * PAIR, PAIR), PAIR)


def pair_lanes(device):
    return pl.ds(pl.multiple_of(device * PAIR, PAIR), PAIR)


def token_rows(device):
    return pl.ds(pl.multiple_of(device * LOCAL, LOCAL), LOCAL)


def ring(me):
    return [(step, (me + step) % SHARDS, (me + SHARDS - step) % SHARDS) for step in range(1, SHARDS)]


def greet_all(me, others=()):
    barrier = pltpu.get_barrier_semaphore()
    ids = peer_ids()
    for device in [{"fsdp": target} for _, target, _ in ring(me)] + [ids[name] for name in others]:
        pl.semaphore_signal(barrier, inc=1, device_id=device, device_id_type=MESH)
    pl.semaphore_wait(barrier, SHARDS - 1 + len(others))


def turned(values):
    lane = lax.broadcasted_iota(jnp.int32, values.shape, 1)
    half = HEAD_WIDTH // 2
    ahead, behind = pltpu.roll(values, PAIR - half, 1), pltpu.roll(values, half, 1)
    return jnp.where(lane % HEAD_WIDTH < half, -ahead, behind)


def sent(source, target, send_sem, recv_sem, device):
    return pltpu.make_async_remote_copy(
        src_ref=source,
        dst_ref=target,
        send_sem=send_sem,
        recv_sem=recv_sem,
        device_id={"fsdp": device},
        device_id_type=MESH,
    )


def causal_mask(values):
    length = values.shape[1]
    row = lax.broadcasted_iota(jnp.int32, (BLOCK, BLOCK), 0)
    column = lax.broadcasted_iota(jnp.int32, (BLOCK, BLOCK), 1)
    own = jnp.where(column <= row, values[:, length - BLOCK :], NEGATIVE)
    if length == BLOCK:
        return own
    return jnp.concatenate([values[:, : length - BLOCK], own], 1)


def dot_t(left, right):
    return lax.dot_general(
        left, right, (((1,), (1,)), ((), ())), preferred_element_type=jnp.float32
    )


def dot_first(left, right):
    return lax.dot_general(
        left, right, (((0,), (0,)), ((), ())), preferred_element_type=jnp.float32
    )


def attend_kernel(with_gather, *refs):
    count = len(FEED_FORWARD) if with_gather else 0
    norm_ref, weight_ref, table_ref = refs[:3]
    mixed_out, q_kept, kv_kept, lse_kept = refs[3 + count : 7 + count]
    scratch = refs[7 + 2 * count :]
    mixed_ref, q_ref, kv_ref, q_all, kv_all, lse_all, mixed_all = scratch[:7]
    local_sem, send_sem, recv_sem = scratch[7:10]
    background = None
    if with_gather:
        background = Gather(
            FEED_FORWARD, 0, refs[3 : 3 + count], refs[7 + count : 7 + 2 * count], refs[-3:]
        )
    me = lax.axis_index("fsdp")
    both = two_groups(me)
    second = jnp.where(both, 1, 0)

    def incoming(slot, step, device, sender):
        rows = token_rows(sender)
        return [
            sent(
                q_ref.at[slot, :, pair_lanes(device)], q_all.at[slot, rows, :],
                send_sem.at[0, slot, step], recv_sem.at[0, slot, step], device,
            ),
            sent(
                kv_ref.at[slot, :, group_lanes(device, 0)], kv_all.at[0, slot, rows, :],
                send_sem.at[1, slot, step], recv_sem.at[1, slot, step], device,
            ),
        ]

    def extra(slot, step, device, sender):
        group = jnp.where(two_groups(device), 1, 0)
        return sent(
            kv_ref.at[slot, :, group_lanes(device, group)], kv_all.at[1, slot, token_rows(sender), :],
            send_sem.at[2, slot, step], recv_sem.at[2, slot, step], device,
        )

    def outgoing(slot, step, device, sender):
        return sent(
            mixed_all.at[slot, token_rows(device), :], mixed_ref.at[slot, :, pair_lanes(sender)],
            send_sem.at[3, slot, step], recv_sem.at[3, slot, step], device,
        )

    def own_copies(slot):
        rows = token_rows(me)
        group = jnp.where(both, 1, 0)
        return [
            pltpu.make_async_copy(
                q_ref.at[slot, :, pair_lanes(me)], q_all.at[slot, rows, :], local_sem.at[0, slot]
            ),
            pltpu.make_async_copy(
                kv_ref.at[slot, :, group_lanes(me, 0)], kv_all.at[0, slot, rows, :],
                local_sem.at[1, slot],
            ),
            pltpu.make_async_copy(
                kv_ref.at[slot, :, group_lanes(me, group)], kv_all.at[1, slot, rows, :],
                local_sem.at[2, slot],
            ),
        ]

    def own_result(slot):
        return pltpu.make_async_copy(
            mixed_all.at[slot, token_rows(me), :], mixed_ref.at[slot, :, pair_lanes(me)],
            local_sem.at[3, slot],
        )

    greet_all(me, ("C", "Z1", "Z3") if background else ())
    pending = []
    if background:
        background.start()
        pending = background.steps()
    for first in range(0, WIDE, 2 * PAIR):
        width = min(2 * PAIR, WIDE - first)
        projected = jnp.dot(
            norm_ref[...], weight_ref[:, first : first + width], preferred_element_type=jnp.float32
        )
        for lane in range(first, first + width, PAIR):
            is_query = lane < FULL
            for slot in range(SLOTS):
                values = projected[
                    slot * LOCAL : (slot + 1) * LOCAL, lane - first : lane - first + PAIR
                ]
                cosine, sine = (table_ref[(0 if is_query else 2) + which, slot] for which in (0, 1))
                rotated = values * cosine + turned(values) * sine
                if is_query:
                    q_ref[slot, :, lane : lane + PAIR] = (rotated * HEAD_WIDTH ** (-0.5)).astype(
                        jnp.bfloat16
                    )
                else:
                    kv_ref[slot, :, lane - FULL : lane - FULL + PAIR] = rotated.astype(jnp.bfloat16)
    for slot in range(SLOTS):
        for step, target, _ in ring(me):
            for copy in incoming(slot, step, target, me):
                copy.start()

            @pl.when(two_groups(target))
            def _():
                extra(slot, step, target, me).start()

        for copy in own_copies(slot):
            copy.start()

    def do_pending(number):
        for _ in range(min(number, len(pending))):
            pending.pop(0)()

    def work(slot):
        for step, _, source in ring(me):
            for copy in incoming(slot, step, source, source):
                copy.wait_recv()

            @pl.when(both)
            def _():
                extra(slot, step, source, source).wait_recv()

        for copy in own_copies(slot):
            copy.wait()
        for block in range(TOKENS // BLOCK):
            rows = pl.ds(block * BLOCK, BLOCK)
            length = (block + 1) * BLOCK
            outs, totals = [], []
            for head in range(2):
                group = 0 if head == 0 else second
                lanes = slice(head * HEAD_WIDTH, (head + 1) * HEAD_WIDTH)
                query = q_all[slot, rows, lanes]
                keys = kv_all[group, slot, :length, :HEAD_WIDTH]
                values = kv_all[group, slot, :length, HEAD_WIDTH:]
                scores = causal_mask(dot_t(query, keys))
                highest = jnp.max(scores, -1, keepdims=True)
                weights = jnp.exp(scores - highest)
                total = jnp.sum(weights, -1, keepdims=True)
                out = jnp.dot(
                    weights.astype(jnp.bfloat16), values, preferred_element_type=jnp.float32
                )
                outs.append(out / total)
                totals.append(
                    jnp.broadcast_to(highest + jnp.log(total), (BLOCK, HEAD_WIDTH))
                )
            mixed_all[slot, rows, :] = jnp.concatenate(outs, 1).astype(jnp.bfloat16)
            lse_all[slot, rows, :] = jnp.concatenate(totals, 1)
        for step, target, _ in ring(me):
            outgoing(slot, step, target, me).start()
        own_result(slot).start()

    if background:
        do_pending(2)
        work(0)
        do_pending(3)
        work(1)
    else:
        pl.loop(0, SLOTS)(work)
    do_pending(len(pending))
    keep = [
        pltpu.make_async_copy(q_all, q_kept, local_sem.at[4, 0]),
        pltpu.make_async_copy(kv_all, kv_kept, local_sem.at[4, 1]),
        pltpu.make_async_copy(lse_all, lse_kept, local_sem.at[5, 0]),
    ]
    for copy in keep:
        copy.start()
    for slot in range(SLOTS):
        for step, target, source in ring(me):
            outgoing(slot, step, source, source).wait_recv()
            outgoing(slot, step, target, me).wait_send()
            for copy in incoming(slot, step, target, me):
                copy.wait_send()

            @pl.when(two_groups(target))
            def _():
                extra(slot, step, target, me).wait_send()

        own_result(slot).wait()
    mixed_out[...] = jnp.zeros_like(mixed_out)
    for slot in range(SLOTS):
        for shard in range(SHARDS):
            mixed_out[
                slot * LOCAL : (slot + 1) * LOCAL, shard * PADDED : shard * PADDED + ROWS
            ] = mixed_ref[slot, :, shard * ROWS : (shard + 1) * ROWS]
    for copy in keep:
        copy.wait()


Q_ALL = (SLOTS, TOKENS, PAIR)
KV_ALL = (2, SLOTS, TOKENS, PAIR)


def attend(norm, weight, tables, shards=()):
    bf16 = jnp.bfloat16
    with_gather = bool(shards)
    return pl.pallas_call(
        functools.partial(attend_kernel, with_gather),
        name="attend_gather" if with_gather else "attend",
        out_shape=[
            jax.ShapeDtypeStruct((ROWS_HERE, MODEL), bf16),
            jax.ShapeDtypeStruct(Q_ALL, bf16),
            jax.ShapeDtypeStruct(KV_ALL, bf16),
            jax.ShapeDtypeStruct(Q_ALL, jnp.float32),
        ]
        + (Gather.out_shapes(FEED_FORWARD) if with_gather else []),
        in_specs=[VMEM] * (3 + len(shards)),
        out_specs=[VMEM] + [ANY] * (3 + len(shards)),
        scratch_shapes=[
            pltpu.VMEM((SLOTS, LOCAL, FULL), bf16),
            pltpu.VMEM((SLOTS, LOCAL, FULL), bf16),
            pltpu.VMEM((SLOTS, LOCAL, WIDE - FULL), bf16),
            pltpu.VMEM(Q_ALL, bf16),
            pltpu.VMEM(KV_ALL, bf16),
            pltpu.VMEM(Q_ALL, jnp.float32),
            pltpu.VMEM(Q_ALL, bf16),
            pltpu.SemaphoreType.DMA((6, SLOTS)),
            pltpu.SemaphoreType.DMA((4, SLOTS, SHARDS)),
            pltpu.SemaphoreType.DMA((4, SLOTS, SHARDS)),
        ]
        + (Gather.scratch(FEED_FORWARD, 0) if with_gather else []),
        compiler_params=pltpu.CompilerParams(
            collective_id=4 if with_gather else 2,
            has_side_effects=True,
            vmem_limit_bytes=40 * 2**20,
        ),
    )(norm, weight, tables, *shards)


def attend_back_kernel(with_reduce, *refs):
    count = len(FEED_FORWARD) if with_reduce else 0
    slope_in, q_ref, kv_ref, lse_ref, weight_ref, table_ref = refs[:6]
    dqkv_ref, norm_slope_ref = refs[6 + 2 * count : 8 + 2 * count]
    scratch = refs[8 + 3 * count :]
    slope_all, q_all, kv_all, lse_all, dq_all, dkv_total, dkv_all = scratch[:7]
    dq_ref, dkv_ref, dkv_extra_ref, slope_ref, local_sem, send_sem, recv_sem = scratch[7:14]
    background = None
    if with_reduce:
        background = Reduce(
            FEED_FORWARD_BACK,
            REDUCE_SPREAD,
            refs[6 : 6 + count],
            refs[6 + count : 6 + 2 * count],
            None,
            refs[8 + 2 * count : 8 + 3 * count],
            scratch[14:],
        )
    me = lax.axis_index("fsdp")
    both = two_groups(me)
    second = jnp.where(both, 1, 0)
    extra_at = me // 4

    def incoming(slot, step, device, sender):
        return sent(
            slope_ref.at[slot, :, pair_lanes(device)], slope_all.at[slot, token_rows(sender), :],
            send_sem.at[0, slot, step], recv_sem.at[0, slot, step], device,
        )

    def outgoing(slot, step, device, sender):
        rows = token_rows(device)
        return [
            sent(
                dq_all.at[slot, rows, :], dq_ref.at[slot, :, pair_lanes(sender)],
                send_sem.at[1, slot, step], recv_sem.at[1, slot, step], device,
            ),
            sent(
                dkv_all.at[0, slot, rows, :], dkv_ref.at[sender, slot],
                send_sem.at[2, slot, step], recv_sem.at[2, slot, step], device,
            ),
        ]

    def extra(slot, step, device, sender):
        return sent(
            dkv_all.at[1, slot, token_rows(device), :], dkv_extra_ref.at[sender // 4, slot],
            send_sem.at[3, slot, step], recv_sem.at[3, slot, step], device,
        )

    def own_slope(slot):
        return pltpu.make_async_copy(
            slope_ref.at[slot, :, pair_lanes(me)], slope_all.at[slot, token_rows(me), :],
            local_sem.at[0, slot],
        )

    def own_results(slot):
        rows = token_rows(me)
        return [
            pltpu.make_async_copy(
                dq_all.at[slot, rows, :], dq_ref.at[slot, :, pair_lanes(me)], local_sem.at[1, slot]
            ),
            pltpu.make_async_copy(
                dkv_all.at[0, slot, rows, :], dkv_ref.at[me, slot], local_sem.at[2, slot]
            ),
        ]

    def own_extra(slot):
        return pltpu.make_async_copy(
            dkv_all.at[1, slot, token_rows(me), :], dkv_extra_ref.at[extra_at, slot],
            local_sem.at[3, slot],
        )

    loads = [
        pltpu.make_async_copy(q_ref, q_all, local_sem.at[4, 0]),
        pltpu.make_async_copy(kv_ref, kv_all, local_sem.at[4, 1]),
        pltpu.make_async_copy(lse_ref, lse_all, local_sem.at[5, 0]),
    ]
    for copy in loads:
        copy.start()
    if background:
        background.start_loads()
    slope_ref[...] = jnp.zeros_like(slope_ref)
    for slot in range(SLOTS):
        for shard in range(SHARDS):
            slope_ref[slot, :, shard * ROWS : (shard + 1) * ROWS] = slope_in[
                slot * LOCAL : (slot + 1) * LOCAL, shard * PADDED : shard * PADDED + ROWS
            ]
    greet_all(me, ("C", "Z1", "Z2", "Z3") if background else ())
    for slot in range(SLOTS):
        for step, target, _ in ring(me):
            incoming(slot, step, target, me).start()
        own_slope(slot).start()
    pending = []
    if background:
        background.start_exchange()
        background.start()
        pending = background.steps()
    for copy in loads:
        copy.wait()

    def work(slot):
        for step, _, source in ring(me):
            incoming(slot, step, source, source).wait_recv()
        own_slope(slot).wait()
        dkv_total[...] = jnp.zeros_like(dkv_total)
        for block in range(TOKENS // BLOCK):
            rows = pl.ds(block * BLOCK, BLOCK)
            length = (block + 1) * BLOCK
            outs = []
            for head in range(2):
                group = 0 if head == 0 else second
                lanes = slice(head * HEAD_WIDTH, (head + 1) * HEAD_WIDTH)
                query = q_all[slot, rows, lanes]
                slope = slope_all[slot, rows, lanes]
                lse = lse_all[slot, rows, head * HEAD_WIDTH : head * HEAD_WIDTH + 1]
                keys = kv_all[group, slot, :length, :HEAD_WIDTH]
                values = kv_all[group, slot, :length, HEAD_WIDTH:]
                probs = jnp.exp(causal_mask(dot_t(query, keys)) - lse)
                prob_slope = dot_t(slope, values)
                inner = jnp.sum(probs * prob_slope, -1, keepdims=True)
                score_slope = (probs * (prob_slope - inner)).astype(jnp.bfloat16)
                outs.append(
                    jnp.dot(score_slope, keys, preferred_element_type=jnp.float32)
                    * HEAD_WIDTH ** (-0.5)
                )
                dkv_total[group, :length, :] += jnp.concatenate(
                    [dot_first(score_slope, query), dot_first(probs.astype(jnp.bfloat16), slope)], 1
                )
            dq_all[slot, rows, :] = jnp.concatenate(outs, 1).astype(jnp.bfloat16)
        dkv_all[0, slot] = dkv_total[0].astype(jnp.bfloat16)
        dkv_all[1, slot] = dkv_total[1].astype(jnp.bfloat16)
        for step, target, _ in ring(me):
            for copy in outgoing(slot, step, target, me):
                copy.start()

            @pl.when(both)
            def _():
                extra(slot, step, target, me).start()

        for copy in own_results(slot):
            copy.start()

        @pl.when(both)
        def _():
            own_extra(slot).start()

    if background:
        work(0)
        for step in pending[:BACK_POINT]:
            step()
        work(1)
    else:
        pl.loop(0, SLOTS)(work)

    def collect():
        for slot in range(SLOTS):
            for step, _, source in ring(me):
                for copy in outgoing(slot, step, source, source):
                    copy.wait_recv()

                @pl.when(two_groups(source))
                def _():
                    extra(slot, step, source, source).wait_recv()

            for copy in own_results(slot):
                copy.wait()

            @pl.when(both)
            def _():
                own_extra(slot).wait()

            rows = pl.ds(slot * LOCAL, LOCAL)

            def reversed_rotation(values, table):
                return values * table_ref[table, slot] - turned(values * table_ref[table + 1, slot])

            for lane in range(0, FULL, PAIR):
                values = dq_ref[slot, :, lane : lane + PAIR].astype(jnp.float32)
                dqkv_ref[rows, lane : lane + PAIR] = reversed_rotation(values, 0).astype(
                    jnp.bfloat16
                )
            pairs = (
                (dkv_ref[0, slot], dkv_ref[1, slot]),
                (dkv_extra_ref[0, slot], dkv_ref[2, slot]),
                (dkv_ref[3, slot], dkv_ref[4, slot]),
                (dkv_extra_ref[1, slot], dkv_ref[5, slot]),
                (dkv_ref[6, slot], dkv_ref[7, slot]),
            )
            for group, (one, two) in enumerate(pairs):
                values = one.astype(jnp.float32) + two.astype(jnp.float32)
                lane = FULL + group * PAIR
                dqkv_ref[rows, lane : lane + PAIR] = reversed_rotation(values, 2).astype(
                    jnp.bfloat16
                )
        for first in range(0, FULL, 2 * PAIR):
            norm_slope_ref[:, first : first + 2 * PAIR] = dot_t(
                dqkv_ref[...], weight_ref[first : first + 2 * PAIR, :]
            )

    if background:
        for step in pending[BACK_POINT:BACK_COLLECT]:
            step()
        collect()
        for step in pending[BACK_COLLECT:]:
            step()
    else:
        collect()
    for slot in range(SLOTS):
        for step, target, source in ring(me):
            incoming(slot, step, target, me).wait_send()
            for copy in outgoing(slot, step, target, me):
                copy.wait_send()

            @pl.when(both)
            def _():
                extra(slot, step, target, me).wait_send()


REDUCE_SPREAD = 2
BACK_POINT = 5
BACK_COLLECT = 13


def attend_back(slope, kept, weight, tables, lefts=(), rights=()):
    bf16 = jnp.bfloat16
    with_reduce = bool(lefts)
    return pl.pallas_call(
        functools.partial(attend_back_kernel, with_reduce),
        name="attend_back_reduce" if with_reduce else "attend_back",
        out_shape=[
            jax.ShapeDtypeStruct((ROWS_HERE, WIDE), bf16),
            jax.ShapeDtypeStruct((ROWS_HERE, FULL), jnp.float32),
        ]
        + (Reduce.out_shapes(FEED_FORWARD) if with_reduce else []),
        in_specs=[VMEM] + [ANY] * 3 + [VMEM] * 2 + [ANY] * (2 * len(lefts)),
        out_specs=[VMEM] * 2 + [ANY] * len(lefts),
        scratch_shapes=[
            pltpu.VMEM(Q_ALL, bf16),
            pltpu.VMEM(Q_ALL, bf16),
            pltpu.VMEM(KV_ALL, bf16),
            pltpu.VMEM(Q_ALL, jnp.float32),
            pltpu.VMEM(Q_ALL, bf16),
            pltpu.VMEM((2, TOKENS, PAIR), jnp.float32),
            pltpu.VMEM(KV_ALL, bf16),
            pltpu.VMEM((SLOTS, LOCAL, FULL), bf16),
            pltpu.VMEM((SHARDS, SLOTS, LOCAL, PAIR), bf16),
            pltpu.VMEM((2, SLOTS, LOCAL, PAIR), bf16),
            pltpu.VMEM((SLOTS, LOCAL, FULL), bf16),
            pltpu.SemaphoreType.DMA((6, SLOTS)),
            pltpu.SemaphoreType.DMA((4, SLOTS, SHARDS)),
            pltpu.SemaphoreType.DMA((4, SLOTS, SHARDS)),
        ]
        + (Reduce.scratch(FEED_FORWARD_BACK, REDUCE_SPREAD) if with_reduce else []),
        compiler_params=pltpu.CompilerParams(
            collective_id=5 if with_reduce else 3,
            has_side_effects=True,
            vmem_limit_bytes=(58 if with_reduce else 48) * 2**20,
        ),
    )(slope, *kept, weight, tables, *lefts, *rights)


FF_BLOCK = 512


def feed_back_kernel(slope_ref, down_ref, gate_w_ref, up_w_ref, gate_ref, up_ref, out_ref, norm_ref):
    slope = dot_t(slope_ref[...], down_ref[...])
    gate, up = gate_ref[...], up_ref[...]
    sigma = jax.nn.sigmoid(gate)
    gate_slope = (slope * up * sigma * (1.0 + gate * (1.0 - sigma))).astype(jnp.bfloat16)
    up_slope = (slope * gate * sigma).astype(jnp.bfloat16)
    out_ref[0] = gate_slope
    out_ref[1] = up_slope
    norm_slope = dot_t(gate_slope, gate_w_ref[...]) + dot_t(up_slope, up_w_ref[...])

    @pl.when(pl.program_id(0) == 0)
    def _():
        norm_ref[...] = norm_slope

    @pl.when(pl.program_id(0) > 0)
    def _():
        norm_ref[...] += norm_slope


def feed_back(down_in, down_weight, gate_up, gated):
    blocks = FF // FF_BLOCK
    tall = pl.BlockSpec((ROWS_HERE, MODEL), lambda i: (0, 0))
    return pl.pallas_call(
        feed_back_kernel,
        name="feed_back",
        grid=(blocks,),
        out_shape=[
            jax.ShapeDtypeStruct((2, ROWS_HERE, FF), jnp.bfloat16),
            jax.ShapeDtypeStruct((ROWS_HERE, MODEL), jnp.float32),
        ],
        in_specs=[
            tall,
            pl.BlockSpec((FF_BLOCK, MODEL), lambda i: (i, 0)),
            pl.BlockSpec((MODEL, FF_BLOCK), lambda i: (0, i)),
            pl.BlockSpec((MODEL, FF_BLOCK), lambda i: (0, i + blocks)),
            pl.BlockSpec((ROWS_HERE, FF_BLOCK), lambda i: (0, i)),
            pl.BlockSpec((ROWS_HERE, FF_BLOCK), lambda i: (0, i + blocks)),
        ],
        out_specs=[pl.BlockSpec((2, ROWS_HERE, FF_BLOCK), lambda i: (0, 0, i)), tall],
        compiler_params=pltpu.CompilerParams(vmem_limit_bytes=40 * 2**20),
    )(down_in, down_weight, gate_up, gate_up, gated, gated)


def finish_kernel(
    flags_ref, hidden_slope_ref, values_ref, slope_ref, gain_ref, result_ref,
    grads_ref, outputs_ref, gain_slope_ref,
):
    swapped, first = flags_ref[0], flags_ref[1]
    slopes, gain_slope = norm_backward(values_ref[...], gain_ref[...], slope_ref[...])
    slopes += hidden_slope_ref[...]
    low = slopes.astype(jnp.bfloat16).astype(jnp.float32)
    slopes = jnp.where(first == 1, slopes, low)
    gain_slope_ref[...] = gain_slope.reshape(1, MODEL)
    for slot in range(SLOTS):
        place = jnp.where(swapped == 1, 1 - slot, slot)
        rows = slice(slot * LOCAL, (slot + 1) * LOCAL)
        for shard in range(SHARDS):
            into = slice(shard * ROWS, (shard + 1) * ROWS)
            have = slice(shard * PADDED, shard * PADDED + ROWS)
            grads_ref[place, :, into] = slopes[rows, have]
            outputs_ref[slot, :, into] = result_ref[rows, have]


def finish(flags, hidden_slope, values, slope, gain, result):
    return pl.pallas_call(
        finish_kernel,
        name="finish",
        out_shape=[
            jax.ShapeDtypeStruct((SLOTS, LOCAL, D), jnp.float32),
            jax.ShapeDtypeStruct((SLOTS, LOCAL, D), jnp.bfloat16),
            jax.ShapeDtypeStruct((1, MODEL), jnp.float32),
        ],
        in_specs=[pl.BlockSpec(memory_space=pltpu.SMEM)] + [VMEM] * 5,
        out_specs=[VMEM] * 3,
        compiler_params=pltpu.CompilerParams(vmem_limit_bytes=40 * 2**20),
    )(flags, hidden_slope, values, slope, gain, result)


def rotary_tables(positions):
    half = HEAD_WIDTH // 2
    frequency = BASE ** (-(jnp.arange(half).astype(jnp.float32) * (2.0 / HEAD_WIDTH)))
    angle = positions.astype(jnp.float32)[..., None] * frequency
    cosine, sine = jnp.cos(angle), jnp.sin(angle)
    one, zero = jnp.ones_like(cosine), jnp.zeros_like(sine)
    return jnp.stack(
        [
            jnp.concatenate(parts, -1)
            for parts in (
                [cosine] * 4,
                [sine] * 4,
                [cosine, cosine, one, one],
                [sine, sine, zero, zero],
            )
        ]
    )


def widened(values):
    lead = values.shape[:-1]
    split = values[..., QUERY_WIDTH:].reshape(lead + (2, KEY_VALUE_HEADS, HEAD_WIDTH))
    return jnp.concatenate(
        [
            values[..., :QUERY_WIDTH],
            jnp.zeros(lead + (FULL - QUERY_WIDTH,), values.dtype),
            jnp.swapaxes(split, -2, -3).reshape(lead + (2 * KEY_WIDTH,)),
        ],
        -1,
    )


def narrowed(values):
    lead = values.shape[:-1]
    split = values[..., FULL:].reshape(lead + (KEY_VALUE_HEADS, 2, HEAD_WIDTH))
    return jnp.concatenate(
        [values[..., :QUERY_WIDTH], jnp.swapaxes(split, -2, -3).reshape(lead + (2 * KEY_WIDTH,))],
        -1,
    )


def mean(values):
    return jnp.sum(values, -1, keepdims=True) * (1.0 / D)


def normed(values, gain):
    return values * lax.rsqrt(mean(values * values) + EPSILON) * gain


def norm_backward(values, gain, upstream):
    row_scale = lax.rsqrt(mean(values * values) + EPSILON)
    unit = values * row_scale
    gain_slope = jnp.sum(upstream * unit, 0)
    inner = upstream * gain
    return (row_scale * (inner - unit * mean(inner * unit)), gain_slope)


def padded(values):
    split = values.reshape(values.shape[:-1] + (SHARDS, ROWS))
    widths = ((0, 0),) * (split.ndim - 1) + ((0, PADDED - ROWS),)
    return jnp.pad(split, widths).reshape(values.shape[:-1] + (MODEL,))


def unpadded(values):
    split = values.reshape(values.shape[:-1] + (SHARDS, PADDED))
    return split[..., :ROWS].reshape(values.shape[:-1] + (D,))


def forward_layer(layer_in, tables, weights, shards=()):
    attend_in, attend_out, gate_up, down_weight, gains = weights
    rows = ROWS_HERE
    values = layer_in.reshape(rows, MODEL).astype(jnp.float32)
    first_norm = normed(values, gains[0]).astype(jnp.bfloat16)
    mixed, *attended = attend(first_norm, attend_in, tables, shards)
    if shards:
        *attended, gate_up, down_weight = attended
        gate_up = gate_up.reshape(-1, 2 * FF)
        down_weight = down_weight.reshape(-1, MODEL)
    hidden = values + jnp.dot(mixed, attend_out, preferred_element_type=jnp.float32)
    second_norm = normed(hidden, gains[1]).astype(jnp.bfloat16)
    gated = jnp.dot(second_norm, gate_up, preferred_element_type=jnp.float32)
    act = (jax.nn.silu(gated[:, :FF]) * gated[:, FF:]).astype(jnp.bfloat16)
    result = hidden + jnp.dot(act, down_weight, preferred_element_type=jnp.float32)
    kept = (
        values,
        first_norm,
        attended,
        mixed,
        hidden,
        second_norm,
        gated,
        act,
    )
    weights = (attend_in, attend_out, gate_up, down_weight, gains)
    return (result.astype(jnp.bfloat16).reshape(layer_in.shape), kept, weights)


def backward_layer(upstream, kept, tables, weights, ending=None):
    last = ending is not None
    attend_in, attend_out, gate_up, down_weight, gains = weights
    (
        values,
        first_norm,
        attended,
        mixed,
        hidden,
        second_norm,
        gated,
        act,
    ) = kept
    batches, local_count = upstream.shape[:2]
    rows = batches * local_count
    down_in = upstream.reshape(rows, MODEL)
    upstream = down_in.astype(jnp.float32)
    gated_slope, second_slope = feed_back(down_in, down_weight, gate_up, gated)
    hidden_part, second_gain = norm_backward(hidden, gains[1], second_slope)
    hidden_slope = upstream + hidden_part
    branch_slope = hidden_slope.astype(jnp.bfloat16)
    mixed_gradient = jnp.einsum(
        "td,qd->tq", branch_slope, attend_out, preferred_element_type=jnp.float32
    ).astype(jnp.bfloat16)
    lefts, rights = (), ()
    if last:
        lefts = (second_norm, by_shard(act))
        rights = (gated_slope, down_in)
    projected_slope, first_slope, *summed = attend_back(
        mixed_gradient,
        attended,
        attend_in,
        tables,
        lefts,
        rights,
    )
    if not last:
        input_part, _ = norm_backward(values, gains[0], first_slope)
        return (hidden_slope + input_part).reshape(batches, local_count, MODEL)
    flags, result = ending
    input_grads, outputs, first_gain = finish(
        flags, hidden_slope, values, first_slope, gains[:1], result.reshape(rows, MODEL)
    )
    gain_slopes = jnp.stack([first_gain[0], second_gain])
    lefts = (by_core(first_norm), by_core(mixed))
    rights = (projected_slope, branch_slope)
    summed = (*reduce_gradients(lefts, rights, spare_rows(gain_slopes)), *summed)
    return (input_grads, outputs, summed)


def passed_along(value, steps):
    return lax.ppermute(value, "section", [(0, 1)] if steps > 0 else [(1, 0)])


def with_other_core(value):
    size = lax.axis_size("dp")
    other = lax.ppermute(value, "dp", [(index, index ^ 1) for index in range(size)])
    return other


def by_shard(values):
    return values.reshape(ROWS_HERE, SHARDS, -1).swapaxes(0, 1)


def by_core(values):
    return values.reshape(ROWS_HERE, SHARDS, 2, -1).transpose(2, 1, 0, 3)


def spare_rows(gain_slopes):
    core = lax.axis_index("dp") % 2
    gains = (gain_slopes + with_other_core(gain_slopes)).reshape(2, SHARDS, PADDED).swapaxes(0, 1)
    gains = jnp.where(core == 1, gains, 0.0).astype(jnp.bfloat16)
    return jnp.pad(gains, ((0, 0), (8, 6), (0, 0)))


def body(
    inputs, positions, plan, attend_in, attend_out, gate_up, down_weight, norm_gains, cotangent
):
    section_index = lax.axis_index("section")
    extra = PADDED - ROWS
    in_shard = jnp.concatenate(
        [
            widened(attend_in[0]),
            jnp.pad(norm_gains[0], ((0, extra - 2), (0, WIDE - ROWS))),
        ],
        0,
    )
    gathered = gather_weights((in_shard, jnp.pad(padded(attend_out[0]), ((0, extra), (0, 0)))))
    gains = gathered[0][:, ROWS : ROWS + 2, :PADDED].swapaxes(0, 1).reshape(2, MODEL)
    weights = (
        gathered[0].reshape(-1, WIDE),
        gathered[1].reshape(-1, MODEL),
        None,
        None,
        gains.astype(jnp.float32),
    )
    shards = (
        jnp.pad(gate_up[0], ((0, extra), (0, 0))),
        padded(down_weight[0]),
    )
    plan_row = plan[0]
    swap = plan_row[0] == 1

    def in_slots(values):
        return jnp.where(swap, values[::-1, 0], values[:, 0])

    fresh = padded(in_slots(inputs))
    tables = rotary_tables(in_slots(positions))
    given = padded(cotangent[:, 0])
    result, _, weights = forward_layer(fresh, tables, weights, shards)
    layer_in = jnp.where(section_index == 0, fresh, passed_along(result, 1))
    outputs, kept, _ = forward_layer(layer_in, tables, weights)
    input_slope = backward_layer(given, kept, tables, weights)
    back = passed_along(input_slope.astype(jnp.bfloat16), -1)
    upstream = jnp.where(section_index == 1, given, back)
    flags = jnp.stack([swap, section_index == 0]).astype(jnp.int32)
    input_slopes, outputs, summed = backward_layer(
        upstream, kept, tables, weights, (flags, outputs)
    )
    full = [value.astype(jnp.float32) for value in summed]
    return (
        outputs[None, :, None],
        input_slopes[None, :, None],
        narrowed(full[0])[None, :ROWS],
        unpadded(full[1][:ROWS])[None],
        full[2][None, :ROWS],
        unpadded(full[3])[None],
        full[0][None, ROWS : ROWS + 2, :ROWS],
    )


def solution(mesh):
    in_specs = (
        P(None, "dp", "fsdp", None),
        P(None, "dp", "fsdp"),
        P("dp", None),
        P("section", "fsdp", None),
        P("section", "fsdp", None),
        P("section", "fsdp", None),
        P("section", "fsdp", None),
        P("section", None, "fsdp"),
        P(None, "dp", "fsdp", None),
    )
    out_specs = (
        P("section", None, "dp", "fsdp", None),
        P("section", None, "dp", "fsdp", None),
        P("section", "fsdp", None),
        P("section", "fsdp", None),
        P("section", "fsdp", None),
        P("section", "fsdp", None),
        P("section", None, "fsdp"),
    )
    return jax.shard_map(body, mesh=mesh, in_specs=in_specs, out_specs=out_specs, check_vma=False)
```
